32 devices in a mesh: seq: 4 (over z), dp: 8 (over y, x, core).
Axes of the slice: x: 2, y: 2, z: 4, core: 2. Of those that a mesh axis runs over, the one named last changes fastest.
Arguments:
- tokens: bfloat16 [8, 3072, 512], P('dp', 'seq'), may hold values from -6 to 6
- cotangent: bfloat16 [8, 3072, 512], P('dp', 'seq'), may hold values from -6 to 6
- first_length: int32 [8], P('dp'), may hold values from 384 to 2688, as said below
- ln1_gain: bfloat16 [512], P(('seq', 'dp')), may hold values from 0.099609375 to 1.8984375
- ln2_gain: bfloat16 [512], P(('seq', 'dp')), may hold values from 0.099609375 to 1.8984375
- ln3_gain: bfloat16 [2048], P(('seq', 'dp')), may hold values from 0.099609375 to 1.8984375
- ln4_gain: bfloat16 [512], P(('seq', 'dp')), may hold values from 0.099609375 to 1.8984375
- ln5_gain: bfloat16 [512], P(('seq', 'dp')), may hold values from 0.099609375 to 1.8984375
- glu_weight: bfloat16 [512, 1024], P(('seq', 'dp')), may hold values from -0.25 to 0.25
- wide_weight: bfloat16 [512, 2048], P(('seq', 'dp')), may hold values from -0.25 to 0.25
- narrow_weight: bfloat16 [1536, 256], P(('seq', 'dp')), may hold values from -0.15625 to 0.15625
- depth_weight: bfloat16 [18432], P(('seq', 'dp')), may hold values from -2 to 2
- point_weight: bfloat16 [2048, 256], P(('seq', 'dp')), may hold values from -0.125 to 0.125
- qkv_weight: bfloat16 [512, 1536], P(('seq', 'dp')), may hold values from -0.25 to 0.25
- attn_weight: bfloat16 [512, 512], P(('seq', 'dp')), may hold values from -6 to 6
- up_weight: bfloat16 [512, 2048], P(('seq', 'dp')), may hold values from -0.25 to 0.25
- down_weight: bfloat16 [2048, 512], P(('seq', 'dp')), may hold values from -0.125 to 0.125
Outputs:
- mixed: bfloat16 [8, 3072, 512], P('dp', 'seq')
- tokens_grad: float32 [8, 3072, 512], P('dp', 'seq')
- ln1_grad: float32 [512], P(('seq', 'dp'))
- ln2_grad: float32 [512], P(('seq', 'dp'))
- ln3_grad: float32 [2048], P(('seq', 'dp'))
- ln4_grad: float32 [512], P(('seq', 'dp'))
- ln5_grad: float32 [512], P(('seq', 'dp'))
- glu_grad: float32 [512, 1024], P(('seq', 'dp'))
- wide_grad: float32 [512, 2048], P(('seq', 'dp'))
- narrow_grad: float32 [1536, 256], P(('seq', 'dp'))
- depth_grad: float32 [18432], P(('seq', 'dp'))
- point_grad: float32 [2048, 256], P(('seq', 'dp'))
- qkv_grad: float32 [512, 1536], P(('seq', 'dp'))
- attn_grad: float32 [512, 512], P(('seq', 'dp'))
- up_grad: float32 [512, 2048], P(('seq', 'dp'))
- down_grad: float32 [2048, 512], P(('seq', 'dp'))
The draws below stay inside these ranges and needn't reach their ends.
Inputs may be any that keep to these rules, and one draw needn't show every extreme that they name: A group's first sequence has first_length tokens and its second the remaining 3072 minus first_length; the shorter of the two has half of 768 to 767 tokens.
All inputs are finite; a program needn't handle non-finite values.
Results may differ from the reference program's by a relative error of at most 0.017.
Values may be sent and summed in bfloat16 or wider, within the bound.
No kernel may reach another device: no remote copies, remote signals or barrier semaphores. Data moves between devices by JAX's collectives and lax.ppermute only.
A program may use at most 256 MiB of HBM per device.

```python
import jax
import jax.numpy as jnp
from jax import lax

D = 512
HEADS = 8
FF = 2048
KERNEL = 9
TOK_DEV = 768
HEAD = 64
NARROW = 256
GROUP = 3072
N_DP = 8


def draw_first_length(key, part):
    short_key, order_key = jax.random.split(jax.random.fold_in(key, 7))
    short_len = jax.random.randint(short_key, (N_DP,), TOK_DEV // 2, TOK_DEV, dtype=jnp.int32)
    order_bits = jax.random.randint(order_key, (N_DP,), 0, 2, dtype=jnp.int32)
    first_len = jnp.where(order_bits == 1, GROUP - short_len, short_len)
    first_len = first_len.at[0].set(TOK_DEV // 2)
    first_len = first_len.at[1].set(GROUP - TOK_DEV // 2)
    return first_len.astype(jnp.int32)


def block_scale(rng, dims, cuts, least, largest):
    def one(dim, blocks):
        steps = jax.random.uniform(jax.random.fold_in(jax.random.fold_in(rng, 6), dim), (blocks,), jnp.float32, least / len(cuts), largest / len(cuts))
        return jnp.repeat(jnp.exp(steps), dims[dim] // blocks).reshape((-1,) + (1,) * (len(dims) - dim - 1))

    level = one(*cuts[0])
    for cut in cuts[1:]:
        level = level * one(*cut)
    return level


def normal_values(key, shape, scale, limit, shards=(), kind=jnp.bfloat16):
    level = block_scale(key, shape, shards, -0.22, 0.18) if shards else 1.0
    values = jax.random.normal(key, shape, jnp.float32) * scale * level
    return jnp.minimum(jnp.maximum(values, -limit), limit).astype(kind)


def setup_inputs(seed: int = 0) -> dict:
    seeds = jax.random.split(jax.random.key(seed), 18)
    return {
        "tokens": normal_values(seeds[0], (N_DP, GROUP, D), 1.0, 6.0, ((0, 8), (1, 4))),
        "cotangent": normal_values(seeds[1], (N_DP, GROUP, D), 1.0, 6.0, ((0, 8), (1, 4))),
        "first_length": draw_first_length(jax.random.fold_in(seeds[17], 71), 0),
        "ln1_gain": jnp.clip(1.0 + 0.18 * jax.random.normal(seeds[3], (D,), jnp.float32), 0.099609375, 1.8984375).astype(jnp.bfloat16),
        "ln2_gain": jnp.clip(1.0 + 0.18 * jax.random.normal(seeds[4], (D,), jnp.float32), 0.099609375, 1.8984375).astype(jnp.bfloat16),
        "ln3_gain": jnp.clip(1.0 + 0.18 * jax.random.normal(seeds[5], (FF,), jnp.float32), 0.099609375, 1.8984375).astype(jnp.bfloat16),
        "ln4_gain": jnp.clip(1.0 + 0.18 * jax.random.normal(seeds[6], (D,), jnp.float32), 0.099609375, 1.8984375).astype(jnp.bfloat16),
        "ln5_gain": jnp.clip(1.0 + 0.18 * jax.random.normal(seeds[7], (D,), jnp.float32), 0.099609375, 1.8984375).astype(jnp.bfloat16),
        "glu_weight": normal_values(seeds[8], (D, 2 * D), D ** -0.5, 0.25, ((0, 32),)),
        "wide_weight": normal_values(seeds[9], (D, FF), D ** -0.5, 0.25, ((0, 32),)),
        "narrow_weight": normal_values(seeds[10], (3 * D, NARROW), (3 * D) ** -0.5, 0.15625, ((0, 32),)),
        "depth_weight": normal_values(seeds[11], (KERNEL * FF,), KERNEL ** -0.5, 2.0, ((0, 32),)),
        "point_weight": normal_values(seeds[12], (FF, NARROW), FF ** -0.5, 0.125, ((0, 32),)),
        "qkv_weight": normal_values(seeds[13], (D, 3 * D), D ** -0.5, 0.25, ((0, 32),)),
        "attn_weight": normal_values(seeds[14], (D, D), (max(1, 4 * D // GROUP)) ** -0.5, 6.0, ((0, 32),)),
        "up_weight": normal_values(seeds[15], (D, FF), D ** -0.5, 0.25, ((0, 32),)),
        "down_weight": normal_values(seeds[16], (FF, D), FF ** -0.5, 0.125, ((0, 32),)),
    }


@jax.custom_vjp
def low(v):
    return lax.optimization_barrier(v.astype(jnp.bfloat16)).astype(jnp.float32)

@jax.custom_vjp
def low_back(v):
    return v

def low_keep(v):
    return (low(v), None)

def low_pass(kept, grad):
    return (grad,)

def back_keep(v):
    return (v, None)

def back_low(kept, grad):
    return (low(grad),)
low.defvjp(low_keep, low_pass)
low_back.defvjp(back_keep, back_low)

def product(left, right):
    return jnp.dot(left, right, precision=lax.Precision.HIGHEST)

def norm_rows(values, gain):
    row_mean = lax.optimization_barrier(jnp.mean(values, axis=-1, keepdims=True))
    centred = values - row_mean
    spread = lax.optimization_barrier(jnp.mean(centred * centred, axis=-1, keepdims=True))
    return centred * lax.rsqrt(spread + 1e-05) * gain

def from_padded(padded, ids_pad, width, offset):
    count = padded.shape[0] - 2 * width
    moved = padded[width + offset:width + offset + count]
    own_ids = ids_pad[width:width + count]
    there_ids = ids_pad[width + offset:width + offset + count]
    return jnp.where((there_ids == own_ids)[:, None], moved, 0.0)

def first_part(inputs, params):
    normed = low(norm_rows(inputs, params[0]))
    joined = low_back(product(normed, params[5]))
    hidden1 = inputs + joined[:, :D] * jax.nn.sigmoid(joined[:, D:])
    return (hidden1, low(norm_rows(hidden1, params[1])))

def second_part(padded, ids_pad, params):
    normed = padded[1:-1]
    left = jax.nn.gelu(low_back(product(normed, params[6])))
    stacked = jnp.concatenate([from_padded(padded, ids_pad, 1, -1), normed, from_padded(padded, ids_pad, 1, 1)], axis=1)
    right = jax.nn.gelu(low_back(product(stacked, params[7])))
    joined = left + jnp.pad(right, ((0, 0), (0, FF - NARROW)))
    return low(norm_rows(joined, params[2]))

def third_part(hidden1, padded, ids_pad, params):
    half = KERNEL // 2
    taps = params[8].reshape(KERNEL, FF)
    spread = from_padded(padded, ids_pad, half, -half) * taps[0]
    for offset in range(1, KERNEL):
        spread = spread + from_padded(padded, ids_pad, half, offset - half) * taps[offset]
    branch = low_back(product(low(spread), params[9]))
    hidden2 = hidden1 + jnp.pad(branch, ((0, 0), (0, D - NARROW)))
    qkv = low(low_back(product(low(norm_rows(hidden2, params[3])), params[10])))
    return (hidden2, qkv)

def fourth_part(hidden2, attended, params):
    hidden3 = hidden2 + low_back(product(low(low_back(attended)), params[11]))
    inner = low(jax.nn.gelu(low_back(product(low(norm_rows(hidden3, params[4])), params[12]))))
    return hidden3 + low_back(product(inner, params[13]))

def attend_block(query, keys, values, query_ids, key_ids):
    scores = jnp.einsum('qhd,khd->hqk', query, keys, precision=lax.Precision.HIGHEST)
    scores = low_back(scores * HEAD ** (-0.5))
    same = (query_ids[:, None] == key_ids[None, :])[None]
    probs = low(jax.nn.softmax(jnp.where(same, scores, -1e+30), axis=-1))
    return jnp.einsum('hqk,khd->qhd', probs, values, precision=lax.Precision.HIGHEST)

def attention(qkv, ids):
    total_rows = qkv.shape[0]
    heads_view = qkv.reshape(total_rows, 3, HEADS, HEAD)
    query = heads_view[:, 0]
    keys = heads_view[:, 1]
    values = heads_view[:, 2]
    block = 512 if total_rows % 512 == 0 else total_rows
    count = total_rows // block
    checked = jax.checkpoint(attend_block)

    def one_block(item):
        return checked(item[0], keys, values, item[1], ids)
    result = lax.map(one_block, (query.reshape(count, block, HEADS, HEAD), ids.reshape(count, block)))
    return result.reshape(total_rows, D)

def pad_rows(values, ids, width):
    padded = jnp.pad(values, ((width, width), (0, 0)))
    ids_pad = jnp.pad(ids, (width, width), constant_values=-1)
    return (padded, ids_pad)

def cell_forward(inputs, params, first_len):
    total_rows = inputs.shape[0]
    ids = (jnp.arange(total_rows) >= first_len).astype(jnp.int32)
    hidden1, normed2 = first_part(inputs, params)
    padded, ids_pad = pad_rows(normed2, ids, 1)
    middle = second_part(padded, ids_pad, params)
    padded, ids_pad = pad_rows(middle, ids, KERNEL // 2)
    hidden2, qkv = third_part(hidden1, padded, ids_pad, params)
    attended = attention(qkv, ids)
    return fourth_part(hidden2, attended, params)

def reference(tokens, cotangent, first_length, ln1_gain, ln2_gain, ln3_gain, ln4_gain, ln5_gain, glu_weight, wide_weight, narrow_weight, depth_weight, point_weight, qkv_weight, attn_weight, up_weight, down_weight):
    params = tuple((weight.astype(jnp.float32) for weight in (ln1_gain, ln2_gain, ln3_gain, ln4_gain, ln5_gain, glu_weight, wide_weight, narrow_weight, depth_weight, point_weight, qkv_weight, attn_weight, up_weight, down_weight)))

    def group_step(totals, item):
        group_tokens, group_cot, group_first = item

        def cell(inputs, weights):
            return cell_forward(inputs, weights, group_first)
        output, pullback = jax.vjp(cell, group_tokens.astype(jnp.float32), params)
        input_grad, weight_grads = pullback(group_cot.astype(jnp.float32))
        totals = tuple((total + extra for total, extra in zip(totals, weight_grads)))
        return (totals, (output.astype(jnp.bfloat16), input_grad))
    zeros = tuple((jnp.zeros_like(weight) for weight in params))
    totals, (mixed, input_grad) = lax.scan(group_step, zeros, (tokens, cotangent, first_length))
    return (mixed, input_grad, totals[0], totals[1], totals[2], totals[3], totals[4], totals[5], totals[6], totals[7], totals[8], totals[9], totals[10], totals[11], totals[12], totals[13])
```

```python
import jax
import jax.numpy as jnp
from jax import lax
from jax.sharding import PartitionSpec as P

D = 512
HEADS = 8
FF = 2048
KERNEL = 9
HEAD = 64
NARROW = 256


PACK = 256


def pack_block(block):
    rows, columns = block.shape
    return block.reshape(rows, columns // PACK, PACK).transpose(1, 0, 2).reshape(-1, PACK)


def pack_small(blocks):
    flat = jnp.concatenate(blocks, axis=-1)
    rows = -(-flat.shape[-1] // (16 * PACK)) * 16
    pad = [(0, 0)] * (flat.ndim - 1) + [(0, rows * PACK - flat.shape[-1])]
    return jnp.pad(flat, pad).reshape(flat.shape[:-1] + (rows, PACK))


def gather_all(weights):
    small = [w for w in weights if w.ndim == 1]
    packed = [pack_block(w) for w in weights if w.ndim == 2] + [pack_small(small)]
    local = jnp.concatenate(packed, axis=0)
    whole = lax.all_gather(local, ("seq", "dp"), axis=0, tiled=False)
    count = whole.shape[0]
    tail = whole[:, -packed[-1].shape[0] :].reshape(count, -1)
    result, start, place = [], 0, 0
    for w in weights:
        if w.ndim == 1:
            result.append(tail[:, place : place + w.shape[0]].reshape(-1))
            place += w.shape[0]
        else:
            rows, columns = w.shape
            chunks = columns // PACK
            part = whole[:, start : start + rows * chunks].reshape(count, chunks, rows, PACK)
            result.append(part.transpose(0, 2, 1, 3).reshape(count * rows, columns))
            start += rows * chunks
    return result


def scatter_all(grads, weights):
    count = lax.axis_size("seq") * lax.axis_size("dp")
    packed, small = [], []
    for grad, w in zip(grads, weights):
        if w.ndim == 1:
            small.append(grad.reshape(count, -1))
        else:
            rows, columns = w.shape
            chunks = columns // PACK
            part = grad.astype(jnp.bfloat16).reshape(count, rows, chunks, PACK)
            packed.append(part.transpose(0, 2, 1, 3).reshape(count, rows * chunks, PACK))
    packed.append(pack_small(small).astype(jnp.bfloat16))
    send = jnp.concatenate(packed, axis=1)
    total = lax.psum_scatter(send, ("seq", "dp"), scatter_dimension=0, tiled=False)
    total = total.astype(jnp.float32)
    tail = total[-packed[-1].shape[1] :].reshape(-1)
    result, start, place = [], 0, 0
    for w in weights:
        if w.ndim == 1:
            result.append(tail[place : place + w.shape[0]])
            place += w.shape[0]
        else:
            rows, columns = w.shape
            chunks = columns // PACK
            part = total[start : start + rows * chunks].reshape(chunks, rows, PACK)
            result.append(part.transpose(1, 0, 2).reshape(rows, columns))
            start += rows * chunks
    return result


def with_halo(block, sides, width):
    for axis, dim in sides:
        count = lax.axis_size(axis)
        forward = [(i, i + 1) for i in range(count - 1)]
        backward = [(target, source) for source, target in forward]
        low = lax.ppermute(
            lax.slice_in_dim(block, block.shape[dim] - width, None, axis=dim), axis, forward
        )
        high = lax.ppermute(lax.slice_in_dim(block, 0, width, axis=dim), axis, backward)
        block = jnp.concatenate([low, block, high], axis=dim)
    return block


def for_sending(value):
    return jax.tree.map(lambda a: a.astype(jnp.bfloat16) if a.dtype == jnp.float32 else a, value)


def value_rounding(v):
    return lax.optimization_barrier(v.astype(jnp.bfloat16)).astype(jnp.float32)


def value_passing(v):
    return v


def make_rounders():
    rounding = jax.custom_vjp(value_rounding)
    back_rounder = jax.custom_vjp(value_passing)

    def rounding_keep(v):
        return (rounding(v), None)

    def rounding_pass(kept, grad):
        return (grad,)

    def back_keep(v):
        return (v, None)

    def back_apply(kept, grad):
        return (rounding(grad),)

    rounding.defvjp(rounding_keep, rounding_pass)
    back_rounder.defvjp(back_keep, back_apply)
    return (rounding, back_rounder)


def low(v):
    return make_rounders()[0](v)


def low_back(v):
    return make_rounders()[1](v)


def product(left, right):
    return jnp.dot(left, right, preferred_element_type=jnp.float32)


def norm_rows(values, gain):
    row_mean = jnp.mean(values, axis=-1, keepdims=True)
    centred = values - row_mean
    spread = jnp.mean(centred * centred, axis=-1, keepdims=True)
    return centred * lax.rsqrt(spread + 1e-05) * gain


def from_padded(padded, ids_pad, width, offset):
    count = padded.shape[0] - 2 * width
    moved = padded[width + offset : width + offset + count]
    own_ids = ids_pad[width : width + count]
    there_ids = ids_pad[width + offset : width + offset + count]
    return jnp.where((there_ids == own_ids)[:, None], moved, 0.0)


def first_part(inputs, params):
    normed = low(norm_rows(inputs, params[0]))
    joined = low_back(product(normed, params[5]))
    hidden1 = inputs + joined[:, :D] * jax.nn.sigmoid(joined[:, D:])
    return (hidden1, low(norm_rows(hidden1, params[1])))


def second_part(padded, ids_pad, params):
    normed = padded[1:-1]
    left = jax.nn.gelu(low_back(product(normed, params[6])))
    stacked = jnp.concatenate(
        [from_padded(padded, ids_pad, 1, -1), normed, from_padded(padded, ids_pad, 1, 1)], axis=1
    )
    right = jax.nn.gelu(low_back(product(stacked, params[7])))
    joined = left + jnp.pad(right, ((0, 0), (0, FF - NARROW)))
    return low(norm_rows(joined, params[2]))


def third_part(hidden1, padded, ids_pad, params):
    half = KERNEL // 2
    taps = params[8].reshape(KERNEL, FF)
    spread = from_padded(padded, ids_pad, half, -half) * taps[0]
    for offset in range(1, KERNEL):
        spread = spread + from_padded(padded, ids_pad, half, offset - half) * taps[offset]
    branch = low_back(product(low(spread), params[9]))
    hidden2 = hidden1 + jnp.pad(branch, ((0, 0), (0, D - NARROW)))
    qkv = low(low_back(product(low(norm_rows(hidden2, params[3])), params[10])))
    return (hidden2, qkv)


def fourth_part(hidden2, attended, params):
    hidden3 = hidden2 + low_back(product(low(low_back(attended)), params[11]))
    inner = low(jax.nn.gelu(low_back(product(low(norm_rows(hidden3, params[4])), params[12]))))
    return hidden3 + low_back(product(inner, params[13]))


def padded_ids(first_len, width, local_rows):
    places = lax.axis_index("seq") * local_rows + jnp.arange(-width, local_rows + width)
    group_rows = local_rows * lax.axis_size("seq")
    inside = (places >= 0) & (places < group_rows)
    return jnp.where(inside, (places >= first_len).astype(jnp.int32), -1)


def fold_rims(grad_pad, arrived, width):
    core = grad_pad[width:-width]
    upper = core[:width] + arrived[:width]
    lower = core[-width:] + arrived[3 * width :]
    return jnp.concatenate([upper, core[width:-width], lower])


def scores_of(query, keys, query_ids, key_ids):
    scores = jnp.einsum("qhd,khd->hqk", query, keys, preferred_element_type=jnp.float32) * HEAD ** (
        -0.5
    )
    same = (query_ids[:, None] == key_ids[None, :])[None]
    return (scores, same)


def key_blocks_of(keys, values, key_ids):
    total_rows = keys.shape[0]
    block = 512 if total_rows % 512 == 0 else total_rows
    count = total_rows // block
    return (
        keys.reshape(count, block, HEADS, HEAD),
        values.reshape(count, block, HEADS, HEAD),
        key_ids.reshape(count, block),
    )


def attend_forward(query, keys, values, query_ids, key_ids):
    blocks = key_blocks_of(keys, values, key_ids)
    start = jnp.full((HEADS, query.shape[0]), -1e30, jnp.float32)

    def peak_step(carry, item):
        peak, total = carry
        scores, same = scores_of(query, item[0], query_ids, item[2])
        new_peak = jnp.maximum(peak, jnp.max(jnp.where(same, scores, -1e30), axis=-1))
        weights = jnp.where(same, jnp.exp(scores - new_peak[..., None]), 0.0)
        return ((new_peak, total * jnp.exp(peak - new_peak) + jnp.sum(weights, axis=-1)), None)

    (peak, total), unused = lax.scan(peak_step, (start, jnp.zeros_like(start)), blocks)
    log_total = peak + jnp.log(total)

    def value_step(acc, item):
        scores, same = scores_of(query, item[0], query_ids, item[2])
        probs = jnp.where(same, jnp.exp(scores - log_total[..., None]), 0.0).astype(jnp.bfloat16)
        return (
            acc + jnp.einsum("hqk,khd->qhd", probs, item[1], preferred_element_type=jnp.float32),
            None,
        )

    attended, unused = lax.scan(value_step, jnp.zeros(query.shape, jnp.float32), blocks)
    return (attended.reshape(query.shape[0], D), log_total)


def probs_and_grads(query, key_block, value_block, query_ids, key_ids, log_total, grad_out):
    scores, same = scores_of(query, key_block, query_ids, key_ids)
    probs = jnp.where(same, jnp.exp(scores - log_total[..., None]), 0.0)
    grad_probs = jnp.einsum(
        "qhd,khd->hqk", grad_out, value_block, preferred_element_type=jnp.float32
    )
    return (probs, grad_probs)


def inner_of(query, blocks, query_ids, log_total, grad_out):

    def inner_step(acc, item):
        probs, grad_probs = probs_and_grads(
            query, item[0], item[1], query_ids, item[2], log_total, grad_out
        )
        return (acc + jnp.sum(probs * grad_probs, axis=-1), None)

    inner_sum, unused = lax.scan(
        inner_step, jnp.zeros((HEADS, query.shape[0]), jnp.float32), blocks
    )
    return inner_sum


def attend_backward(query, keys, values, query_ids, key_ids, log_total, grad_out):
    blocks = key_blocks_of(keys, values, key_ids)
    scale = HEAD ** (-0.5)
    inner_sum = inner_of(query, blocks, query_ids, log_total, grad_out)

    def grad_step(acc, item):
        probs, grad_probs = probs_and_grads(
            query, item[0], item[1], query_ids, item[2], log_total, grad_out
        )
        grad_scores = (probs * (grad_probs - inner_sum[..., None])).astype(jnp.bfloat16)
        acc = acc + scale * jnp.einsum(
            "hqk,khd->qhd", grad_scores, item[0], preferred_element_type=jnp.float32
        )
        key_grad = scale * jnp.einsum(
            "hqk,qhd->khd", grad_scores, query, preferred_element_type=jnp.float32
        )
        value_grad = jnp.einsum(
            "hqk,qhd->khd", probs.astype(jnp.bfloat16), grad_out, preferred_element_type=jnp.float32
        )
        block_rows = item[0].shape[0]
        return (
            acc,
            jnp.concatenate(
                [key_grad.reshape(block_rows, D), value_grad.reshape(block_rows, D)], axis=1
            ),
        )

    query_grad, pieces = lax.scan(grad_step, jnp.zeros(query.shape, jnp.float32), blocks)
    return (query_grad.reshape(query.shape[0], D), pieces.reshape(keys.shape[0], 2 * D))


def on_device(
    tokens,
    cotangent,
    first_length,
    ln1_gain,
    ln2_gain,
    ln3_gain,
    ln4_gain,
    ln5_gain,
    glu_weight,
    wide_weight,
    narrow_weight,
    depth_weight,
    point_weight,
    qkv_weight,
    attn_weight,
    up_weight,
    down_weight,
):
    inputs = tokens[0].astype(jnp.float32)
    local_rows = inputs.shape[0]
    first_len = first_length[0]
    half = KERNEL // 2
    narrow_ids = padded_ids(first_len, 1, local_rows)
    wide_ids = padded_ids(first_len, half, local_rows)
    own_ids = narrow_ids[1:-1]
    group_rows = local_rows * lax.axis_size("seq")
    key_ids = (jnp.arange(group_rows) >= first_len).astype(jnp.int32)
    weights = (
        ln1_gain,
        ln2_gain,
        ln3_gain,
        ln4_gain,
        ln5_gain,
        glu_weight,
        wide_weight,
        narrow_weight,
        depth_weight,
        point_weight,
        qkv_weight,
        attn_weight,
        up_weight,
        down_weight,
    )
    gathered = gather_all(weights)
    params = tuple((weight.astype(jnp.float32) for weight in gathered))
    hidden1, normed2 = first_part(inputs, params)
    narrow_pad = with_halo(normed2.astype(jnp.bfloat16), (("seq", 0),), 1).astype(jnp.float32)
    middle = second_part(narrow_pad, narrow_ids, params)
    wide_pad = with_halo(middle.astype(jnp.bfloat16), (("seq", 0),), half).astype(jnp.float32)
    hidden2, qkv = third_part(hidden1, wide_pad, wide_ids, params)
    qkv_low = qkv.astype(jnp.bfloat16)
    query = qkv_low[:, :D].reshape(local_rows, HEADS, HEAD)
    keys_all, values_all = (
        lax.all_gather(qkv_low[:, D : 2 * D], "seq", axis=0, tiled=True),
        lax.all_gather(qkv_low[:, 2 * D :], "seq", axis=0, tiled=True),
    )
    attended, log_total = attend_forward(
        query,
        keys_all.reshape(group_rows, HEADS, HEAD),
        values_all.reshape(group_rows, HEADS, HEAD),
        own_ids,
        key_ids,
    )
    output = fourth_part(hidden2, attended, params)
    cot_out = cotangent[0].astype(jnp.float32)
    unused, pull_fourth = jax.vjp(fourth_part, hidden2, attended, params)
    grad_hidden2, grad_attended, grads_fourth = pull_fourth(cot_out)
    grad_low = grad_attended.astype(jnp.bfloat16)
    query_grad, key_terms = attend_backward(
        query,
        keys_all.reshape(group_rows, HEADS, HEAD),
        values_all.reshape(group_rows, HEADS, HEAD),
        own_ids,
        key_ids,
        log_total,
        grad_low.reshape(local_rows, HEADS, HEAD),
    )
    key_grads = lax.psum_scatter(
        key_terms.astype(jnp.bfloat16), "seq", scatter_dimension=0, tiled=True
    ).astype(jnp.float32)
    unused, pull_third = jax.vjp(
        lambda first, padded, weights: third_part(first, padded, wide_ids, weights),
        hidden1,
        wide_pad,
        params,
    )
    grad_hidden1, grad_wide_pad, grads_third = pull_third(
        (grad_hidden2, jnp.concatenate([query_grad, key_grads], axis=1))
    )
    rim_rows = jnp.concatenate([grad_wide_pad[:half], grad_wide_pad[-half:]])
    arrived = with_halo(for_sending(rim_rows), (("seq", 0),), half).astype(rim_rows.dtype)
    grad_middle = fold_rims(grad_wide_pad, arrived, half)
    unused, pull_second = jax.vjp(
        lambda padded, weights: second_part(padded, narrow_ids, weights), narrow_pad, params
    )
    grad_narrow_pad, grads_second = pull_second(grad_middle)
    rim_rows = jnp.concatenate([grad_narrow_pad[:1], grad_narrow_pad[-1:]])
    arrived = with_halo(rim_rows, (("seq", 0),), 1)
    grad_normed2 = fold_rims(grad_narrow_pad, arrived, 1)
    unused, pull_first = jax.vjp(first_part, inputs, params)
    grad_inputs, grads_first = pull_first((grad_hidden1, grad_normed2))
    totals = jax.tree.map(
        lambda a, b, c, e: a + b + c + e, grads_first, grads_second, grads_third, grads_fourth
    )
    summed = scatter_all(totals, weights)
    return (
        output.astype(jnp.bfloat16)[None],
        grad_inputs[None],
        summed[0],
        summed[1],
        summed[2],
        summed[3],
        summed[4],
        summed[5],
        summed[6],
        summed[7],
        summed[8],
        summed[9],
        summed[10],
        summed[11],
        summed[12],
        summed[13],
    )


def solution(mesh):
    in_specs = (
        P("dp", "seq", None),
        P("dp", "seq", None),
        P("dp"),
        P(("seq", "dp")),
        P(("seq", "dp")),
        P(("seq", "dp")),
        P(("seq", "dp")),
        P(("seq", "dp")),
        P(("seq", "dp"), None),
        P(("seq", "dp"), None),
        P(("seq", "dp"), None),
        P(("seq", "dp")),
        P(("seq", "dp"), None),
        P(("seq", "dp"), None),
        P(("seq", "dp"), None),
        P(("seq", "dp"), None),
        P(("seq", "dp"), None),
    )
    out_specs = (
        P("dp", "seq", None),
        P("dp", "seq", None),
        P(("seq", "dp")),
        P(("seq", "dp")),
        P(("seq", "dp")),
        P(("seq", "dp")),
        P(("seq", "dp")),
        P(("seq", "dp"), None),
        P(("seq", "dp"), None),
        P(("seq", "dp"), None),
        P(("seq", "dp")),
        P(("seq", "dp"), None),
        P(("seq", "dp"), None),
        P(("seq", "dp"), None),
        P(("seq", "dp"), None),
        P(("seq", "dp"), None),
    )
    return jax.shard_map(
        on_device, mesh=mesh, in_specs=in_specs, out_specs=out_specs, check_vma=False
    )
```

```python
import functools
import math

import jax
import jax.numpy as jnp
import numpy as np
from jax import lax
from jax.experimental import pallas as pl
from jax.experimental.pallas import tpu as pltpu
from jax.sharding import PartitionSpec as P

D = 512
HEADS = 8
FF = 2048
KERNEL = 9
HEAD = 64
NARROW = 256
HALF = KERNEL // 2
LANES = 128
PACK = 256
RIM = 16
BLOCKS = 32
F32 = jnp.float32
BF = jnp.bfloat16
LOG2E = math.log2(math.e)
BIG = -1e30
AXES = ("seq", "dp")
VMEM = 58 << 20


def nt(a, b):
    return lax.dot_general(a, b, (((1,), (1,)), ((), ())), preferred_element_type=F32)


def nn(a, b):
    return lax.dot_general(a, b, (((1,), (0,)), ((), ())), preferred_element_type=F32)


def tn(a, b):
    return lax.dot_general(a, b, (((0,), (0,)), ((), ())), preferred_element_type=F32)


def whole_call(kernel, outs, args, scratch=(), scalars=1, flops=0):
    vm = pl.BlockSpec(memory_space=pltpu.VMEM)
    sm = pl.BlockSpec(memory_space=pltpu.SMEM)
    outs = [jax.ShapeDtypeStruct(shape, dtype) for shape, dtype in outs]
    moved = sum(math.prod(a.shape) * a.dtype.itemsize for a in list(args) + outs)
    return pl.pallas_call(
        kernel,
        out_shape=outs,
        in_specs=[sm] * scalars + [vm] * (len(args) - scalars),
        out_specs=[vm] * len(outs),
        scratch_shapes=[pltpu.VMEM(shape, dtype) for shape, dtype in scratch],
        compiler_params=pltpu.CompilerParams(vmem_limit_bytes=VMEM),
        cost_estimate=pl.CostEstimate(flops=flops, bytes_accessed=moved, transcendentals=0),
    )(*args)


def normalise(v):
    mean = jnp.mean(v, axis=1, keepdims=True)
    c = v - mean
    r = lax.rsqrt(jnp.mean(c * c, axis=1, keepdims=True) + 1e-05)
    return c * r, r


def norm_back(grad, hat, r, gain):
    g = grad * gain
    a = jnp.mean(g, axis=1, keepdims=True)
    b = jnp.mean(g * hat, axis=1, keepdims=True)
    return r * (g - a - hat * b)


C0 = math.sqrt(2.0 / math.pi)
C1 = 0.044715


def gelu(x):
    return 0.5 * x * (1.0 + jnp.tanh(x * (C0 + C0 * C1 * (x * x))))


def gelu_and_slope(x):
    xx = x * x
    t = jnp.tanh(x * (C0 + C0 * C1 * xx))
    half = 0.5 * (1.0 + t)
    return x * half, half + (0.5 * x) * (1.0 - t * t) * (C0 + 3.0 * C0 * C1 * xx)


def sigmoid(x):
    return 0.5 * jnp.tanh(0.5 * x) + 0.5


def fold8(v):
    return jnp.sum(v.reshape(v.shape[0] // 8, 8, v.shape[1]), axis=0)


def rows_at(i, tile, start=0):
    return pl.ds(pl.multiple_of(start + i * tile, 16), tile)


def places(base, rows, lanes=LANES):
    return base + lax.broadcasted_iota(jnp.int32, (rows, lanes), 0)


def blocks_of(value):
    return value.astype(BF).reshape(BLOCKS, value.shape[0] // BLOCKS, value.shape[1])


def front1_kernel(tile, x_ref, g1, glu, g2, h1_ref, y2_ref, joined_ref):
    def step(i, carry):
        at = rows_at(i, tile)
        x = x_ref[at, :].astype(F32)
        hat, _ = normalise(x)
        joined = nn((hat * g1[...]).astype(BF), glu[...])
        joined_ref[at, :] = joined
        h1 = x + joined[:, :D] * sigmoid(joined[:, D:])
        h1_ref[at, :] = h1
        hat2, _ = normalise(h1)
        y2_ref[at, :] = (hat2 * g2[...]).astype(BF)
        return carry

    lax.fori_loop(0, x_ref.shape[0] // tile, step, 0)


def front1(x, g1, glu, g2):
    rows = x.shape[0]
    return whole_call(
        functools.partial(front1_kernel, 160),
        [((rows, D), F32), ((rows, D), BF), ((rows, 2 * D), F32)],
        [x, g1, glu, g2],
        scalars=0,
        flops=4 * rows * D * D,
    )


def front2_kernel(tile, group, scal, y2_ref, wide, narrow, g3, left_ref, right_ref, mid_ref, u_ref):
    rows = y2_ref.shape[0]
    base = scal[0] * (rows - 2 * RIM) - RIM
    first = scal[1]
    u_ref[0:RIM, :] = jnp.zeros((RIM, 3 * NARROW), F32)
    u_ref[RIM + rows : 2 * RIM + rows, :] = jnp.zeros((RIM, 3 * NARROW), F32)

    def narrow_step(i, carry):
        y = y2_ref[rows_at(i, tile), :]
        for k in range(3):
            u_ref[rows_at(i, tile, RIM), k * NARROW : (k + 1) * NARROW] = nn(
                y, narrow[k * D : (k + 1) * D, :]
            )
        return carry

    lax.fori_loop(0, rows // tile, narrow_step, 0)

    def step(i, carry):
        at = rows_at(i, tile)
        around = pl.ds(pl.multiple_of(i * tile, 16), tile + 2 * RIM)
        left = nn(y2_ref[at, :], wide[...])
        left_ref[at, :] = left
        pos = places(base + i * tile, tile, NARROW)
        before = pltpu.roll(u_ref[around, 0:NARROW], 1, 0)[RIM : RIM + tile]
        after = pltpu.roll(u_ref[around, 2 * NARROW :], tile + 2 * RIM - 1, 0)[RIM : RIM + tile]
        right = u_ref[rows_at(i, tile, RIM), NARROW : 2 * NARROW]
        right = right + jnp.where((pos == first) | (pos == 0), 0.0, before)
        right = right + jnp.where((pos + 1 == first) | (pos + 1 == group), 0.0, after)
        right_ref[at, :] = right
        left = gelu(left)
        joined = jnp.concatenate([left[:, :NARROW] + gelu(right), left[:, NARROW:]], axis=1)
        hat, _ = normalise(joined)
        row = base + i * tile + lax.broadcasted_iota(jnp.int32, (tile, 1), 0)
        inside = ((row >= 0) & (row < group)).astype(F32)
        mid_ref[at, :] = (hat * inside * g3[...]).astype(BF)
        return carry

    lax.fori_loop(0, rows // tile, step, 0)


def front2(scal, y2, wide, narrow, g3, group):
    rows = y2.shape[0]
    return whole_call(
        functools.partial(front2_kernel, 160, group),
        [((rows, FF), F32), ((rows, NARROW), F32), ((rows, FF), BF)],
        [scal, y2, wide, narrow, g3],
        scratch=[((rows + 2 * RIM, 3 * NARROW), F32)],
        flops=2 * rows * D * (FF + 3 * NARROW),
    )


def crosses(pos, offset, first):
    if offset > 0:
        return (pos < first) & (pos + offset >= first)
    return (pos >= first) & (pos + offset < first)


def conv(win, tile, taps, lanes, pos, first, masked, sign):
    total = None
    for k in range(KERNEL):
        o = sign * (k - HALF)
        v = win[RIM + o : RIM + o + tile, :]
        if masked and o != 0:
            v = jnp.where(crosses(pos, o, first), 0.0, v)
        v = v * taps[k : k + 1, lanes]
        total = v if total is None else total + v
    return total


def front3_kernel(tile, n, share, scal, mid_ref, taps, point, h1_ref, g4, qkv_w, *refs):
    spread_ref, h2_ref, y4_ref = refs[:3]
    outs = refs[3 : 3 + n]
    win, qkv_s = refs[3 + n :]
    rows = h2_ref.shape[0]
    s, first = scal[0], scal[1]
    base = s * rows

    def step(i, carry):
        at = rows_at(i, tile)
        begin = base + i * tile
        near = (first > begin - HALF) & (first < begin + tile + HALF)

        def chunk(c, carry2):
            lanes = pl.ds(pl.multiple_of(c * LANES, LANES), LANES)
            around = pl.ds(pl.multiple_of(i * tile, 16), tile + 2 * RIM)
            win[...] = mid_ref[around, lanes].astype(F32)
            pos = places(begin, tile)
            for masked in (False, True):

                @pl.when(near if masked else jnp.logical_not(near))
                def _():
                    spread_ref[at, lanes] = conv(
                        win, tile, taps, lanes, pos, first, masked, 1
                    ).astype(BF)

            return carry2

        lax.fori_loop(0, FF // LANES, chunk, 0)
        h1 = h1_ref[rows_at(i, tile, RIM), :]
        branch = nn(spread_ref[at, :], point[...])
        h2 = jnp.concatenate([h1[:, :NARROW] + branch, h1[:, NARROW:]], axis=1)
        h2_ref[at, :] = h2
        hat, _ = normalise(h2)
        y4 = (hat * g4[...]).astype(BF)
        y4_ref[at, :] = y4
        qkv_s[...] = nn(y4, qkv_w[...]).astype(BF)
        for k in range(n):
            block = (s ^ k) // share
            for part in range(3):
                outs[k][at, part * LANES : (part + 1) * LANES] = qkv_s[
                    :, pl.ds(pl.multiple_of(part * D + block * LANES, LANES), LANES)
                ]
        return carry

    lax.fori_loop(0, rows // tile, step, 0)


def front3(scal, mid, taps, point, h1, g4, qkv_w, n, share):
    rows = mid.shape[0] - 2 * RIM
    tile = 128
    return whole_call(
        functools.partial(front3_kernel, tile, n, share),
        [((rows, FF), BF), ((rows, D), F32), ((rows, D), BF)] + [((rows, 3 * LANES), BF)] * n,
        [scal, mid, taps, point, h1, g4, qkv_w],
        scratch=[((tile + 2 * RIM, LANES), F32), ((tile, 3 * D), BF)],
        flops=2 * rows * (FF * NARROW + 3 * D * D),
    )


def middle_kernel(tile, n, share, scal, h2_ref, *refs):
    att = refs[:n]
    cot_ref, g5, wa, wup, wdown, mixed_ref, dh3_ref = refs[n : n + 7]
    datt = refs[n + 7 : 2 * n + 7]
    ga_ref, gup_ref, gdown_ref, ln_ref = refs[2 * n + 7 : 2 * n + 11]
    att_s, y5_s, inner_s, du_s, db_s = refs[2 * n + 11 :]
    rows = h2_ref.shape[0]
    s = scal[0]
    for k in range(n):
        block = (s ^ k) // share
        lanes = pl.ds(pl.multiple_of(block * LANES, LANES), LANES)
        if share == 1:
            att_s[:, lanes] = att[k][...]
        else:
            seen = (s ^ k) % share
            before = att_s[:, lanes].astype(F32)
            lane = lax.broadcasted_iota(jnp.int32, (rows, LANES), 1)
            mine = lane // (LANES // share) == seen
            att_s[:, lanes] = jnp.where(mine, att[k][...].astype(F32), before).astype(BF)
    ln_ref[...] = jnp.zeros_like(ln_ref)

    def step(i, carry):
        at = rows_at(i, tile)
        h3 = h2_ref[at, :] + nn(att_s[at, :], wa[...])
        hat, r = normalise(h3)
        y5 = (hat * g5[...]).astype(BF)
        y5_s[at, :] = y5
        value, slope = gelu_and_slope(nn(y5, wup[...]))
        inner = value.astype(BF)
        inner_s[at, :] = inner
        mixed_ref[at, :] = (h3 + nn(inner, wdown[...])).astype(BF)
        cot = cot_ref[at, :]
        du = (nt(cot, wdown[...]) * slope).astype(BF)
        du_s[at, :] = du
        dy5 = nt(du, wup[...])
        ln_ref[...] += fold8(dy5 * hat)
        dh3 = cot.astype(F32) + norm_back(dy5, hat, r, g5[...])
        dh3_ref[at, :] = dh3
        db = dh3.astype(BF)
        db_s[at, :] = db
        da = nt(db, wa[...]).astype(BF)
        for j in range(D // LANES):
            for k in range(n):

                @pl.when((s ^ k) // share == j)
                def _():
                    datt[k][at, :] = da[:, j * LANES : (j + 1) * LANES]

        return carry

    lax.fori_loop(0, rows // tile, step, 0)
    att_t = att_s[...].T
    for j in range(D // PACK):
        ga_ref[:, j * 16 : (j + 1) * 16, :] = blocks_of(
            nn(att_t, db_s[:, j * PACK : (j + 1) * PACK])
        )
    y5_t = y5_s[...].T
    for j in range(FF // PACK):
        cols = slice(j * PACK, (j + 1) * PACK)
        gup_ref[:, j * 16 : (j + 1) * 16, :] = blocks_of(nn(y5_t, du_s[:, cols]))
        down = tn(inner_s[:, cols], cot_ref[...]).astype(BF)
        for m in range(D // PACK):
            gdown_ref[j * 4 : (j + 1) * 4, m * 64 : (m + 1) * 64, :] = down[
                :, m * PACK : (m + 1) * PACK
            ].reshape(4, 64, PACK)


def middle(scal, h2, att, cot, g5, wa, wup, wdown, n, share):
    rows = h2.shape[0]
    return whole_call(
        functools.partial(middle_kernel, 128, n, share),
        [((rows, D), BF), ((rows, D), F32)]
        + [((rows, LANES), BF)] * n
        + [((BLOCKS, 32, PACK), BF), ((BLOCKS, 128, PACK), BF), ((BLOCKS, 128, PACK), BF)]
        + [((8, D), F32)],
        [scal, h2, *att, cot, g5, wa, wup, wdown],
        scratch=[
            ((rows, D), BF),
            ((rows, D), BF),
            ((rows, FF), BF),
            ((rows, FF), BF),
            ((rows, D), BF),
        ],
        flops=6 * rows * (2 * D * FF + D * D),
    )


def back3_kernel(tile, n, share, scal, *refs):
    blocks = refs[:n]
    dh3_ref, h2_ref, y4_ref, spread_ref, g4, qkv_w = refs[n : n + 6]
    dh2_ref, db_ref, gqkv_ref, gpoint_ref, ln_ref = refs[n + 6 : n + 11]
    (dqkv_s,) = refs[n + 11 :]
    rows = h2_ref.shape[0]
    s = scal[0]
    for k in range(n):
        block = (s ^ k) // share
        for part in range(3):
            lanes = pl.ds(pl.multiple_of(part * D + block * LANES, LANES), LANES)
            new = blocks[k][:, part * LANES : (part + 1) * LANES]
            if share > 1:
                lane = lax.broadcasted_iota(jnp.int32, (rows, LANES), 1)
                mine = lane // (LANES // share) == (s ^ k) % share
                new = jnp.where(mine, new.astype(F32), dqkv_s[:, lanes].astype(F32)).astype(BF)
            dqkv_s[:, lanes] = new
    ln_ref[...] = jnp.zeros_like(ln_ref)

    def step(i, carry):
        at = rows_at(i, tile)
        dy4 = nt(dqkv_s[at, :], qkv_w[...])
        hat, r = normalise(h2_ref[at, :])
        ln_ref[...] += fold8(dy4 * hat)
        dh2 = dh3_ref[at, :] + norm_back(dy4, hat, r, g4[...])
        dh2_ref[at, :] = dh2
        db_ref[at, :] = dh2[:, :NARROW].astype(BF)
        return carry

    lax.fori_loop(0, rows // tile, step, 0)
    y4_t = y4_ref[...].T
    for j in range(3 * D // PACK):
        gqkv_ref[:, j * 16 : (j + 1) * 16, :] = blocks_of(
            nn(y4_t, dqkv_s[:, j * PACK : (j + 1) * PACK])
        )
    for j in range(FF // PACK):
        gpoint_ref[j * PACK : (j + 1) * PACK, :] = tn(
            spread_ref[:, j * PACK : (j + 1) * PACK], db_ref[...]
        ).astype(BF)


def back3(scal, blocks, dh3, h2, y4, spread, g4, qkv_w, n, share):
    rows = h2.shape[0]
    return whole_call(
        functools.partial(back3_kernel, 128, n, share),
        [((rows, D), F32), ((rows, NARROW), BF), ((BLOCKS, 96, PACK), BF)]
        + [((FF, PACK), BF), ((8, D), F32)],
        [scal, *blocks, dh3, h2, y4, spread, g4, qkv_w],
        scratch=[((rows, 3 * D), BF)],
        flops=4 * rows * D * 3 * D + 2 * rows * FF * NARROW,
    )


def back2_kernel(tile, group, scal, low_ref, db_ref, high_ref, *refs):
    point, taps, mid_ref, left_ref, right_ref, wide, narrow, y2_ref, g3 = refs[:9]
    dy2_ref, gwide_ref, gnarrow_ref, gdepth_ref, ln_ref = refs[9:14]
    dbx, dsp, win, dmid, dl, dr, st = refs[14:]
    rows = db_ref.shape[0]
    ext = rows + 2 * RIM
    base = scal[0] * rows - RIM
    first = scal[1]
    dbx[0:RIM, :] = low_ref[...]
    dbx[RIM : RIM + rows, :] = db_ref[...]
    dbx[RIM + rows :, :] = high_ref[...]
    dsp[0:RIM, :] = jnp.zeros((RIM, FF), F32)
    dsp[RIM + ext :, :] = jnp.zeros((RIM, FF), F32)
    dr[0:RIM, :] = jnp.zeros((RIM, NARROW), F32)
    dr[RIM + ext :, :] = jnp.zeros((RIM, NARROW), F32)
    gdepth_ref[...] = jnp.zeros_like(gdepth_ref)
    ln_ref[...] = jnp.zeros_like(ln_ref)

    def spread_step(i, carry):
        dsp[rows_at(i, tile, RIM), :] = nt(dbx[rows_at(i, tile), :], point[...])
        return carry

    lax.fori_loop(0, ext // tile, spread_step, 0)

    def step(i, carry):
        at = rows_at(i, tile)
        begin = base + i * tile
        near = (first > begin - HALF) & (first < begin + tile + HALF)
        near = near | (i == 0) | (i == ext // tile - 1)

        def chunk(c, carry2):
            lanes = pl.ds(pl.multiple_of(c * LANES, LANES), LANES)
            around = pl.ds(pl.multiple_of(i * tile, 16), tile + 2 * RIM)
            win[...] = dsp[around, lanes]
            local = i * tile + lax.broadcasted_iota(jnp.int32, (tile, LANES), 0)
            mid = mid_ref[at, lanes].astype(F32)
            pos = places(begin, tile)
            for masked in (False, True):

                @pl.when(near if masked else jnp.logical_not(near))
                def _():
                    total = None
                    for k in range(KERNEL):
                        o = HALF - k
                        v = win[RIM + o : RIM + o + tile, :]
                        if masked and o != 0:
                            v = jnp.where(crosses(pos, o, first), 0.0, v)
                        counted = v
                        if masked:
                            kept = (local + o >= RIM) & (local + o < RIM + rows)
                            counted = jnp.where(kept, v, 0.0)
                        gdepth_ref[k * 8 : (k + 1) * 8, lanes] += fold8(counted * mid)
                        v = v * taps[k : k + 1, lanes]
                        total = v if total is None else total + v
                    dmid[:, lanes] = total

            return carry2

        lax.fori_loop(0, FF // LANES, chunk, 0)
        left, slope = gelu_and_slope(left_ref[at, :])
        right, slope_r = gelu_and_slope(right_ref[at, :])
        joined = jnp.concatenate([left[:, :NARROW] + right, left[:, NARROW:]], axis=1)
        hat, r = normalise(joined)
        local = i * tile + lax.broadcasted_iota(jnp.int32, (tile, 1), 0)
        own = ((local >= RIM) & (local < RIM + rows)).astype(F32)
        pos = base + local
        grad = dmid[...] * ((pos >= 0) & (pos < group)).astype(F32)
        ln_ref[...] += fold8(grad * hat * own)
        dj = norm_back(grad, hat, r, g3[...])
        dl[at, :] = (dj * slope).astype(BF)
        dr[rows_at(i, tile, RIM), :] = (dj[:, :NARROW] * slope_r).astype(BF).astype(F32)
        return carry

    lax.fori_loop(0, ext // tile, step, 0)
    part = 128

    def gather_step(i, carry):
        at = rows_at(i, part)
        around = pl.ds(pl.multiple_of(RIM + i * part, 16), part + 2 * RIM)
        pos = places(base + RIM + i * part, part, NARROW)
        v = dr[around, :]
        after = pltpu.roll(v, part + 2 * RIM - 1, 0)[RIM : RIM + part]
        before = pltpu.roll(v, 1, 0)[RIM : RIM + part]
        after = jnp.where((pos + 1 == first) | (pos + 1 == group), 0.0, after).astype(BF)
        before = jnp.where((pos == first) | (pos == 0), 0.0, before).astype(BF)
        here = v[RIM : RIM + part].astype(BF)
        st[at, 0:NARROW] = after
        st[at, NARROW : 2 * NARROW] = here
        st[at, 2 * NARROW :] = before
        dy2 = nt(dl[rows_at(i, part, RIM), :], wide[...])
        for k, v in enumerate((after, here, before)):
            dy2 = dy2 + nt(v, narrow[k * D : (k + 1) * D, :])
        dy2_ref[at, :] = dy2
        return carry

    lax.fori_loop(0, rows // part, gather_step, 0)
    y2_t = y2_ref[RIM : RIM + rows, :].T
    for j in range(FF // PACK):
        gwide_ref[:, j * 16 : (j + 1) * 16, :] = blocks_of(
            nn(y2_t, dl[RIM : RIM + rows, j * PACK : (j + 1) * PACK])
        )
    for k in range(3):
        gnarrow_ref[k * D : (k + 1) * D, :] = nn(
            y2_t, st[:, k * NARROW : (k + 1) * NARROW]
        ).astype(BF)


def back2(scal, low, db, high, point, taps, mid, left, right, wide, narrow, y2, g3, group):
    rows = db.shape[0]
    ext = rows + 2 * RIM
    tile = 160
    return whole_call(
        functools.partial(back2_kernel, tile, group),
        [((rows, D), F32), ((BLOCKS, 128, PACK), BF), ((3 * D, NARROW), BF)]
        + [((8 * KERNEL, FF), F32), ((8, FF), F32)],
        [scal, low, db, high, point, taps, mid, left, right, wide, narrow, y2, g3],
        scratch=[
            ((ext, NARROW), BF),
            ((ext + 2 * RIM, FF), F32),
            ((tile + 2 * RIM, LANES), F32),
            ((tile, FF), F32),
            ((ext, FF), BF),
            ((ext + 2 * RIM, NARROW), F32),
            ((rows, 3 * NARROW), BF),
        ],
        flops=2 * rows * (FF * NARROW + 2 * FF * D + 6 * D * NARROW),
    )


def back1_kernel(tile, dy2_ref, dh2_ref, h1_ref, joined_ref, x_ref, g1, g2, glu, *refs):
    dx_ref, gglu_ref, ln1_ref, ln2_ref, y1_s, dj_s = refs
    rows = dy2_ref.shape[0]
    ln1_ref[...] = jnp.zeros_like(ln1_ref)
    ln2_ref[...] = jnp.zeros_like(ln2_ref)

    def step(i, carry):
        at = rows_at(i, tile)
        ext = rows_at(i, tile, RIM)
        hat2, r2 = normalise(h1_ref[ext, :])
        dy2 = dy2_ref[at, :]
        ln2_ref[...] += fold8(dy2 * hat2)
        dh1 = dh2_ref[at, :] + norm_back(dy2, hat2, r2, g2[...])
        gate = sigmoid(joined_ref[ext, D:])
        value = joined_ref[ext, :D]
        da = (dh1 * gate).astype(BF)
        db = (dh1 * value * gate * (1.0 - gate)).astype(BF)
        dj_s[at, :D] = da
        dj_s[at, D:] = db
        x = x_ref[ext, :].astype(F32)
        hat1, r1 = normalise(x)
        y1_s[at, :] = (hat1 * g1[...]).astype(BF)
        dy1 = nt(dj_s[at, :], glu[...])
        ln1_ref[...] += fold8(dy1 * hat1)
        dx_ref[at, :] = (dh1 + norm_back(dy1, hat1, r1, g1[...])).astype(dx_ref.dtype)
        return carry

    lax.fori_loop(0, rows // tile, step, 0)
    y1_t = y1_s[...].T
    for j in range(2 * D // PACK):
        gglu_ref[:, j * 16 : (j + 1) * 16, :] = blocks_of(
            nn(y1_t, dj_s[:, j * PACK : (j + 1) * PACK])
        )


def back1(dy2, dh2, h1, joined, x, g1, g2, glu):
    rows = dy2.shape[0]
    return whole_call(
        functools.partial(back1_kernel, 128),
        [((rows, D), BF), ((BLOCKS, 64, PACK), BF), ((8, D), F32), ((8, D), F32)],
        [dy2, dh2, h1, joined, x, g1, g2, glu],
        scratch=[((rows, D), BF), ((rows, 2 * D), BF)],
        scalars=0,
        flops=8 * rows * D * D,
    )


def lane_maps(rows, head):
    lane = lax.broadcasted_iota(jnp.int32,(rows,LANES),1)
    own = (lane >= head*HEAD) & (lane < (head+1)*HEAD)
    rel = lane - (1-head)*HEAD
    return own, rel

def id_column(base, rows, first):
    pos = base + lax.broadcasted_iota(jnp.int32,(rows,LANES),0)
    return pos >= first

def split3(v):
    hi = v.astype(BF).astype(F32)
    mid = (v-hi).astype(BF).astype(F32)
    return hi, mid, v-hi-mid

def tile_ids(start, rows, first):
    return start < first, start+rows > first

def overlap(a_start,a_rows,b_start,b_rows,first):
    a0,a1 = tile_ids(a_start,a_rows,first); b0,b1=tile_ids(b_start,b_rows,first)
    return (a0&b0)|(a1&b1)

def attend_kernel(n, heads, share, tq, tk, scal, *refs):
    qkv = refs[:n]; att = refs[n:2*n]; lse_ref = refs[2*n]
    qa, ka, va, mx_ref, m_ref, q2_ref, acc_ref = refs[2*n+1:]
    s = scal[0]; first = scal[1]
    rows = qkv[0].shape[0]
    for k in range(n):
        base = (s ^ k)*rows
        id1 = id_column(base, rows, first).astype(F32)
        q = qkv[k][:, 0:LANES].astype(F32)*(HEAD**-0.5)
        key = qkv[k][:, LANES:2*LANES].astype(F32)
        v = qkv[k][:, 2*LANES:3*LANES].astype(F32)
        for i in range(heads):
            h = i if share==1 else s % share
            own, rel = lane_maps(rows, h)
            qx = jnp.where(rel==0, 1.0-id1, jnp.where(rel==1, id1, 0.0))
            kx = jnp.where(rel==0, id1*BIG, jnp.where(rel==1, (1.0-id1)*BIG, jnp.where(rel<5,1.0,0.0)))
            qa[i, k*rows:(k+1)*rows,:] = jnp.where(own, q, qx).astype(BF)
            ka[i, k*rows:(k+1)*rows,:] = jnp.where(own, key, kx).astype(BF)
            va[i, k*rows:(k+1)*rows,:] = jnp.where(own, v, 1.0).astype(BF)
    per = rows//tq; per_k = rows//tk
    def fold(sc, best):
        for j in range(tk//LANES):
            best = jnp.maximum(best, sc[:, j*LANES:(j+1)*LANES])
        return best
    def q_step(it, carry):
        kq = it//per
        r0 = pl.multiple_of((it % per)*tq, tq)
        g0 = pl.multiple_of(it*tq, tq)
        own0 = pl.multiple_of((g0//tk)*tk, tk)
        q_start = (s ^ kq)*rows + r0
        for i in range(heads):
            for j in range(max(1,tq//tk)):
                sc = nt(qa[i, pl.ds(g0,tq),:], ka[i, pl.ds(own0+j*tk,tk),:])
                best = fold(sc, sc[:, :LANES] if j==0 else best)
            mx_ref[i] = best
            m_ref[i] = jnp.zeros((tq,LANES),F32)
        def attempt(again):
            for i in range(heads):
                h = i if share==1 else s % share
                own, rel = lane_maps(tq, h)
                m = jnp.max(mx_ref[i], axis=1, keepdims=True)
                mb = m_ref[i] + jnp.broadcast_to(m, (tq,LANES))
                m_ref[i] = mb
                hi,mid,lo = split3(-mb)
                q = qa[i, pl.ds(g0,tq),:].astype(F32)
                q2_ref[i] = jnp.where(rel==2,hi,jnp.where(rel==3,mid,jnp.where(rel==4,lo,q))).astype(BF)
            mx_ref[...] = jnp.full_like(mx_ref, -3e38)
            acc_ref[...] = jnp.zeros_like(acc_ref)
            for kt in range(n*per_k):
                k_start = (s ^ (kt//per_k))*rows + (kt%per_k)*tk
                @pl.when(overlap(q_start,tq,k_start,tk,first))
                def _():
                    for i in range(heads):
                        sc = nt(q2_ref[i], ka[i, kt*tk:(kt+1)*tk,:])
                        mx_ref[i] = fold(sc, mx_ref[i])
                        p = jnp.exp2(sc*LOG2E).astype(BF)
                        acc_ref[i] += nn(p, va[i, kt*tk:(kt+1)*tk,:])
            return (jnp.max(mx_ref[...]) > 40.0).astype(jnp.int32)
        lax.while_loop(lambda again: again > 0, attempt, jnp.int32(1))
        out = jnp.zeros((tq,LANES),F32); lse = jnp.zeros((tq,LANES),F32)
        for i in range(heads):
            h = i if share==1 else s % share
            own,_ = lane_maps(tq,h)
            acc = acc_ref[i]
            total = pltpu.roll(acc, HEAD, 1)
            out = jnp.where(own, acc/total, out)
            lse = jnp.where(own, m_ref[i]+jnp.log(total), lse)
        lse_ref[pl.ds(g0,tq),:] = lse
        for k in range(n):
            @pl.when(kq==k)
            def _():
                att[k][pl.ds(r0,tq),:] = out.astype(BF)
        return carry
    lax.fori_loop(0, n*per, q_step, 0)

def attend(scal, blocks, n, share, tq=768, tk=384):
    rows = blocks[0].shape[0]
    heads = 2 // share
    return whole_call(
        functools.partial(attend_kernel, n, heads, share, tq, tk),
        [((rows, LANES), BF)] * n + [((n * rows, LANES), F32)],
        [scal, *blocks],
        scratch=[((heads, n * rows, LANES), BF)] * 3
        + [((heads, tq, LANES), F32)] * 2
        + [((heads, tq, LANES), BF), ((heads, tq, LANES), F32)],
        flops=4 * n * rows * n * rows * HEAD * heads,
    )


def attend_back_kernel(n, heads, share, tq, tk, scal, *refs):
    qkv = refs[:n]; att = refs[n:2*n]; dat = refs[2*n:3*n]; lse_ref = refs[3*n]
    out = refs[3*n+1:4*n+1]
    qa, ka, va, da, dq_ref, dk_ref, dv_ref = refs[4*n+1:]
    s = scal[0]; first = scal[1]
    rows = qkv[0].shape[0]
    for k in range(n):
        base = (s ^ k)*rows
        sl = slice(k*rows,(k+1)*rows)
        id1 = id_column(base, rows, first).astype(F32)
        q = qkv[k][:, 0:LANES].astype(F32)*(HEAD**-0.5)
        key = qkv[k][:, LANES:2*LANES].astype(F32)
        v = qkv[k][:, 2*LANES:3*LANES].astype(F32)
        do = dat[k][...].astype(F32)
        prod = do*att[k][...].astype(F32)
        for i in range(heads):
            h = i if share==1 else s % share
            own, rel = lane_maps(rows, h)
            lse = pltpu.roll(lse_ref[sl,:], HEAD, 1)
            hi,mid,lo = split3(-lse)
            delta = jnp.sum(jnp.where(own,prod,0.0),axis=1,keepdims=True)
            dhi,dmid,dlo = split3(-delta)
            qx = jnp.where(rel==0, 1.0-id1, jnp.where(rel==1, id1, jnp.where(rel==2,hi,jnp.where(rel==3,mid,jnp.where(rel==4,lo,0.0)))))
            kx = jnp.where(rel==0, id1*BIG, jnp.where(rel==1, (1.0-id1)*BIG, jnp.where(rel<5,1.0,0.0)))
            vx = jnp.where(rel<3,1.0,0.0)
            dx = jnp.where(rel==0,dhi,jnp.where(rel==1,dmid,jnp.where(rel==2,dlo,0.0)))
            qa[i,sl,:] = jnp.where(own,q,qx).astype(BF)
            ka[i,sl,:] = jnp.where(own,key,kx).astype(BF)
            va[i,sl,:] = jnp.where(own,v,vx).astype(BF)
            da[i,sl,:] = jnp.where(own,do,dx).astype(BF)
    dq_ref[...] = jnp.zeros_like(dq_ref)
    per_q = rows//tq; per_k = rows//tk
    def k_step(kt, carry):
        k0 = pl.multiple_of(kt*tk, tk)
        kk = kt//per_k
        k_start = (s ^ kk)*rows + (kt % per_k)*tk
        for i in range(heads):
            dk_ref[i] = jnp.zeros((tk,LANES),F32)
            dv_ref[i] = jnp.zeros((tk,LANES),F32)
        def q_step(qt, c2):
            q0 = pl.multiple_of(qt*tq, tq)
            q_start = (s ^ (qt//per_q))*rows + (qt % per_q)*tq
            @pl.when(overlap(q_start,tq,k_start,tk,first))
            def _():
                for i in range(heads):
                    qq = qa[i,pl.ds(q0,tq),:]; kx = ka[i,pl.ds(k0,tk),:]; dd = da[i,pl.ds(q0,tq),:]
                    st = nt(kx, qq)
                    p = jnp.exp2(st*LOG2E)
                    dp = nt(va[i,pl.ds(k0,tk),:], dd)
                    ds = (p*dp).astype(BF)
                    dv_ref[i] += nn(p.astype(BF), dd)
                    dk_ref[i] += nn(ds, qq)
                    dq_ref[i,pl.ds(q0,tq),:] += tn(ds, kx)
            return c2
        lax.fori_loop(0, n*per_q, q_step, 0)
        dk = jnp.zeros((tk,LANES),F32); dv = jnp.zeros((tk,LANES),F32)
        for i in range(heads):
            h = i if share==1 else s % share
            own,_ = lane_maps(tk,h)
            dk = jnp.where(own, dk_ref[i], dk); dv = jnp.where(own, dv_ref[i], dv)
        r0 = pl.multiple_of((kt % per_k)*tk, tk)
        for k in range(n):
            @pl.when(kk==k)
            def _():
                out[k][pl.ds(r0,tk),LANES:2*LANES] = dk.astype(BF)
                out[k][pl.ds(r0,tk),2*LANES:3*LANES] = dv.astype(BF)
        return carry
    lax.fori_loop(0, n*per_k, k_step, 0)
    for k in range(n):
        sl = slice(k*rows,(k+1)*rows)
        dq = jnp.zeros((rows,LANES),F32)
        for i in range(heads):
            h = i if share==1 else s % share
            own,_ = lane_maps(rows,h)
            dq = jnp.where(own, dq_ref[i,sl,:], dq)
        out[k][:, 0:LANES] = (dq*(HEAD**-0.5)).astype(BF)

def attend_back(scal, blocks, att, datt, lse, n, share, tq=384, tk=384):
    rows = blocks[0].shape[0]
    heads = 2 // share
    return whole_call(
        functools.partial(attend_back_kernel, n, heads, share, tq, tk),
        [((rows, 3 * LANES), BF)] * n,
        [scal, *blocks, *att, *datt, lse],
        scratch=[((heads, n * rows, LANES), BF)] * 4
        + [((heads, n * rows, LANES), F32)]
        + [((heads, tk, LANES), F32)] * 2,
        flops=10 * n * rows * n * rows * HEAD * heads,
    )


def pack_block(block):
    rows, columns = block.shape
    return block.reshape(rows, columns // PACK, PACK).transpose(1, 0, 2).reshape(-1, PACK)


def pack_small(blocks):
    flat = jnp.concatenate(blocks, axis=-1)
    rows = -(-flat.shape[-1] // (16 * PACK)) * 16
    pad = [(0, 0)] * (flat.ndim - 1) + [(0, rows * PACK - flat.shape[-1])]
    return jnp.pad(flat, pad).reshape(flat.shape[:-1] + (rows, PACK))


def gather_all(weights):
    small = [w for w in weights if w.ndim == 1]
    packed = [pack_block(w) for w in weights if w.ndim == 2] + [pack_small(small)]
    local = jnp.concatenate(packed, axis=0)
    whole = lax.all_gather(local, AXES, axis=0, tiled=False)
    count = whole.shape[0]
    tail = whole[:, -packed[-1].shape[0] :].reshape(count, -1)
    result, start, place = [], 0, 0
    for w in weights:
        if w.ndim == 1:
            result.append(tail[:, place : place + w.shape[0]].reshape(-1))
            place += w.shape[0]
        else:
            rows, columns = w.shape
            chunks = columns // PACK
            part = whole[:, start : start + rows * chunks].reshape(count, chunks, rows, PACK)
            result.append(part.transpose(0, 2, 1, 3).reshape(count * rows, columns))
            start += rows * chunks
    return result


def to_owners(grad, w, count):
    if grad.ndim == 2:
        return grad.reshape(count, -1, PACK)
    finer = count // BLOCKS
    if finer == 1:
        return grad
    rows, columns = w.shape
    part = grad.reshape(BLOCKS, columns // PACK, finer, rows, PACK)
    return part.transpose(0, 2, 1, 3, 4).reshape(count, -1, PACK)


def scatter_all(grads, weights):
    count = lax.axis_size("seq") * lax.axis_size("dp")
    small = [g.reshape(count, -1) for g, w in zip(grads, weights) if w.ndim == 1]
    packed = [to_owners(g, w, count) for g, w in zip(grads, weights) if w.ndim == 2]
    packed.append(pack_small(small).astype(BF))
    send = jnp.concatenate(packed, axis=1)
    total = lax.psum_scatter(send, AXES, scatter_dimension=0, tiled=False).astype(F32)
    tail = total[-packed[-1].shape[1] :].reshape(-1)
    result, start, place = [], 0, 0
    for w in weights:
        if w.ndim == 1:
            result.append(tail[place : place + w.shape[0]])
            place += w.shape[0]
        else:
            rows, columns = w.shape
            chunks = columns // PACK
            part = total[start : start + rows * chunks].reshape(chunks, rows, PACK)
            result.append(part.transpose(1, 0, 2).reshape(rows, columns))
            start += rows * chunks
    return result


class Layout:
    def __init__(self, n_seq, n_dp):
        self.n_seq, self.n_dp = n_seq, n_dp
        self.where = {}
        for g in range(n_dp):
            for s in range(n_seq):
                self.where[g, s] = self.place(g, s)
        self.block = np.zeros(n_seq * n_dp, np.int32)
        for (g, s), device in self.where.items():
            self.block[device] = s

    def place(self, g, s):
        if (self.n_seq, self.n_dp) == (4, 8):
            y, x, c = g >> 2, g >> 1 & 1, g & 1
            return (2 * c + y) * 8 + (s & 1) * 4 + x * 2 + (s >> 1)
        return s * self.n_dp + g

    def pairs(self, source, target):
        return [
            (source(g, s), target(g, s))
            for g in range(self.n_dp)
            for s in range(self.n_seq)
            if target(g, s) is not None and source(g, s) is not None
        ]

    def at(self, g, s):
        return self.where.get((g, s))

    def home(self, g, s):
        return s * self.n_dp + g

    def bring(self, value):
        return lax.ppermute(value, AXES, self.pairs(self.home, self.at))

    def bring_to(self, value, step):
        return lax.ppermute(
            value, AXES, self.pairs(self.home, lambda g, s: self.at(g, s + step))
        )

    def send_home(self, value):
        return lax.ppermute(value, AXES, self.pairs(self.at, self.home))

    def to_neighbour(self, value, step):
        return lax.ppermute(value, AXES, self.pairs(self.at, lambda g, s: self.at(g, s + step)))

    def swap(self, values):
        return [values[0]] + [
            lax.ppermute(values[k], AXES, self.pairs(self.at, lambda g, s: self.at(g, s ^ k)))
            for k in range(1, self.n_seq)
        ]


def on_device(tokens, cotangent, first_length, *weights):
    n = lax.axis_size("seq")
    n_dp = lax.axis_size("dp")
    share = n * LANES // D
    layout = Layout(n, n_dp)
    rows = tokens.shape[1]
    group = n * rows
    me = lax.axis_index("seq") * n_dp + lax.axis_index("dp")
    s = jnp.asarray(layout.block)[me]

    tokens = tokens[0]
    x = layout.bring(tokens)
    low = layout.bring_to(tokens[-RIM:], 1)
    high = layout.bring_to(tokens[:RIM], -1)
    first = layout.bring(first_length)[0]
    scal = jnp.stack([s.astype(jnp.int32), first])
    cot = layout.bring(cotangent[0])
    x_ext = jnp.concatenate([low, x, high], axis=0)

    params = gather_all(weights)
    g1, g2, g3, g4, g5 = (p.astype(F32)[None] for p in params[:5])
    glu, wide, narrow, depth, point, qkv_w, wa, wup, wdown = params[5:]
    taps = depth.reshape(KERNEL, FF).astype(F32)

    h1, y2, joined = front1(x_ext, g1, glu, g2)
    left, right, mid = front2(scal, y2, wide, narrow, g3, group)
    spread, h2, y4, *qkv = front3(scal, mid, taps, point, h1, g4, qkv_w, n, share)
    qkv = layout.swap(qkv)
    *att, lse = attend(scal, qkv, n, share)
    mixed, dh3, *rest = middle(
        scal, h2, layout.swap(att), cot, g5, wa, wup, wdown, n, share
    )
    datt, (ga, gup, gdown, ln5) = rest[:n], rest[n:]
    dqkv = attend_back(scal, qkv, att, layout.swap(datt), lse, n, share)
    dh2, db, gqkv, gpoint, ln4 = back3(
        scal, layout.swap(dqkv), dh3, h2, y4, spread, g4, qkv_w, n, share
    )
    dy2, gwide, gnarrow, gdepth, ln3 = back2(
        scal,
        layout.to_neighbour(db[-RIM:], 1),
        db,
        layout.to_neighbour(db[:RIM], -1),
        point,
        taps,
        mid,
        left,
        right,
        wide,
        narrow,
        y2,
        g3,
        group,
    )
    dx, gglu, ln1, ln2 = back1(dy2, dh2, h1, joined, x_ext, g1, g2, glu)
    ln1, ln2, ln3, ln4, ln5 = (jnp.sum(v, axis=0) for v in (ln1, ln2, ln3, ln4, ln5))
    gdepth = jnp.sum(gdepth.reshape(KERNEL, 8, FF), axis=1).reshape(-1)
    grads = [ln1, ln2, ln3, ln4, ln5, gglu, gwide, gnarrow, gdepth, gpoint, gqkv, ga, gup, gdown]
    summed = scatter_all(grads, weights)
    return (
        layout.send_home(mixed)[None],
        layout.send_home(dx).astype(F32)[None],
        *summed,
    )


def solution(mesh):
    token, owner, rows = P("dp", "seq", None), P(AXES), P(AXES, None)
    params = (owner,) * 5 + (rows,) * 3 + (owner,) + (rows,) * 5
    return jax.shard_map(
        on_device,
        mesh=mesh,
        in_specs=(token, token, P("dp")) + params,
        out_specs=(token, token) + params,
        check_vma=False,
    )
```

```python
import functools
import math

import jax
import jax.numpy as jnp
import numpy as np
from jax import lax
from jax.experimental import pallas as pl
from jax.experimental.pallas import tpu as pltpu
from jax.sharding import PartitionSpec as P

D = 512
HEADS = 8
FF = 2048
KERNEL = 9
HEAD = 64
NARROW = 256
HALF = KERNEL // 2
LANES = 128
PACK = 256
RIM = 16
BLOCKS = 32
F32 = jnp.float32
BF = jnp.bfloat16
LOG2E = math.log2(math.e)
BIG = -1e30
AXES = ("seq", "dp")
VMEM = 58 << 20


def nt(a, b):
    return lax.dot_general(a, b, (((1,), (1,)), ((), ())), preferred_element_type=F32)


def nn(a, b):
    return lax.dot_general(a, b, (((1,), (0,)), ((), ())), preferred_element_type=F32)


def tn(a, b):
    return lax.dot_general(a, b, (((0,), (0,)), ((), ())), preferred_element_type=F32)


def whole_call(kernel, outs, args, scratch=(), scalars=1, micros=0, ties=()):
    if ties:
        inner, fixed, count = kernel, len(args), len(ties)

        def kernel(*refs):
            inner(*refs[:fixed], *refs[fixed + count :])

    vm = pl.BlockSpec(memory_space=pltpu.VMEM)
    sm = pl.BlockSpec(memory_space=pltpu.SMEM)
    outs = [jax.ShapeDtypeStruct(shape, dtype) for shape, dtype in outs]
    moved = sum(math.prod(a.shape) * a.dtype.itemsize for a in list(args) + outs)
    return pl.pallas_call(
        kernel,
        out_shape=outs,
        in_specs=[sm] * scalars + [vm] * (len(args) - scalars)
        + [pl.BlockSpec(memory_space=pl.ANY)] * len(ties),
        out_specs=[vm] * len(outs),
        scratch_shapes=[pltpu.VMEM(shape, dtype) for shape, dtype in scratch],
        compiler_params=pltpu.CompilerParams(vmem_limit_bytes=VMEM),
        cost_estimate=pl.CostEstimate(
            flops=int(micros * 1.15e9), bytes_accessed=moved, transcendentals=0
        ),
    )(*args, *ties)


def normalise(v):
    mean = jnp.mean(v, axis=1, keepdims=True)
    c = v - mean
    r = lax.rsqrt(jnp.mean(c * c, axis=1, keepdims=True) + 1e-05)
    return c * r, r


def norm_back(grad, hat, r, gain):
    g = grad * gain
    a = jnp.mean(g, axis=1, keepdims=True)
    b = jnp.mean(g * hat, axis=1, keepdims=True)
    return r * (g - a - hat * b)


C0 = math.sqrt(2.0 / math.pi)
C1 = 0.044715


def gelu(x):
    return 0.5 * x * (1.0 + jnp.tanh(x * (C0 + C0 * C1 * (x * x))))


def gelu_and_slope(x):
    xx = x * x
    t = jnp.tanh(x * (C0 + C0 * C1 * xx))
    half = 0.5 * (1.0 + t)
    return x * half, half + (0.5 * x) * (1.0 - t * t) * (C0 + 3.0 * C0 * C1 * xx)


def sigmoid(x):
    return 0.5 * jnp.tanh(0.5 * x) + 0.5


def fold8(v):
    return jnp.sum(v.reshape(v.shape[0] // 8, 8, v.shape[1]), axis=0)


def rows_at(i, tile, start=0):
    return pl.ds(pl.multiple_of(start + i * tile, 16), tile)


def places(base, rows, lanes=LANES):
    return base + lax.broadcasted_iota(jnp.int32, (rows, lanes), 0)


ROWS = {"glu": 16, "wide": 16, "narrow": 48, "point": 64, "qkv": 16, "attn": 16, "up": 16, "down": 64, "small": 16}


def columns_of(name, *chunks):
    return [(name, j) for j in chunks]


WIDE, GLU, QKV, UP = (columns_of(n, *range(k)) for n, k in (("wide", 8), ("glu", 4), ("qkv", 6), ("up", 8)))
NARROW_0, POINT_0, SMALL_0 = (columns_of(n, 0) for n in ("narrow", "point", "small"))
ATTN, DOWN = columns_of("attn", 0, 1), columns_of("down", 0, 1)
LAST = (UP + ATTN[:1], ATTN[1:] + DOWN)
GATHERS = ((WIDE + QKV[:5], GLU + NARROW_0 + SMALL_0 + QKV[5:] + POINT_0), LAST)
SUMS = (
    LAST,
    (QKV[:5], QKV[5:] + POINT_0),
    (WIDE[:6], WIDE[6:] + NARROW_0),
    (GLU[:2], GLU[2:] + SMALL_0),
)


def height(items):
    return sum(ROWS[name] for name, _ in items)


def row_of(items, item):
    return height(items[: items.index(item)])


def slot_bits(half, r):
    high, low, z = r >> 3, r >> 2 & 1, r & 3
    x, y = (high, low) if half == 0 else (low, high)
    return z * 8 + y * 4 + x * 2


def slot_of(half, rel):
    z, y, x, c = rel >> 3, rel >> 2 & 1, rel >> 1 & 1, rel & 1
    high, low = (x, y) if half == 0 else (y, x)
    return c * 16 + high * 8 + low * 4 + z


def unpack(me, group, pieces, wanted):
    for half, items in enumerate(GATHERS[group]):
        for core in range(2):
            piece = pieces[half * 2 + core]
            for r in range(BLOCKS // 2):
                owner = (slot_bits(half, r) + core) ^ me
                for name, j in items:
                    if name in wanted:
                        b, off = ROWS[name], row_of(items, (name, j))
                        wanted[name][
                            pl.ds(pl.multiple_of(owner * b, 16), b), j * PACK : (j + 1) * PACK
                        ] = piece[r, off : off + b, :]


def put(me, group, ref, item, value, start=0):
    half = int(item in SUMS[group][1])
    off = row_of(SUMS[group][half], item) + half * height(SUMS[group][0])
    b = ROWS[item[0]]
    for k in range(value.shape[0] // b):
        slot = slot_of(half, (start + k) ^ me)
        ref[slot, off : off + b, :] = value[k * b : (k + 1) * b]


def group_grads(group):
    return [((BLOCKS, height(sum(SUMS[group], [])), PACK), BF)]


def front1_kernel(tile, scal, x_ref, g1, g2, p0, p1, p2, p3, h1_ref, y2_ref, joined_ref, glu):
    unpack(scal[2], 0, (p0, p1, p2, p3), {"glu": glu})

    def step(i, carry):
        at = rows_at(i, tile)
        x = x_ref[at, :].astype(F32)
        hat, _ = normalise(x)
        joined = nn((hat * g1[...]).astype(BF), glu[...])
        joined_ref[at, :] = joined
        h1 = x + joined[:, :D] * sigmoid(joined[:, D:])
        h1_ref[at, :] = h1
        hat2, _ = normalise(h1)
        y2_ref[at, :] = (hat2 * g2[...]).astype(BF)
        return carry

    lax.fori_loop(0, x_ref.shape[0] // tile, step, 0)


def front1(scal, x, g1, g2, pieces, ties=()):
    rows = x.shape[0]
    return whole_call(
        functools.partial(front1_kernel, 160),
        [((rows, D), F32), ((rows, D), BF), ((rows, 2 * D), F32)],
        [scal, x, g1, g2, *pieces],
        scratch=[((D, 2 * D), BF)],
        ties=ties,
        micros=9,
    )


def front2_kernel(tile, group, scal, y2_ref, g3, p0, p1, p2, p3, *refs):
    left_ref, right_ref, mid_ref, u_ref, wide, narrow = refs
    unpack(scal[2], 0, (p0, p1, p2, p3), {"wide": wide, "narrow": narrow})
    rows = y2_ref.shape[0]
    base = scal[0] * (rows - 2 * RIM) - RIM
    first = scal[1]
    u_ref[0:RIM, :] = jnp.zeros((RIM, 3 * NARROW), F32)
    u_ref[RIM + rows : 2 * RIM + rows, :] = jnp.zeros((RIM, 3 * NARROW), F32)

    def narrow_step(i, carry):
        y = y2_ref[rows_at(i, tile), :]
        for k in range(3):
            u_ref[rows_at(i, tile, RIM), k * NARROW : (k + 1) * NARROW] = nn(
                y, narrow[k * D : (k + 1) * D, :]
            )
        return carry

    lax.fori_loop(0, rows // tile, narrow_step, 0)

    def step(i, carry):
        at = rows_at(i, tile)
        around = pl.ds(pl.multiple_of(i * tile, 16), tile + 2 * RIM)
        left = nn(y2_ref[at, :], wide[...])
        left_ref[at, :] = left
        pos = places(base + i * tile, tile, NARROW)
        before = pltpu.roll(u_ref[around, 0:NARROW], 1, 0)[RIM : RIM + tile]
        after = pltpu.roll(u_ref[around, 2 * NARROW :], tile + 2 * RIM - 1, 0)[RIM : RIM + tile]
        right = u_ref[rows_at(i, tile, RIM), NARROW : 2 * NARROW]
        right = right + jnp.where((pos == first) | (pos == 0), 0.0, before)
        right = right + jnp.where((pos + 1 == first) | (pos + 1 == group), 0.0, after)
        right_ref[at, :] = right
        left = gelu(left)
        joined = jnp.concatenate([left[:, :NARROW] + gelu(right), left[:, NARROW:]], axis=1)
        hat, _ = normalise(joined)
        row = base + i * tile + lax.broadcasted_iota(jnp.int32, (tile, 1), 0)
        inside = ((row >= 0) & (row < group)).astype(F32)
        mid_ref[at, :] = (hat * inside * g3[...]).astype(BF)
        return carry

    lax.fori_loop(0, rows // tile, step, 0)


def front2(scal, y2, g3, pieces, group, ties=()):
    rows = y2.shape[0]
    return whole_call(
        functools.partial(front2_kernel, 160, group),
        [((rows, FF), F32), ((rows, NARROW), F32), ((rows, FF), BF)],
        [scal, y2, g3, *pieces],
        scratch=[((rows + 2 * RIM, 3 * NARROW), F32), ((D, FF), BF), ((3 * D, NARROW), BF)],
        ties=ties,
        micros=14,
    )


def crosses(pos, offset, first):
    if offset > 0:
        return (pos < first) & (pos + offset >= first)
    return (pos >= first) & (pos + offset < first)


def conv(win, tile, taps, lanes, pos, first, masked, sign):
    total = None
    for k in range(KERNEL):
        o = sign * (k - HALF)
        v = win[RIM + o : RIM + o + tile, :]
        if masked and o != 0:
            v = jnp.where(crosses(pos, o, first), 0.0, v)
        v = v * taps[k : k + 1, lanes]
        total = v if total is None else total + v
    return total


def front3_kernel(tile, n, share, scal, mid_ref, taps, h1_ref, g4, p0, p1, p2, p3, *refs):
    spread_ref, h2_ref, y4_ref = refs[:3]
    outs = refs[3 : 3 + n]
    win, qkv_s, point, qkv_w = refs[3 + n :]
    unpack(scal[2], 0, (p0, p1, p2, p3), {"point": point, "qkv": qkv_w})
    rows = h2_ref.shape[0]
    s, first = scal[0], scal[1]
    base = s * rows

    def step(i, carry):
        at = rows_at(i, tile)
        begin = base + i * tile
        near = (first > begin - HALF) & (first < begin + tile + HALF)

        def chunk(c, carry2):
            lanes = pl.ds(pl.multiple_of(c * LANES, LANES), LANES)
            around = pl.ds(pl.multiple_of(i * tile, 16), tile + 2 * RIM)
            win[...] = mid_ref[around, lanes].astype(F32)
            pos = places(begin, tile)
            for masked in (False, True):

                @pl.when(near if masked else jnp.logical_not(near))
                def _():
                    spread_ref[at, lanes] = conv(
                        win, tile, taps, lanes, pos, first, masked, 1
                    ).astype(BF)

            return carry2

        lax.fori_loop(0, FF // LANES, chunk, 0)
        h1 = h1_ref[rows_at(i, tile, RIM), :]
        branch = nn(spread_ref[at, :], point[...])
        h2 = jnp.concatenate([h1[:, :NARROW] + branch, h1[:, NARROW:]], axis=1)
        h2_ref[at, :] = h2
        hat, _ = normalise(h2)
        y4 = (hat * g4[...]).astype(BF)
        y4_ref[at, :] = y4
        qkv_s[...] = nn(y4, qkv_w[...]).astype(BF)
        for k in range(n):
            block = (s ^ k) // share
            for part in range(3):
                outs[k][at, part * LANES : (part + 1) * LANES] = qkv_s[
                    :, pl.ds(pl.multiple_of(part * D + block * LANES, LANES), LANES)
                ]
        return carry

    lax.fori_loop(0, rows // tile, step, 0)


def front3(scal, mid, taps, h1, g4, pieces, n, share, ties=()):
    rows = mid.shape[0] - 2 * RIM
    tile = 128
    return whole_call(
        functools.partial(front3_kernel, tile, n, share),
        [((rows, FF), BF), ((rows, D), F32), ((rows, D), BF)] + [((rows, 3 * LANES), BF)] * n,
        [scal, mid, taps, h1, g4, *pieces],
        scratch=[((tile + 2 * RIM, LANES), F32), ((tile, 3 * D), BF)]
        + [((FF, NARROW), BF), ((D, 3 * D), BF)],
        ties=ties,
        micros=22,
    )


def middle_kernel(tile, n, share, scal, h2_ref, *refs):
    att = refs[:n]
    cot_ref, g5, p0, p1, p2, p3, mixed_ref, dh3_ref = refs[n : n + 8]
    datt = refs[n + 8 : 2 * n + 8]
    grads, ln_out = refs[2 * n + 8 : 2 * n + 10]
    att_s, y5_s, inner_s, du_s, db_s, wa, wup, wdown, ln_ref = refs[2 * n + 10 :]
    me = scal[2]
    unpack(me, 1, (p0, p1, p2, p3), {"attn": wa, "up": wup, "down": wdown})
    rows = h2_ref.shape[0]
    s = scal[0]
    for k in range(n):
        block = (s ^ k) // share
        lanes = pl.ds(pl.multiple_of(block * LANES, LANES), LANES)
        if share == 1:
            att_s[:, lanes] = att[k][...]
        else:
            seen = (s ^ k) % share
            before = att_s[:, lanes].astype(F32)
            lane = lax.broadcasted_iota(jnp.int32, (rows, LANES), 1)
            mine = lane // (LANES // share) == seen
            att_s[:, lanes] = jnp.where(mine, att[k][...].astype(F32), before).astype(BF)
    ln_ref[...] = jnp.zeros_like(ln_ref)

    def step(i, carry):
        at = rows_at(i, tile)
        h3 = h2_ref[at, :] + nn(att_s[at, :], wa[...])
        hat, r = normalise(h3)
        y5 = (hat * g5[...]).astype(BF)
        y5_s[at, :] = y5
        value, slope = gelu_and_slope(nn(y5, wup[...]))
        inner = value.astype(BF)
        inner_s[at, :] = inner
        mixed_ref[at, :] = (h3 + nn(inner, wdown[...])).astype(BF)
        cot = cot_ref[at, :]
        du = (nt(cot, wdown[...]) * slope).astype(BF)
        du_s[at, :] = du
        dy5 = nt(du, wup[...])
        ln_ref[...] += fold8(dy5 * hat)
        dh3 = cot.astype(F32) + norm_back(dy5, hat, r, g5[...])
        dh3_ref[at, :] = dh3
        db = dh3.astype(BF)
        db_s[at, :] = db
        da = nt(db, wa[...]).astype(BF)
        for j in range(D // LANES):
            for k in range(n):

                @pl.when((s ^ k) // share == j)
                def _():
                    datt[k][at, :] = da[:, j * LANES : (j + 1) * LANES]

        return carry

    lax.fori_loop(0, rows // tile, step, 0)
    ln_out[...] = jnp.sum(ln_ref[...], axis=0, keepdims=True)
    att_t = att_s[...].T
    for j in range(D // PACK):
        put(me, 0, grads, ("attn", j), nn(att_t, db_s[:, j * PACK : (j + 1) * PACK]).astype(BF))
    y5_t = y5_s[...].T
    for j in range(FF // PACK):
        cols = slice(j * PACK, (j + 1) * PACK)
        put(me, 0, grads, ("up", j), nn(y5_t, du_s[:, cols]).astype(BF))
        down = tn(inner_s[:, cols], cot_ref[...]).astype(BF)
        for m in range(D // PACK):
            put(me, 0, grads, ("down", m), down[:, m * PACK : (m + 1) * PACK], j * PACK // 64)


def middle(scal, h2, att, cot, g5, pieces, n, share, ties=()):
    rows = h2.shape[0]
    return whole_call(
        functools.partial(middle_kernel, 128, n, share),
        [((rows, D), BF), ((rows, D), F32)]
        + [((rows, LANES), BF)] * n
        + group_grads(0)
        + [((1, D), F32)],
        [scal, h2, *att, cot, g5, *pieces],
        scratch=[
            ((rows, D), BF),
            ((rows, D), BF),
            ((rows, FF), BF),
            ((rows, FF), BF),
            ((rows, D), BF),
            ((D, D), BF),
            ((D, FF), BF),
            ((FF, D), BF),
            ((8, D), F32),
        ],
        ties=ties,
        micros=29,
    )


def back3_kernel(tile, n, share, scal, *refs):
    blocks = refs[:n]
    dh3_ref, h2_ref, y4_ref, spread_ref, g4, p0, p1, p2, p3 = refs[n : n + 9]
    dh2_ref, db_ref, grads, ln_out = refs[n + 9 : n + 13]
    dqkv_s, qkv_w, ln_ref = refs[n + 13 :]
    me = scal[2]
    unpack(me, 0, (p0, p1, p2, p3), {"qkv": qkv_w})
    rows = h2_ref.shape[0]
    s = scal[0]
    for k in range(n):
        block = (s ^ k) // share
        for part in range(3):
            lanes = pl.ds(pl.multiple_of(part * D + block * LANES, LANES), LANES)
            new = blocks[k][:, part * LANES : (part + 1) * LANES]
            if share > 1:
                lane = lax.broadcasted_iota(jnp.int32, (rows, LANES), 1)
                mine = lane // (LANES // share) == (s ^ k) % share
                new = jnp.where(mine, new.astype(F32), dqkv_s[:, lanes].astype(F32)).astype(BF)
            dqkv_s[:, lanes] = new
    ln_ref[...] = jnp.zeros_like(ln_ref)

    def step(i, carry):
        at = rows_at(i, tile)
        dy4 = nt(dqkv_s[at, :], qkv_w[...])
        hat, r = normalise(h2_ref[at, :])
        ln_ref[...] += fold8(dy4 * hat)
        dh2 = dh3_ref[at, :] + norm_back(dy4, hat, r, g4[...])
        dh2_ref[at, :] = dh2
        db_ref[at, :] = dh2[:, :NARROW].astype(BF)
        return carry

    lax.fori_loop(0, rows // tile, step, 0)
    ln_out[...] = jnp.sum(ln_ref[...], axis=0, keepdims=True)
    y4_t = y4_ref[...].T
    for j in range(3 * D // PACK):
        put(me, 1, grads, ("qkv", j), nn(y4_t, dqkv_s[:, j * PACK : (j + 1) * PACK]).astype(BF))
    for j in range(FF // PACK):
        part = tn(spread_ref[:, j * PACK : (j + 1) * PACK], db_ref[...]).astype(BF)
        put(me, 1, grads, ("point", 0), part, j * PACK // 64)


def back3(scal, blocks, dh3, h2, y4, spread, g4, pieces, n, share, ties=()):
    rows = h2.shape[0]
    return whole_call(
        functools.partial(back3_kernel, 128, n, share),
        [((rows, D), F32), ((rows, NARROW), BF)] + group_grads(1) + [((1, D), F32)],
        [scal, *blocks, dh3, h2, y4, spread, g4, *pieces],
        scratch=[((rows, 3 * D), BF), ((D, 3 * D), BF), ((8, D), F32)],
        ties=ties,
        micros=15,
    )


def back2_kernel(tile, group, scal, low_ref, db_ref, high_ref, *refs):
    taps, mid_ref, left_ref, right_ref, g3 = refs[:5]
    pieces, (dl, st, gdepth_out, ln_out) = refs[5:9], refs[9:13]
    dbx, dsp, win, dmid, dr, point, gdepth_ref, ln_ref = refs[13:]
    unpack(scal[2], 0, pieces, {"point": point})
    rows = db_ref.shape[0]
    ext = rows + 2 * RIM
    base = scal[0] * rows - RIM
    first = scal[1]
    dbx[0:RIM, :] = low_ref[...]
    dbx[RIM : RIM + rows, :] = db_ref[...]
    dbx[RIM + rows :, :] = high_ref[...]
    dsp[0:RIM, :] = jnp.zeros((RIM, FF), F32)
    dsp[RIM + ext :, :] = jnp.zeros((RIM, FF), F32)
    dr[0:RIM, :] = jnp.zeros((RIM, NARROW), F32)
    dr[RIM + ext :, :] = jnp.zeros((RIM, NARROW), F32)
    gdepth_ref[...] = jnp.zeros_like(gdepth_ref)
    ln_ref[...] = jnp.zeros_like(ln_ref)

    def spread_step(i, carry):
        dsp[rows_at(i, tile, RIM), :] = nt(dbx[rows_at(i, tile), :], point[...])
        return carry

    lax.fori_loop(0, ext // tile, spread_step, 0)

    def step(i, carry):
        at = rows_at(i, tile)
        begin = base + i * tile
        near = (first > begin - HALF) & (first < begin + tile + HALF)
        near = near | (i == 0) | (i == ext // tile - 1)

        def chunk(c, carry2):
            lanes = pl.ds(pl.multiple_of(c * LANES, LANES), LANES)
            around = pl.ds(pl.multiple_of(i * tile, 16), tile + 2 * RIM)
            win[...] = dsp[around, lanes]
            local = i * tile + lax.broadcasted_iota(jnp.int32, (tile, LANES), 0)
            mid = mid_ref[at, lanes].astype(F32)
            pos = places(begin, tile)
            for masked in (False, True):

                @pl.when(near if masked else jnp.logical_not(near))
                def _():
                    total = None
                    for k in range(KERNEL):
                        o = HALF - k
                        v = win[RIM + o : RIM + o + tile, :]
                        if masked and o != 0:
                            v = jnp.where(crosses(pos, o, first), 0.0, v)
                        counted = v
                        if masked:
                            kept = (local + o >= RIM) & (local + o < RIM + rows)
                            counted = jnp.where(kept, v, 0.0)
                        gdepth_ref[k * 8 : (k + 1) * 8, lanes] += fold8(counted * mid)
                        v = v * taps[k : k + 1, lanes]
                        total = v if total is None else total + v
                    dmid[:, lanes] = total

            return carry2

        lax.fori_loop(0, FF // LANES, chunk, 0)
        left, slope = gelu_and_slope(left_ref[at, :])
        right, slope_r = gelu_and_slope(right_ref[at, :])
        joined = jnp.concatenate([left[:, :NARROW] + right, left[:, NARROW:]], axis=1)
        hat, r = normalise(joined)
        local = i * tile + lax.broadcasted_iota(jnp.int32, (tile, 1), 0)
        own = ((local >= RIM) & (local < RIM + rows)).astype(F32)
        pos = base + local
        grad = dmid[...] * ((pos >= 0) & (pos < group)).astype(F32)
        ln_ref[...] += fold8(grad * hat * own)
        dj = norm_back(grad, hat, r, g3[...])
        dl[at, :] = (dj * slope).astype(BF)
        dr[rows_at(i, tile, RIM), :] = (dj[:, :NARROW] * slope_r).astype(BF).astype(F32)
        return carry

    lax.fori_loop(0, ext // tile, step, 0)
    for k in range(KERNEL):
        gdepth_out[k : k + 1, :] = jnp.sum(gdepth_ref[k * 8 : (k + 1) * 8, :], axis=0, keepdims=True)
    ln_out[...] = jnp.sum(ln_ref[...], axis=0, keepdims=True)
    part = 128

    def gather_step(i, carry):
        at = rows_at(i, part)
        around = pl.ds(pl.multiple_of(RIM + i * part, 16), part + 2 * RIM)
        pos = places(base + RIM + i * part, part, NARROW)
        v = dr[around, :]
        after = pltpu.roll(v, part + 2 * RIM - 1, 0)[RIM : RIM + part]
        before = pltpu.roll(v, 1, 0)[RIM : RIM + part]
        after = jnp.where((pos + 1 == first) | (pos + 1 == group), 0.0, after)
        before = jnp.where((pos == first) | (pos == 0), 0.0, before)
        st[at, 0:NARROW] = after.astype(BF)
        st[at, NARROW : 2 * NARROW] = v[RIM : RIM + part].astype(BF)
        st[at, 2 * NARROW :] = before.astype(BF)
        return carry

    lax.fori_loop(0, rows // part, gather_step, 0)


def back2(scal, low, db, high, taps, mid, left, right, g3, pieces, group, ties=()):
    rows = db.shape[0]
    ext = rows + 2 * RIM
    tile = 160
    return whole_call(
        functools.partial(back2_kernel, tile, group),
        [((ext, FF), BF), ((rows, 3 * NARROW), BF), ((KERNEL, FF), F32), ((1, FF), F32)],
        [scal, low, db, high, taps, mid, left, right, g3, *pieces],
        scratch=[
            ((ext, NARROW), BF),
            ((ext + 2 * RIM, FF), F32),
            ((tile + 2 * RIM, LANES), F32),
            ((tile, FF), F32),
            ((ext + 2 * RIM, NARROW), F32),
            ((FF, NARROW), BF),
            ((8 * KERNEL, FF), F32),
            ((8, FF), F32),
        ],
        ties=ties,
        micros=49,
    )


def weigh2_kernel(scal, dl, st, y2_ref, grads, gn):
    me = scal[2]
    rows = st.shape[0]
    y2_t = y2_ref[RIM : RIM + rows, :].T
    for j in range(FF // PACK):
        part = nn(y2_t, dl[RIM : RIM + rows, j * PACK : (j + 1) * PACK]).astype(BF)
        put(me, 2, grads, ("wide", j), part)
    for k in range(3):
        gn[k * D : (k + 1) * D, :] = nn(y2_t, st[:, k * NARROW : (k + 1) * NARROW]).astype(BF)
    put(me, 2, grads, ("narrow", 0), gn[...])


def weigh2(scal, dl, st, y2, ties=()):
    return whole_call(
        weigh2_kernel,
        group_grads(2),
        [scal, dl, st, y2],
        scratch=[((3 * D, NARROW), BF)],
        ties=ties,
        micros=7,
    )


def back1_kernel(tile, scal, dl, st, dh2_ref, h1_ref, joined_ref, x_ref, g1, g2, *refs):
    p0, p1, p2, p3, dx_ref, grads, ln1_out, ln2_out = refs[:8]
    y1_s, dj_s, glu, wide, narrow, ln1_ref, ln2_ref = refs[8:]
    rows = st.shape[0]
    me = scal[2]
    unpack(me, 0, (p0, p1, p2, p3), {"glu": glu, "wide": wide, "narrow": narrow})
    ln1_ref[...] = jnp.zeros_like(ln1_ref)
    ln2_ref[...] = jnp.zeros_like(ln2_ref)

    def step(i, carry):
        at = rows_at(i, tile)
        ext = rows_at(i, tile, RIM)
        dy2 = nt(dl[ext, :], wide[...])
        for k in range(3):
            dy2 = dy2 + nt(
                st[at, k * NARROW : (k + 1) * NARROW], narrow[k * D : (k + 1) * D, :]
            )
        hat2, r2 = normalise(h1_ref[ext, :])
        ln2_ref[...] += fold8(dy2 * hat2)
        dh1 = dh2_ref[at, :] + norm_back(dy2, hat2, r2, g2[...])
        gate = sigmoid(joined_ref[ext, D:])
        value = joined_ref[ext, :D]
        da = (dh1 * gate).astype(BF)
        db = (dh1 * value * gate * (1.0 - gate)).astype(BF)
        dj_s[at, :D] = da
        dj_s[at, D:] = db
        x = x_ref[ext, :].astype(F32)
        hat1, r1 = normalise(x)
        y1_s[at, :] = (hat1 * g1[...]).astype(BF)
        dy1 = nt(dj_s[at, :], glu[...])
        ln1_ref[...] += fold8(dy1 * hat1)
        dx_ref[at, :] = (dh1 + norm_back(dy1, hat1, r1, g1[...])).astype(dx_ref.dtype)
        return carry

    lax.fori_loop(0, rows // tile, step, 0)
    ln1_out[...] = jnp.sum(ln1_ref[...], axis=0, keepdims=True)
    ln2_out[...] = jnp.sum(ln2_ref[...], axis=0, keepdims=True)
    y1_t = y1_s[...].T
    for j in range(2 * D // PACK):
        put(me, 3, grads, ("glu", j), nn(y1_t, dj_s[:, j * PACK : (j + 1) * PACK]).astype(BF))


def back1(scal, dl, st, dh2, h1, joined, x, g1, g2, pieces, ties=()):
    rows = st.shape[0]
    return whole_call(
        functools.partial(back1_kernel, 128),
        [((rows, D), BF), ((BLOCKS, height(GLU), PACK), BF), ((1, D), F32), ((1, D), F32)],
        [scal, dl, st, dh2, h1, joined, x, g1, g2, *pieces],
        scratch=[((rows, D), BF), ((rows, 2 * D), BF), ((D, 2 * D), BF)]
        + [((D, FF), BF), ((3 * D, NARROW), BF), ((8, D), F32), ((8, D), F32)],
        ties=ties,
        micros=20,
    )


def lane_maps(rows, head):
    lane = lax.broadcasted_iota(jnp.int32,(rows,LANES),1)
    own = (lane >= head*HEAD) & (lane < (head+1)*HEAD)
    rel = lane - (1-head)*HEAD
    return own, rel

def id_column(base, rows, first):
    pos = base + lax.broadcasted_iota(jnp.int32,(rows,LANES),0)
    return pos >= first

def split3(v):
    hi = v.astype(BF).astype(F32)
    mid = (v-hi).astype(BF).astype(F32)
    return hi, mid, v-hi-mid

def tile_ids(start, rows, first):
    return start < first, start+rows > first

def overlap(a_start,a_rows,b_start,b_rows,first):
    a0,a1 = tile_ids(a_start,a_rows,first); b0,b1=tile_ids(b_start,b_rows,first)
    return (a0&b0)|(a1&b1)

def attend_kernel(n, heads, share, tq, tk, scal, *refs):
    qkv = refs[:n]; att = refs[n:2*n]; lse_ref = refs[2*n]
    qa, ka, va, mx_ref, m_ref, q2_ref, acc_ref = refs[2*n+1:]
    s = scal[0]; first = scal[1]
    rows = qkv[0].shape[0]
    for k in range(n):
        base = (s ^ k)*rows
        id1 = id_column(base, rows, first).astype(F32)
        q = qkv[k][:, 0:LANES].astype(F32)*(HEAD**-0.5)
        key = qkv[k][:, LANES:2*LANES].astype(F32)
        v = qkv[k][:, 2*LANES:3*LANES].astype(F32)
        for i in range(heads):
            h = i if share==1 else s % share
            own, rel = lane_maps(rows, h)
            qx = jnp.where(rel==0, 1.0-id1, jnp.where(rel==1, id1, 0.0))
            kx = jnp.where(rel==0, id1*BIG, jnp.where(rel==1, (1.0-id1)*BIG, jnp.where(rel<5,1.0,0.0)))
            qa[i, k*rows:(k+1)*rows,:] = jnp.where(own, q, qx).astype(BF)
            ka[i, k*rows:(k+1)*rows,:] = jnp.where(own, key, kx).astype(BF)
            va[i, k*rows:(k+1)*rows,:] = jnp.where(own, v, 1.0).astype(BF)
    per = rows//tq; per_k = rows//tk
    def fold(sc, best):
        for j in range(tk//LANES):
            best = jnp.maximum(best, sc[:, j*LANES:(j+1)*LANES])
        return best
    def q_step(it, carry):
        kq = it//per
        r0 = pl.multiple_of((it % per)*tq, tq)
        g0 = pl.multiple_of(it*tq, tq)
        own0 = pl.multiple_of((g0//tk)*tk, tk)
        q_start = (s ^ kq)*rows + r0
        for i in range(heads):
            for j in range(max(1,tq//tk)):
                sc = nt(qa[i, pl.ds(g0,tq),:], ka[i, pl.ds(own0+j*tk,tk),:])
                best = fold(sc, sc[:, :LANES] if j==0 else best)
            mx_ref[i] = best
            m_ref[i] = jnp.zeros((tq,LANES),F32)
        def attempt(again):
            for i in range(heads):
                h = i if share==1 else s % share
                own, rel = lane_maps(tq, h)
                m = jnp.max(mx_ref[i], axis=1, keepdims=True)
                mb = m_ref[i] + jnp.broadcast_to(m, (tq,LANES))
                m_ref[i] = mb
                hi,mid,lo = split3(-mb)
                q = qa[i, pl.ds(g0,tq),:].astype(F32)
                q2_ref[i] = jnp.where(rel==2,hi,jnp.where(rel==3,mid,jnp.where(rel==4,lo,q))).astype(BF)
            mx_ref[...] = jnp.full_like(mx_ref, -3e38)
            acc_ref[...] = jnp.zeros_like(acc_ref)
            for kt in range(n*per_k):
                k_start = (s ^ (kt//per_k))*rows + (kt%per_k)*tk
                @pl.when(overlap(q_start,tq,k_start,tk,first))
                def _():
                    for i in range(heads):
                        sc = nt(q2_ref[i], ka[i, kt*tk:(kt+1)*tk,:])
                        mx_ref[i] = fold(sc, mx_ref[i])
                        p = jnp.exp2(sc*LOG2E).astype(BF)
                        acc_ref[i] += nn(p, va[i, kt*tk:(kt+1)*tk,:])
            return (jnp.max(mx_ref[...]) > 40.0).astype(jnp.int32)
        lax.while_loop(lambda again: again > 0, attempt, jnp.int32(1))
        out = jnp.zeros((tq,LANES),F32); lse = jnp.zeros((tq,LANES),F32)
        for i in range(heads):
            h = i if share==1 else s % share
            own,_ = lane_maps(tq,h)
            acc = acc_ref[i]
            total = pltpu.roll(acc, HEAD, 1)
            out = jnp.where(own, acc/total, out)
            lse = jnp.where(own, m_ref[i]+jnp.log(total), lse)
        lse_ref[pl.ds(g0,tq),:] = lse
        for k in range(n):
            @pl.when(kq==k)
            def _():
                att[k][pl.ds(r0,tq),:] = out.astype(BF)
        return carry
    lax.fori_loop(0, n*per, q_step, 0)

def attend(scal, blocks, n, share, tq=768, tk=384, ties=()):
    rows = blocks[0].shape[0]
    heads = 2 // share
    return whole_call(
        functools.partial(attend_kernel, n, heads, share, tq, tk),
        [((rows, LANES), BF)] * n + [((n * rows, LANES), F32)],
        [scal, *blocks],
        scratch=[((heads, n * rows, LANES), BF)] * 3
        + [((heads, tq, LANES), F32)] * 2
        + [((heads, tq, LANES), BF), ((heads, tq, LANES), F32)],
        ties=ties,
        micros=36,
    )


def attend_back_kernel(n, heads, share, tq, tk, scal, *refs):
    qkv = refs[:n]; att = refs[n:2*n]; dat = refs[2*n:3*n]; lse_ref = refs[3*n]
    out = refs[3*n+1:4*n+1]
    qa, ka, va, da, dq_ref, dk_ref, dv_ref = refs[4*n+1:]
    s = scal[0]; first = scal[1]
    rows = qkv[0].shape[0]
    for k in range(n):
        base = (s ^ k)*rows
        sl = slice(k*rows,(k+1)*rows)
        id1 = id_column(base, rows, first).astype(F32)
        q = qkv[k][:, 0:LANES].astype(F32)*(HEAD**-0.5)
        key = qkv[k][:, LANES:2*LANES].astype(F32)
        v = qkv[k][:, 2*LANES:3*LANES].astype(F32)
        do = dat[k][...].astype(F32)
        prod = do*att[k][...].astype(F32)
        for i in range(heads):
            h = i if share==1 else s % share
            own, rel = lane_maps(rows, h)
            lse = pltpu.roll(lse_ref[sl,:], HEAD, 1)
            hi,mid,lo = split3(-lse)
            delta = jnp.sum(jnp.where(own,prod,0.0),axis=1,keepdims=True)
            dhi,dmid,dlo = split3(-delta)
            qx = jnp.where(rel==0, 1.0-id1, jnp.where(rel==1, id1, jnp.where(rel==2,hi,jnp.where(rel==3,mid,jnp.where(rel==4,lo,0.0)))))
            kx = jnp.where(rel==0, id1*BIG, jnp.where(rel==1, (1.0-id1)*BIG, jnp.where(rel<5,1.0,0.0)))
            vx = jnp.where(rel<3,1.0,0.0)
            dx = jnp.where(rel==0,dhi,jnp.where(rel==1,dmid,jnp.where(rel==2,dlo,0.0)))
            qa[i,sl,:] = jnp.where(own,q,qx).astype(BF)
            ka[i,sl,:] = jnp.where(own,key,kx).astype(BF)
            va[i,sl,:] = jnp.where(own,v,vx).astype(BF)
            da[i,sl,:] = jnp.where(own,do,dx).astype(BF)
    dq_ref[...] = jnp.zeros_like(dq_ref)
    per_q = rows//tq; per_k = rows//tk
    def k_step(kt, carry):
        k0 = pl.multiple_of(kt*tk, tk)
        kk = kt//per_k
        k_start = (s ^ kk)*rows + (kt % per_k)*tk
        for i in range(heads):
            dk_ref[i] = jnp.zeros((tk,LANES),F32)
            dv_ref[i] = jnp.zeros((tk,LANES),F32)
        def q_step(qt, c2):
            q0 = pl.multiple_of(qt*tq, tq)
            q_start = (s ^ (qt//per_q))*rows + (qt % per_q)*tq
            @pl.when(overlap(q_start,tq,k_start,tk,first))
            def _():
                for i in range(heads):
                    qq = qa[i,pl.ds(q0,tq),:]; kx = ka[i,pl.ds(k0,tk),:]; dd = da[i,pl.ds(q0,tq),:]
                    st = nt(kx, qq)
                    p = jnp.exp2(st*LOG2E)
                    dp = nt(va[i,pl.ds(k0,tk),:], dd)
                    ds = (p*dp).astype(BF)
                    dv_ref[i] += nn(p.astype(BF), dd)
                    dk_ref[i] += nn(ds, qq)
                    dq_ref[i,pl.ds(q0,tq),:] += tn(ds, kx)
            return c2
        lax.fori_loop(0, n*per_q, q_step, 0)
        dk = jnp.zeros((tk,LANES),F32); dv = jnp.zeros((tk,LANES),F32)
        for i in range(heads):
            h = i if share==1 else s % share
            own,_ = lane_maps(tk,h)
            dk = jnp.where(own, dk_ref[i], dk); dv = jnp.where(own, dv_ref[i], dv)
        r0 = pl.multiple_of((kt % per_k)*tk, tk)
        for k in range(n):
            @pl.when(kk==k)
            def _():
                out[k][pl.ds(r0,tk),LANES:2*LANES] = dk.astype(BF)
                out[k][pl.ds(r0,tk),2*LANES:3*LANES] = dv.astype(BF)
        return carry
    lax.fori_loop(0, n*per_k, k_step, 0)
    for k in range(n):
        sl = slice(k*rows,(k+1)*rows)
        dq = jnp.zeros((rows,LANES),F32)
        for i in range(heads):
            h = i if share==1 else s % share
            own,_ = lane_maps(rows,h)
            dq = jnp.where(own, dq_ref[i,sl,:], dq)
        out[k][:, 0:LANES] = (dq*(HEAD**-0.5)).astype(BF)

def attend_back(scal, blocks, att, datt, lse, n, share, tq=384, tk=384, ties=()):
    rows = blocks[0].shape[0]
    heads = 2 // share
    return whole_call(
        functools.partial(attend_back_kernel, n, heads, share, tq, tk),
        [((rows, 3 * LANES), BF)] * n,
        [scal, *blocks, *att, *datt, lse],
        scratch=[((heads, n * rows, LANES), BF)] * 4
        + [((heads, n * rows, LANES), F32)]
        + [((heads, tk, LANES), F32)] * 2,
        ties=ties,
        micros=58,
    )


class Links:
    def __init__(self, n_seq, n_dp):
        self.count = n_seq * n_dp
        self.direct = (n_seq, n_dp) == (4, 8)

    def flip(self, value, mask):
        return lax.ppermute(value, AXES, [(i, i ^ mask) for i in range(self.count)])

    def near(self, group, weights):
        blocks = [
            weights[name][:, j * PACK : (j + 1) * PACK] for name, j in sum(GATHERS[group], [])
        ]
        block = jnp.concatenate(blocks, axis=0)
        return jnp.stack([block] + [self.flip(block, k << 3) for k in range(1, 4)])

    def part(self, group, held):
        low = height(GATHERS[group][0])
        return [held[:, :low], held[:, low:]]

    def spread(self, held, stage):
        masks = ((4, 2), (2, 4))[stage]
        return [jnp.concatenate([h, self.flip(h, m)]) for h, m in zip(held, masks)]

    def across(self, held):
        return [held[0], self.flip(held[0], 1), held[1], self.flip(held[1], 1)]

    def gather_whole(self, group, weights):
        whole = {
            name: lax.all_gather(weights[name], AXES, axis=0, tiled=True)
            for name in dict(sum(GATHERS[group], []))
        }
        pieces = []
        for half, items in enumerate(GATHERS[group]):
            blocks = [
                whole[name][:, j * PACK : (j + 1) * PACK].reshape(BLOCKS, -1, PACK)
                for name, j in items
            ]
            pieces += list(self.by_slot(jnp.concatenate(blocks, axis=1), half))
        return pieces

    def by_slot(self, blocks, half):
        shape = blocks.shape[1:]
        order = ((3, 2, 1, 0), (3, 1, 2, 0))[half]
        return blocks.reshape(4, 2, 2, 2, *shape).transpose(*order, 4, 5).reshape(2, 16, *shape)

    def by_owner(self, slots, half):
        shape = slots.shape[1:]
        order = ((3, 2, 1, 0), (3, 1, 2, 0))[half]
        return slots.reshape(2, 2, 2, 4, *shape).transpose(*order, 4, 5).reshape(BLOCKS, *shape)

    def add(self, a, b):
        return (a.astype(F32) + b.astype(F32)).astype(BF)

    def fold(self, slots, mask):
        middle = slots.shape[0] // 2
        return self.add(slots[:middle], self.flip(slots[middle:], mask))

    def first(self, group, slots):
        held = self.fold(slots, 1)
        low = height(SUMS[group][0])
        return [held[:, :low], held[:, low:]]

    def next(self, held, stage):
        masks = ((2, 4), (4, 2))[stage]
        return [self.fold(h, m) for h, m in zip(held, masks)]

    def finish(self, held):
        held = jnp.concatenate(held, axis=1)
        total = held[0].astype(F32)
        for k in range(1, 4):
            total = total + self.flip(held[k], k << 3).astype(F32)
        return total

    def rows_of(self, items, total):
        parts, at = {}, 0
        for name, j in items:
            b = ROWS[name] * BLOCKS // self.count
            parts.setdefault(name, []).append(total[at : at + b])
            at += b
        return {name: jnp.concatenate(p, axis=1) for name, p in parts.items()}

    def scatter_whole(self, group, slots):
        sent, at = [], 0
        for half, items in enumerate(SUMS[group]):
            for name, _ in items:
                blocks = self.by_owner(slots[:, at : at + ROWS[name]], half)
                sent.append(blocks.reshape(self.count, -1, PACK))
                at += ROWS[name]
        sent = jnp.concatenate(sent, axis=1)
        return lax.psum_scatter(sent, AXES, scatter_dimension=0, tiled=False).astype(F32)


def small_block(arrays, blocks):
    flat = jnp.concatenate([a.reshape(blocks, -1) for a in arrays], axis=1)
    flat = jnp.pad(flat, ((0, 0), (0, 16 * PACK - flat.shape[1])))
    return flat.reshape(blocks * 16, PACK)


def slot_matrix(me, half):
    slots = slot_of(half, lax.iota(jnp.int32, BLOCKS) ^ me)
    return (slots[:, None] == lax.iota(jnp.int32, BLOCKS)[None, :]).astype(BF)


def small_from(pieces, me, sizes):
    off = row_of(GATHERS[0][1], SMALL_0[0])
    used = -(-sum(sizes) // PACK)
    rows = jnp.concatenate([pieces[2][:, off : off + used], pieces[3][:, off : off + used]])
    rows = nn(slot_matrix(me, 1), rows.reshape(BLOCKS, used * PACK))
    result, at = [], 0
    for size in sizes:
        result.append(rows[:, at : at + size].reshape(-1))
        at += size
    return result


def small_to(arrays, me):
    flat = jnp.concatenate([a.reshape(BLOCKS, -1) for a in arrays], axis=1).astype(BF)
    flat = tn(slot_matrix(me, 1), flat).astype(BF)
    flat = jnp.pad(flat, ((0, 0), (0, 16 * PACK - flat.shape[1])))
    return flat.reshape(BLOCKS, 16, PACK)


class Layout:
    def __init__(self, n_seq, n_dp):
        self.n_seq, self.n_dp = n_seq, n_dp
        self.where = {}
        for g in range(n_dp):
            for s in range(n_seq):
                self.where[g, s] = self.place(g, s)
        self.block = np.zeros(n_seq * n_dp, np.int32)
        for (g, s), device in self.where.items():
            self.block[device] = s

    def place(self, g, s):
        if (self.n_seq, self.n_dp) == (4, 8):
            y, x, c = g >> 2, g >> 1 & 1, g & 1
            return (2 * c + y) * 8 + (s & 1) * 4 + x * 2 + (s >> 1)
        return s * self.n_dp + g

    def pairs(self, source, target):
        return [
            (source(g, s), target(g, s))
            for g in range(self.n_dp)
            for s in range(self.n_seq)
            if target(g, s) is not None and source(g, s) is not None
        ]

    def at(self, g, s):
        return self.where.get((g, s))

    def home(self, g, s):
        return s * self.n_dp + g

    def bring(self, value):
        return lax.ppermute(value, AXES, self.pairs(self.home, self.at))

    def bring_to(self, value, step):
        return lax.ppermute(
            value, AXES, self.pairs(self.home, lambda g, s: self.at(g, s + step))
        )

    def send_home(self, value):
        return lax.ppermute(value, AXES, self.pairs(self.at, self.home))

    def to_neighbour(self, value, step):
        return lax.ppermute(value, AXES, self.pairs(self.at, lambda g, s: self.at(g, s + step)))

    def swap(self, values):
        return [values[0]] + [
            lax.ppermute(values[k], AXES, self.pairs(self.at, lambda g, s: self.at(g, s ^ k)))
            for k in range(1, self.n_seq)
        ]


NAMES = ("ln1", "ln2", "ln3", "ln4", "ln5", "glu", "wide", "narrow", "depth", "point", "qkv", "attn", "up", "down")
SMALL = ("ln1", "ln2", "ln3", "ln4", "ln5", "depth")


def after(value, *others):
    return lax.optimization_barrier((value, *others))[0]


def on_device(tokens, cotangent, first_length, *weights):
    n = lax.axis_size("seq")
    n_dp = lax.axis_size("dp")
    share = n * LANES // D
    layout = Layout(n, n_dp)
    links = Links(n, n_dp)
    rows = tokens.shape[1]
    group = n * rows
    me = lax.axis_index("seq") * n_dp + lax.axis_index("dp")
    s = jnp.asarray(layout.block)[me]
    mine = dict(zip(NAMES, weights))
    if links.direct:
        mine["small"] = small_block([mine[k] for k in SMALL], 1)
    else:
        me = jnp.zeros_like(me)
        small = [lax.all_gather(mine[k], AXES, axis=0, tiled=True) for k in SMALL]
        small = small_block(small, BLOCKS).reshape(links.count, -1, PACK)
        mine["small"] = small[lax.axis_index("seq") * n_dp + lax.axis_index("dp")]

    direct = links.direct
    tokens = tokens[0]
    lane = lax.broadcasted_iota(jnp.int32, (RIM, D), 1)
    digits = jnp.where(lane < LANES, first_length[0] // LANES, first_length[0] % LANES)
    held = links.near(0, mine) if direct else ()
    x = layout.bring(jnp.concatenate([tokens, digits.astype(BF)], axis=0))
    digits = x[rows, 0 : 2 * LANES : LANES].astype(F32).astype(jnp.int32)
    first = digits[0] * LANES + digits[1]
    low = layout.bring_to(tokens[-RIM:], 1)
    high = layout.bring_to(tokens[:RIM], -1)
    scal = jnp.stack([s.astype(jnp.int32), first, me.astype(jnp.int32)])
    x_ext = jnp.concatenate([low, x[:rows], high], axis=0)
    if direct:
        held = links.spread(links.part(0, held), 0)
        held = [after(h, x_ext) for h in held]
        pieces1 = links.across(links.spread(held, 1))
    else:
        pieces1, pieces2 = (links.gather_whole(k, mine) for k in range(2))
    sizes = [mine[k].shape[0] * links.count // BLOCKS for k in SMALL]
    g1, g2, g3, g4, g5, depth = small_from(pieces1, me, sizes)
    g1, g2, g3, g4, g5 = (g.astype(F32)[None] for g in (g1, g2, g3, g4, g5))
    taps = depth.reshape(KERNEL, FF).astype(F32)

    ties = ()
    if direct:
        late = dict(mine)
        for name in ("attn", "up", "down"):
            late[name] = after(mine[name], *pieces1)
        ties = held = (links.near(1, late),)
    h1, y2, joined = front1(scal, x_ext, g1, g2, pieces1)
    left, right, mid = front2(scal, y2, g3, pieces1, group)
    spread, h2, y4, *qkv = front3(scal, mid, taps, h1, g4, pieces1, n, share, ties=ties)
    cot = layout.bring(after(cotangent, mid)[0])
    if direct:
        ties = held = links.spread(links.part(1, held[0]), 0)
    qkv = layout.swap(qkv)
    *att, lse = attend(scal, qkv, n, share, ties=ties)
    if direct:
        pieces2 = links.across(links.spread(held, 1))
    mixed, dh3, *rest = middle(scal, h2, layout.swap(att), cot, g5, pieces2, n, share)
    datt, sum0, ln5 = rest[:n], rest[n], rest[n + 1]
    mixed = layout.send_home(mixed)
    ties = ()
    if direct:
        ties = sum0 = links.first(0, sum0)
    dqkv = attend_back(scal, qkv, att, layout.swap(datt), lse, n, share, ties=ties)
    if direct:
        sum0 = links.next(sum0, 0)
        ties = (mixed, *sum0)
    dqkv = layout.swap(dqkv)
    dh2, db, sum1, ln4 = back3(
        scal, dqkv, dh3, h2, y4, spread, g4, pieces1, n, share, ties=ties
    )
    low = layout.to_neighbour(db[-RIM:], 1)
    high = layout.to_neighbour(db[:RIM], -1)
    if direct:
        sum0 = links.next(sum0, 1)
        sum1 = links.first(1, sum1)
        ties = (*sum0, *sum1)
    dl, st, gdepth, ln3 = back2(
        scal, low, db, high, taps, mid, left, right, g3, pieces1, group, ties=ties
    )
    if direct:
        sum0 = links.finish([after(v, low, high, *sum1) for v in sum0])
        sum1 = links.next(sum1, 0)
        ties = (sum0, *sum1)
    (sum2,) = weigh2(scal, dl, st, y2, ties=ties)
    if direct:
        sum1 = links.next(sum1, 1)
        ties = sum1
    dx, sum3, ln1, ln2 = back1(scal, dl, st, dh2, h1, joined, x_ext, g1, g2, pieces1, ties=ties)
    dx = layout.send_home(dx)
    sum3 = jnp.concatenate([sum3, small_to([ln1, ln2, ln3, ln4, ln5, gdepth], me)], axis=1)
    if direct:
        sum1 = links.finish(sum1)
        sum2 = links.first(2, sum2)
        sum3 = links.first(3, sum3)
        held = [jnp.concatenate(v, axis=1) for v in zip(sum2, sum3)]
        tail = links.finish(links.next(links.next(held, 0), 1))
        sums = (sum0, sum1, tail)
        tables = (sum(SUMS[0], []), sum(SUMS[1], []))
        tables += (SUMS[2][0] + SUMS[3][0] + SUMS[2][1] + SUMS[3][1],)
    else:
        sums = [links.scatter_whole(k, v) for k, v in enumerate((sum0, sum1, sum2, sum3))]
        tables = [sum(items, []) for items in SUMS]
    out = {}
    for items, total in zip(tables, sums):
        out.update(links.rows_of(items, total))
    flat = out.pop("small")
    if not links.direct:
        flat = lax.all_gather(flat, AXES, axis=0, tiled=True).reshape(BLOCKS, -1)
    else:
        flat = flat.reshape(1, -1)
    at = 0
    for name, size in zip(SMALL, sizes):
        part = flat[:, at : at + size]
        at += size
        if not links.direct:
            own = mine[name].shape[0]
            here = lax.axis_index("seq") * n_dp + lax.axis_index("dp")
            part = lax.dynamic_slice(part.reshape(-1), (here * own,), (own,))
        out[name] = part.reshape(-1)
    return (
        mixed[None],
        dx.astype(F32)[None],
        *(out[name] for name in NAMES),
    )


def solution(mesh):
    token, owner, rows = P("dp", "seq", None), P(AXES), P(AXES, None)
    params = (owner,) * 5 + (rows,) * 3 + (owner,) + (rows,) * 5
    return jax.shard_map(
        on_device,
        mesh=mesh,
        in_specs=(token, token, P("dp")) + params,
        out_specs=(token, token) + params,
        check_vma=False,
    )
```

```python
import functools
import math

import jax
import jax.numpy as jnp
import numpy as np
from jax import lax
from jax.experimental import pallas as pl
from jax.experimental.pallas import tpu as pltpu
from jax.sharding import PartitionSpec as P

D = 512
HEADS = 8
FF = 2048
KERNEL = 9
HEAD = 64
NARROW = 256
HALF = KERNEL // 2
LANES = 128
PACK = 256
RIM = 16
BLOCKS = 32
F32 = jnp.float32
BF = jnp.bfloat16
LOG2E = math.log2(math.e)
BIG = -1e30
AXES = ("seq", "dp")
VMEM = 58 << 20


def nt(a, b):
    return lax.dot_general(a, b, (((1,), (1,)), ((), ())), preferred_element_type=F32)


def nn(a, b):
    return lax.dot_general(a, b, (((1,), (0,)), ((), ())), preferred_element_type=F32)


def tn(a, b):
    return lax.dot_general(a, b, (((0,), (0,)), ((), ())), preferred_element_type=F32)


def call(kernel, ins, outs, scratch=(), micros=0, ties=(), steps=None):
    if ties:
        inner, fixed, count = kernel, len(ins), len(ties)

        def kernel(*refs):
            inner(*refs[:fixed], *refs[fixed + count :])

    def spec(shape, how, once):
        if how == "s":
            return pl.BlockSpec(memory_space=pltpu.SMEM)
        if steps is None:
            return pl.BlockSpec(memory_space=pltpu.VMEM)
        if how is None:
            zeros = (0,) * len(shape)
            mode = pl.Buffered(1) if once else None
            return pl.BlockSpec(shape, lambda i: zeros, pipeline_mode=mode)
        return pl.BlockSpec((how, *shape[1:]), lambda i: (i, *(0,) * (len(shape) - 1)))

    args = [a for a, _ in ins]
    shapes = [jax.ShapeDtypeStruct(shape, dtype) for shape, dtype, _ in outs]
    moved = sum(math.prod(a.shape) * a.dtype.itemsize for a in args + shapes)
    return pl.pallas_call(
        kernel,
        out_shape=shapes,
        grid=() if steps is None else (steps,),
        in_specs=[spec(a.shape, how, True) for a, how in ins]
        + [pl.BlockSpec(memory_space=pl.ANY)] * len(ties),
        out_specs=[spec(shape, how, False) for shape, _, how in outs],
        scratch_shapes=[pltpu.VMEM(shape, dtype) for shape, dtype in scratch],
        compiler_params=pltpu.CompilerParams(vmem_limit_bytes=VMEM),
        cost_estimate=pl.CostEstimate(
            flops=int(micros * 1.15e9), bytes_accessed=moved, transcendentals=0
        ),
    )(*args, *ties)


def whole_call(kernel, outs, args, scratch=(), micros=0, ties=()):
    ins = [(a, "s" if i == 0 else None) for i, a in enumerate(args)]
    outs = [(shape, dtype, None) for shape, dtype in outs]
    return call(kernel, ins, outs, scratch, micros, ties)


def normalise(v):
    mean = jnp.mean(v, axis=1, keepdims=True)
    c = v - mean
    r = lax.rsqrt(jnp.mean(c * c, axis=1, keepdims=True) + 1e-05)
    return c * r, r


def norm_back(grad, hat, r, gain):
    g = grad * gain
    a = jnp.mean(g, axis=1, keepdims=True)
    b = jnp.mean(g * hat, axis=1, keepdims=True)
    return r * (g - a - hat * b)


C0 = math.sqrt(2.0 / math.pi)
C1 = 0.044715


def gelu(x):
    return 0.5 * x * (1.0 + jnp.tanh(x * (C0 + C0 * C1 * (x * x))))


def gelu_and_slope(x):
    xx = x * x
    t = jnp.tanh(x * (C0 + C0 * C1 * xx))
    half = 0.5 * (1.0 + t)
    return x * half, half + (0.5 * x) * (1.0 - t * t) * (C0 + 3.0 * C0 * C1 * xx)


def sigmoid(x):
    return 0.5 * jnp.tanh(0.5 * x) + 0.5


def fold8(v):
    return jnp.sum(v.reshape(v.shape[0] // 8, 8, v.shape[1]), axis=0)


def rows_at(i, tile, start=0):
    return pl.ds(pl.multiple_of(start + i * tile, 16), tile)


def places(base, rows, lanes=LANES):
    return base + lax.broadcasted_iota(jnp.int32, (rows, lanes), 0)


ROWS = {"glu": 16, "wide": 16, "narrow": 48, "point": 64, "qkv": 16, "attn": 16, "up": 16, "down": 64, "small": 16}


def columns_of(name, *chunks):
    return [(name, j) for j in chunks]


WIDE, GLU, QKV, UP = (columns_of(n, *range(k)) for n, k in (("wide", 8), ("glu", 4), ("qkv", 6), ("up", 8)))
NARROW_0, POINT_0, SMALL_0 = (columns_of(n, 0) for n in ("narrow", "point", "small"))
ATTN, DOWN = columns_of("attn", 0, 1), columns_of("down", 0, 1)
LAST = (UP + ATTN[:1], ATTN[1:] + DOWN)
GATHERS = ((WIDE + QKV[:5], GLU + NARROW_0 + SMALL_0 + QKV[5:] + POINT_0), LAST)
SUMS = (
    LAST,
    (QKV[:5], QKV[5:] + POINT_0),
    (WIDE[:6], WIDE[6:] + NARROW_0),
    (GLU[:2], GLU[2:] + SMALL_0),
)


def height(items):
    return sum(ROWS[name] for name, _ in items)


def row_of(items, item):
    return height(items[: items.index(item)])


def slot_bits(half, r):
    high, low, z = r >> 3, r >> 2 & 1, r & 3
    x, y = (high, low) if half == 0 else (low, high)
    return z * 8 + y * 4 + x * 2


def slot_of(half, rel):
    z, y, x, c = rel >> 3, rel >> 2 & 1, rel >> 1 & 1, rel & 1
    high, low = (x, y) if half == 0 else (y, x)
    return c * 16 + high * 8 + low * 4 + z


def unpack(me, group, pieces, wanted):
    for half, items in enumerate(GATHERS[group]):
        for core in range(2):
            piece = pieces[half * 2 + core]
            for r in range(BLOCKS // 2):
                owner = (slot_bits(half, r) + core) ^ me
                for name, j in items:
                    if name in wanted:
                        b, off = ROWS[name], row_of(items, (name, j))
                        wanted[name][
                            pl.ds(pl.multiple_of(owner * b, 16), b), j * PACK : (j + 1) * PACK
                        ] = piece[r, off : off + b, :]


def put(me, group, ref, item, value, start=0):
    half = int(item in SUMS[group][1])
    off = row_of(SUMS[group][half], item) + half * height(SUMS[group][0])
    b = ROWS[item[0]]
    for k in range(value.shape[0] // b):
        slot = slot_of(half, (start + k) ^ me)
        ref[slot, off : off + b, :] = value[k * b : (k + 1) * b]


def group_grads(group):
    return [((BLOCKS, height(sum(SUMS[group], [])), PACK), BF)]


SHAPES = {"glu": (D, 2 * D), "wide": (D, FF), "narrow": (3 * D, NARROW), "qkv": (D, 3 * D), "point": (FF, NARROW)}

GAINS = ((0, 16), (16, 16), (32, 64), (96, 16), (112, 16))
TAPS = 128
TAP_RUN = KERNEL * FF // BLOCKS
SMALL_ROWS = 3


def iota(shape, dim):
    return lax.broadcasted_iota(jnp.int32, shape, dim)


def owner_slots(me):
    shape = (BLOCKS, BLOCKS)
    return (slot_of(1, iota(shape, 0) ^ me) == iota(shape, 1)).astype(F32).astype(BF)


def gain_maps(offset, width):
    total = BLOCKS * width
    owner = iota((BLOCKS, total), 1) // width == iota((BLOCKS, total), 0)
    value = iota((LANES, total), 0) == offset + iota((LANES, total), 1) % width
    return owner, value.astype(F32).astype(BF)


def tap_runs():
    for b in range(KERNEL * FF // 64):
        f = b * 64
        yield f // FF, f % FF, f // TAP_RUN, TAPS + f % TAP_RUN


def read_small(me, pieces, gains, taps, table):
    off = row_of(GATHERS[0][1], SMALL_0[0])
    for core in range(2):
        for r in range(BLOCKS // 2):
            rows = pieces[2 + core][r, off : off + 16, :].astype(F32)
            slot = core * 16 + r
            for q in range(SMALL_ROWS):
                table[slot : slot + 1, q * PACK : (q + 1) * PACK] = rows[q : q + 1, :]
    table[...] = nn(owner_slots(me), table[...].astype(BF))
    for ref, (offset, width) in zip(gains, GAINS):
        owner, value = gain_maps(offset, width)
        spread = nn(table[:, :LANES].astype(BF), value)
        ref[...] = jnp.sum(jnp.where(owner, spread, 0.0), axis=0, keepdims=True)
    for tap, channel, who, place in tap_runs():
        taps[tap : tap + 1, channel : channel + 64] = table[who : who + 1, place : place + 64]


def write_small(me, gains, taps, table, block, grads):
    table[...] = jnp.zeros_like(table)
    total = jnp.zeros((BLOCKS, LANES), F32)
    for gain, (offset, width) in zip(gains, GAINS):
        owner, value = gain_maps(offset, width)
        total = total + nt(jnp.where(owner, gain[...], 0.0).astype(BF), value)
    table[:, :LANES] = total
    for tap, channel, who, place in tap_runs():
        table[who : who + 1, place : place + 64] = taps[tap : tap + 1, channel : channel + 64]
    table[...] = tn(owner_slots(me), table[...].astype(BF))
    block[...] = jnp.zeros_like(block)
    for slot in range(BLOCKS):
        for q in range(SMALL_ROWS):
            block[slot, q : q + 1, :] = table[slot : slot + 1, q * PACK : (q + 1) * PACK]
    at = height(GLU)
    grads[:, at : at + 16, :] = block[...].astype(BF)


def pack_kernel(names, *refs):
    shards = dict(zip(names, refs))
    for ref, halves in zip(refs[len(names) :], GATHERS):
        at = 0
        for name, j in sum(halves, []):
            b = ROWS[name]
            if name == "small":
                ref[at : at + b, :] = shards[name][...]
            else:
                ref[at : at + b, :] = shards[name][:, j * PACK : (j + 1) * PACK]
            at += b


def pack(shards):
    names = tuple(shards)
    return call(
        functools.partial(pack_kernel, names),
        [(shards[k], None) for k in names],
        [((height(sum(halves, [])), PACK), BF, None) for halves in GATHERS],
        micros=2,
    )


def front1_kernel(scal, x_ref, p0, p1, p2, p3, h1_ref, y2_ref, joined_ref, *refs):
    weights, gains, taps, table = refs[:5], refs[5:10], refs[10], refs[11]
    g1, g2 = gains[:2]

    @pl.when(pl.program_id(0) == 0)
    def _():
        read_small(scal[2], (p0, p1, p2, p3), gains, taps, table)
        unpack(scal[2], 0, (p0, p1, p2, p3), dict(zip(SHAPES, weights)))

    x = x_ref[...].astype(F32)
    hat, _ = normalise(x)
    joined = nn((hat * g1[...]).astype(BF), weights[0][...])
    joined_ref[...] = joined
    h1 = x + joined[:, :D] * sigmoid(joined[:, D:])
    h1_ref[...] = h1
    hat2, _ = normalise(h1)
    y2_ref[...] = (hat2 * g2[...]).astype(BF)


def front1(scal, x, pieces, ties=()):
    rows = x.shape[0]
    tile = 160
    return call(
        front1_kernel,
        [(scal, "s"), (x, tile)] + [(p, None) for p in pieces],
        [((rows, D), F32, tile), ((rows, D), BF, tile), ((rows, 2 * D), F32, tile)]
        + [(shape, BF, None) for shape in SHAPES.values()]
        + [((1, BLOCKS * width), F32, None) for _, width in GAINS]
        + [((KERNEL, FF), F32, None)],
        scratch=[((BLOCKS, SMALL_ROWS * PACK), F32)],
        micros=12,
        ties=ties,
        steps=rows // tile,
    )


def front2_kernel(tile, group, scal, y2_ref, g3, wide, narrow, left_ref, right_ref, mid_ref, u_ref):
    rows = y2_ref.shape[0]
    base = scal[0] * (rows - 2 * RIM) - RIM
    first = scal[1]
    i = pl.program_id(0)

    @pl.when(i == 0)
    def _():
        u_ref[0:RIM, :] = jnp.zeros((RIM, 3 * NARROW), F32)
        u_ref[RIM + rows : 2 * RIM + rows, :] = jnp.zeros((RIM, 3 * NARROW), F32)

        def narrow_step(j, carry):
            y = y2_ref[rows_at(j, tile), :]
            for k in range(3):
                u_ref[rows_at(j, tile, RIM), k * NARROW : (k + 1) * NARROW] = nn(
                    y, narrow[k * D : (k + 1) * D, :]
                )
            return carry

        lax.fori_loop(0, rows // tile, narrow_step, 0)

    around = pl.ds(pl.multiple_of(i * tile, 16), tile + 2 * RIM)
    left = nn(y2_ref[rows_at(i, tile), :], wide[...])
    left_ref[...] = left
    pos = places(base + i * tile, tile, NARROW)
    before = pltpu.roll(u_ref[around, 0:NARROW], 1, 0)[RIM : RIM + tile]
    after = pltpu.roll(u_ref[around, 2 * NARROW :], tile + 2 * RIM - 1, 0)[RIM : RIM + tile]
    right = u_ref[rows_at(i, tile, RIM), NARROW : 2 * NARROW]
    right = right + jnp.where((pos == first) | (pos == 0), 0.0, before)
    right = right + jnp.where((pos + 1 == first) | (pos + 1 == group), 0.0, after)
    right_ref[...] = right
    left = gelu(left)
    joined = jnp.concatenate([left[:, :NARROW] + gelu(right), left[:, NARROW:]], axis=1)
    hat, _ = normalise(joined)
    row = base + i * tile + lax.broadcasted_iota(jnp.int32, (tile, 1), 0)
    inside = ((row >= 0) & (row < group)).astype(F32)
    mid_ref[...] = (hat * inside * g3[...]).astype(BF)


def front2(scal, y2, g3, wide, narrow, group, ties=()):
    rows = y2.shape[0]
    tile = 160
    return call(
        functools.partial(front2_kernel, tile, group),
        [(scal, "s"), (y2, None), (g3, None), (wide, None), (narrow, None)],
        [((rows, FF), F32, tile), ((rows, NARROW), F32, tile), ((rows, FF), BF, tile)],
        scratch=[((rows + 2 * RIM, 3 * NARROW), F32)],
        micros=12,
        ties=ties,
        steps=rows // tile,
    )


def crosses(pos, offset, first):
    if offset > 0:
        return (pos < first) & (pos + offset >= first)
    return (pos >= first) & (pos + offset < first)


def conv(win, tile, taps, lanes, pos, first, masked, sign):
    total = None
    for k in range(KERNEL):
        o = sign * (k - HALF)
        v = win[RIM + o : RIM + o + tile, :]
        if masked and o != 0:
            v = jnp.where(crosses(pos, o, first), 0.0, v)
        v = v * taps[k : k + 1, lanes]
        total = v if total is None else total + v
    return total


def front3_kernel(tile, n, share, scal, mid_ref, taps, h1_ref, g4, point, qkv_w, *refs):
    spread_ref, h2_ref, y4_ref = refs[:3]
    outs = refs[3 : 3 + n]
    win, qkv_s = refs[3 + n :]
    i = pl.program_id(0)
    s, first = scal[0], scal[1]
    begin = s * (mid_ref.shape[0] - 2 * RIM) + i * tile
    near = (first > begin - HALF) & (first < begin + tile + HALF)

    def chunk(c, carry):
        lanes = pl.ds(pl.multiple_of(c * LANES, LANES), LANES)
        around = pl.ds(pl.multiple_of(i * tile, 16), tile + 2 * RIM)
        win[...] = mid_ref[around, lanes].astype(F32)
        pos = places(begin, tile)
        for masked in (False, True):

            @pl.when(near if masked else jnp.logical_not(near))
            def _():
                spread_ref[:, lanes] = conv(win, tile, taps, lanes, pos, first, masked, 1).astype(BF)

        return carry

    lax.fori_loop(0, FF // LANES, chunk, 0)
    h1 = h1_ref[rows_at(i, tile, RIM), :]
    branch = nn(spread_ref[...], point[...])
    h2 = jnp.concatenate([h1[:, :NARROW] + branch, h1[:, NARROW:]], axis=1)
    h2_ref[...] = h2
    hat, _ = normalise(h2)
    y4 = (hat * g4[...]).astype(BF)
    y4_ref[...] = y4
    qkv_s[...] = nn(y4, qkv_w[...]).astype(BF)
    for k in range(n):
        block = (s ^ k) // share
        for part in range(3):
            outs[k][:, part * LANES : (part + 1) * LANES] = qkv_s[
                :, pl.ds(pl.multiple_of(part * D + block * LANES, LANES), LANES)
            ]


def front3(scal, mid, taps, h1, g4, point, qkv_w, n, share, ties=()):
    rows = mid.shape[0] - 2 * RIM
    tile = 128
    return call(
        functools.partial(front3_kernel, tile, n, share),
        [(scal, "s")] + [(a, None) for a in (mid, taps, h1, g4, point, qkv_w)],
        [((rows, FF), BF, tile), ((rows, D), F32, tile), ((rows, D), BF, tile)]
        + [((rows, 3 * LANES), BF, tile)] * n,
        scratch=[((tile + 2 * RIM, LANES), F32), ((tile, 3 * D), BF)],
        micros=20,
        ties=ties,
        steps=rows // tile,
    )


def gather_lanes(wide_ref, n, share, s, blocks, parts):
    rows = wide_ref.shape[0]
    for k in range(n):
        block = (s ^ k) // share
        for part in range(parts):
            lanes = pl.ds(pl.multiple_of(part * D + block * LANES, LANES), LANES)
            new = blocks[k][:, part * LANES : (part + 1) * LANES]
            if share > 1:
                lane = lax.broadcasted_iota(jnp.int32, (rows, LANES), 1)
                mine = lane // (LANES // share) == (s ^ k) % share
                new = jnp.where(mine, new.astype(F32), wide_ref[:, lanes].astype(F32)).astype(BF)
            wide_ref[:, lanes] = new


def middle_kernel(n, share, scal, h2_ref, *refs):
    att = refs[:n]
    cot_ref, g5, p0, p1, p2, p3, mixed_ref, dh3_ref = refs[n : n + 8]
    datt = refs[n + 8 : 2 * n + 8]
    att_s, y5_s, inner_s, du_s, ln_out = refs[2 * n + 8 : 2 * n + 13]
    wa, wup, wdown, ln_ref = refs[2 * n + 13 :]
    s = scal[0]
    i = pl.program_id(0)

    @pl.when(i == 0)
    def _():
        unpack(scal[2], 1, (p0, p1, p2, p3), {"attn": wa, "up": wup, "down": wdown})
        ln_ref[...] = jnp.zeros_like(ln_ref)

    gather_lanes(att_s, n, share, s, att, 1)
    h3 = h2_ref[...] + nn(att_s[...], wa[...])
    hat, r = normalise(h3)
    y5 = (hat * g5[...]).astype(BF)
    y5_s[...] = y5
    value, slope = gelu_and_slope(nn(y5, wup[...]))
    inner = value.astype(BF)
    inner_s[...] = inner
    mixed_ref[...] = (h3 + nn(inner, wdown[...])).astype(BF)
    cot = cot_ref[...]
    du = (nt(cot, wdown[...]) * slope).astype(BF)
    du_s[...] = du
    dy5 = nt(du, wup[...])
    ln_ref[...] += fold8(dy5 * hat)
    dh3 = cot.astype(F32) + norm_back(dy5, hat, r, g5[...])
    dh3_ref[...] = dh3
    da = nt(dh3.astype(BF), wa[...]).astype(BF)
    for j in range(D // LANES):
        for k in range(n):

            @pl.when((s ^ k) // share == j)
            def _():
                datt[k][...] = da[:, j * LANES : (j + 1) * LANES]

    ln_out[...] = jnp.sum(ln_ref[...], axis=0, keepdims=True)


def middle(scal, h2, att, cot, g5, pieces, n, share, ties=()):
    rows = h2.shape[0]
    tile = 128
    return call(
        functools.partial(middle_kernel, n, share),
        [(scal, "s"), (h2, tile)]
        + [(a, tile) for a in (*att, cot)]
        + [(a, None) for a in (g5, *pieces)],
        [((rows, D), BF, tile), ((rows, D), F32, tile)]
        + [((rows, LANES), BF, tile)] * n
        + [((rows, c), BF, tile) for c in (D, D, FF, FF)]
        + [((1, D), F32, None)],
        scratch=[((D, D), BF), ((D, FF), BF), ((FF, D), BF), ((8, D), F32)],
        micros=20,
        ties=ties,
        steps=rows // tile,
    )


def weigh0_kernel(scal, att_s, y5_s, inner_s, du_s, cot_ref, dh3_ref, grads):
    me = scal[2]
    att_t = att_s[...].T
    for j in range(D // PACK):
        part = nn(att_t, dh3_ref[:, j * PACK : (j + 1) * PACK].astype(BF))
        put(me, 0, grads, ("attn", j), part.astype(BF))
    y5_t = y5_s[...].T
    for j in range(FF // PACK):
        cols = slice(j * PACK, (j + 1) * PACK)
        put(me, 0, grads, ("up", j), nn(y5_t, du_s[:, cols]).astype(BF))
        down = tn(inner_s[:, cols], cot_ref[...]).astype(BF)
        for m in range(D // PACK):
            put(me, 0, grads, ("down", m), down[:, m * PACK : (m + 1) * PACK], j * PACK // 64)


def weigh0(scal, att, y5, inner, du, cot, dh3, ties=()):
    return whole_call(
        weigh0_kernel, group_grads(0), [scal, att, y5, inner, du, cot, dh3], micros=10, ties=ties
    )


def back3_kernel(n, share, scal, *refs):
    blocks = refs[:n]
    dh3_ref, h2_ref, g4, qkv_w = refs[n : n + 4]
    dh2_ref, db_ref, dqkv_s, ln_out, ln_ref = refs[n + 4 :]

    @pl.when(pl.program_id(0) == 0)
    def _():
        ln_ref[...] = jnp.zeros_like(ln_ref)

    gather_lanes(dqkv_s, n, share, scal[0], blocks, 3)
    dy4 = nt(dqkv_s[...], qkv_w[...])
    hat, r = normalise(h2_ref[...])
    ln_ref[...] += fold8(dy4 * hat)
    dh2 = dh3_ref[...] + norm_back(dy4, hat, r, g4[...])
    dh2_ref[...] = dh2
    db_ref[...] = dh2[:, :NARROW].astype(BF)
    ln_out[...] = jnp.sum(ln_ref[...], axis=0, keepdims=True)


def back3(scal, blocks, dh3, h2, g4, qkv_w, n, share, ties=()):
    rows = h2.shape[0]
    tile = 128
    return call(
        functools.partial(back3_kernel, n, share),
        [(scal, "s")] + [(a, tile) for a in (*blocks, dh3, h2)] + [(g4, None), (qkv_w, None)],
        [((rows, D), F32, tile), ((rows, NARROW), BF, tile), ((rows, 3 * D), BF, tile)]
        + [((1, D), F32, None)],
        scratch=[((8, D), F32)],
        micros=6,
        ties=ties,
        steps=rows // tile,
    )


def weigh1_kernel(scal, y4_ref, dqkv_s, spread_ref, db_ref, grads):
    me = scal[2]
    y4_t = y4_ref[...].T
    for j in range(3 * D // PACK):
        part = nn(y4_t, dqkv_s[:, j * PACK : (j + 1) * PACK])
        put(me, 1, grads, ("qkv", j), part.astype(BF))
    for j in range(FF // PACK):
        part = tn(spread_ref[:, j * PACK : (j + 1) * PACK], db_ref[...]).astype(BF)
        put(me, 1, grads, ("point", 0), part, j * PACK // 64)


def weigh1(scal, y4, dqkv, spread, db, ties=()):
    return whole_call(
        weigh1_kernel, group_grads(1), [scal, y4, dqkv, spread, db], micros=8, ties=ties
    )


def back2_kernel(tile, group, scal, low_ref, db_ref, high_ref, *refs):
    taps, mid_ref, left_ref, right_ref, g3, point = refs[:6]
    dl, st, gdepth_out, ln_out = refs[6:10]
    dbx, dsp, win, dmid, dr, gdepth_ref, ln_ref = refs[10:]
    rows = db_ref.shape[0]
    ext = rows + 2 * RIM
    base = scal[0] * rows - RIM
    first = scal[1]
    i = pl.program_id(0)
    last = ext // tile - 1

    @pl.when(i == 0)
    def _():
        dbx[0:RIM, :] = low_ref[...]
        dbx[RIM : RIM + rows, :] = db_ref[...]
        dbx[RIM + rows :, :] = high_ref[...]
        dsp[0:RIM, :] = jnp.zeros((RIM, FF), F32)
        dsp[RIM + ext :, :] = jnp.zeros((RIM, FF), F32)
        dr[0:RIM, :] = jnp.zeros((RIM, NARROW), F32)
        dr[RIM + ext :, :] = jnp.zeros((RIM, NARROW), F32)
        gdepth_ref[...] = jnp.zeros_like(gdepth_ref)
        ln_ref[...] = jnp.zeros_like(ln_ref)

        def spread_step(j, carry):
            dsp[rows_at(j, tile, RIM), :] = nt(dbx[rows_at(j, tile), :], point[...])
            return carry

        lax.fori_loop(0, ext // tile, spread_step, 0)

    begin = base + i * tile
    near = (first > begin - HALF) & (first < begin + tile + HALF)
    near = near | (i == 0) | (i == last)

    def chunk(c, carry):
        lanes = pl.ds(pl.multiple_of(c * LANES, LANES), LANES)
        around = pl.ds(pl.multiple_of(i * tile, 16), tile + 2 * RIM)
        win[...] = dsp[around, lanes]
        local = i * tile + lax.broadcasted_iota(jnp.int32, (tile, LANES), 0)
        mid = mid_ref[:, lanes].astype(F32)
        pos = places(begin, tile)
        for masked in (False, True):

            @pl.when(near if masked else jnp.logical_not(near))
            def _():
                total = None
                for k in range(KERNEL):
                    o = HALF - k
                    v = win[RIM + o : RIM + o + tile, :]
                    if masked and o != 0:
                        v = jnp.where(crosses(pos, o, first), 0.0, v)
                    counted = v
                    if masked:
                        kept = (local + o >= RIM) & (local + o < RIM + rows)
                        counted = jnp.where(kept, v, 0.0)
                    gdepth_ref[k * 8 : (k + 1) * 8, lanes] += fold8(counted * mid)
                    v = v * taps[k : k + 1, lanes]
                    total = v if total is None else total + v
                dmid[:, lanes] = total

        return carry

    lax.fori_loop(0, FF // LANES, chunk, 0)
    left, slope = gelu_and_slope(left_ref[...])
    right, slope_r = gelu_and_slope(right_ref[...])
    joined = jnp.concatenate([left[:, :NARROW] + right, left[:, NARROW:]], axis=1)
    hat, r = normalise(joined)
    local = i * tile + lax.broadcasted_iota(jnp.int32, (tile, 1), 0)
    own = ((local >= RIM) & (local < RIM + rows)).astype(F32)
    pos = base + local
    grad = dmid[...] * ((pos >= 0) & (pos < group)).astype(F32)
    ln_ref[...] += fold8(grad * hat * own)
    dj = norm_back(grad, hat, r, g3[...])
    dl[...] = (dj * slope).astype(BF)
    dr[rows_at(i, tile, RIM), :] = (dj[:, :NARROW] * slope_r).astype(BF).astype(F32)

    @pl.when(i == last)
    def _():
        for k in range(KERNEL):
            gdepth_out[k : k + 1, :] = jnp.sum(
                gdepth_ref[k * 8 : (k + 1) * 8, :], axis=0, keepdims=True
            )
        ln_out[...] = jnp.sum(ln_ref[...], axis=0, keepdims=True)
        part = 128

        def gather_step(j, carry):
            at = rows_at(j, part)
            around = pl.ds(pl.multiple_of(RIM + j * part, 16), part + 2 * RIM)
            pos = places(base + RIM + j * part, part, NARROW)
            v = dr[around, :]
            after = pltpu.roll(v, part + 2 * RIM - 1, 0)[RIM : RIM + part]
            before = pltpu.roll(v, 1, 0)[RIM : RIM + part]
            after = jnp.where((pos + 1 == first) | (pos + 1 == group), 0.0, after)
            before = jnp.where((pos == first) | (pos == 0), 0.0, before)
            st[at, 0:NARROW] = after.astype(BF)
            st[at, NARROW : 2 * NARROW] = v[RIM : RIM + part].astype(BF)
            st[at, 2 * NARROW :] = before.astype(BF)
            return carry

        lax.fori_loop(0, rows // part, gather_step, 0)


def back2(scal, low, db, high, taps, mid, left, right, g3, point, group, ties=()):
    rows = db.shape[0]
    ext = rows + 2 * RIM
    tile = 160
    return call(
        functools.partial(back2_kernel, tile, group),
        [(scal, "s")]
        + [(a, None) for a in (low, db, high, taps)]
        + [(a, tile) for a in (mid, left, right)]
        + [(g3, None), (point, None)],
        [((ext, FF), BF, tile), ((rows, 3 * NARROW), BF, None)]
        + [((KERNEL, FF), F32, None), ((1, FF), F32, None)],
        scratch=[
            ((ext, NARROW), BF),
            ((ext + 2 * RIM, FF), F32),
            ((tile + 2 * RIM, LANES), F32),
            ((tile, FF), F32),
            ((ext + 2 * RIM, NARROW), F32),
            ((8 * KERNEL, FF), F32),
            ((8, FF), F32),
        ],
        micros=44,
        ties=ties,
        steps=ext // tile,
    )


def weigh2_kernel(scal, dl, st, y2_ref, grads, gn):
    me = scal[2]
    rows = st.shape[0]
    y2_t = y2_ref[RIM : RIM + rows, :].T
    for j in range(FF // PACK):
        part = nn(y2_t, dl[RIM : RIM + rows, j * PACK : (j + 1) * PACK]).astype(BF)
        put(me, 2, grads, ("wide", j), part)
    for k in range(3):
        gn[k * D : (k + 1) * D, :] = nn(y2_t, st[:, k * NARROW : (k + 1) * NARROW]).astype(BF)
    put(me, 2, grads, ("narrow", 0), gn[...])


def weigh2(scal, dl, st, y2, ties=()):
    return whole_call(
        weigh2_kernel,
        group_grads(2),
        [scal, dl, st, y2],
        scratch=[((3 * D, NARROW), BF)],
        ties=ties,
        micros=7,
    )


def back1_kernel(tile, scal, dl, st, dh2_ref, h1_ref, joined_ref, x_ref, g1, g2, *refs):
    glu, wide, narrow, ln3, ln4, ln5, gdepth, dx_ref, grads = refs[:9]
    y1_s, dj_s, ln1_ref, ln2_ref, ln1, ln2, table, block = refs[9:]
    i = pl.program_id(0)

    @pl.when(i == 0)
    def _():
        ln1_ref[...] = jnp.zeros_like(ln1_ref)
        ln2_ref[...] = jnp.zeros_like(ln2_ref)

    at = rows_at(i, tile)
    ext = rows_at(i, tile, RIM)
    dy2 = nt(dl[ext, :], wide[...])
    for k in range(3):
        dy2 = dy2 + nt(st[:, k * NARROW : (k + 1) * NARROW], narrow[k * D : (k + 1) * D, :])
    hat2, r2 = normalise(h1_ref[ext, :])
    ln2_ref[...] += fold8(dy2 * hat2)
    dh1 = dh2_ref[...] + norm_back(dy2, hat2, r2, g2[...])
    gate = sigmoid(joined_ref[ext, D:])
    value = joined_ref[ext, :D]
    da = (dh1 * gate).astype(BF)
    db = (dh1 * value * gate * (1.0 - gate)).astype(BF)
    dj_s[at, :D] = da
    dj_s[at, D:] = db
    x = x_ref[ext, :].astype(F32)
    hat1, r1 = normalise(x)
    y1_s[at, :] = (hat1 * g1[...]).astype(BF)
    dy1 = nt(dj_s[at, :], glu[...])
    ln1_ref[...] += fold8(dy1 * hat1)
    dx_ref[...] = (dh1 + norm_back(dy1, hat1, r1, g1[...])).astype(dx_ref.dtype)

    @pl.when(i == pl.num_programs(0) - 1)
    def _():
        ln1[...] = jnp.sum(ln1_ref[...], axis=0, keepdims=True)
        ln2[...] = jnp.sum(ln2_ref[...], axis=0, keepdims=True)
        write_small(scal[2], (ln1, ln2, ln3, ln4, ln5), gdepth, table, block, grads)
        y1_t = y1_s[...].T
        for j in range(2 * D // PACK):
            part = nn(y1_t, dj_s[:, j * PACK : (j + 1) * PACK]).astype(BF)
            put(scal[2], 3, grads, ("glu", j), part)


def back1(scal, dl, st, dh2, h1, joined, x, g1, g2, glu, wide, narrow, small, ties=()):
    rows = st.shape[0]
    tile = 128
    return call(
        functools.partial(back1_kernel, tile),
        [(scal, "s"), (dl, None), (st, tile), (dh2, tile)]
        + [(a, None) for a in (h1, joined, x, g1, g2, glu, wide, narrow, *small)],
        [((rows, D), BF, tile), (*group_grads(3)[0], None)],
        scratch=[((rows, D), BF), ((rows, 2 * D), BF), ((8, D), F32), ((8, D), F32)]
        + [((1, D), F32), ((1, D), F32), ((BLOCKS, SMALL_ROWS * PACK), F32), ((BLOCKS, 16, PACK), F32)],
        micros=18,
        ties=ties,
        steps=rows // tile,
    )


def lane_maps(rows, head):
    lane = lax.broadcasted_iota(jnp.int32,(rows,LANES),1)
    own = (lane >= head*HEAD) & (lane < (head+1)*HEAD)
    rel = lane - (1-head)*HEAD
    return own, rel

def id_column(base, rows, first):
    pos = base + lax.broadcasted_iota(jnp.int32,(rows,LANES),0)
    return pos >= first

def split3(v):
    hi = v.astype(BF).astype(F32)
    mid = (v-hi).astype(BF).astype(F32)
    return hi, mid, v-hi-mid

def tile_ids(start, rows, first):
    return start < first, start+rows > first

def overlap(a_start,a_rows,b_start,b_rows,first):
    a0,a1 = tile_ids(a_start,a_rows,first); b0,b1=tile_ids(b_start,b_rows,first)
    return (a0&b0)|(a1&b1)

def attend_kernel(n, heads, share, tq, tk, scal, *refs):
    qkv = refs[:n]; att = refs[n:2*n]; lse_ref = refs[2*n]
    qa, ka, va, mx_ref, m_ref, q2_ref, acc_ref = refs[2*n+1:]
    s = scal[0]; first = scal[1]
    rows = qkv[0].shape[0]
    for k in range(n):
        base = (s ^ k)*rows
        id1 = id_column(base, rows, first).astype(F32)
        q = qkv[k][:, 0:LANES].astype(F32)*(HEAD**-0.5)
        key = qkv[k][:, LANES:2*LANES].astype(F32)
        v = qkv[k][:, 2*LANES:3*LANES].astype(F32)
        for i in range(heads):
            h = i if share==1 else s % share
            own, rel = lane_maps(rows, h)
            qx = jnp.where(rel==0, 1.0-id1, jnp.where(rel==1, id1, 0.0))
            kx = jnp.where(rel==0, id1*BIG, jnp.where(rel==1, (1.0-id1)*BIG, jnp.where(rel<5,1.0,0.0)))
            qa[i, k*rows:(k+1)*rows,:] = jnp.where(own, q, qx).astype(BF)
            ka[i, k*rows:(k+1)*rows,:] = jnp.where(own, key, kx).astype(BF)
            va[i, k*rows:(k+1)*rows,:] = jnp.where(own, v, 1.0).astype(BF)
    per = rows//tq; per_k = rows//tk
    def fold(sc, best):
        for j in range(tk//LANES):
            best = jnp.maximum(best, sc[:, j*LANES:(j+1)*LANES])
        return best
    def q_step(it, carry):
        kq = it//per
        r0 = pl.multiple_of((it % per)*tq, tq)
        g0 = pl.multiple_of(it*tq, tq)
        own0 = pl.multiple_of((g0//tk)*tk, tk)
        q_start = (s ^ kq)*rows + r0
        for i in range(heads):
            for j in range(max(1,tq//tk)):
                sc = nt(qa[i, pl.ds(g0,tq),:], ka[i, pl.ds(own0+j*tk,tk),:])
                best = fold(sc, sc[:, :LANES] if j==0 else best)
            mx_ref[i] = best
            m_ref[i] = jnp.zeros((tq,LANES),F32)
        def attempt(again):
            for i in range(heads):
                h = i if share==1 else s % share
                own, rel = lane_maps(tq, h)
                m = jnp.max(mx_ref[i], axis=1, keepdims=True)
                mb = m_ref[i] + jnp.broadcast_to(m, (tq,LANES))
                m_ref[i] = mb
                hi,mid,lo = split3(-mb)
                q = qa[i, pl.ds(g0,tq),:].astype(F32)
                q2_ref[i] = jnp.where(rel==2,hi,jnp.where(rel==3,mid,jnp.where(rel==4,lo,q))).astype(BF)
            mx_ref[...] = jnp.full_like(mx_ref, -3e38)
            acc_ref[...] = jnp.zeros_like(acc_ref)
            for kt in range(n*per_k):
                k_start = (s ^ (kt//per_k))*rows + (kt%per_k)*tk
                @pl.when(overlap(q_start,tq,k_start,tk,first))
                def _():
                    for i in range(heads):
                        sc = nt(q2_ref[i], ka[i, kt*tk:(kt+1)*tk,:])
                        mx_ref[i] = fold(sc, mx_ref[i])
                        p = jnp.exp2(sc*LOG2E).astype(BF)
                        acc_ref[i] += nn(p, va[i, kt*tk:(kt+1)*tk,:])
            return (jnp.max(mx_ref[...]) > 40.0).astype(jnp.int32)
        lax.while_loop(lambda again: again > 0, attempt, jnp.int32(1))
        out = jnp.zeros((tq,LANES),F32); lse = jnp.zeros((tq,LANES),F32)
        for i in range(heads):
            h = i if share==1 else s % share
            own,_ = lane_maps(tq,h)
            acc = acc_ref[i]
            total = pltpu.roll(acc, HEAD, 1)
            out = jnp.where(own, acc/total, out)
            lse = jnp.where(own, m_ref[i]+jnp.log(total), lse)
        lse_ref[pl.ds(g0,tq),:] = lse
        for k in range(n):
            @pl.when(kq==k)
            def _():
                att[k][pl.ds(r0,tq),:] = out.astype(BF)
        return carry
    lax.fori_loop(0, n*per, q_step, 0)

def attend(scal, blocks, n, share, tq=768, tk=384, ties=()):
    rows = blocks[0].shape[0]
    heads = 2 // share
    return whole_call(
        functools.partial(attend_kernel, n, heads, share, tq, tk),
        [((rows, LANES), BF)] * n + [((n * rows, LANES), F32)],
        [scal, *blocks],
        scratch=[((heads, n * rows, LANES), BF)] * 3
        + [((heads, tq, LANES), F32)] * 2
        + [((heads, tq, LANES), BF), ((heads, tq, LANES), F32)],
        ties=ties,
        micros=36,
    )


def attend_back_kernel(n, heads, share, tq, tk, scal, *refs):
    qkv = refs[:n]; att = refs[n:2*n]; dat = refs[2*n:3*n]; lse_ref = refs[3*n]
    out = refs[3*n+1:4*n+1]
    qa, ka, va, da, dq_ref, dk_ref, dv_ref = refs[4*n+1:]
    s = scal[0]; first = scal[1]
    rows = qkv[0].shape[0]
    for k in range(n):
        base = (s ^ k)*rows
        sl = slice(k*rows,(k+1)*rows)
        id1 = id_column(base, rows, first).astype(F32)
        q = qkv[k][:, 0:LANES].astype(F32)*(HEAD**-0.5)
        key = qkv[k][:, LANES:2*LANES].astype(F32)
        v = qkv[k][:, 2*LANES:3*LANES].astype(F32)
        do = dat[k][...].astype(F32)
        prod = do*att[k][...].astype(F32)
        for i in range(heads):
            h = i if share==1 else s % share
            own, rel = lane_maps(rows, h)
            lse = pltpu.roll(lse_ref[sl,:], HEAD, 1)
            hi,mid,lo = split3(-lse)
            delta = jnp.sum(jnp.where(own,prod,0.0),axis=1,keepdims=True)
            dhi,dmid,dlo = split3(-delta)
            qx = jnp.where(rel==0, 1.0-id1, jnp.where(rel==1, id1, jnp.where(rel==2,hi,jnp.where(rel==3,mid,jnp.where(rel==4,lo,0.0)))))
            kx = jnp.where(rel==0, id1*BIG, jnp.where(rel==1, (1.0-id1)*BIG, jnp.where(rel<5,1.0,0.0)))
            vx = jnp.where(rel<3,1.0,0.0)
            dx = jnp.where(rel==0,dhi,jnp.where(rel==1,dmid,jnp.where(rel==2,dlo,0.0)))
            qa[i,sl,:] = jnp.where(own,q,qx).astype(BF)
            ka[i,sl,:] = jnp.where(own,key,kx).astype(BF)
            va[i,sl,:] = jnp.where(own,v,vx).astype(BF)
            da[i,sl,:] = jnp.where(own,do,dx).astype(BF)
    dq_ref[...] = jnp.zeros_like(dq_ref)
    per_q = rows//tq; per_k = rows//tk
    def k_step(kt, carry):
        k0 = pl.multiple_of(kt*tk, tk)
        kk = kt//per_k
        k_start = (s ^ kk)*rows + (kt % per_k)*tk
        for i in range(heads):
            dk_ref[i] = jnp.zeros((tk,LANES),F32)
            dv_ref[i] = jnp.zeros((tk,LANES),F32)
        def q_step(qt, c2):
            q0 = pl.multiple_of(qt*tq, tq)
            q_start = (s ^ (qt//per_q))*rows + (qt % per_q)*tq
            @pl.when(overlap(q_start,tq,k_start,tk,first))
            def _():
                for i in range(heads):
                    qq = qa[i,pl.ds(q0,tq),:]; kx = ka[i,pl.ds(k0,tk),:]; dd = da[i,pl.ds(q0,tq),:]
                    st = nt(kx, qq)
                    p = jnp.exp2(st*LOG2E)
                    dp = nt(va[i,pl.ds(k0,tk),:], dd)
                    ds = (p*dp).astype(BF)
                    dv_ref[i] += nn(p.astype(BF), dd)
                    dk_ref[i] += nn(ds, qq)
                    dq_ref[i,pl.ds(q0,tq),:] += tn(ds, kx)
            return c2
        lax.fori_loop(0, n*per_q, q_step, 0)
        dk = jnp.zeros((tk,LANES),F32); dv = jnp.zeros((tk,LANES),F32)
        for i in range(heads):
            h = i if share==1 else s % share
            own,_ = lane_maps(tk,h)
            dk = jnp.where(own, dk_ref[i], dk); dv = jnp.where(own, dv_ref[i], dv)
        r0 = pl.multiple_of((kt % per_k)*tk, tk)
        for k in range(n):
            @pl.when(kk==k)
            def _():
                out[k][pl.ds(r0,tk),LANES:2*LANES] = dk.astype(BF)
                out[k][pl.ds(r0,tk),2*LANES:3*LANES] = dv.astype(BF)
        return carry
    lax.fori_loop(0, n*per_k, k_step, 0)
    for k in range(n):
        sl = slice(k*rows,(k+1)*rows)
        dq = jnp.zeros((rows,LANES),F32)
        for i in range(heads):
            h = i if share==1 else s % share
            own,_ = lane_maps(rows,h)
            dq = jnp.where(own, dq_ref[i,sl,:], dq)
        out[k][:, 0:LANES] = (dq*(HEAD**-0.5)).astype(BF)

def attend_back(scal, blocks, att, datt, lse, n, share, tq=384, tk=384, ties=()):
    rows = blocks[0].shape[0]
    heads = 2 // share
    return whole_call(
        functools.partial(attend_back_kernel, n, heads, share, tq, tk),
        [((rows, 3 * LANES), BF)] * n,
        [scal, *blocks, *att, *datt, lse],
        scratch=[((heads, n * rows, LANES), BF)] * 4
        + [((heads, n * rows, LANES), F32)]
        + [((heads, tk, LANES), F32)] * 2,
        ties=ties,
        micros=58,
    )


class Links:
    def __init__(self, n_seq, n_dp):
        self.count = n_seq * n_dp
        self.direct = (n_seq, n_dp) == (4, 8)

    def flip(self, value, mask):
        return lax.ppermute(value, AXES, [(i, i ^ mask) for i in range(self.count)])

    def near(self, block):
        return jnp.stack([block] + [self.flip(block, k << 3) for k in range(1, 4)])

    def part(self, group, held):
        low = height(GATHERS[group][0])
        return [held[:, :low], held[:, low:]]

    def spread(self, held, stage):
        masks = ((4, 2), (2, 4))[stage]
        return [jnp.concatenate([h, self.flip(h, m)]) for h, m in zip(held, masks)]

    def across(self, held):
        return [held[0], self.flip(held[0], 1), held[1], self.flip(held[1], 1)]

    def gather_whole(self, group, weights):
        whole = {
            name: lax.all_gather(weights[name], AXES, axis=0, tiled=True)
            for name in dict(sum(GATHERS[group], []))
        }
        pieces = []
        for half, items in enumerate(GATHERS[group]):
            blocks = [
                whole[name][:, j * PACK : (j + 1) * PACK].reshape(BLOCKS, -1, PACK)
                for name, j in items
            ]
            pieces += list(self.by_slot(jnp.concatenate(blocks, axis=1), half))
        return pieces

    def by_slot(self, blocks, half):
        shape = blocks.shape[1:]
        order = ((3, 2, 1, 0), (3, 1, 2, 0))[half]
        return blocks.reshape(4, 2, 2, 2, *shape).transpose(*order, 4, 5).reshape(2, 16, *shape)

    def by_owner(self, slots, half):
        shape = slots.shape[1:]
        order = ((3, 2, 1, 0), (3, 1, 2, 0))[half]
        return slots.reshape(2, 2, 2, 4, *shape).transpose(*order, 4, 5).reshape(BLOCKS, *shape)

    def add(self, a, b):
        return (a.astype(F32) + b.astype(F32)).astype(BF)

    def fold(self, slots, mask):
        middle = slots.shape[0] // 2
        return self.add(slots[:middle], self.flip(slots[middle:], mask))

    def first(self, group, slots):
        held = self.fold(slots, 1)
        low = height(SUMS[group][0])
        return [held[:, :low], held[:, low:]]

    def next(self, held, stage):
        masks = ((2, 4), (4, 2))[stage]
        return [self.fold(h, m) for h, m in zip(held, masks)]

    def finish(self, held):
        held = jnp.concatenate(held, axis=1)
        total = held[0].astype(F32)
        for k in range(1, 4):
            total = total + self.flip(held[k], k << 3).astype(F32)
        return total

    def rows_of(self, items, total):
        parts, at = {}, 0
        for name, j in items:
            b = ROWS[name] * BLOCKS // self.count
            parts.setdefault(name, []).append(total[at : at + b])
            at += b
        return {name: jnp.concatenate(p, axis=1) for name, p in parts.items()}

    def scatter_whole(self, group, slots):
        sent, at = [], 0
        for half, items in enumerate(SUMS[group]):
            for name, _ in items:
                blocks = self.by_owner(slots[:, at : at + ROWS[name]], half)
                sent.append(blocks.reshape(self.count, -1, PACK))
                at += ROWS[name]
        sent = jnp.concatenate(sent, axis=1)
        return lax.psum_scatter(sent, AXES, scatter_dimension=0, tiled=False).astype(F32)


class Layout:
    def __init__(self, n_seq, n_dp):
        self.n_seq, self.n_dp = n_seq, n_dp
        self.where = {}
        for g in range(n_dp):
            for s in range(n_seq):
                self.where[g, s] = self.place(g, s)
        self.block = np.zeros(n_seq * n_dp, np.int32)
        for (g, s), device in self.where.items():
            self.block[device] = s

    def place(self, g, s):
        if (self.n_seq, self.n_dp) == (4, 8):
            y, x, c = g >> 2, g >> 1 & 1, g & 1
            return (2 * c + y) * 8 + (s & 1) * 4 + x * 2 + (s >> 1)
        return s * self.n_dp + g

    def pairs(self, source, target):
        return [
            (source(g, s), target(g, s))
            for g in range(self.n_dp)
            for s in range(self.n_seq)
            if target(g, s) is not None and source(g, s) is not None
        ]

    def at(self, g, s):
        return self.where.get((g, s))

    def home(self, g, s):
        return s * self.n_dp + g

    def bring(self, value):
        return lax.ppermute(value, AXES, self.pairs(self.home, self.at))

    def bring_to(self, value, step):
        return lax.ppermute(
            value, AXES, self.pairs(self.home, lambda g, s: self.at(g, s + step))
        )

    def send_home(self, value):
        return lax.ppermute(value, AXES, self.pairs(self.at, self.home))

    def to_neighbour(self, value, step):
        return lax.ppermute(value, AXES, self.pairs(self.at, lambda g, s: self.at(g, s + step)))

    def swap(self, values):
        return [values[0]] + [
            lax.ppermute(values[k], AXES, self.pairs(self.at, lambda g, s: self.at(g, s ^ k)))
            for k in range(1, self.n_seq)
        ]


NAMES = ("ln1", "ln2", "ln3", "ln4", "ln5", "glu", "wide", "narrow", "depth", "point", "qkv", "attn", "up", "down")
SMALL = ("ln1", "ln2", "ln3", "ln4", "ln5", "depth")


def sync(*values):
    return lax.optimization_barrier(values)


def small_block(arrays, blocks):
    flat = jnp.concatenate([a.reshape(blocks, -1) for a in arrays], axis=1)
    flat = jnp.pad(flat, ((0, 0), (0, 16 * PACK - flat.shape[1])))
    return flat.reshape(blocks * 16, PACK)


def on_device(tokens, cotangent, first_length, *weights):
    n = lax.axis_size("seq")
    n_dp = lax.axis_size("dp")
    share = n * LANES // D
    layout = Layout(n, n_dp)
    links = Links(n, n_dp)
    direct = links.direct
    rows = tokens.shape[1]
    group = n * rows
    here = lax.axis_index("seq") * n_dp + lax.axis_index("dp")
    me = here if direct else jnp.zeros_like(here)
    s = jnp.asarray(layout.block)[here]
    mine = dict(zip(NAMES, weights))
    if direct:
        mine["small"] = small_block([mine[k] for k in SMALL], 1)
    else:
        small = [lax.all_gather(mine[k], AXES, axis=0, tiled=True) for k in SMALL]
        mine["small"] = small_block(small, BLOCKS).reshape(links.count, -1, PACK)[here]

    tokens = tokens[0]
    digits = jnp.where(
        lax.broadcasted_iota(jnp.int32, (RIM, D), 1) < LANES,
        first_length[0] // LANES,
        first_length[0] % LANES,
    )
    sent = jnp.concatenate([tokens, digits.astype(BF)], axis=0)
    if direct:
        packed, packed_late = pack({k: mine[k] for k in mine if k not in SMALL})
        packed, sent, packed_late = sync(packed, sent, packed_late)
        held = links.near(packed)
    x = layout.bring(sent)
    if direct:
        held, x = sync(held, x)
        held = links.spread(links.part(0, held), 0)
    low = layout.bring_to(tokens[-RIM:], 1)
    high = layout.bring_to(tokens[:RIM], -1)
    if direct:
        held, x, low, high = sync(held, x, low, high)
        held, packed_late = sync(links.spread(held, 1), packed_late)
        pieces1 = links.across(held)
        late = links.near(packed_late)
    else:
        pieces1, pieces2 = (links.gather_whole(k, mine) for k in range(2))
    digits = x[rows, 0 : 2 * LANES : LANES].astype(F32).astype(jnp.int32)
    first = digits[0] * LANES + digits[1]
    scal = jnp.stack([s.astype(jnp.int32), first, me.astype(jnp.int32)])
    x_ext = jnp.concatenate([low, x[:rows], high], axis=0)

    h1, y2, joined, *rest = front1(scal, x_ext, pieces1)
    (glu, wide, narrow, qkv_w, point), (g1, g2, g3, g4, g5, taps) = rest[:5], rest[5:]
    left, right, mid = front2(scal, y2, g3, wide, narrow, group)
    if direct:
        mid, late = sync(mid, late)
        late = links.spread(links.part(1, late), 0)
    spread, h2, y4, *qkv = front3(scal, mid, taps, h1, g4, point, qkv_w, n, share)
    if direct:
        qkv, late = sync(qkv, late)
    qkv = layout.swap(qkv)
    qkv, cot = sync(qkv, cotangent[0])
    cot = layout.bring(cot)
    if direct:
        late, qkv = sync(late, qkv)
        late = links.spread(late, 1)
    *att, lse = attend(scal, qkv, n, share)
    if direct:
        att, late, cot = sync(att, late, cot)
        pieces2 = links.across(late)
    else:
        att, cot = sync(att, cot)
    arrived = layout.swap(att)
    mixed, dh3, *rest = middle(scal, h2, arrived, cot, g5, pieces2, n, share)
    datt, (att_all, y5, inner, du, ln5) = rest[:n], rest[n:]
    datt, du = sync(datt, du)
    datt = layout.swap(datt)
    (sum0,) = weigh0(scal, att_all, y5, inner, du, cot, dh3)
    datt, sum0 = sync(datt, sum0)
    if direct:
        sum0 = links.first(0, sum0)
    dqkv = attend_back(scal, qkv, att, datt, lse, n, share)
    dqkv, sum0 = sync(dqkv, sum0)
    dqkv = layout.swap(dqkv)
    dqkv, sum0 = sync(dqkv, sum0)
    if direct:
        sum0 = links.next(sum0, 0)
    dh2, db, dqkv, ln4 = back3(scal, dqkv, dh3, h2, g4, qkv_w, n, share)
    db, dqkv = sync(db, dqkv)
    low = layout.to_neighbour(db[-RIM:], 1)
    high = layout.to_neighbour(db[:RIM], -1)
    (sum1,) = weigh1(scal, y4, dqkv, spread, db)
    low, high, sum1, sum0 = sync(low, high, sum1, sum0)
    if direct:
        sum1 = links.first(1, sum1)
        low, high, sum1, sum0, mixed = sync(low, high, sum1, sum0, mixed)
        sum0 = links.next(sum0, 1)
        sum1 = links.next(sum1, 0)
    mixed = layout.send_home(mixed)
    dl, st, gdepth, ln3 = back2(scal, low, db, high, taps, mid, left, right, g3, point, group)
    dl, st, sum0, sum1, mixed = sync(dl, st, sum0, sum1, mixed)
    if direct:
        sum1 = links.next(sum1, 1)
    (sum2,) = weigh2(scal, dl, st, y2)
    sum2, sum1, sum0 = sync(sum2, sum1, sum0)
    if direct:
        tail0 = links.finish([*sum0, *sum1])
        sum2 = links.first(2, sum2)
    small = (ln3, ln4, ln5, gdepth)
    dx, sum3 = back1(
        scal, dl, st, dh2, h1, joined, x_ext, g1, g2, glu, wide, narrow, small
    )
    if direct:
        dx, sum3, sum2, tail0 = sync(dx, sum3, sum2, tail0)
        sum3 = links.first(3, sum3)
        held = sync(*(jnp.concatenate(v, axis=1) for v in zip(sum2, sum3)))
        held = sync(*links.next(held, 0))
        held = sync(*links.next(held, 1))
        sums = (tail0, links.finish(held))
        tables = (sum([*SUMS[0], *SUMS[1]], []),)
        tables += (SUMS[2][0] + SUMS[3][0] + SUMS[2][1] + SUMS[3][1],)
    else:
        sums = [links.scatter_whole(k, v) for k, v in enumerate((sum0, sum1, sum2, sum3))]
        tables = [sum(items, []) for items in SUMS]
    dx = layout.send_home(dx)
    out = {}
    for items, total in zip(tables, sums):
        out.update(links.rows_of(items, total))
    flat = out.pop("small")
    if not direct:
        flat = lax.all_gather(flat, AXES, axis=0, tiled=True)
    flat = flat.reshape(-1, 16 * PACK)
    sizes = [width for _, width in GAINS] + [TAP_RUN]
    at = 0
    for name, size in zip(SMALL, sizes):
        part = flat[:, at : at + size].reshape(-1)
        at += size
        if not direct:
            own = mine[name].shape[0]
            part = lax.dynamic_slice(part, (here * own,), (own,))
        out[name] = part
    return (mixed[None], dx.astype(F32)[None], *(out[name] for name in NAMES))


def solution(mesh):
    token, owner, rows = P("dp", "seq", None), P(AXES), P(AXES, None)
    params = (owner,) * 5 + (rows,) * 3 + (owner,) + (rows,) * 5
    return jax.shard_map(
        on_device,
        mesh=mesh,
        in_specs=(token, token, P("dp")) + params,
        out_specs=(token, token) + params,
        check_vma=False,
    )
```

```python
import functools
import math

import jax
import jax.numpy as jnp
import numpy as np
from jax import lax
from jax.experimental import pallas as pl
from jax.experimental.pallas import tpu as pltpu
from jax.sharding import PartitionSpec as P

D = 512
HEADS = 8
FF = 2048
KERNEL = 9
HEAD = 64
NARROW = 256
HALF = KERNEL // 2
LANES = 128
PACK = 256
RIM = 16
BLOCKS = 32
F32 = jnp.float32
BF = jnp.bfloat16
LOG2E = math.log2(math.e)
BIG = -1e30
AXES = ("seq", "dp")
VMEM = 58 << 20


def nt(a, b):
    return lax.dot_general(a, b, (((1,), (1,)), ((), ())), preferred_element_type=F32)


def nn(a, b):
    return lax.dot_general(a, b, (((1,), (0,)), ((), ())), preferred_element_type=F32)


def tn(a, b):
    return lax.dot_general(a, b, (((0,), (0,)), ((), ())), preferred_element_type=F32)


def call(kernel, ins, outs, scratch=(), micros=0, ties=(), steps=None):
    if ties:
        inner, fixed, count = kernel, len(ins), len(ties)

        def kernel(*refs):
            inner(*refs[:fixed], *refs[fixed + count :])

    def spec(shape, how, once):
        if how == "s":
            return pl.BlockSpec(memory_space=pltpu.SMEM)
        if steps is None:
            return pl.BlockSpec(memory_space=pltpu.VMEM)
        if isinstance(how, tuple):
            tile, start = how
            block = tuple(pl.Element(b) for b in (tile, *shape[1:]))
            rest = (0,) * (len(shape) - 1)
            return pl.BlockSpec(block, lambda i: (pl.multiple_of(start + i * tile, 16), *rest))
        if how is None:
            zeros = (0,) * len(shape)
            mode = pl.Buffered(1) if once else None
            return pl.BlockSpec(shape, lambda i: zeros, pipeline_mode=mode)
        return pl.BlockSpec((how, *shape[1:]), lambda i: (i, *(0,) * (len(shape) - 1)))

    args = [a for a, _ in ins]
    shapes = [jax.ShapeDtypeStruct(shape, dtype) for shape, dtype, _ in outs]
    moved = sum(math.prod(a.shape) * a.dtype.itemsize for a in args + shapes) if micros else 0
    return pl.pallas_call(
        kernel,
        out_shape=shapes,
        grid=() if steps is None else (steps,),
        in_specs=[spec(a.shape, how, True) for a, how in ins]
        + [pl.BlockSpec(memory_space=pl.ANY)] * len(ties),
        out_specs=[spec(shape, how, False) for shape, _, how in outs],
        scratch_shapes=[pltpu.VMEM(shape, dtype) for shape, dtype in scratch],
        compiler_params=pltpu.CompilerParams(vmem_limit_bytes=VMEM),
        cost_estimate=pl.CostEstimate(
            flops=int(micros * 1.15e9), bytes_accessed=moved, transcendentals=0
        ),
    )(*args, *ties)


def whole_call(kernel, outs, args, scratch=(), micros=0, ties=()):
    ins = [(a, "s" if i == 0 else None) for i, a in enumerate(args)]
    outs = [(shape, dtype, None) for shape, dtype in outs]
    return call(kernel, ins, outs, scratch, micros, ties)


def normalise(v):
    mean = jnp.mean(v, axis=1, keepdims=True)
    c = v - mean
    r = lax.rsqrt(jnp.mean(c * c, axis=1, keepdims=True) + 1e-05)
    return c * r, r


def norm_back(grad, hat, r, gain):
    g = grad * gain
    a = jnp.mean(g, axis=1, keepdims=True)
    b = jnp.mean(g * hat, axis=1, keepdims=True)
    return r * (g - a - hat * b)


C0 = math.sqrt(2.0 / math.pi)
C1 = 0.044715


def gelu(x):
    return 0.5 * x * (1.0 + jnp.tanh(x * (C0 + C0 * C1 * (x * x))))


def gelu_and_slope(x):
    xx = x * x
    t = jnp.tanh(x * (C0 + C0 * C1 * xx))
    half = 0.5 * (1.0 + t)
    return x * half, half + (0.5 * x) * (1.0 - t * t) * (C0 + 3.0 * C0 * C1 * xx)


def sigmoid(x):
    return 0.5 * jnp.tanh(0.5 * x) + 0.5


def fold8(v):
    return jnp.sum(v.reshape(v.shape[0] // 8, 8, v.shape[1]), axis=0)


def rows_at(i, tile, start=0):
    return pl.ds(pl.multiple_of(start + i * tile, 16), tile)


def places(base, rows, lanes=LANES):
    return base + lax.broadcasted_iota(jnp.int32, (rows, lanes), 0)


ROWS = {"glu": 16, "wide": 16, "narrow": 48, "point": 64, "qkv": 16, "attn": 16, "up": 16, "down": 64, "small": 16}


def columns_of(name, *chunks):
    return [(name, j) for j in chunks]


WIDE, GLU, QKV, UP = (columns_of(n, *range(k)) for n, k in (("wide", 8), ("glu", 4), ("qkv", 6), ("up", 8)))
NARROW_0, POINT_0, SMALL_0 = (columns_of(n, 0) for n in ("narrow", "point", "small"))
ATTN, DOWN = columns_of("attn", 0, 1), columns_of("down", 0, 1)
LAST = (UP + ATTN[:1], ATTN[1:] + DOWN)
GATHERS = ((WIDE, GLU + NARROW_0 + SMALL_0), (QKV[:5], QKV[5:] + POINT_0), LAST)
SUMS = (
    LAST,
    (QKV[:5], QKV[5:] + POINT_0),
    (WIDE[:6], WIDE[6:] + NARROW_0),
    (GLU[:2], GLU[2:] + SMALL_0),
)

SPLIT = (1, 2)


def height(items):
    return sum(ROWS[name] for name, _ in items)


def row_of(items, item):
    return height(items[: items.index(item)])


def slot_bits(half, r):
    high, low, z = r >> 3, r >> 2 & 1, r & 3
    x, y = (high, low) if half == 0 else (low, high)
    return z * 8 + y * 4 + x * 2


def slot_of(half, rel):
    z, y, x, c = rel >> 3, rel >> 2 & 1, rel >> 1 & 1, rel & 1
    high, low = (x, y) if half == 0 else (y, x)
    return c * 16 + high * 8 + low * 4 + z


def unpack(me, group, pieces, wanted):
    for half, items in enumerate(GATHERS[group]):
        for core in range(2):
            piece = pieces[half * 2 + core]
            for r in range(BLOCKS // 2):
                owner = (slot_bits(half, r) + core) ^ me
                for name, j in items:
                    if name in wanted:
                        b, off = ROWS[name], row_of(items, (name, j))
                        wanted[name][
                            pl.ds(pl.multiple_of(owner * b, 16), b), j * PACK : (j + 1) * PACK
                        ] = piece[r, off : off + b, :]


def put(me, group, ref, item, value, start=0):
    half = int(item in SUMS[group][1])
    off = row_of(SUMS[group][half], item) + half * height(SUMS[group][0])
    b = ROWS[item[0]]
    for k in range(value.shape[0] // b):
        slot = slot_of(half if group in SPLIT else 0, (start + k) ^ me)
        ref[slot, off : off + b, :] = value[k * b : (k + 1) * b]


def group_grads(group):
    rows = height(sum(SUMS[group], []))
    return [((BLOCKS // 2, rows, PACK), BF)] * 2


def group_slots(group):
    return ((BLOCKS, height(sum(SUMS[group], [])), PACK), BF)


def part_slots(slots, kept, given):
    kept[...] = slots[: BLOCKS // 2]
    given[...] = slots[BLOCKS // 2 :]


SHAPES = ({"glu": (D, 2 * D), "wide": (D, FF), "narrow": (3 * D, NARROW)}, {"qkv": (D, 3 * D), "point": (FF, NARROW)})

GAINS = ((0, 16), (16, 16), (32, 64), (96, 16), (112, 16))
TAPS = 128
TAP_RUN = KERNEL * FF // BLOCKS
SMALL_ROWS = 3


def iota(shape, dim):
    return lax.broadcasted_iota(jnp.int32, shape, dim)


def owner_slots(me, half):
    shape = (BLOCKS, BLOCKS)
    return (slot_of(half, iota(shape, 0) ^ me) == iota(shape, 1)).astype(F32).astype(BF)


def gain_maps(offset, width):
    total = BLOCKS * width
    owner = iota((BLOCKS, total), 1) // width == iota((BLOCKS, total), 0)
    value = iota((LANES, total), 0) == offset + iota((LANES, total), 1) % width
    return owner, value.astype(F32).astype(BF)


def tap_runs():
    for b in range(KERNEL * FF // 64):
        f = b * 64
        yield f // FF, f % FF, f // TAP_RUN, TAPS + f % TAP_RUN


def read_small(me, pieces, gains, taps, table):
    off = row_of(GATHERS[0][1], SMALL_0[0])
    for core in range(2):
        for r in range(BLOCKS // 2):
            rows = pieces[2 + core][r, off : off + 16, :].astype(F32)
            slot = core * 16 + r
            for q in range(SMALL_ROWS):
                table[slot : slot + 1, q * PACK : (q + 1) * PACK] = rows[q : q + 1, :]
    table[...] = nn(owner_slots(me, 1), table[...].astype(BF))
    for ref, (offset, width) in zip(gains, GAINS):
        owner, value = gain_maps(offset, width)
        spread = nn(table[:, :LANES].astype(BF), value)
        ref[...] = jnp.sum(jnp.where(owner, spread, 0.0), axis=0, keepdims=True)
    for tap, channel, who, place in tap_runs():
        taps[tap : tap + 1, channel : channel + 64] = table[who : who + 1, place : place + 64]


def write_small(me, gains, taps, table, block, grads):
    table[...] = jnp.zeros_like(table)
    total = jnp.zeros((BLOCKS, LANES), F32)
    for gain, (offset, width) in zip(gains, GAINS):
        owner, value = gain_maps(offset, width)
        total = total + nt(jnp.where(owner, gain[...], 0.0).astype(BF), value)
    table[:, :LANES] = total
    for tap, channel, who, place in tap_runs():
        table[who : who + 1, place : place + 64] = taps[tap : tap + 1, channel : channel + 64]
    table[...] = tn(owner_slots(me, 0), table[...].astype(BF))
    block[...] = jnp.zeros_like(block)
    for slot in range(BLOCKS):
        for q in range(SMALL_ROWS):
            block[slot, q : q + 1, :] = table[slot : slot + 1, q * PACK : (q + 1) * PACK]
    at = height(sum(SUMS[3], [])) - 16
    grads[:, at : at + 16, :] = block[...].astype(BF)


def pack_kernel(names, *refs):
    shards = dict(zip(names, refs))
    for ref, halves in zip(refs[len(names) :], GATHERS):
        at = 0
        for name, j in sum(halves, []):
            b = ROWS[name]
            if name == "small":
                ref[at : at + b, :] = shards[name][...]
            else:
                ref[at : at + b, :] = shards[name][:, j * PACK : (j + 1) * PACK]
            at += b


def pack(shards):
    names = tuple(shards)
    return call(
        functools.partial(pack_kernel, names),
        [(shards[k], None) for k in names],
        [((height(sum(halves, [])), PACK), BF, None) for halves in GATHERS],
        micros=2,
    )


def front1_kernel(scal, x_ref, p0, p1, p2, p3, h1_ref, y2_ref, joined_ref, *refs):
    weights, gains, taps, table = refs[:3], refs[3:8], refs[8], refs[9]
    g1, g2 = gains[:2]

    @pl.when(pl.program_id(0) == 0)
    def _():
        read_small(scal[2], (p0, p1, p2, p3), gains, taps, table)
        unpack(scal[2], 0, (p0, p1, p2, p3), dict(zip(SHAPES[0], weights)))

    x = x_ref[...].astype(F32)
    hat, _ = normalise(x)
    joined = nn((hat * g1[...]).astype(BF), weights[0][...])
    joined_ref[...] = joined
    h1 = x + joined[:, :D] * sigmoid(joined[:, D:])
    h1_ref[...] = h1
    hat2, _ = normalise(h1)
    y2_ref[...] = (hat2 * g2[...]).astype(BF)


def front1(scal, x, pieces, ties=()):
    rows = x.shape[0]
    tile = 160
    return call(
        front1_kernel,
        [(scal, "s"), (x, tile)] + [(p, None) for p in pieces],
        [((rows, D), F32, tile), ((rows, D), BF, tile), ((rows, 2 * D), F32, tile)]
        + [(shape, BF, None) for shape in SHAPES[0].values()]
        + [((1, BLOCKS * width), F32, None) for _, width in GAINS]
        + [((KERNEL, FF), F32, None)],
        scratch=[((BLOCKS, SMALL_ROWS * PACK), F32)],
        micros=12,
        ties=ties,
        steps=rows // tile,
    )


def front2_kernel(tile, group, scal, y2_ref, g3, wide, narrow, left_ref, right_ref, mid_ref, u_ref):
    rows = y2_ref.shape[0]
    base = scal[0] * (rows - 2 * RIM) - RIM
    first = scal[1]
    i = pl.program_id(0)

    @pl.when(i == 0)
    def _():
        u_ref[0:RIM, :] = jnp.zeros((RIM, 3 * NARROW), F32)
        u_ref[RIM + rows : 2 * RIM + rows, :] = jnp.zeros((RIM, 3 * NARROW), F32)

        def narrow_step(j, carry):
            y = y2_ref[rows_at(j, tile), :]
            for k in range(3):
                u_ref[rows_at(j, tile, RIM), k * NARROW : (k + 1) * NARROW] = nn(
                    y, narrow[k * D : (k + 1) * D, :]
                )
            return carry

        lax.fori_loop(0, rows // tile, narrow_step, 0)

    around = pl.ds(pl.multiple_of(i * tile, 16), tile + 2 * RIM)
    left = nn(y2_ref[rows_at(i, tile), :], wide[...])
    left_ref[...] = left
    pos = places(base + i * tile, tile, NARROW)
    before = pltpu.roll(u_ref[around, 0:NARROW], 1, 0)[RIM : RIM + tile]
    after = pltpu.roll(u_ref[around, 2 * NARROW :], tile + 2 * RIM - 1, 0)[RIM : RIM + tile]
    right = u_ref[rows_at(i, tile, RIM), NARROW : 2 * NARROW]
    right = right + jnp.where((pos == first) | (pos == 0), 0.0, before)
    right = right + jnp.where((pos + 1 == first) | (pos + 1 == group), 0.0, after)
    right_ref[...] = right
    left = gelu(left)
    joined = jnp.concatenate([left[:, :NARROW] + gelu(right), left[:, NARROW:]], axis=1)
    hat, _ = normalise(joined)
    row = base + i * tile + lax.broadcasted_iota(jnp.int32, (tile, 1), 0)
    inside = ((row >= 0) & (row < group)).astype(F32)
    mid_ref[...] = (hat * inside * g3[...]).astype(BF)


def front2(scal, y2, g3, wide, narrow, group, ties=()):
    rows = y2.shape[0]
    tile = 160
    return call(
        functools.partial(front2_kernel, tile, group),
        [(scal, "s"), (y2, None), (g3, None), (wide, None), (narrow, None)],
        [((rows, FF), F32, tile), ((rows, NARROW), F32, tile), ((rows, FF), BF, tile)],
        scratch=[((rows + 2 * RIM, 3 * NARROW), F32)],
        micros=12,
        ties=ties,
        steps=rows // tile,
    )


def crosses(pos, offset, first):
    if offset > 0:
        return (pos < first) & (pos + offset >= first)
    return (pos >= first) & (pos + offset < first)


def conv(win, tile, taps, lanes, pos, first, masked, sign):
    total = None
    for k in range(KERNEL):
        o = sign * (k - HALF)
        v = win[RIM + o : RIM + o + tile, :]
        if masked and o != 0:
            v = jnp.where(crosses(pos, o, first), 0.0, v)
        v = v * taps[k : k + 1, lanes]
        total = v if total is None else total + v
    return total


def front3_kernel(tile, n, share, scal, mid_ref, taps, h1_ref, g4, p0, p1, p2, p3, *refs):
    spread_ref, h2_ref, y4_ref = refs[:3]
    outs = refs[3 : 3 + n]
    qkv_w, point, win, qkv_s = refs[3 + n :]
    i = pl.program_id(0)

    @pl.when(i == 0)
    def _():
        unpack(scal[2], 1, (p0, p1, p2, p3), {"qkv": qkv_w, "point": point})

    s, first = scal[0], scal[1]
    begin = s * (mid_ref.shape[0] - 2 * RIM) + i * tile
    near = (first > begin - HALF) & (first < begin + tile + HALF)

    def chunk(c, carry):
        lanes = pl.ds(pl.multiple_of(c * LANES, LANES), LANES)
        around = pl.ds(pl.multiple_of(i * tile, 16), tile + 2 * RIM)
        win[...] = mid_ref[around, lanes].astype(F32)
        pos = places(begin, tile)
        for masked in (False, True):

            @pl.when(near if masked else jnp.logical_not(near))
            def _():
                spread_ref[:, lanes] = conv(win, tile, taps, lanes, pos, first, masked, 1).astype(BF)

        return carry

    lax.fori_loop(0, FF // LANES, chunk, 0)
    h1 = h1_ref[rows_at(i, tile, RIM), :]
    branch = nn(spread_ref[...], point[...])
    h2 = jnp.concatenate([h1[:, :NARROW] + branch, h1[:, NARROW:]], axis=1)
    h2_ref[...] = h2
    hat, _ = normalise(h2)
    y4 = (hat * g4[...]).astype(BF)
    y4_ref[...] = y4
    qkv_s[...] = nn(y4, qkv_w[...]).astype(BF)
    for k in range(n):
        block = (s ^ k) // share
        for part in range(3):
            outs[k][:, part * LANES : (part + 1) * LANES] = qkv_s[
                :, pl.ds(pl.multiple_of(part * D + block * LANES, LANES), LANES)
            ]


def front3(scal, mid, taps, h1, g4, pieces, n, share, ties=()):
    rows = mid.shape[0] - 2 * RIM
    tile = 128
    return call(
        functools.partial(front3_kernel, tile, n, share),
        [(scal, "s")] + [(a, None) for a in (mid, taps, h1, g4, *pieces)],
        [((rows, FF), BF, tile), ((rows, D), F32, tile), ((rows, D), BF, tile)]
        + [((rows, 3 * LANES), BF, tile)] * n
        + [(shape, BF, None) for shape in SHAPES[1].values()],
        scratch=[((tile + 2 * RIM, LANES), F32), ((tile, 3 * D), BF)],
        micros=20,
        ties=ties,
        steps=rows // tile,
    )


def gather_lanes(wide_ref, n, share, s, blocks, parts):
    rows = wide_ref.shape[0]
    for k in range(n):
        block = (s ^ k) // share
        for part in range(parts):
            lanes = pl.ds(pl.multiple_of(part * D + block * LANES, LANES), LANES)
            new = blocks[k][:, part * LANES : (part + 1) * LANES]
            if share > 1:
                lane = lax.broadcasted_iota(jnp.int32, (rows, LANES), 1)
                mine = lane // (LANES // share) == (s ^ k) % share
                new = jnp.where(mine, new.astype(F32), wide_ref[:, lanes].astype(F32)).astype(BF)
            wide_ref[:, lanes] = new


def middle_kernel(n, share, scal, h2_ref, *refs):
    att = refs[:n]
    cot_ref, g5, p0, p1, p2, p3, mixed_ref, dh3_ref = refs[n : n + 8]
    datt = refs[n + 8 : 2 * n + 8]
    att_s, y5_s, inner_s, du_s, ln_out = refs[2 * n + 8 : 2 * n + 13]
    wa, wup, wdown, ln_ref = refs[2 * n + 13 :]
    s = scal[0]
    i = pl.program_id(0)

    @pl.when(i == 0)
    def _():
        unpack(scal[2], 2, (p0, p1, p2, p3), {"attn": wa, "up": wup, "down": wdown})
        ln_ref[...] = jnp.zeros_like(ln_ref)

    gather_lanes(att_s, n, share, s, att, 1)
    h3 = h2_ref[...] + nn(att_s[...], wa[...])
    hat, r = normalise(h3)
    y5 = (hat * g5[...]).astype(BF)
    y5_s[...] = y5
    value, slope = gelu_and_slope(nn(y5, wup[...]))
    inner = value.astype(BF)
    inner_s[...] = inner
    mixed_ref[...] = (h3 + nn(inner, wdown[...])).astype(BF)
    cot = cot_ref[...]
    du = (nt(cot, wdown[...]) * slope).astype(BF)
    du_s[...] = du
    dy5 = nt(du, wup[...])
    ln_ref[...] += fold8(dy5 * hat)
    dh3 = cot.astype(F32) + norm_back(dy5, hat, r, g5[...])
    dh3_ref[...] = dh3
    da = nt(dh3.astype(BF), wa[...]).astype(BF)
    for j in range(D // LANES):
        for k in range(n):

            @pl.when((s ^ k) // share == j)
            def _():
                datt[k][...] = da[:, j * LANES : (j + 1) * LANES]

    ln_out[...] = jnp.sum(ln_ref[...], axis=0, keepdims=True)


def middle(scal, h2, att, cot, g5, pieces, n, share, ties=()):
    rows = h2.shape[0]
    tile = 128
    return call(
        functools.partial(middle_kernel, n, share),
        [(scal, "s"), (h2, tile)]
        + [(a, tile) for a in (*att, cot)]
        + [(a, None) for a in (g5, *pieces)],
        [((rows, D), BF, tile), ((rows, D), F32, tile)]
        + [((rows, LANES), BF, tile)] * n
        + [((rows, c), BF, tile) for c in (D, D, FF, FF)]
        + [((1, D), F32, None)],
        scratch=[((D, D), BF), ((D, FF), BF), ((FF, D), BF), ((8, D), F32)],
        micros=20,
        ties=ties,
        steps=rows // tile,
    )


def weigh0_kernel(scal, att_s, y5_s, inner_s, du_s, cot_ref, dh3_ref, kept, given, grads):
    me = scal[2]
    att_t = att_s[...].T
    for j in range(D // PACK):
        part = nn(att_t, dh3_ref[:, j * PACK : (j + 1) * PACK].astype(BF))
        put(me, 0, grads, ("attn", j), part.astype(BF))
    y5_t = y5_s[...].T
    for j in range(FF // PACK):
        cols = slice(j * PACK, (j + 1) * PACK)
        put(me, 0, grads, ("up", j), nn(y5_t, du_s[:, cols]).astype(BF))
        down = tn(inner_s[:, cols], cot_ref[...]).astype(BF)
        for m in range(D // PACK):
            put(me, 0, grads, ("down", m), down[:, m * PACK : (m + 1) * PACK], j * PACK // 64)
    part_slots(grads, kept, given)


def weigh0(scal, att, y5, inner, du, cot, dh3, ties=()):
    return whole_call(
        weigh0_kernel,
        group_grads(0),
        [scal, att, y5, inner, du, cot, dh3],
        scratch=[group_slots(0)],
        micros=10,
        ties=ties,
    )


def back3_kernel(n, share, scal, *refs):
    blocks = refs[:n]
    dh3_ref, h2_ref, g4, qkv_w = refs[n : n + 4]
    dh2_ref, db_ref, dqkv_s, ln_out, ln_ref = refs[n + 4 :]

    @pl.when(pl.program_id(0) == 0)
    def _():
        ln_ref[...] = jnp.zeros_like(ln_ref)

    gather_lanes(dqkv_s, n, share, scal[0], blocks, 3)
    dy4 = nt(dqkv_s[...], qkv_w[...])
    hat, r = normalise(h2_ref[...])
    ln_ref[...] += fold8(dy4 * hat)
    dh2 = dh3_ref[...] + norm_back(dy4, hat, r, g4[...])
    dh2_ref[...] = dh2
    db_ref[...] = dh2[:, :NARROW].astype(BF)
    ln_out[...] = jnp.sum(ln_ref[...], axis=0, keepdims=True)


def back3(scal, blocks, dh3, h2, g4, qkv_w, n, share, ties=()):
    rows = h2.shape[0]
    tile = 128
    return call(
        functools.partial(back3_kernel, n, share),
        [(scal, "s")] + [(a, tile) for a in (*blocks, dh3, h2)] + [(g4, None), (qkv_w, None)],
        [((rows, D), F32, tile), ((rows, NARROW), BF, tile), ((rows, 3 * D), BF, tile)]
        + [((1, D), F32, None)],
        scratch=[((8, D), F32)],
        micros=6,
        ties=ties,
        steps=rows // tile,
    )


def weigh1_kernel(scal, y4_ref, dqkv_s, spread_ref, db_ref, kept, given, grads):
    me = scal[2]
    y4_t = y4_ref[...].T
    for j in range(3 * D // PACK):
        part = nn(y4_t, dqkv_s[:, j * PACK : (j + 1) * PACK])
        put(me, 1, grads, ("qkv", j), part.astype(BF))
    for j in range(FF // PACK):
        part = tn(spread_ref[:, j * PACK : (j + 1) * PACK], db_ref[...]).astype(BF)
        put(me, 1, grads, ("point", 0), part, j * PACK // 64)
    part_slots(grads, kept, given)


def weigh1(scal, y4, dqkv, spread, db, ties=()):
    return whole_call(
        weigh1_kernel,
        group_grads(1),
        [scal, y4, dqkv, spread, db],
        scratch=[group_slots(1)],
        micros=3,
        ties=ties,
    )


def back2_kernel(tile, group, scal, low_ref, db_ref, high_ref, *refs):
    taps, mid_ref, left_ref, right_ref, g3, point = refs[:6]
    dl, st, gdepth_out, ln_out = refs[6:10]
    dbx, dsp, win, dmid, dr, gdepth_ref, ln_ref = refs[10:]
    rows = db_ref.shape[0]
    ext = rows + 2 * RIM
    base = scal[0] * rows - RIM
    first = scal[1]
    i = pl.program_id(0)
    last = ext // tile - 1

    @pl.when(i == 0)
    def _():
        dbx[0:RIM, :] = low_ref[...]
        dbx[RIM : RIM + rows, :] = db_ref[...]
        dbx[RIM + rows :, :] = high_ref[...]
        dsp[0:RIM, :] = jnp.zeros((RIM, FF), F32)
        dsp[RIM + ext :, :] = jnp.zeros((RIM, FF), F32)
        dr[0:RIM, :] = jnp.zeros((RIM, NARROW), F32)
        dr[RIM + ext :, :] = jnp.zeros((RIM, NARROW), F32)
        gdepth_ref[...] = jnp.zeros_like(gdepth_ref)
        ln_ref[...] = jnp.zeros_like(ln_ref)

        def spread_step(j, carry):
            dsp[rows_at(j, tile, RIM), :] = nt(dbx[rows_at(j, tile), :], point[...])
            return carry

        lax.fori_loop(0, ext // tile, spread_step, 0)

    begin = base + i * tile
    near = (first > begin - HALF) & (first < begin + tile + HALF)
    near = near | (i == 0) | (i == last)

    def chunk(c, carry):
        lanes = pl.ds(pl.multiple_of(c * LANES, LANES), LANES)
        around = pl.ds(pl.multiple_of(i * tile, 16), tile + 2 * RIM)
        win[...] = dsp[around, lanes]
        local = i * tile + lax.broadcasted_iota(jnp.int32, (tile, LANES), 0)
        mid = mid_ref[:, lanes].astype(F32)
        pos = places(begin, tile)
        for masked in (False, True):

            @pl.when(near if masked else jnp.logical_not(near))
            def _():
                total = None
                for k in range(KERNEL):
                    o = HALF - k
                    v = win[RIM + o : RIM + o + tile, :]
                    if masked and o != 0:
                        v = jnp.where(crosses(pos, o, first), 0.0, v)
                    counted = v
                    if masked:
                        kept = (local + o >= RIM) & (local + o < RIM + rows)
                        counted = jnp.where(kept, v, 0.0)
                    gdepth_ref[k * 8 : (k + 1) * 8, lanes] += fold8(counted * mid)
                    v = v * taps[k : k + 1, lanes]
                    total = v if total is None else total + v
                dmid[:, lanes] = total

        return carry

    lax.fori_loop(0, FF // LANES, chunk, 0)
    left, slope = gelu_and_slope(left_ref[...])
    right, slope_r = gelu_and_slope(right_ref[...])
    joined = jnp.concatenate([left[:, :NARROW] + right, left[:, NARROW:]], axis=1)
    hat, r = normalise(joined)
    local = i * tile + lax.broadcasted_iota(jnp.int32, (tile, 1), 0)
    own = ((local >= RIM) & (local < RIM + rows)).astype(F32)
    pos = base + local
    grad = dmid[...] * ((pos >= 0) & (pos < group)).astype(F32)
    ln_ref[...] += fold8(grad * hat * own)
    dj = norm_back(grad, hat, r, g3[...])
    dl[...] = (dj * slope).astype(BF)
    dr[rows_at(i, tile, RIM), :] = (dj[:, :NARROW] * slope_r).astype(BF).astype(F32)

    @pl.when(i == last)
    def _():
        for k in range(KERNEL):
            gdepth_out[k : k + 1, :] = jnp.sum(
                gdepth_ref[k * 8 : (k + 1) * 8, :], axis=0, keepdims=True
            )
        ln_out[...] = jnp.sum(ln_ref[...], axis=0, keepdims=True)
        part = 128

        def gather_step(j, carry):
            at = rows_at(j, part)
            around = pl.ds(pl.multiple_of(RIM + j * part, 16), part + 2 * RIM)
            pos = places(base + RIM + j * part, part, NARROW)
            v = dr[around, :]
            after = pltpu.roll(v, part + 2 * RIM - 1, 0)[RIM : RIM + part]
            before = pltpu.roll(v, 1, 0)[RIM : RIM + part]
            after = jnp.where((pos + 1 == first) | (pos + 1 == group), 0.0, after)
            before = jnp.where((pos == first) | (pos == 0), 0.0, before)
            st[at, 0:NARROW] = after.astype(BF)
            st[at, NARROW : 2 * NARROW] = v[RIM : RIM + part].astype(BF)
            st[at, 2 * NARROW :] = before.astype(BF)
            return carry

        lax.fori_loop(0, rows // part, gather_step, 0)


def back2(scal, low, db, high, taps, mid, left, right, g3, point, group, ties=()):
    rows = db.shape[0]
    ext = rows + 2 * RIM
    tile = 160
    return call(
        functools.partial(back2_kernel, tile, group),
        [(scal, "s")]
        + [(a, None) for a in (low, db, high, taps)]
        + [(a, tile) for a in (mid, left, right)]
        + [(g3, None), (point, None)],
        [((ext, FF), BF, tile), ((rows, 3 * NARROW), BF, None)]
        + [((KERNEL, FF), F32, None), ((1, FF), F32, None)],
        scratch=[
            ((ext, NARROW), BF),
            ((ext + 2 * RIM, FF), F32),
            ((tile + 2 * RIM, LANES), F32),
            ((tile, FF), F32),
            ((ext + 2 * RIM, NARROW), F32),
            ((8 * KERNEL, FF), F32),
            ((8, FF), F32),
        ],
        micros=44,
        ties=ties,
        steps=ext // tile,
    )


def back1_kernel(scal, dl, st, dh2_ref, h1_ref, joined_ref, x_ref, g1, g2, *refs):
    glu, wide, narrow, dx_ref, y1_ref, dj_ref, ln1_out, ln2_out, ln1_ref, ln2_ref = refs
    i = pl.program_id(0)

    @pl.when(i == 0)
    def _():
        ln1_ref[...] = jnp.zeros_like(ln1_ref)
        ln2_ref[...] = jnp.zeros_like(ln2_ref)

    dy2 = nt(dl[...], wide[...])
    for k in range(3):
        dy2 = dy2 + nt(st[:, k * NARROW : (k + 1) * NARROW], narrow[k * D : (k + 1) * D, :])
    hat2, r2 = normalise(h1_ref[...])
    ln2_ref[...] += fold8(dy2 * hat2)
    dh1 = dh2_ref[...] + norm_back(dy2, hat2, r2, g2[...])
    gate = sigmoid(joined_ref[:, D:])
    value = joined_ref[:, :D]
    dj_ref[:, :D] = (dh1 * gate).astype(BF)
    dj_ref[:, D:] = (dh1 * value * gate * (1.0 - gate)).astype(BF)
    x = x_ref[...].astype(F32)
    hat1, r1 = normalise(x)
    y1_ref[...] = (hat1 * g1[...]).astype(BF)
    dy1 = nt(dj_ref[...], glu[...])
    ln1_ref[...] += fold8(dy1 * hat1)
    dx_ref[...] = (dh1 + norm_back(dy1, hat1, r1, g1[...])).astype(dx_ref.dtype)
    ln1_out[...] = jnp.sum(ln1_ref[...], axis=0, keepdims=True)
    ln2_out[...] = jnp.sum(ln2_ref[...], axis=0, keepdims=True)


def back1(scal, dl, st, dh2, h1, joined, x, g1, g2, glu, wide, narrow, start, rows):
    tile = 128
    own, ext = (tile, start), (tile, start + RIM)
    return call(
        back1_kernel,
        [(scal, "s"), (dl, ext), (st, own), (dh2, own), (h1, ext), (joined, ext), (x, ext)]
        + [(a, None) for a in (g1, g2, glu, wide, narrow)],
        [((rows, D), BF, tile), ((rows, D), BF, tile), ((rows, 2 * D), BF, tile)]
        + [((1, D), F32, None)] * 2,
        scratch=[((8, D), F32), ((8, D), F32)],
        micros=5,
        steps=rows // tile,
    )


def weigh2_kernel(scal, dl, st, y2_ref, kept, given, grads, gn):
    me = scal[2]
    rows = st.shape[0]
    y2_t = y2_ref[RIM : RIM + rows, :].T
    for j in range(FF // PACK):
        part = nn(y2_t, dl[RIM : RIM + rows, j * PACK : (j + 1) * PACK]).astype(BF)
        put(me, 2, grads, ("wide", j), part)
    for k in range(3):
        gn[k * D : (k + 1) * D, :] = nn(y2_t, st[:, k * NARROW : (k + 1) * NARROW]).astype(BF)
    put(me, 2, grads, ("narrow", 0), gn[...])
    part_slots(grads, kept, given)


def weigh2(scal, dl, st, y2):
    return whole_call(
        weigh2_kernel,
        group_grads(2),
        [scal, dl, st, y2],
        scratch=[group_slots(2), ((3 * D, NARROW), BF)],
        micros=3,
    )


def weigh3_kernel(halves, scal, *refs):
    y1, dj, ln1, ln2 = (refs[i * halves : (i + 1) * halves] for i in range(4))
    gains, taps, kept, given = refs[4 * halves : 4 * halves + 3], *refs[4 * halves + 3 : 4 * halves + 6]
    grads, table, block, ln1_s, ln2_s = refs[4 * halves + 6 :]
    me = scal[2]
    for total, parts in ((ln1_s, ln1), (ln2_s, ln2)):
        total[...] = sum(p[...] for p in parts[1:]) + parts[0][...]
    write_small(me, (ln1_s, ln2_s, *gains), taps, table, block, grads)
    turned = [y[...].T for y in y1]
    for j in range(2 * D // PACK):
        part = None
        for y, d in zip(turned, dj):
            more = nn(y, d[:, j * PACK : (j + 1) * PACK])
            part = more if part is None else part + more
        put(me, 3, grads, ("glu", j), part.astype(BF))
    part_slots(grads, kept, given)


def weigh3(scal, y1, dj, ln1, ln2, gains, taps):
    return whole_call(
        functools.partial(weigh3_kernel, len(y1)),
        group_grads(3),
        [scal, *y1, *dj, *ln1, *ln2, *gains, taps],
        scratch=[group_slots(3), ((BLOCKS, SMALL_ROWS * PACK), F32), ((BLOCKS, 16, PACK), F32)]
        + [((1, D), F32)] * 2,
        micros=0,
    )


def lane_maps(rows, head):
    lane = lax.broadcasted_iota(jnp.int32,(rows,LANES),1)
    own = (lane >= head*HEAD) & (lane < (head+1)*HEAD)
    rel = lane - (1-head)*HEAD
    return own, rel

def id_column(base, rows, first):
    pos = base + lax.broadcasted_iota(jnp.int32,(rows,LANES),0)
    return pos >= first

def split3(v):
    hi = v.astype(BF).astype(F32)
    mid = (v-hi).astype(BF).astype(F32)
    return hi, mid, v-hi-mid

def tile_ids(start, rows, first):
    return start < first, start+rows > first

def overlap(a_start,a_rows,b_start,b_rows,first):
    a0,a1 = tile_ids(a_start,a_rows,first); b0,b1=tile_ids(b_start,b_rows,first)
    return (a0&b0)|(a1&b1)

def attend_kernel(n, heads, share, tq, tk, scal, *refs):
    qkv = refs[:n]; att = refs[n:2*n]; lse_ref = refs[2*n]
    qa, ka, va, mx_ref, m_ref, q2_ref, acc_ref = refs[2*n+1:]
    s = scal[0]; first = scal[1]
    rows = qkv[0].shape[0]
    for k in range(n):
        base = (s ^ k)*rows
        id1 = id_column(base, rows, first).astype(F32)
        q = qkv[k][:, 0:LANES].astype(F32)*(HEAD**-0.5)
        key = qkv[k][:, LANES:2*LANES].astype(F32)
        v = qkv[k][:, 2*LANES:3*LANES].astype(F32)
        for i in range(heads):
            h = i if share==1 else s % share
            own, rel = lane_maps(rows, h)
            qx = jnp.where(rel==0, 1.0-id1, jnp.where(rel==1, id1, 0.0))
            kx = jnp.where(rel==0, id1*BIG, jnp.where(rel==1, (1.0-id1)*BIG, jnp.where(rel<5,1.0,0.0)))
            qa[i, k*rows:(k+1)*rows,:] = jnp.where(own, q, qx).astype(BF)
            ka[i, k*rows:(k+1)*rows,:] = jnp.where(own, key, kx).astype(BF)
            va[i, k*rows:(k+1)*rows,:] = jnp.where(own, v, 1.0).astype(BF)
    per = rows//tq; per_k = rows//tk
    def fold(sc, best):
        for j in range(tk//LANES):
            best = jnp.maximum(best, sc[:, j*LANES:(j+1)*LANES])
        return best
    def q_step(it, carry):
        kq = it//per
        r0 = pl.multiple_of((it % per)*tq, tq)
        g0 = pl.multiple_of(it*tq, tq)
        own0 = pl.multiple_of((g0//tk)*tk, tk)
        q_start = (s ^ kq)*rows + r0
        for i in range(heads):
            for j in range(max(1,tq//tk)):
                sc = nt(qa[i, pl.ds(g0,tq),:], ka[i, pl.ds(own0+j*tk,tk),:])
                best = fold(sc, sc[:, :LANES] if j==0 else best)
            mx_ref[i] = best
            m_ref[i] = jnp.zeros((tq,LANES),F32)
        def attempt(again):
            for i in range(heads):
                h = i if share==1 else s % share
                own, rel = lane_maps(tq, h)
                m = jnp.max(mx_ref[i], axis=1, keepdims=True)
                mb = m_ref[i] + jnp.broadcast_to(m, (tq,LANES))
                m_ref[i] = mb
                hi,mid,lo = split3(-mb)
                q = qa[i, pl.ds(g0,tq),:].astype(F32)
                q2_ref[i] = jnp.where(rel==2,hi,jnp.where(rel==3,mid,jnp.where(rel==4,lo,q))).astype(BF)
            mx_ref[...] = jnp.full_like(mx_ref, -3e38)
            acc_ref[...] = jnp.zeros_like(acc_ref)
            for kt in range(n*per_k):
                k_start = (s ^ (kt//per_k))*rows + (kt%per_k)*tk
                @pl.when(overlap(q_start,tq,k_start,tk,first))
                def _():
                    for i in range(heads):
                        sc = nt(q2_ref[i], ka[i, kt*tk:(kt+1)*tk,:])
                        mx_ref[i] = fold(sc, mx_ref[i])
                        p = jnp.exp2(sc*LOG2E).astype(BF)
                        acc_ref[i] += nn(p, va[i, kt*tk:(kt+1)*tk,:])
            return (jnp.max(mx_ref[...]) > 40.0).astype(jnp.int32)
        lax.while_loop(lambda again: again > 0, attempt, jnp.int32(1))
        out = jnp.zeros((tq,LANES),F32); lse = jnp.zeros((tq,LANES),F32)
        for i in range(heads):
            h = i if share==1 else s % share
            own,_ = lane_maps(tq,h)
            acc = acc_ref[i]
            total = pltpu.roll(acc, HEAD, 1)
            out = jnp.where(own, acc/total, out)
            lse = jnp.where(own, m_ref[i]+jnp.log(total), lse)
        lse_ref[pl.ds(g0,tq),:] = lse
        for k in range(n):
            @pl.when(kq==k)
            def _():
                att[k][pl.ds(r0,tq),:] = out.astype(BF)
        return carry
    lax.fori_loop(0, n*per, q_step, 0)

def attend(scal, blocks, n, share, tq=768, tk=384, ties=()):
    rows = blocks[0].shape[0]
    heads = 2 // share
    return whole_call(
        functools.partial(attend_kernel, n, heads, share, tq, tk),
        [((rows, LANES), BF)] * n + [((n * rows, LANES), F32)],
        [scal, *blocks],
        scratch=[((heads, n * rows, LANES), BF)] * 3
        + [((heads, tq, LANES), F32)] * 2
        + [((heads, tq, LANES), BF), ((heads, tq, LANES), F32)],
        ties=ties,
        micros=36,
    )


def attend_back_kernel(n, heads, share, tq, tk, scal, *refs):
    qkv = refs[:n]; att = refs[n:2*n]; dat = refs[2*n:3*n]; lse_ref = refs[3*n]
    out = refs[3*n+1:4*n+1]
    qa, ka, va, da, dq_ref, dk_ref, dv_ref = refs[4*n+1:]
    s = scal[0]; first = scal[1]
    rows = qkv[0].shape[0]
    for k in range(n):
        base = (s ^ k)*rows
        sl = slice(k*rows,(k+1)*rows)
        id1 = id_column(base, rows, first).astype(F32)
        q = qkv[k][:, 0:LANES].astype(F32)*(HEAD**-0.5)
        key = qkv[k][:, LANES:2*LANES].astype(F32)
        v = qkv[k][:, 2*LANES:3*LANES].astype(F32)
        do = dat[k][...].astype(F32)
        prod = do*att[k][...].astype(F32)
        for i in range(heads):
            h = i if share==1 else s % share
            own, rel = lane_maps(rows, h)
            lse = pltpu.roll(lse_ref[sl,:], HEAD, 1)
            hi,mid,lo = split3(-lse)
            delta = jnp.sum(jnp.where(own,prod,0.0),axis=1,keepdims=True)
            dhi,dmid,dlo = split3(-delta)
            qx = jnp.where(rel==0, 1.0-id1, jnp.where(rel==1, id1, jnp.where(rel==2,hi,jnp.where(rel==3,mid,jnp.where(rel==4,lo,0.0)))))
            kx = jnp.where(rel==0, id1*BIG, jnp.where(rel==1, (1.0-id1)*BIG, jnp.where(rel<5,1.0,0.0)))
            vx = jnp.where(rel<3,1.0,0.0)
            dx = jnp.where(rel==0,dhi,jnp.where(rel==1,dmid,jnp.where(rel==2,dlo,0.0)))
            qa[i,sl,:] = jnp.where(own,q,qx).astype(BF)
            ka[i,sl,:] = jnp.where(own,key,kx).astype(BF)
            va[i,sl,:] = jnp.where(own,v,vx).astype(BF)
            da[i,sl,:] = jnp.where(own,do,dx).astype(BF)
    dq_ref[...] = jnp.zeros_like(dq_ref)
    per_q = rows//tq; per_k = rows//tk
    def k_step(kt, carry):
        k0 = pl.multiple_of(kt*tk, tk)
        kk = kt//per_k
        k_start = (s ^ kk)*rows + (kt % per_k)*tk
        for i in range(heads):
            dk_ref[i] = jnp.zeros((tk,LANES),F32)
            dv_ref[i] = jnp.zeros((tk,LANES),F32)
        def q_step(qt, c2):
            q0 = pl.multiple_of(qt*tq, tq)
            q_start = (s ^ (qt//per_q))*rows + (qt % per_q)*tq
            @pl.when(overlap(q_start,tq,k_start,tk,first))
            def _():
                for i in range(heads):
                    qq = qa[i,pl.ds(q0,tq),:]; kx = ka[i,pl.ds(k0,tk),:]; dd = da[i,pl.ds(q0,tq),:]
                    st = nt(kx, qq)
                    p = jnp.exp2(st*LOG2E)
                    dp = nt(va[i,pl.ds(k0,tk),:], dd)
                    ds = (p*dp).astype(BF)
                    dv_ref[i] += nn(p.astype(BF), dd)
                    dk_ref[i] += nn(ds, qq)
                    dq_ref[i,pl.ds(q0,tq),:] += tn(ds, kx)
            return c2
        lax.fori_loop(0, n*per_q, q_step, 0)
        dk = jnp.zeros((tk,LANES),F32); dv = jnp.zeros((tk,LANES),F32)
        for i in range(heads):
            h = i if share==1 else s % share
            own,_ = lane_maps(tk,h)
            dk = jnp.where(own, dk_ref[i], dk); dv = jnp.where(own, dv_ref[i], dv)
        r0 = pl.multiple_of((kt % per_k)*tk, tk)
        for k in range(n):
            @pl.when(kk==k)
            def _():
                out[k][pl.ds(r0,tk),LANES:2*LANES] = dk.astype(BF)
                out[k][pl.ds(r0,tk),2*LANES:3*LANES] = dv.astype(BF)
        return carry
    lax.fori_loop(0, n*per_k, k_step, 0)
    for k in range(n):
        sl = slice(k*rows,(k+1)*rows)
        dq = jnp.zeros((rows,LANES),F32)
        for i in range(heads):
            h = i if share==1 else s % share
            own,_ = lane_maps(rows,h)
            dq = jnp.where(own, dq_ref[i,sl,:], dq)
        out[k][:, 0:LANES] = (dq*(HEAD**-0.5)).astype(BF)

def attend_back(scal, blocks, att, datt, lse, n, share, tq=384, tk=384, ties=()):
    rows = blocks[0].shape[0]
    heads = 2 // share
    return whole_call(
        functools.partial(attend_back_kernel, n, heads, share, tq, tk),
        [((rows, 3 * LANES), BF)] * n,
        [scal, *blocks, *att, *datt, lse],
        scratch=[((heads, n * rows, LANES), BF)] * 4
        + [((heads, n * rows, LANES), F32)]
        + [((heads, tk, LANES), F32)] * 2,
        ties=ties,
        micros=58,
    )


class Links:
    def __init__(self, n_seq, n_dp):
        self.count = n_seq * n_dp
        self.direct = (n_seq, n_dp) == (4, 8)

    def flip(self, value, mask):
        return lax.ppermute(value, AXES, [(i, i ^ mask) for i in range(self.count)])

    def near(self, block):
        return jnp.stack([block] + [self.flip(block, k << 3) for k in range(1, 4)])

    def part(self, group, held):
        low = height(GATHERS[group][0])
        return [held[:, :low], held[:, low:]]

    def spread(self, held, stage):
        masks = ((4, 2), (2, 4))[stage]
        return [jnp.concatenate([h, self.flip(h, m)]) for h, m in zip(held, masks)]

    def across(self, held):
        return [held[0], self.flip(held[0], 1), held[1], self.flip(held[1], 1)]

    def gather_whole(self, group, weights):
        whole = {
            name: lax.all_gather(weights[name], AXES, axis=0, tiled=True)
            for name in dict(sum(GATHERS[group], []))
        }
        pieces = []
        for half, items in enumerate(GATHERS[group]):
            blocks = [
                whole[name][:, j * PACK : (j + 1) * PACK].reshape(BLOCKS, -1, PACK)
                for name, j in items
            ]
            pieces += list(self.by_slot(jnp.concatenate(blocks, axis=1), half))
        return pieces

    def by_slot(self, blocks, half):
        shape = blocks.shape[1:]
        order = ((3, 2, 1, 0), (3, 1, 2, 0))[half]
        return blocks.reshape(4, 2, 2, 2, *shape).transpose(*order, 4, 5).reshape(2, 16, *shape)

    def by_owner(self, slots, half):
        shape = slots.shape[1:]
        order = ((3, 2, 1, 0), (3, 1, 2, 0))[half]
        return slots.reshape(2, 2, 2, 4, *shape).transpose(*order, 4, 5).reshape(BLOCKS, *shape)

    def add(self, a, b):
        return (a.astype(F32) + b.astype(F32)).astype(BF)

    def fold(self, slots, mask):
        middle = slots.shape[0] // 2
        return self.add(slots[:middle], self.flip(slots[middle:], mask))

    def cores(self, kept, given):
        return self.add(kept, self.flip(given, 1))

    def first(self, group, kept, given):
        held = self.cores(kept, given)
        low = height(SUMS[group][0])
        return [held[:, :low], held[:, low:]]

    def straight(self, held, stage):
        return self.fold(held, (2, 4)[stage])

    def flips(self, values, mask):
        flat = self.flip(jnp.concatenate([v.reshape(-1, PACK) for v in values], axis=0), mask)
        result, at = [], 0
        for v in values:
            count = v.size // PACK
            result.append(flat[at : at + count].reshape(v.shape))
            at += count
        return result

    def next_two(self, late, early):
        a, b = (v.shape[0] // 2 for v in late)
        c, d = (v.shape[0] // 2 for v in early)
        got_y = self.flips([late[0][a:], early[1][d:]], 4)
        got_x = self.flips([late[1][b:], early[0][c:]], 2)
        late = [self.add(late[0][:a], got_y[0]), self.add(late[1][:b], got_x[0])]
        early = [self.add(early[0][:c], got_x[1]), self.add(early[1][:d], got_y[1])]
        return late, early

    def next_and_plane(self, late, held):
        a, b = (v.shape[0] // 2 for v in late)
        got_y = self.flips([late[0][a:], held[4:8]], 4)
        got_x = self.flips([late[1][b:], held[8:12]], 2)
        total = held[:4].astype(F32) + got_y[1].astype(F32) + got_x[1].astype(F32)
        total = total + self.flip(held[12:], 6).astype(F32)
        late = [self.add(late[0][:a], got_y[0]), self.add(late[1][:b], got_x[0])]
        return late, total.astype(BF)

    def next(self, held, stage):
        masks = ((2, 4), (4, 2))[stage]
        return [self.fold(h, m) for h, m in zip(held, masks)]

    def finish(self, held):
        held = jnp.concatenate(held, axis=1)
        total = held[0].astype(F32)
        for k in range(1, 4):
            total = total + self.flip(held[k], k << 3).astype(F32)
        return total

    def rows_of(self, items, total):
        parts, at = {}, 0
        for name, j in items:
            b = ROWS[name] * BLOCKS // self.count
            parts.setdefault(name, []).append(total[at : at + b])
            at += b
        return {name: jnp.concatenate(p, axis=1) for name, p in parts.items()}

    def scatter_whole(self, group, parts):
        slots = jnp.concatenate(parts)
        sent, at = [], 0
        for half, items in enumerate(SUMS[group]):
            for name, _ in items:
                blocks = self.by_owner(slots[:, at : at + ROWS[name]], half if group in SPLIT else 0)
                sent.append(blocks.reshape(self.count, -1, PACK))
                at += ROWS[name]
        sent = jnp.concatenate(sent, axis=1)
        return lax.psum_scatter(sent, AXES, scatter_dimension=0, tiled=False).astype(F32)


class Layout:
    def __init__(self, n_seq, n_dp):
        self.n_seq, self.n_dp = n_seq, n_dp
        self.where = {}
        for g in range(n_dp):
            for s in range(n_seq):
                self.where[g, s] = self.place(g, s)
        self.block = np.zeros(n_seq * n_dp, np.int32)
        for (g, s), device in self.where.items():
            self.block[device] = s

    def place(self, g, s):
        if (self.n_seq, self.n_dp) == (4, 8):
            y, x, c = g >> 2, g >> 1 & 1, g & 1
            return (2 * c + y) * 8 + (s & 1) * 4 + x * 2 + (s >> 1)
        return s * self.n_dp + g

    def pairs(self, source, target):
        return [
            (source(g, s), target(g, s))
            for g in range(self.n_dp)
            for s in range(self.n_seq)
            if target(g, s) is not None and source(g, s) is not None
        ]

    def at(self, g, s):
        return self.where.get((g, s))

    def home(self, g, s):
        return s * self.n_dp + g

    def bring(self, value):
        return lax.ppermute(value, AXES, self.pairs(self.home, self.at))

    def bring_to(self, value, step):
        return lax.ppermute(
            value, AXES, self.pairs(self.home, lambda g, s: self.at(g, s + step))
        )

    def send_home(self, value):
        return lax.ppermute(value, AXES, self.pairs(self.at, self.home))

    def to_neighbour(self, value, step):
        return lax.ppermute(value, AXES, self.pairs(self.at, lambda g, s: self.at(g, s + step)))

    def swap(self, values):
        return [values[0]] + [
            lax.ppermute(values[k], AXES, self.pairs(self.at, lambda g, s: self.at(g, s ^ k)))
            for k in range(1, self.n_seq)
        ]


NAMES = ("ln1", "ln2", "ln3", "ln4", "ln5", "glu", "wide", "narrow", "depth", "point", "qkv", "attn", "up", "down")
SMALL = ("ln1", "ln2", "ln3", "ln4", "ln5", "depth")


def sync(*values):
    return lax.optimization_barrier(values)


def small_block(arrays, blocks):
    flat = jnp.concatenate([a.reshape(blocks, -1) for a in arrays], axis=1)
    flat = jnp.pad(flat, ((0, 0), (0, 16 * PACK - flat.shape[1])))
    return flat.reshape(blocks * 16, PACK)


def on_device(tokens, cotangent, first_length, *weights):
    n = lax.axis_size("seq")
    n_dp = lax.axis_size("dp")
    share = n * LANES // D
    layout = Layout(n, n_dp)
    links = Links(n, n_dp)
    direct = links.direct
    rows = tokens.shape[1]
    group = n * rows
    here = lax.axis_index("seq") * n_dp + lax.axis_index("dp")
    me = here if direct else jnp.zeros_like(here)
    s = jnp.asarray(layout.block)[here]
    mine = dict(zip(NAMES, weights))
    if direct:
        mine["small"] = small_block([mine[k] for k in SMALL], 1)
    else:
        small = [lax.all_gather(mine[k], AXES, axis=0, tiled=True) for k in SMALL]
        mine["small"] = small_block(small, BLOCKS).reshape(links.count, -1, PACK)[here]

    tokens = tokens[0]
    digits = jnp.where(
        lax.broadcasted_iota(jnp.int32, (RIM, D), 1) < LANES,
        first_length[0] // LANES,
        first_length[0] % LANES,
    )
    sent = jnp.concatenate([tokens, digits.astype(BF)], axis=0)
    if direct:
        blocks = pack({k: mine[k] for k in mine if k not in SMALL})
        sent, blocks = sync(sent, blocks)
        held1 = links.near(blocks[0])
    x = layout.bring(sent)
    if direct:
        held1 = links.spread(links.part(0, *sync(held1)), 0)
    low = layout.bring_to(tokens[-RIM:], 1)
    high = layout.bring_to(tokens[:RIM], -1)
    if direct:
        held1, x, low, high, blocks = sync(held1, x, low, high, blocks)
        held1 = links.spread(held1, 1)
        held2 = links.near(blocks[1])
        held1, held2 = sync(held1, held2)
        pieces1 = links.across(held1)
        held2 = links.spread(links.part(1, held2), 0)
        pieces1, held2 = sync(pieces1, held2)
        held2 = links.spread(held2, 1)
    else:
        pieces1, pieces2, pieces3 = (links.gather_whole(k, mine) for k in range(3))
    digits = x[rows, 0 : 2 * LANES : LANES].astype(F32).astype(jnp.int32)
    first = digits[0] * LANES + digits[1]
    scal = jnp.stack([s.astype(jnp.int32), first, me.astype(jnp.int32)])
    x_ext = jnp.concatenate([low, x[:rows], high], axis=0)

    h1, y2, joined, *rest = front1(scal, x_ext, pieces1)
    (glu, wide, narrow), (g1, g2, g3, g4, g5, taps) = rest[:3], rest[3:]
    if direct:
        y2, held2, blocks = sync(y2, held2, blocks)
        pieces2 = links.across(held2)
        held3 = links.near(blocks[2])
    left, right, mid = front2(scal, y2, g3, wide, narrow, group)
    if direct:
        mid, pieces2, held3 = sync(mid, pieces2, held3)
        held3 = links.spread(links.part(2, held3), 0)
    spread, h2, y4, *rest = front3(scal, mid, taps, h1, g4, pieces2, n, share)
    qkv, (qkv_w, point) = rest[:n], rest[n:]
    if direct:
        qkv, held3 = sync(qkv, held3)
    qkv = layout.swap(qkv)
    qkv, cot = sync(qkv, cotangent[0])
    cot = layout.bring(cot)
    if direct:
        held3, qkv = sync(held3, qkv)
        held3 = links.spread(held3, 1)
    *att, lse = attend(scal, qkv, n, share)
    if direct:
        att, held3, cot = sync(att, held3, cot)
        pieces3 = links.across(held3)
    else:
        att, cot = sync(att, cot)
    arrived = layout.swap(att)
    mixed, dh3, *rest = middle(scal, h2, arrived, cot, g5, pieces3, n, share)
    datt, (att_all, y5, inner, du, ln5) = rest[:n], rest[n:]
    datt, du = sync(datt, du)
    datt = layout.swap(datt)
    sum0 = weigh0(scal, att_all, y5, inner, du, cot, dh3)
    datt, sum0 = sync(datt, sum0)
    if direct:
        sum0 = links.cores(*sum0)
    dqkv = attend_back(scal, qkv, att, datt, lse, n, share)
    dqkv, sum0 = sync(dqkv, sum0)
    dqkv = layout.swap(dqkv)
    if direct:
        sum0 = links.straight(sum0, 0)
        dqkv, sum0 = sync(dqkv, sum0)
        sum0 = links.straight(sum0, 1)
    dh2, db, dqkv, ln4 = back3(scal, dqkv, dh3, h2, g4, qkv_w, n, share)
    db, dqkv = sync(db, dqkv)
    low = layout.to_neighbour(db[-RIM:], 1)
    high = layout.to_neighbour(db[:RIM], -1)
    sum1 = weigh1(scal, y4, dqkv, spread, db)
    low, high, sum1, sum0, mixed = sync(low, high, sum1, sum0, mixed)
    if direct:
        total0 = links.finish([sum0])
        sum1 = links.first(1, *sum1)
    mixed = layout.send_home(mixed)
    dl, st, gdepth, ln3 = back2(scal, low, db, high, taps, mid, left, right, g3, point, group)
    if direct:
        dl, st, total0, sum1, mixed = sync(dl, st, total0, sum1, mixed)
        sum1 = links.next(sum1, 0)
    sum2 = weigh2(scal, dl, st, y2)
    if direct:
        (dl, sum2) = sync(dl, sum2)
        sum2 = links.first(2, *sum2)
    half = rows // 2
    fixed = (scal, dl, st, dh2, h1, joined, x_ext, g1, g2, glu, wide, narrow)
    dx_a, y1_a, dj_a, ln1_a, ln2_a = back1(*fixed, 0, half)
    if direct:
        dx_a, dl, sum1, sum2 = sync(dx_a, dl, sum1, sum2)
        sum1, sum2 = links.next_two(sum1, sum2)
        fixed = (scal, dl, *fixed[2:])
    dx_a = layout.send_home(dx_a)
    dx_b, y1_b, dj_b, ln1_b, ln2_b = back1(*fixed, half, rows - half)
    if direct:
        dx_b, dj_b = sync(dx_b, dj_b)
    dx_b = layout.send_home(dx_b)
    gains = (ln3, ln4, ln5)
    sum3 = weigh3(scal, (y1_a, y1_b), (dj_a, dj_b), (ln1_a, ln1_b), (ln2_a, ln2_b), gains, gdepth)
    if direct:
        sum3, sum2, sum1, dx_a = sync(sum3, sum2, sum1, dx_a)
        sum3 = links.cores(*sum3)
    if direct:
        sum3, sum2 = sync(sum3, sum2)
        sum2, sum3 = links.next_and_plane(sum2, sum3)
        *held, dx_b = sync(*sum2, sum3, dx_b)
        sums = (total0, links.finish([*sum1, *held]))
        tables = (sum(SUMS[0], []), sum([*SUMS[1], *SUMS[2], *SUMS[3]], []))
    else:
        sums = [links.scatter_whole(k, v) for k, v in enumerate((sum0, sum1, sum2, sum3))]
        tables = [sum(items, []) for items in SUMS]
    dx = jnp.concatenate([dx_a, dx_b], axis=0)
    out = {}
    for items, total in zip(tables, sums):
        out.update(links.rows_of(items, total))
    flat = out.pop("small")
    if not direct:
        flat = lax.all_gather(flat, AXES, axis=0, tiled=True)
    flat = flat.reshape(-1, 16 * PACK)
    sizes = [width for _, width in GAINS] + [TAP_RUN]
    at = 0
    for name, size in zip(SMALL, sizes):
        part = flat[:, at : at + size].reshape(-1)
        at += size
        if not direct:
            own = mine[name].shape[0]
            part = lax.dynamic_slice(part, (here * own,), (own,))
        out[name] = part
    return (mixed[None], dx.astype(F32)[None], *(out[name] for name in NAMES))


def solution(mesh):
    token, owner, rows = P("dp", "seq", None), P(AXES), P(AXES, None)
    params = (owner,) * 5 + (rows,) * 3 + (owner,) + (rows,) * 5
    return jax.shard_map(
        on_device,
        mesh=mesh,
        in_specs=(token, token, P("dp")) + params,
        out_specs=(token, token) + params,
        check_vma=False,
    )
```

```python
import functools
import math

import jax
import jax.numpy as jnp
import numpy as np
from jax import lax
from jax.experimental import pallas as pl
from jax.experimental.pallas import tpu as pltpu
from jax.sharding import PartitionSpec as P

D = 512
HEADS = 8
FF = 2048
KERNEL = 9
HEAD = 64
NARROW = 256
HALF = KERNEL // 2
LANES = 128
PACK = 256
RIM = 16
BLOCKS = 32
F32 = jnp.float32
BF = jnp.bfloat16
LOG2E = math.log2(math.e)
BIG = -1e30
AXES = ("seq", "dp")
VMEM = 58 << 20


def nt(a, b):
    return lax.dot_general(a, b, (((1,), (1,)), ((), ())), preferred_element_type=F32)


def nn(a, b):
    return lax.dot_general(a, b, (((1,), (0,)), ((), ())), preferred_element_type=F32)


def tn(a, b):
    return lax.dot_general(a, b, (((0,), (0,)), ((), ())), preferred_element_type=F32)


def call(kernel, ins, outs, scratch=(), micros=0, ties=(), steps=None):
    if ties:
        inner, fixed, count = kernel, len(ins), len(ties)

        def kernel(*refs):
            inner(*refs[:fixed], *refs[fixed + count :])

    def spec(shape, how, once):
        if how == "s":
            return pl.BlockSpec(memory_space=pltpu.SMEM)
        if steps is None:
            return pl.BlockSpec(memory_space=pltpu.VMEM)
        if isinstance(how, tuple):
            tile, start = how
            block = tuple(pl.Element(b) for b in (tile, *shape[1:]))
            rest = (0,) * (len(shape) - 1)
            return pl.BlockSpec(block, lambda i: (pl.multiple_of(start + i * tile, 16), *rest))
        if how is None:
            zeros = (0,) * len(shape)
            mode = pl.Buffered(1) if once else None
            return pl.BlockSpec(shape, lambda i: zeros, pipeline_mode=mode)
        return pl.BlockSpec((how, *shape[1:]), lambda i: (i, *(0,) * (len(shape) - 1)))

    args = [a for a, _ in ins]
    shapes = [jax.ShapeDtypeStruct(shape, dtype) for shape, dtype, _ in outs]
    moved = sum(math.prod(a.shape) * a.dtype.itemsize for a in args + shapes) if micros else 0
    return pl.pallas_call(
        kernel,
        out_shape=shapes,
        grid=() if steps is None else (steps,),
        in_specs=[spec(a.shape, how, True) for a, how in ins]
        + [pl.BlockSpec(memory_space=pl.ANY)] * len(ties),
        out_specs=[spec(shape, how, False) for shape, _, how in outs],
        scratch_shapes=[pltpu.VMEM(shape, dtype) for shape, dtype in scratch],
        compiler_params=pltpu.CompilerParams(vmem_limit_bytes=VMEM),
        cost_estimate=pl.CostEstimate(
            flops=int(micros * 1.15e9), bytes_accessed=moved, transcendentals=0
        ),
    )(*args, *ties)


def whole_call(kernel, outs, args, scratch=(), micros=0, ties=()):
    ins = [(a, "s" if i == 0 else None) for i, a in enumerate(args)]
    outs = [(shape, dtype, None) for shape, dtype in outs]
    return call(kernel, ins, outs, scratch, micros, ties)


def normalise(v):
    mean = jnp.mean(v, axis=1, keepdims=True)
    c = v - mean
    r = lax.rsqrt(jnp.mean(c * c, axis=1, keepdims=True) + 1e-05)
    return c * r, r


def norm_back(grad, hat, r, gain):
    g = grad * gain
    a = jnp.mean(g, axis=1, keepdims=True)
    b = jnp.mean(g * hat, axis=1, keepdims=True)
    return r * (g - a - hat * b)


C0 = math.sqrt(2.0 / math.pi)
C1 = 0.044715


def gelu(x):
    return 0.5 * x * (1.0 + jnp.tanh(x * (C0 + C0 * C1 * (x * x))))


def gelu_and_slope(x):
    xx = x * x
    t = jnp.tanh(x * (C0 + C0 * C1 * xx))
    half = 0.5 * (1.0 + t)
    return x * half, half + (0.5 * x) * (1.0 - t * t) * (C0 + 3.0 * C0 * C1 * xx)


def sigmoid(x):
    return 0.5 * jnp.tanh(0.5 * x) + 0.5


def fold8(v):
    return jnp.sum(v.reshape(v.shape[0] // 8, 8, v.shape[1]), axis=0)


def rows_at(i, tile, start=0, count=None):
    return pl.ds(pl.multiple_of(start + i * tile, 16), count or tile)


def places(base, rows, lanes=LANES):
    return base + lax.broadcasted_iota(jnp.int32, (rows, lanes), 0)


ROWS = {"glu": 16, "wide": 16, "narrow": 48, "point": 64, "qkv": 16, "attn": 16, "up": 16, "down": 64, "small": 16}


def columns_of(name, *chunks):
    return [(name, j) for j in chunks]


WIDE, GLU, QKV, UP = (columns_of(n, *range(k)) for n, k in (("wide", 8), ("glu", 4), ("qkv", 6), ("up", 8)))
NARROW_0, POINT_0, SMALL_0 = (columns_of(n, 0) for n in ("narrow", "point", "small"))
ATTN, DOWN = columns_of("attn", 0, 1), columns_of("down", 0, 1)
LAST = (UP + ATTN[:1], ATTN[1:] + DOWN)
GATHERS = ((WIDE, GLU + NARROW_0 + SMALL_0), (QKV[:5], QKV[5:] + POINT_0), LAST)
SUMS = (
    LAST,
    (QKV[:5], QKV[5:] + POINT_0),
    (WIDE[:6], WIDE[6:] + NARROW_0),
    (GLU[:2], GLU[2:] + SMALL_0),
)

SPLIT = (1, 2)


def height(items):
    return sum(ROWS[name] for name, _ in items)


def row_of(items, item):
    return height(items[: items.index(item)])


def slot_bits(half, r):
    high, low, z = r >> 3, r >> 2 & 1, r & 3
    x, y = (high, low) if half == 0 else (low, high)
    return z * 8 + y * 4 + x * 2


def slot_of(half, rel):
    z, y, x, c = rel >> 3, rel >> 2 & 1, rel >> 1 & 1, rel & 1
    high, low = (x, y) if half == 0 else (y, x)
    return c * 16 + high * 8 + low * 4 + z


def unpack(me, group, pieces, wanted):
    for half, items in enumerate(GATHERS[group]):
        for core in range(2):
            piece = pieces[half * 2 + core]
            for r in range(BLOCKS // 2):
                owner = (slot_bits(half, r) + core) ^ me
                for name, j in items:
                    if name in wanted:
                        b, off = ROWS[name], row_of(items, (name, j))
                        wanted[name][
                            pl.ds(pl.multiple_of(owner * b, 16), b), j * PACK : (j + 1) * PACK
                        ] = piece[r, off : off + b, :]


def put(me, group, ref, item, value, start=0):
    half = int(item in SUMS[group][1])
    off = row_of(SUMS[group][half], item) + half * height(SUMS[group][0])
    b = ROWS[item[0]]
    for k in range(value.shape[0] // b):
        slot = slot_of(half if group in SPLIT else 0, (start + k) ^ me)
        ref[slot, off : off + b, :] = value[k * b : (k + 1) * b]


def group_grads(group):
    rows = height(sum(SUMS[group], []))
    return [((BLOCKS // 2, rows, PACK), BF)] * 2


def group_slots(group):
    return ((BLOCKS, height(sum(SUMS[group], [])), PACK), BF)


def part_slots(slots, kept, given):
    kept[...] = slots[: BLOCKS // 2]
    given[...] = slots[BLOCKS // 2 :]


SHAPES = ({"glu": (D, 2 * D), "wide": (D, FF), "narrow": (3 * D, NARROW)}, {"qkv": (D, 3 * D), "point": (FF, NARROW)})

GAINS = ((0, 16), (16, 16), (32, 64), (96, 16), (112, 16))
TAPS = 128
TAP_RUN = KERNEL * FF // BLOCKS
SMALL_ROWS = 3


def iota(shape, dim):
    return lax.broadcasted_iota(jnp.int32, shape, dim)


def owner_slots(me, half):
    shape = (BLOCKS, BLOCKS)
    return (slot_of(half, iota(shape, 0) ^ me) == iota(shape, 1)).astype(F32).astype(BF)


def gain_maps(offset, width):
    total = BLOCKS * width
    owner = iota((BLOCKS, total), 1) // width == iota((BLOCKS, total), 0)
    value = iota((LANES, total), 0) == offset + iota((LANES, total), 1) % width
    return owner, value.astype(F32).astype(BF)


def tap_runs():
    for b in range(KERNEL * FF // 64):
        f = b * 64
        yield f // FF, f % FF, f // TAP_RUN, TAPS + f % TAP_RUN


def read_small(me, pieces, gains, taps, table):
    off = row_of(GATHERS[0][1], SMALL_0[0])
    for core in range(2):
        for r in range(BLOCKS // 2):
            rows = pieces[2 + core][r, off : off + 16, :].astype(F32)
            slot = core * 16 + r
            for q in range(SMALL_ROWS):
                table[slot : slot + 1, q * PACK : (q + 1) * PACK] = rows[q : q + 1, :]
    table[...] = nn(owner_slots(me, 1), table[...].astype(BF))
    for ref, (offset, width) in zip(gains, GAINS):
        owner, value = gain_maps(offset, width)
        spread = nn(table[:, :LANES].astype(BF), value)
        ref[...] = jnp.sum(jnp.where(owner, spread, 0.0), axis=0, keepdims=True)
    for tap, channel, who, place in tap_runs():
        taps[tap : tap + 1, channel : channel + 64] = table[who : who + 1, place : place + 64]


def write_small(me, gains, taps, table, block, grads):
    table[...] = jnp.zeros_like(table)
    total = jnp.zeros((BLOCKS, LANES), F32)
    for gain, (offset, width) in zip(gains, GAINS):
        owner, value = gain_maps(offset, width)
        total = total + nt(jnp.where(owner, gain[...], 0.0).astype(BF), value)
    table[:, :LANES] = total
    for tap, channel, who, place in tap_runs():
        table[who : who + 1, place : place + 64] = taps[tap : tap + 1, channel : channel + 64]
    table[...] = tn(owner_slots(me, 0), table[...].astype(BF))
    block[...] = jnp.zeros_like(block)
    for slot in range(BLOCKS):
        for q in range(SMALL_ROWS):
            block[slot, q : q + 1, :] = table[slot : slot + 1, q * PACK : (q + 1) * PACK]
    at = height(sum(SUMS[3], [])) - 16
    grads[:, at : at + 16, :] = block[...].astype(BF)


def pack_kernel(names, *refs):
    shards = dict(zip(names, refs))
    for ref, halves in zip(refs[len(names) :], GATHERS):
        at = 0
        for name, j in sum(halves, []):
            b = ROWS[name]
            if name == "small":
                ref[at : at + b, :] = shards[name][...]
            else:
                ref[at : at + b, :] = shards[name][:, j * PACK : (j + 1) * PACK]
            at += b


def pack(shards):
    names = tuple(shards)
    return call(
        functools.partial(pack_kernel, names),
        [(shards[k], None) for k in names],
        [((height(sum(halves, [])), PACK), BF, None) for halves in GATHERS],
        micros=2,
    )


def front1_kernel(scal, x_ref, p0, p1, p2, p3, h1_ref, y2_ref, joined_ref, *refs):
    weights, gains, taps, table = refs[:3], refs[3:8], refs[8], refs[9]
    g1, g2 = gains[:2]

    @pl.when(pl.program_id(0) == 0)
    def _():
        read_small(scal[2], (p0, p1, p2, p3), gains, taps, table)
        unpack(scal[2], 0, (p0, p1, p2, p3), dict(zip(SHAPES[0], weights)))

    x = x_ref[...].astype(F32)
    hat, _ = normalise(x)
    joined = nn((hat * g1[...]).astype(BF), weights[0][...])
    joined_ref[...] = joined
    h1 = x + joined[:, :D] * sigmoid(joined[:, D:])
    h1_ref[...] = h1
    hat2, _ = normalise(h1)
    y2_ref[...] = (hat2 * g2[...]).astype(BF)


def front1(scal, x, pieces, ties=()):
    rows = x.shape[0]
    tile = 160
    return call(
        front1_kernel,
        [(scal, "s"), (x, tile)] + [(p, None) for p in pieces],
        [((rows, D), F32, tile), ((rows, D), BF, tile), ((rows, 2 * D), F32, tile)]
        + [(shape, BF, None) for shape in SHAPES[0].values()]
        + [((1, BLOCKS * width), F32, None) for _, width in GAINS]
        + [((KERNEL, FF), F32, None)],
        scratch=[((BLOCKS, SMALL_ROWS * PACK), F32)],
        micros=12,
        ties=ties,
        steps=rows // tile,
    )


def front2_kernel(tile, group, scal, y2_ref, g3, wide, narrow, left_ref, right_ref, mid_ref, u_ref):
    rows = y2_ref.shape[0]
    base = scal[0] * (rows - 2 * RIM) - RIM
    first = scal[1]
    i = pl.program_id(0)

    @pl.when(i == 0)
    def _():
        u_ref[0:RIM, :] = jnp.zeros((RIM, 3 * NARROW), F32)
        u_ref[RIM + rows : 2 * RIM + rows, :] = jnp.zeros((RIM, 3 * NARROW), F32)

        def narrow_step(j, carry):
            y = y2_ref[rows_at(j, tile), :]
            for k in range(3):
                u_ref[rows_at(j, tile, RIM), k * NARROW : (k + 1) * NARROW] = nn(
                    y, narrow[k * D : (k + 1) * D, :]
                )
            return carry

        lax.fori_loop(0, rows // tile, narrow_step, 0)

    around = pl.ds(pl.multiple_of(i * tile, 16), tile + 2 * RIM)
    left = nn(y2_ref[rows_at(i, tile), :], wide[...])
    left_ref[...] = left
    pos = places(base + i * tile, tile, NARROW)
    before = pltpu.roll(u_ref[around, 0:NARROW], 1, 0)[RIM : RIM + tile]
    after = pltpu.roll(u_ref[around, 2 * NARROW :], tile + 2 * RIM - 1, 0)[RIM : RIM + tile]
    right = u_ref[rows_at(i, tile, RIM), NARROW : 2 * NARROW]
    right = right + jnp.where((pos == first) | (pos == 0), 0.0, before)
    right = right + jnp.where((pos + 1 == first) | (pos + 1 == group), 0.0, after)
    right_ref[...] = right
    for q in range(0, tile, STEP):
        at = slice(q, q + STEP)
        left = gelu(left_ref[at, :])
        joined = jnp.concatenate([left[:, :NARROW] + gelu(right_ref[at, :]), left[:, NARROW:]], axis=1)
        hat, _ = normalise(joined)
        row = base + i * tile + q + iota((STEP, 1), 0)
        inside = ((row >= 0) & (row < group)).astype(F32)
        mid_ref[at, :] = (hat * inside * g3[...]).astype(BF)


def front2(scal, y2, g3, wide, narrow, group, ties=()):
    rows = y2.shape[0]
    tile = 160
    return call(
        functools.partial(front2_kernel, tile, group),
        [(scal, "s"), (y2, None), (g3, None), (wide, None), (narrow, None)],
        [((rows, FF), F32, tile), ((rows, NARROW), F32, tile), ((rows, FF), BF, tile)],
        scratch=[((rows + 2 * RIM, 3 * NARROW), F32)],
        micros=12,
        ties=ties,
        steps=rows // tile,
    )


def crosses(pos, offset, first):
    if offset > 0:
        return (pos < first) & (pos + offset >= first)
    return (pos >= first) & (pos + offset < first)


WIDTH = 4
STEP = 16


def front3_kernel(tile, n, share, scal, mid_ref, taps, h1_ref, g4, p0, p1, p2, p3, *refs):
    spread_ref, h2_ref, y4_ref = refs[:3]
    outs = refs[3 : 3 + n]
    qkv_w, point, win, qkv_s = refs[3 + n :]
    i = pl.program_id(0)

    @pl.when(i == 0)
    def _():
        unpack(scal[2], 1, (p0, p1, p2, p3), {"qkv": qkv_w, "point": point})

    s, first = scal[0], scal[1]
    begin = s * (mid_ref.shape[0] - 2 * RIM) + i * tile
    near = (first > begin - HALF) & (first < begin + tile + HALF)

    def chunk(c, carry):
        around = pl.ds(pl.multiple_of(i * tile, 16), tile + 2 * RIM)
        lanes = [pl.ds(pl.multiple_of((c * WIDTH + w) * LANES, LANES), LANES) for w in range(WIDTH)]
        for w in range(WIDTH):
            win[w] = mid_ref[around, lanes[w]].astype(F32)
        for masked in (False, True):

            @pl.when(near if masked else jnp.logical_not(near))
            def _():
                for w in range(WIDTH):
                    tap = [taps[k : k + 1, lanes[w]] for k in range(KERNEL)]
                    for r in range(0, tile, STEP):
                        pos = places(begin + r, STEP)
                        total = None
                        for k in range(KERNEL):
                            o = k - HALF
                            v = win[w, RIM + o + r : RIM + o + r + STEP, :]
                            if masked and o != 0:
                                v = jnp.where(crosses(pos, o, first), 0.0, v)
                            total = v * tap[k] if total is None else total + v * tap[k]
                        spread_ref[r : r + STEP, lanes[w]] = total.astype(BF)

        return carry

    lax.fori_loop(0, FF // (WIDTH * LANES), chunk, 0)
    h1 = h1_ref[rows_at(i, tile, RIM), :]
    branch = nn(spread_ref[...], point[...])
    h2 = jnp.concatenate([h1[:, :NARROW] + branch, h1[:, NARROW:]], axis=1)
    h2_ref[...] = h2
    hat, _ = normalise(h2)
    y4 = (hat * g4[...]).astype(BF)
    y4_ref[...] = y4
    qkv_s[...] = nn(y4, qkv_w[...]).astype(BF)
    for k in range(n):
        block = (s ^ k) // share
        for part in range(3):
            outs[k][:, part * LANES : (part + 1) * LANES] = qkv_s[
                :, pl.ds(pl.multiple_of(part * D + block * LANES, LANES), LANES)
            ]


def front3(scal, mid, taps, h1, g4, pieces, n, share, ties=()):
    rows = mid.shape[0] - 2 * RIM
    tile = 128
    return call(
        functools.partial(front3_kernel, tile, n, share),
        [(scal, "s")] + [(a, None) for a in (mid, taps, h1, g4, *pieces)],
        [((rows, FF), BF, tile), ((rows, D), F32, tile), ((rows, D), BF, tile)]
        + [((rows, 3 * LANES), BF, tile)] * n
        + [(shape, BF, None) for shape in SHAPES[1].values()],
        scratch=[((WIDTH, tile + 2 * RIM, LANES), F32), ((tile, 3 * D), BF)],
        micros=20,
        ties=ties,
        steps=rows // tile,
    )


def gather_lanes(wide_ref, n, share, s, blocks, parts):
    rows = wide_ref.shape[0]
    for k in range(n):
        block = (s ^ k) // share
        for part in range(parts):
            lanes = pl.ds(pl.multiple_of(part * D + block * LANES, LANES), LANES)
            new = blocks[k][:, part * LANES : (part + 1) * LANES]
            if share > 1:
                lane = lax.broadcasted_iota(jnp.int32, (rows, LANES), 1)
                mine = lane // (LANES // share) == (s ^ k) % share
                new = jnp.where(mine, new.astype(F32), wide_ref[:, lanes].astype(F32)).astype(BF)
            wide_ref[:, lanes] = new


def middle_kernel(n, share, scal, h2_ref, *refs):
    att = refs[:n]
    cot_ref, g5, p0, p1, p2, p3, mixed_ref, dh3_ref = refs[n : n + 8]
    datt = refs[n + 8 : 2 * n + 8]
    att_s, y5_s, inner_s, du_s, ln_out = refs[2 * n + 8 : 2 * n + 13]
    wa, wup, wdown, ln_ref = refs[2 * n + 13 :]
    s = scal[0]
    i = pl.program_id(0)

    @pl.when(i == 0)
    def _():
        unpack(scal[2], 2, (p0, p1, p2, p3), {"attn": wa, "up": wup, "down": wdown})
        ln_ref[...] = jnp.zeros_like(ln_ref)

    gather_lanes(att_s, n, share, s, att, 1)
    h3 = h2_ref[...] + nn(att_s[...], wa[...])
    hat, r = normalise(h3)
    y5 = (hat * g5[...]).astype(BF)
    y5_s[...] = y5
    value, slope = gelu_and_slope(nn(y5, wup[...]))
    inner = value.astype(BF)
    inner_s[...] = inner
    mixed_ref[...] = (h3 + nn(inner, wdown[...])).astype(BF)
    cot = cot_ref[...]
    du = (nt(cot, wdown[...]) * slope).astype(BF)
    du_s[...] = du
    dy5 = nt(du, wup[...])
    ln_ref[...] += fold8(dy5 * hat)
    dh3 = cot.astype(F32) + norm_back(dy5, hat, r, g5[...])
    dh3_ref[...] = dh3
    da = nt(dh3.astype(BF), wa[...]).astype(BF)
    for j in range(D // LANES):
        for k in range(n):

            @pl.when((s ^ k) // share == j)
            def _():
                datt[k][...] = da[:, j * LANES : (j + 1) * LANES]

    ln_out[...] = jnp.sum(ln_ref[...], axis=0, keepdims=True)


def middle(scal, h2, att, cot, g5, pieces, n, share, ties=()):
    rows = h2.shape[0]
    tile = 128
    return call(
        functools.partial(middle_kernel, n, share),
        [(scal, "s"), (h2, tile)]
        + [(a, tile) for a in (*att, cot)]
        + [(a, None) for a in (g5, *pieces)],
        [((rows, D), BF, tile), ((rows, D), F32, tile)]
        + [((rows, LANES), BF, tile)] * n
        + [((rows, c), BF, tile) for c in (D, D, FF, FF)]
        + [((1, D), F32, None)],
        scratch=[((D, D), BF), ((D, FF), BF), ((FF, D), BF), ((8, D), F32)],
        micros=20,
        ties=ties,
        steps=rows // tile,
    )


def weigh0_kernel(scal, att_s, y5_s, inner_s, du_s, cot_ref, dh3_ref, kept, given, grads):
    me = scal[2]
    att_t = att_s[...].T
    for j in range(D // PACK):
        part = nn(att_t, dh3_ref[:, j * PACK : (j + 1) * PACK].astype(BF))
        put(me, 0, grads, ("attn", j), part.astype(BF))
    y5_t = y5_s[...].T
    for j in range(FF // PACK):
        cols = slice(j * PACK, (j + 1) * PACK)
        put(me, 0, grads, ("up", j), nn(y5_t, du_s[:, cols]).astype(BF))
        down = tn(inner_s[:, cols], cot_ref[...]).astype(BF)
        for m in range(D // PACK):
            put(me, 0, grads, ("down", m), down[:, m * PACK : (m + 1) * PACK], j * PACK // 64)
    part_slots(grads, kept, given)


def weigh0(scal, att, y5, inner, du, cot, dh3, ties=()):
    return whole_call(
        weigh0_kernel,
        group_grads(0),
        [scal, att, y5, inner, du, cot, dh3],
        scratch=[group_slots(0)],
        micros=10,
        ties=ties,
    )


def back3_kernel(n, share, scal, *refs):
    blocks = refs[:n]
    dh3_ref, h2_ref, g4, qkv_w = refs[n : n + 4]
    dh2_ref, db_ref, dqkv_s, ln_out, ln_ref = refs[n + 4 :]

    @pl.when(pl.program_id(0) == 0)
    def _():
        ln_ref[...] = jnp.zeros_like(ln_ref)

    gather_lanes(dqkv_s, n, share, scal[0], blocks, 3)
    dy4 = nt(dqkv_s[...], qkv_w[...])
    hat, r = normalise(h2_ref[...])
    ln_ref[...] += fold8(dy4 * hat)
    dh2 = dh3_ref[...] + norm_back(dy4, hat, r, g4[...])
    dh2_ref[...] = dh2
    db_ref[...] = dh2[:, :NARROW].astype(BF)
    ln_out[...] = jnp.sum(ln_ref[...], axis=0, keepdims=True)


def back3(scal, blocks, dh3, h2, g4, qkv_w, n, share, ties=()):
    rows = h2.shape[0]
    tile = 128
    return call(
        functools.partial(back3_kernel, n, share),
        [(scal, "s")] + [(a, tile) for a in (*blocks, dh3, h2)] + [(g4, None), (qkv_w, None)],
        [((rows, D), F32, tile), ((rows, NARROW), BF, tile), ((rows, 3 * D), BF, tile)]
        + [((1, D), F32, None)],
        scratch=[((8, D), F32)],
        micros=6,
        ties=ties,
        steps=rows // tile,
    )


def weigh1_kernel(scal, y4_ref, dqkv_s, spread_ref, db_ref, kept, given, grads):
    me = scal[2]
    y4_t = y4_ref[...].T
    for j in range(3 * D // PACK):
        part = nn(y4_t, dqkv_s[:, j * PACK : (j + 1) * PACK])
        put(me, 1, grads, ("qkv", j), part.astype(BF))
    for j in range(FF // PACK):
        part = tn(spread_ref[:, j * PACK : (j + 1) * PACK], db_ref[...]).astype(BF)
        put(me, 1, grads, ("point", 0), part, j * PACK // 64)
    part_slots(grads, kept, given)


def weigh1(scal, y4, dqkv, spread, db, ties=()):
    return whole_call(
        weigh1_kernel,
        group_grads(1),
        [scal, y4, dqkv, spread, db],
        scratch=[group_slots(1)],
        micros=3,
        ties=ties,
    )


def back2_kernel(tile, group, scal, low_ref, db_ref, high_ref, *refs):
    taps, mid_ref, left_ref, right_ref, g3, point = refs[:6]
    dl, st, gdepth_out, ln_out = refs[6:10]
    dbx, dsp, win, dmid, dr, gdepth_ref, ln_ref = refs[10:]
    rows = db_ref.shape[0]
    ext = rows + 2 * RIM
    base = scal[0] * rows - RIM
    first = scal[1]
    i = pl.program_id(0)
    last = ext // tile - 1

    @pl.when(i == 0)
    def _():
        dbx[0:RIM, :] = low_ref[...]
        dbx[RIM : RIM + rows, :] = db_ref[...]
        dbx[RIM + rows :, :] = high_ref[...]
        dsp[0:RIM, :] = jnp.zeros((RIM, FF), F32)
        dsp[RIM + ext :, :] = jnp.zeros((RIM, FF), F32)
        dr[0:RIM, :] = jnp.zeros((RIM, NARROW), F32)
        dr[RIM + ext :, :] = jnp.zeros((RIM, NARROW), F32)
        gdepth_ref[...] = jnp.zeros_like(gdepth_ref)
        ln_ref[...] = jnp.zeros_like(ln_ref)

        def spread_step(j, carry):
            dsp[rows_at(j, tile, RIM), :] = nt(dbx[rows_at(j, tile), :], point[...])
            return carry

        lax.fori_loop(0, ext // tile, spread_step, 0)

    begin = base + i * tile
    near = (first > begin - HALF) & (first < begin + tile + HALF)
    near = near | (i == 0) | (i == last)

    def chunk(c, carry):
        around = pl.ds(pl.multiple_of(i * tile, 16), tile + 2 * RIM)
        lanes = [pl.ds(pl.multiple_of((c * WIDTH + w) * LANES, LANES), LANES) for w in range(WIDTH)]
        for w in range(WIDTH):
            win[w] = dsp[around, lanes[w]]
        for masked in (False, True):

            @pl.when(near if masked else jnp.logical_not(near))
            def _():
                for w in range(WIDTH):
                    tap = [taps[k : k + 1, lanes[w]] for k in range(KERNEL)]
                    pairs = [None] * KERNEL
                    for r in range(0, tile, STEP):
                        pos = places(begin + r, STEP)
                        local = i * tile + r + iota((STEP, LANES), 0)
                        mid = mid_ref[r : r + STEP, lanes[w]].astype(F32)
                        total = None
                        for k in range(KERNEL):
                            o = HALF - k
                            v = win[w, RIM + o + r : RIM + o + r + STEP, :]
                            if masked and o != 0:
                                v = jnp.where(crosses(pos, o, first), 0.0, v)
                            counted = v
                            if masked:
                                kept = (local + o >= RIM) & (local + o < RIM + rows)
                                counted = jnp.where(kept, v, 0.0)
                            counted = counted * mid
                            counted = counted[:8] + counted[8:]
                            pairs[k] = counted if pairs[k] is None else pairs[k] + counted
                            total = v * tap[k] if total is None else total + v * tap[k]
                        dmid[r : r + STEP, lanes[w]] = total
                    for k in range(KERNEL):
                        gdepth_ref[k * 8 : (k + 1) * 8, lanes[w]] += pairs[k]

        return carry

    lax.fori_loop(0, FF // (WIDTH * LANES), chunk, 0)
    for q in range(0, tile, STEP):
        at = slice(q, q + STEP)
        left, slope = gelu_and_slope(left_ref[at, :])
        right, slope_r = gelu_and_slope(right_ref[at, :])
        joined = jnp.concatenate([left[:, :NARROW] + right, left[:, NARROW:]], axis=1)
        hat, r = normalise(joined)
        local = i * tile + q + iota((STEP, 1), 0)
        own = ((local >= RIM) & (local < RIM + rows)).astype(F32)
        pos = base + local
        grad = dmid[at, :] * ((pos >= 0) & (pos < group)).astype(F32)
        ln_ref[...] += fold8(grad * hat * own)
        dj = norm_back(grad, hat, r, g3[...])
        dl[at, :] = (dj * slope).astype(BF)
        dr[rows_at(i, tile, RIM + q, STEP), :] = (dj[:, :NARROW] * slope_r).astype(BF).astype(F32)

    @pl.when(i == last)
    def _():
        for k in range(KERNEL):
            gdepth_out[k : k + 1, :] = jnp.sum(
                gdepth_ref[k * 8 : (k + 1) * 8, :], axis=0, keepdims=True
            )
        ln_out[...] = jnp.sum(ln_ref[...], axis=0, keepdims=True)
        part = 128

        def gather_step(j, carry):
            at = rows_at(j, part)
            around = pl.ds(pl.multiple_of(RIM + j * part, 16), part + 2 * RIM)
            pos = places(base + RIM + j * part, part, NARROW)
            v = dr[around, :]
            after = pltpu.roll(v, part + 2 * RIM - 1, 0)[RIM : RIM + part]
            before = pltpu.roll(v, 1, 0)[RIM : RIM + part]
            after = jnp.where((pos + 1 == first) | (pos + 1 == group), 0.0, after)
            before = jnp.where((pos == first) | (pos == 0), 0.0, before)
            st[at, 0:NARROW] = after.astype(BF)
            st[at, NARROW : 2 * NARROW] = v[RIM : RIM + part].astype(BF)
            st[at, 2 * NARROW :] = before.astype(BF)
            return carry

        lax.fori_loop(0, rows // part, gather_step, 0)


def back2(scal, low, db, high, taps, mid, left, right, g3, point, group, ties=()):
    rows = db.shape[0]
    ext = rows + 2 * RIM
    tile = 160
    return call(
        functools.partial(back2_kernel, tile, group),
        [(scal, "s")]
        + [(a, None) for a in (low, db, high, taps)]
        + [(a, tile) for a in (mid, left, right)]
        + [(g3, None), (point, None)],
        [((ext, FF), BF, tile), ((rows, 3 * NARROW), BF, None)]
        + [((KERNEL, FF), F32, None), ((1, FF), F32, None)],
        scratch=[
            ((ext, NARROW), BF),
            ((ext + 2 * RIM, FF), F32),
            ((WIDTH, tile + 2 * RIM, LANES), F32),
            ((tile, FF), F32),
            ((ext + 2 * RIM, NARROW), F32),
            ((8 * KERNEL, FF), F32),
            ((8, FF), F32),
        ],
        micros=44,
        ties=ties,
        steps=ext // tile,
    )


def back1_kernel(scal, dl, st, dh2_ref, h1_ref, joined_ref, x_ref, g1, g2, *refs):
    glu, wide, narrow, dx_ref, y1_ref, dj_ref, ln1_out, ln2_out, ln1_ref, ln2_ref = refs
    i = pl.program_id(0)

    @pl.when(i == 0)
    def _():
        ln1_ref[...] = jnp.zeros_like(ln1_ref)
        ln2_ref[...] = jnp.zeros_like(ln2_ref)

    dy2 = nt(dl[...], wide[...])
    for k in range(3):
        dy2 = dy2 + nt(st[:, k * NARROW : (k + 1) * NARROW], narrow[k * D : (k + 1) * D, :])
    hat2, r2 = normalise(h1_ref[...])
    ln2_ref[...] += fold8(dy2 * hat2)
    dh1 = dh2_ref[...] + norm_back(dy2, hat2, r2, g2[...])
    gate = sigmoid(joined_ref[:, D:])
    value = joined_ref[:, :D]
    dj_ref[:, :D] = (dh1 * gate).astype(BF)
    dj_ref[:, D:] = (dh1 * value * gate * (1.0 - gate)).astype(BF)
    x = x_ref[...].astype(F32)
    hat1, r1 = normalise(x)
    y1_ref[...] = (hat1 * g1[...]).astype(BF)
    dy1 = nt(dj_ref[...], glu[...])
    ln1_ref[...] += fold8(dy1 * hat1)
    dx_ref[...] = (dh1 + norm_back(dy1, hat1, r1, g1[...])).astype(dx_ref.dtype)
    ln1_out[...] = jnp.sum(ln1_ref[...], axis=0, keepdims=True)
    ln2_out[...] = jnp.sum(ln2_ref[...], axis=0, keepdims=True)


def back1(scal, dl, st, dh2, h1, joined, x, g1, g2, glu, wide, narrow, start, rows):
    tile = 128
    own, ext = (tile, start), (tile, start + RIM)
    return call(
        back1_kernel,
        [(scal, "s"), (dl, ext), (st, own), (dh2, own), (h1, ext), (joined, ext), (x, ext)]
        + [(a, None) for a in (g1, g2, glu, wide, narrow)],
        [((rows, D), BF, tile), ((rows, D), BF, tile), ((rows, 2 * D), BF, tile)]
        + [((1, D), F32, None)] * 2,
        scratch=[((8, D), F32), ((8, D), F32)],
        micros=5,
        steps=rows // tile,
    )


def weigh2_kernel(scal, dl, st, y2_ref, kept, given, grads, gn):
    me = scal[2]
    rows = st.shape[0]
    y2_t = y2_ref[RIM : RIM + rows, :].T
    for j in range(FF // PACK):
        part = nn(y2_t, dl[RIM : RIM + rows, j * PACK : (j + 1) * PACK]).astype(BF)
        put(me, 2, grads, ("wide", j), part)
    for k in range(3):
        gn[k * D : (k + 1) * D, :] = nn(y2_t, st[:, k * NARROW : (k + 1) * NARROW]).astype(BF)
    put(me, 2, grads, ("narrow", 0), gn[...])
    part_slots(grads, kept, given)


def weigh2(scal, dl, st, y2):
    return whole_call(
        weigh2_kernel,
        group_grads(2),
        [scal, dl, st, y2],
        scratch=[group_slots(2), ((3 * D, NARROW), BF)],
        micros=3,
    )


def weigh3_kernel(halves, scal, *refs):
    y1, dj, ln1, ln2 = (refs[i * halves : (i + 1) * halves] for i in range(4))
    gains, taps, kept, given = refs[4 * halves : 4 * halves + 3], *refs[4 * halves + 3 : 4 * halves + 6]
    grads, table, block, ln1_s, ln2_s = refs[4 * halves + 6 :]
    me = scal[2]
    for total, parts in ((ln1_s, ln1), (ln2_s, ln2)):
        total[...] = sum(p[...] for p in parts[1:]) + parts[0][...]
    write_small(me, (ln1_s, ln2_s, *gains), taps, table, block, grads)
    turned = [y[...].T for y in y1]
    for j in range(2 * D // PACK):
        part = None
        for y, d in zip(turned, dj):
            more = nn(y, d[:, j * PACK : (j + 1) * PACK])
            part = more if part is None else part + more
        put(me, 3, grads, ("glu", j), part.astype(BF))
    part_slots(grads, kept, given)


def weigh3(scal, y1, dj, ln1, ln2, gains, taps):
    return whole_call(
        functools.partial(weigh3_kernel, len(y1)),
        group_grads(3),
        [scal, *y1, *dj, *ln1, *ln2, *gains, taps],
        scratch=[group_slots(3), ((BLOCKS, SMALL_ROWS * PACK), F32), ((BLOCKS, 16, PACK), F32)]
        + [((1, D), F32)] * 2,
        micros=0,
    )


def lane_maps(rows, head):
    lane = lax.broadcasted_iota(jnp.int32,(rows,LANES),1)
    own = (lane >= head*HEAD) & (lane < (head+1)*HEAD)
    rel = lane - (1-head)*HEAD
    return own, rel

def id_column(base, rows, first):
    pos = base + lax.broadcasted_iota(jnp.int32,(rows,LANES),0)
    return pos >= first

def split3(v):
    hi = v.astype(BF).astype(F32)
    mid = (v-hi).astype(BF).astype(F32)
    return hi, mid, v-hi-mid

def tile_ids(start, rows, first):
    return start < first, start+rows > first

def overlap(a_start,a_rows,b_start,b_rows,first):
    a0,a1 = tile_ids(a_start,a_rows,first); b0,b1=tile_ids(b_start,b_rows,first)
    return (a0&b0)|(a1&b1)

def attend_kernel(n, heads, share, tq, tk, scal, *refs):
    qkv = refs[:n]; att = refs[n:2*n]; lse_ref = refs[2*n]
    qa, ka, va, mx_ref, m_ref, q2_ref, acc_ref = refs[2*n+1:]
    s = scal[0]; first = scal[1]
    rows = qkv[0].shape[0]
    for k in range(n):
        base = (s ^ k)*rows
        id1 = id_column(base, rows, first).astype(F32)
        q = qkv[k][:, 0:LANES].astype(F32)*(HEAD**-0.5)
        key = qkv[k][:, LANES:2*LANES].astype(F32)
        v = qkv[k][:, 2*LANES:3*LANES].astype(F32)
        for i in range(heads):
            h = i if share==1 else s % share
            own, rel = lane_maps(rows, h)
            qx = jnp.where(rel==0, 1.0-id1, jnp.where(rel==1, id1, 0.0))
            kx = jnp.where(rel==0, id1*BIG, jnp.where(rel==1, (1.0-id1)*BIG, jnp.where(rel<5,1.0,0.0)))
            qa[i, k*rows:(k+1)*rows,:] = jnp.where(own, q, qx).astype(BF)
            ka[i, k*rows:(k+1)*rows,:] = jnp.where(own, key, kx).astype(BF)
            va[i, k*rows:(k+1)*rows,:] = jnp.where(own, v, 1.0).astype(BF)
    per = rows//tq; per_k = rows//tk
    def fold(sc, best):
        for j in range(tk//LANES):
            best = jnp.maximum(best, sc[:, j*LANES:(j+1)*LANES])
        return best
    def q_step(it, carry):
        kq = it//per
        r0 = pl.multiple_of((it % per)*tq, tq)
        g0 = pl.multiple_of(it*tq, tq)
        own0 = pl.multiple_of((g0//tk)*tk, tk)
        q_start = (s ^ kq)*rows + r0
        for i in range(heads):
            for j in range(max(1,tq//tk)):
                sc = nt(qa[i, pl.ds(g0,tq),:], ka[i, pl.ds(own0+j*tk,tk),:])
                best = fold(sc, sc[:, :LANES] if j==0 else best)
            mx_ref[i] = best
            m_ref[i] = jnp.zeros((tq,LANES),F32)
        def attempt(again):
            for i in range(heads):
                h = i if share==1 else s % share
                own, rel = lane_maps(tq, h)
                m = jnp.max(mx_ref[i], axis=1, keepdims=True)
                mb = m_ref[i] + jnp.broadcast_to(m, (tq,LANES))
                m_ref[i] = mb
                hi,mid,lo = split3(-mb)
                q = qa[i, pl.ds(g0,tq),:].astype(F32)
                q2_ref[i] = jnp.where(rel==2,hi,jnp.where(rel==3,mid,jnp.where(rel==4,lo,q))).astype(BF)
            mx_ref[...] = jnp.full_like(mx_ref, -3e38)
            acc_ref[...] = jnp.zeros_like(acc_ref)
            for kt in range(n*per_k):
                k_start = (s ^ (kt//per_k))*rows + (kt%per_k)*tk
                @pl.when(overlap(q_start,tq,k_start,tk,first))
                def _():
                    for i in range(heads):
                        sc = nt(q2_ref[i], ka[i, kt*tk:(kt+1)*tk,:])
                        mx_ref[i] = fold(sc, mx_ref[i])
                        p = jnp.exp2(sc*LOG2E).astype(BF)
                        acc_ref[i] += nn(p, va[i, kt*tk:(kt+1)*tk,:])
            return (jnp.max(mx_ref[...]) > 40.0).astype(jnp.int32)
        lax.while_loop(lambda again: again > 0, attempt, jnp.int32(1))
        out = jnp.zeros((tq,LANES),F32); lse = jnp.zeros((tq,LANES),F32)
        for i in range(heads):
            h = i if share==1 else s % share
            own,_ = lane_maps(tq,h)
            acc = acc_ref[i]
            total = pltpu.roll(acc, HEAD, 1)
            out = jnp.where(own, acc/total, out)
            lse = jnp.where(own, m_ref[i]+jnp.log(total), lse)
        lse_ref[pl.ds(g0,tq),:] = lse
        for k in range(n):
            @pl.when(kq==k)
            def _():
                att[k][pl.ds(r0,tq),:] = out.astype(BF)
        return carry
    lax.fori_loop(0, n*per, q_step, 0)

def attend(scal, blocks, n, share, tq=768, tk=768, ties=()):
    rows = blocks[0].shape[0]
    heads = 2 // share
    return whole_call(
        functools.partial(attend_kernel, n, heads, share, tq, tk),
        [((rows, LANES), BF)] * n + [((n * rows, LANES), F32)],
        [scal, *blocks],
        scratch=[((heads, n * rows, LANES), BF)] * 3
        + [((heads, tq, LANES), F32)] * 2
        + [((heads, tq, LANES), BF), ((heads, tq, LANES), F32)],
        ties=ties,
        micros=36,
    )


def attend_back_kernel(n, heads, share, tq, tk, scal, *refs):
    qkv = refs[:n]; att = refs[n:2*n]; dat = refs[2*n:3*n]; lse_ref = refs[3*n]
    out = refs[3*n+1:4*n+1]
    qa, ka, va, da, dq_ref, dk_ref, dv_ref = refs[4*n+1:]
    s = scal[0]; first = scal[1]
    rows = qkv[0].shape[0]
    for k in range(n):
        base = (s ^ k)*rows
        sl = slice(k*rows,(k+1)*rows)
        id1 = id_column(base, rows, first).astype(F32)
        q = qkv[k][:, 0:LANES].astype(F32)*(HEAD**-0.5)
        key = qkv[k][:, LANES:2*LANES].astype(F32)
        v = qkv[k][:, 2*LANES:3*LANES].astype(F32)
        do = dat[k][...].astype(F32)
        prod = do*att[k][...].astype(F32)
        for i in range(heads):
            h = i if share==1 else s % share
            own, rel = lane_maps(rows, h)
            lse = pltpu.roll(lse_ref[sl,:], HEAD, 1)
            hi,mid,lo = split3(-lse)
            delta = jnp.sum(jnp.where(own,prod,0.0),axis=1,keepdims=True)
            dhi,dmid,dlo = split3(-delta)
            qx = jnp.where(rel==0, 1.0-id1, jnp.where(rel==1, id1, jnp.where(rel==2,hi,jnp.where(rel==3,mid,jnp.where(rel==4,lo,0.0)))))
            kx = jnp.where(rel==0, id1*BIG, jnp.where(rel==1, (1.0-id1)*BIG, jnp.where(rel<5,1.0,0.0)))
            vx = jnp.where(rel<3,1.0,0.0)
            dx = jnp.where(rel==0,dhi,jnp.where(rel==1,dmid,jnp.where(rel==2,dlo,0.0)))
            qa[i,sl,:] = jnp.where(own,q,qx).astype(BF)
            ka[i,sl,:] = jnp.where(own,key,kx).astype(BF)
            va[i,sl,:] = jnp.where(own,v,vx).astype(BF)
            da[i,sl,:] = jnp.where(own,do,dx).astype(BF)
    dq_ref[...] = jnp.zeros_like(dq_ref)
    per_q = rows//tq; per_k = rows//tk
    def k_step(kt, carry):
        k0 = pl.multiple_of(kt*tk, tk)
        kk = kt//per_k
        k_start = (s ^ kk)*rows + (kt % per_k)*tk
        for i in range(heads):
            dk_ref[i] = jnp.zeros((tk,LANES),F32)
            dv_ref[i] = jnp.zeros((tk,LANES),F32)
        def q_step(qt, c2):
            q0 = pl.multiple_of(qt*tq, tq)
            q_start = (s ^ (qt//per_q))*rows + (qt % per_q)*tq
            @pl.when(overlap(q_start,tq,k_start,tk,first))
            def _():
                for i in range(heads):
                    qq = qa[i,pl.ds(q0,tq),:]; kx = ka[i,pl.ds(k0,tk),:]; dd = da[i,pl.ds(q0,tq),:]
                    st = nt(kx, qq)
                    p = jnp.exp2(st*LOG2E)
                    dp = nt(va[i,pl.ds(k0,tk),:], dd)
                    ds = (p*dp).astype(BF)
                    dv_ref[i] += nn(p.astype(BF), dd)
                    dk_ref[i] += nn(ds, qq)
                    dq_ref[i,pl.ds(q0,tq),:] += tn(ds, kx)
            return c2
        lax.fori_loop(0, n*per_q, q_step, 0)
        dk = jnp.zeros((tk,LANES),F32); dv = jnp.zeros((tk,LANES),F32)
        for i in range(heads):
            h = i if share==1 else s % share
            own,_ = lane_maps(tk,h)
            dk = jnp.where(own, dk_ref[i], dk); dv = jnp.where(own, dv_ref[i], dv)
        r0 = pl.multiple_of((kt % per_k)*tk, tk)
        for k in range(n):
            @pl.when(kk==k)
            def _():
                out[k][pl.ds(r0,tk),LANES:2*LANES] = dk.astype(BF)
                out[k][pl.ds(r0,tk),2*LANES:3*LANES] = dv.astype(BF)
        return carry
    lax.fori_loop(0, n*per_k, k_step, 0)
    for k in range(n):
        sl = slice(k*rows,(k+1)*rows)
        dq = jnp.zeros((rows,LANES),F32)
        for i in range(heads):
            h = i if share==1 else s % share
            own,_ = lane_maps(rows,h)
            dq = jnp.where(own, dq_ref[i,sl,:], dq)
        out[k][:, 0:LANES] = (dq*(HEAD**-0.5)).astype(BF)

def attend_back(scal, blocks, att, datt, lse, n, share, tq=384, tk=384, ties=()):
    rows = blocks[0].shape[0]
    heads = 2 // share
    return whole_call(
        functools.partial(attend_back_kernel, n, heads, share, tq, tk),
        [((rows, 3 * LANES), BF)] * n,
        [scal, *blocks, *att, *datt, lse],
        scratch=[((heads, n * rows, LANES), BF)] * 4
        + [((heads, n * rows, LANES), F32)]
        + [((heads, tk, LANES), F32)] * 2,
        ties=ties,
        micros=58,
    )


class Links:
    def __init__(self, n_seq, n_dp):
        self.count = n_seq * n_dp
        self.direct = (n_seq, n_dp) == (4, 8)

    def flip(self, value, mask):
        return lax.ppermute(value, AXES, [(i, i ^ mask) for i in range(self.count)])

    def near(self, block):
        return jnp.stack([block] + [self.flip(block, k << 3) for k in range(1, 4)])

    def part(self, group, held):
        low = height(GATHERS[group][0])
        return [held[:, :low], held[:, low:]]

    def spread(self, held, stage):
        masks = ((4, 2), (2, 4))[stage]
        return [jnp.concatenate([h, self.flip(h, m)]) for h, m in zip(held, masks)]

    def across(self, held):
        return [held[0], self.flip(held[0], 1), held[1], self.flip(held[1], 1)]

    def gather_whole(self, group, weights):
        whole = {
            name: lax.all_gather(weights[name], AXES, axis=0, tiled=True)
            for name in dict(sum(GATHERS[group], []))
        }
        pieces = []
        for half, items in enumerate(GATHERS[group]):
            blocks = [
                whole[name][:, j * PACK : (j + 1) * PACK].reshape(BLOCKS, -1, PACK)
                for name, j in items
            ]
            pieces += list(self.by_slot(jnp.concatenate(blocks, axis=1), half))
        return pieces

    def by_slot(self, blocks, half):
        shape = blocks.shape[1:]
        order = ((3, 2, 1, 0), (3, 1, 2, 0))[half]
        return blocks.reshape(4, 2, 2, 2, *shape).transpose(*order, 4, 5).reshape(2, 16, *shape)

    def by_owner(self, slots, half):
        shape = slots.shape[1:]
        order = ((3, 2, 1, 0), (3, 1, 2, 0))[half]
        return slots.reshape(2, 2, 2, 4, *shape).transpose(*order, 4, 5).reshape(BLOCKS, *shape)

    def add(self, a, b):
        return (a.astype(F32) + b.astype(F32)).astype(BF)

    def fold(self, slots, mask):
        middle = slots.shape[0] // 2
        return self.add(slots[:middle], self.flip(slots[middle:], mask))

    def cores(self, kept, given):
        return self.add(kept, self.flip(given, 1))

    def first(self, group, kept, given):
        held = self.cores(kept, given)
        low = height(SUMS[group][0])
        return [held[:, :low], held[:, low:]]

    def straight(self, held, stage):
        return self.fold(held, (2, 4)[stage])

    def flips(self, values, mask):
        flat = self.flip(jnp.concatenate([v.reshape(-1, PACK) for v in values], axis=0), mask)
        result, at = [], 0
        for v in values:
            count = v.size // PACK
            result.append(flat[at : at + count].reshape(v.shape))
            at += count
        return result

    def next_two(self, late, early):
        a, b = (v.shape[0] // 2 for v in late)
        c, d = (v.shape[0] // 2 for v in early)
        got_y = self.flips([late[0][a:], early[1][d:]], 4)
        got_x = self.flips([late[1][b:], early[0][c:]], 2)
        late = [self.add(late[0][:a], got_y[0]), self.add(late[1][:b], got_x[0])]
        early = [self.add(early[0][:c], got_x[1]), self.add(early[1][:d], got_y[1])]
        return late, early

    def next_and_plane(self, late, held):
        a, b = (v.shape[0] // 2 for v in late)
        got_y = self.flips([late[0][a:], held[4:8]], 4)
        got_x = self.flips([late[1][b:], held[8:12]], 2)
        total = held[:4].astype(F32) + got_y[1].astype(F32) + got_x[1].astype(F32)
        total = total + self.flip(held[12:], 6).astype(F32)
        late = [self.add(late[0][:a], got_y[0]), self.add(late[1][:b], got_x[0])]
        return late, total.astype(BF)

    def next(self, held, stage):
        masks = ((2, 4), (4, 2))[stage]
        return [self.fold(h, m) for h, m in zip(held, masks)]

    def finish(self, held):
        held = jnp.concatenate(held, axis=1)
        total = held[0].astype(F32)
        for k in range(1, 4):
            total = total + self.flip(held[k], k << 3).astype(F32)
        return total

    def rows_of(self, items, total):
        parts, at = {}, 0
        for name, j in items:
            b = ROWS[name] * BLOCKS // self.count
            parts.setdefault(name, []).append(total[at : at + b])
            at += b
        return {name: jnp.concatenate(p, axis=1) for name, p in parts.items()}

    def scatter_whole(self, group, parts):
        slots = jnp.concatenate(parts)
        sent, at = [], 0
        for half, items in enumerate(SUMS[group]):
            for name, _ in items:
                blocks = self.by_owner(slots[:, at : at + ROWS[name]], half if group in SPLIT else 0)
                sent.append(blocks.reshape(self.count, -1, PACK))
                at += ROWS[name]
        sent = jnp.concatenate(sent, axis=1)
        return lax.psum_scatter(sent, AXES, scatter_dimension=0, tiled=False).astype(F32)


class Layout:
    def __init__(self, n_seq, n_dp):
        self.n_seq, self.n_dp = n_seq, n_dp
        self.where = {}
        for g in range(n_dp):
            for s in range(n_seq):
                self.where[g, s] = self.place(g, s)
        self.block = np.zeros(n_seq * n_dp, np.int32)
        for (g, s), device in self.where.items():
            self.block[device] = s

    def place(self, g, s):
        if (self.n_seq, self.n_dp) == (4, 8):
            y, x, c = g >> 2, g >> 1 & 1, g & 1
            return (2 * c + y) * 8 + (s & 1) * 4 + x * 2 + (s >> 1)
        return s * self.n_dp + g

    def pairs(self, source, target):
        return [
            (source(g, s), target(g, s))
            for g in range(self.n_dp)
            for s in range(self.n_seq)
            if target(g, s) is not None and source(g, s) is not None
        ]

    def at(self, g, s):
        return self.where.get((g, s))

    def home(self, g, s):
        return s * self.n_dp + g

    def bring(self, value):
        return lax.ppermute(value, AXES, self.pairs(self.home, self.at))

    def bring_to(self, value, step):
        return lax.ppermute(
            value, AXES, self.pairs(self.home, lambda g, s: self.at(g, s + step))
        )

    def send_home(self, value):
        return lax.ppermute(value, AXES, self.pairs(self.at, self.home))

    def to_neighbour(self, value, step):
        return lax.ppermute(value, AXES, self.pairs(self.at, lambda g, s: self.at(g, s + step)))

    def swap(self, values):
        return [values[0]] + [
            lax.ppermute(values[k], AXES, self.pairs(self.at, lambda g, s: self.at(g, s ^ k)))
            for k in range(1, self.n_seq)
        ]


NAMES = ("ln1", "ln2", "ln3", "ln4", "ln5", "glu", "wide", "narrow", "depth", "point", "qkv", "attn", "up", "down")
SMALL = ("ln1", "ln2", "ln3", "ln4", "ln5", "depth")


def sync(*values):
    return lax.optimization_barrier(values)


def small_block(arrays, blocks):
    flat = jnp.concatenate([a.reshape(blocks, -1) for a in arrays], axis=1)
    flat = jnp.pad(flat, ((0, 0), (0, 16 * PACK - flat.shape[1])))
    return flat.reshape(blocks * 16, PACK)


def on_device(tokens, cotangent, first_length, *weights):
    n = lax.axis_size("seq")
    n_dp = lax.axis_size("dp")
    share = n * LANES // D
    layout = Layout(n, n_dp)
    links = Links(n, n_dp)
    direct = links.direct
    rows = tokens.shape[1]
    group = n * rows
    here = lax.axis_index("seq") * n_dp + lax.axis_index("dp")
    me = here if direct else jnp.zeros_like(here)
    s = jnp.asarray(layout.block)[here]
    mine = dict(zip(NAMES, weights))
    if direct:
        mine["small"] = small_block([mine[k] for k in SMALL], 1)
    else:
        small = [lax.all_gather(mine[k], AXES, axis=0, tiled=True) for k in SMALL]
        mine["small"] = small_block(small, BLOCKS).reshape(links.count, -1, PACK)[here]

    tokens = tokens[0]
    digits = jnp.where(
        lax.broadcasted_iota(jnp.int32, (RIM, D), 1) < LANES,
        first_length[0] // LANES,
        first_length[0] % LANES,
    )
    sent = jnp.concatenate([tokens, digits.astype(BF)], axis=0)
    if direct:
        blocks = pack({k: mine[k] for k in mine if k not in SMALL})
        sent, blocks = sync(sent, blocks)
        held1 = links.near(blocks[0])
    x = layout.bring(sent)
    if direct:
        held1 = links.spread(links.part(0, *sync(held1)), 0)
    low = layout.bring_to(tokens[-RIM:], 1)
    high = layout.bring_to(tokens[:RIM], -1)
    if direct:
        held1, x, low, high, blocks = sync(held1, x, low, high, blocks)
        held1 = links.spread(held1, 1)
        held2 = links.near(blocks[1])
    digits = x[rows, 0 : 2 * LANES : LANES].astype(F32).astype(jnp.int32)
    first = digits[0] * LANES + digits[1]
    scal = jnp.stack([s.astype(jnp.int32), first, me.astype(jnp.int32)])
    x_ext = jnp.concatenate([low, x[:rows], high], axis=0)
    if direct:
        held1, held2, scal, x_ext = sync(held1, held2, scal, x_ext)
        pieces1 = links.across(held1)
        held2 = links.spread(links.part(1, held2), 0)
        pieces1, held2 = sync(pieces1, held2)
        held2 = links.spread(held2, 1)
    else:
        pieces1, pieces2, pieces3 = (links.gather_whole(k, mine) for k in range(3))
    h1, y2, joined, *rest = front1(scal, x_ext, pieces1)
    (glu, wide, narrow), (g1, g2, g3, g4, g5, taps) = rest[:3], rest[3:]
    if direct:
        y2, held2, blocks = sync(y2, held2, blocks)
        pieces2 = links.across(held2)
        held3 = links.near(blocks[2])
    left, right, mid = front2(scal, y2, g3, wide, narrow, group)
    if direct:
        mid, pieces2, held3 = sync(mid, pieces2, held3)
        held3 = links.spread(links.part(2, held3), 0)
    spread, h2, y4, *rest = front3(scal, mid, taps, h1, g4, pieces2, n, share)
    qkv, (qkv_w, point) = rest[:n], rest[n:]
    if direct:
        qkv, held3 = sync(qkv, held3)
    qkv = layout.swap(qkv)
    qkv, cot = sync(qkv, cotangent[0])
    cot = layout.bring(cot)
    if direct:
        held3, qkv = sync(held3, qkv)
        held3 = links.spread(held3, 1)
    *att, lse = attend(scal, qkv, n, share)
    if direct:
        att, held3, cot = sync(att, held3, cot)
        pieces3 = links.across(held3)
    else:
        att, cot = sync(att, cot)
    arrived = layout.swap(att)
    mixed, dh3, *rest = middle(scal, h2, arrived, cot, g5, pieces3, n, share)
    datt, (att_all, y5, inner, du, ln5) = rest[:n], rest[n:]
    datt, du = sync(datt, du)
    datt = layout.swap(datt)
    sum0 = weigh0(scal, att_all, y5, inner, du, cot, dh3)
    datt, sum0 = sync(datt, sum0)
    if direct:
        sum0 = links.cores(*sum0)
    dqkv = attend_back(scal, qkv, att, datt, lse, n, share)
    dqkv, sum0 = sync(dqkv, sum0)
    dqkv = layout.swap(dqkv)
    if direct:
        sum0 = links.straight(sum0, 0)
        dqkv, sum0 = sync(dqkv, sum0)
        sum0 = links.straight(sum0, 1)
    dh2, db, dqkv, ln4 = back3(scal, dqkv, dh3, h2, g4, qkv_w, n, share)
    db, dqkv = sync(db, dqkv)
    low = layout.to_neighbour(db[-RIM:], 1)
    high = layout.to_neighbour(db[:RIM], -1)
    sum1 = weigh1(scal, y4, dqkv, spread, db)
    low, high, sum1, sum0, mixed = sync(low, high, sum1, sum0, mixed)
    if direct:
        total0 = links.finish([sum0])
        sum1 = links.first(1, *sum1)
    mixed = layout.send_home(mixed)
    dl, st, gdepth, ln3 = back2(scal, low, db, high, taps, mid, left, right, g3, point, group)
    if direct:
        dl, st, total0, sum1, mixed = sync(dl, st, total0, sum1, mixed)
        sum1 = links.next(sum1, 0)
    sum2 = weigh2(scal, dl, st, y2)
    if direct:
        (dl, sum2) = sync(dl, sum2)
        sum2 = links.first(2, *sum2)
    half = rows // 2
    fixed = (scal, dl, st, dh2, h1, joined, x_ext, g1, g2, glu, wide, narrow)
    dx_a, y1_a, dj_a, ln1_a, ln2_a = back1(*fixed, 0, half)
    if direct:
        dx_a, dl, sum1, sum2 = sync(dx_a, dl, sum1, sum2)
        sum1, sum2 = links.next_two(sum1, sum2)
        fixed = (scal, dl, *fixed[2:])
    dx_a = layout.send_home(dx_a)
    dx_b, y1_b, dj_b, ln1_b, ln2_b = back1(*fixed, half, rows - half)
    if direct:
        dx_b, dj_b = sync(dx_b, dj_b)
    dx_b = layout.send_home(dx_b)
    gains = (ln3, ln4, ln5)
    sum3 = weigh3(scal, (y1_a, y1_b), (dj_a, dj_b), (ln1_a, ln1_b), (ln2_a, ln2_b), gains, gdepth)
    if direct:
        sum3, sum2, sum1, dx_a = sync(sum3, sum2, sum1, dx_a)
        sum3 = links.cores(*sum3)
    if direct:
        sum3, sum2 = sync(sum3, sum2)
        sum2, sum3 = links.next_and_plane(sum2, sum3)
        *held, dx_b = sync(*sum2, sum3, dx_b)
        sums = (total0, links.finish([*sum1, *held]))
        tables = (sum(SUMS[0], []), sum([*SUMS[1], *SUMS[2], *SUMS[3]], []))
    else:
        sums = [links.scatter_whole(k, v) for k, v in enumerate((sum0, sum1, sum2, sum3))]
        tables = [sum(items, []) for items in SUMS]
    dx = jnp.concatenate([dx_a, dx_b], axis=0)
    out = {}
    for items, total in zip(tables, sums):
        out.update(links.rows_of(items, total))
    flat = out.pop("small")
    if not direct:
        flat = lax.all_gather(flat, AXES, axis=0, tiled=True)
    flat = flat.reshape(-1, 16 * PACK)
    sizes = [width for _, width in GAINS] + [TAP_RUN]
    at = 0
    for name, size in zip(SMALL, sizes):
        part = flat[:, at : at + size].reshape(-1)
        at += size
        if not direct:
            own = mine[name].shape[0]
            part = lax.dynamic_slice(part, (here * own,), (own,))
        out[name] = part
    return (mixed[None], dx.astype(F32)[None], *(out[name] for name in NAMES))


def solution(mesh):
    token, owner, rows = P("dp", "seq", None), P(AXES), P(AXES, None)
    params = (owner,) * 5 + (rows,) * 3 + (owner,) + (rows,) * 5
    return jax.shard_map(
        on_device,
        mesh=mesh,
        in_specs=(token, token, P("dp")) + params,
        out_specs=(token, token) + params,
        check_vma=False,
    )
```

```python
import functools
import math

import jax
import jax.numpy as jnp
import numpy as np
from jax import lax
from jax.experimental import pallas as pl
from jax.experimental.pallas import tpu as pltpu
from jax.sharding import PartitionSpec as P

D = 512
HEADS = 8
FF = 2048
KERNEL = 9
HEAD = 64
NARROW = 256
HALF = KERNEL // 2
LANES = 128
PACK = 256
RIM = 16
BLOCKS = 32
F32 = jnp.float32
BF = jnp.bfloat16
LOG2E = math.log2(math.e)
BIG = -1e30
AXES = ("seq", "dp")
VMEM = 58 << 20


def nt(a, b):
    return lax.dot_general(a, b, (((1,), (1,)), ((), ())), preferred_element_type=F32)


def nn(a, b):
    return lax.dot_general(a, b, (((1,), (0,)), ((), ())), preferred_element_type=F32)


def tn(a, b):
    return lax.dot_general(a, b, (((0,), (0,)), ((), ())), preferred_element_type=F32)


def call(kernel, ins, outs, scratch=(), micros=0, ties=(), steps=None):
    if ties:
        inner, fixed, count = kernel, len(ins), len(ties)

        def kernel(*refs):
            inner(*refs[:fixed], *refs[fixed + count :])

    def spec(shape, how, once):
        if how == "s":
            return pl.BlockSpec(memory_space=pltpu.SMEM)
        if steps is None:
            return pl.BlockSpec(memory_space=pltpu.VMEM)
        if isinstance(how, tuple):
            tile, start = how
            block = tuple(pl.Element(b) for b in (tile, *shape[1:]))
            rest = (0,) * (len(shape) - 1)
            return pl.BlockSpec(block, lambda i: (pl.multiple_of(start + i * tile, 16), *rest))
        if how is None:
            zeros = (0,) * len(shape)
            mode = pl.Buffered(1) if once else None
            return pl.BlockSpec(shape, lambda i: zeros, pipeline_mode=mode)
        return pl.BlockSpec((how, *shape[1:]), lambda i: (i, *(0,) * (len(shape) - 1)))

    args = [a for a, _ in ins]
    shapes = [jax.ShapeDtypeStruct(shape, dtype) for shape, dtype, _ in outs]
    moved = sum(math.prod(a.shape) * a.dtype.itemsize for a in args + shapes) if micros else 0
    return pl.pallas_call(
        kernel,
        out_shape=shapes,
        grid=() if steps is None else (steps,),
        in_specs=[spec(a.shape, how, True) for a, how in ins]
        + [pl.BlockSpec(memory_space=pl.ANY)] * len(ties),
        out_specs=[spec(shape, how, False) for shape, _, how in outs],
        scratch_shapes=[pltpu.VMEM(shape, dtype) for shape, dtype in scratch],
        compiler_params=pltpu.CompilerParams(vmem_limit_bytes=VMEM),
        cost_estimate=pl.CostEstimate(
            flops=int(micros * 1.15e9), bytes_accessed=moved, transcendentals=0
        ),
    )(*args, *ties)


def whole_call(kernel, outs, args, scratch=(), micros=0, ties=()):
    ins = [(a, "s" if i == 0 else None) for i, a in enumerate(args)]
    outs = [(shape, dtype, None) for shape, dtype in outs]
    return call(kernel, ins, outs, scratch, micros, ties)


def normalise(v):
    mean = jnp.mean(v, axis=1, keepdims=True)
    c = v - mean
    r = lax.rsqrt(jnp.mean(c * c, axis=1, keepdims=True) + 1e-05)
    return c * r, r


def norm_back(grad, hat, r, gain):
    g = grad * gain
    a = jnp.mean(g, axis=1, keepdims=True)
    b = jnp.mean(g * hat, axis=1, keepdims=True)
    return r * (g - a - hat * b)


C0 = math.sqrt(2.0 / math.pi)
C1 = 0.044715


def gelu(x):
    return 0.5 * x * (1.0 + jnp.tanh(x * (C0 + C0 * C1 * (x * x))))


def gelu_and_slope(x):
    xx = x * x
    t = jnp.tanh(x * (C0 + C0 * C1 * xx))
    half = 0.5 * (1.0 + t)
    return x * half, half + (0.5 * x) * (1.0 - t * t) * (C0 + 3.0 * C0 * C1 * xx)


def sigmoid(x):
    return 0.5 * jnp.tanh(0.5 * x) + 0.5


def fold8(v):
    return jnp.sum(v.reshape(v.shape[0] // 8, 8, v.shape[1]), axis=0)


def rows_at(i, tile, start=0, count=None):
    return pl.ds(pl.multiple_of(start + i * tile, 16), count or tile)


def places(base, rows, lanes=LANES):
    return base + lax.broadcasted_iota(jnp.int32, (rows, lanes), 0)


ROWS = {"glu": 16, "wide": 16, "narrow": 48, "point": 64, "qkv": 16, "attn": 16, "up": 16, "down": 64, "small": 16}


def columns_of(name, *chunks):
    return [(name, j) for j in chunks]


WIDE, GLU, QKV, UP = (columns_of(n, *range(k)) for n, k in (("wide", 8), ("glu", 4), ("qkv", 6), ("up", 8)))
NARROW_0, POINT_0, SMALL_0 = (columns_of(n, 0) for n in ("narrow", "point", "small"))
ATTN, DOWN = columns_of("attn", 0, 1), columns_of("down", 0, 1)
LAST = (UP + ATTN[:1], ATTN[1:] + DOWN)
GATHERS = ((WIDE, GLU + NARROW_0 + SMALL_0), (QKV[:5], QKV[5:] + POINT_0), LAST)
SUMS = (
    LAST,
    (QKV[:5], QKV[5:] + POINT_0),
    (WIDE[:6], WIDE[6:] + NARROW_0),
    (GLU[:2], GLU[2:] + SMALL_0),
)

SPLIT = (1, 2)


def height(items):
    return sum(ROWS[name] for name, _ in items)


def row_of(items, item):
    return height(items[: items.index(item)])


def slot_bits(half, r):
    high, low, z = r >> 3, r >> 2 & 1, r & 3
    x, y = (high, low) if half == 0 else (low, high)
    return z * 8 + y * 4 + x * 2


def slot_of(half, rel):
    z, y, x, c = rel >> 3, rel >> 2 & 1, rel >> 1 & 1, rel & 1
    high, low = (x, y) if half == 0 else (y, x)
    return c * 16 + high * 8 + low * 4 + z


def unpack(me, group, pieces, wanted):
    for half, items in enumerate(GATHERS[group]):
        for core in range(2):
            piece = pieces[half * 2 + core]
            for r in range(BLOCKS // 2):
                owner = (slot_bits(half, r) + core) ^ me
                for name, j in items:
                    if name in wanted:
                        b, off = ROWS[name], row_of(items, (name, j))
                        wanted[name][
                            pl.ds(pl.multiple_of(owner * b, 16), b), j * PACK : (j + 1) * PACK
                        ] = piece[r, off : off + b, :]


def put(me, group, ref, item, value, start=0):
    half = int(item in SUMS[group][1])
    off = row_of(SUMS[group][half], item) + half * height(SUMS[group][0])
    b = ROWS[item[0]]
    for k in range(value.shape[0] // b):
        slot = slot_of(half if group in SPLIT else 0, (start + k) ^ me)
        ref[slot, off : off + b, :] = value[k * b : (k + 1) * b]


def group_grads(group):
    rows = height(sum(SUMS[group], []))
    return [((BLOCKS // 2, rows, PACK), BF)] * 2


def group_slots(group):
    return ((BLOCKS, height(sum(SUMS[group], [])), PACK), BF)


def part_slots(slots, kept, given):
    kept[...] = slots[: BLOCKS // 2]
    given[...] = slots[BLOCKS // 2 :]


SHAPES = ({"glu": (D, 2 * D), "wide": (D, FF), "narrow": (3 * D, NARROW)}, {"qkv": (D, 3 * D), "point": (FF, NARROW)})

GAINS = ((0, 16), (16, 16), (32, 64), (96, 16), (112, 16))
TAPS = 128
TAP_RUN = KERNEL * FF // BLOCKS
SMALL_ROWS = 3


def iota(shape, dim):
    return lax.broadcasted_iota(jnp.int32, shape, dim)


def owner_slots(me, half):
    shape = (BLOCKS, BLOCKS)
    return (slot_of(half, iota(shape, 0) ^ me) == iota(shape, 1)).astype(F32).astype(BF)


def gain_maps(offset, width):
    total = BLOCKS * width
    owner = iota((BLOCKS, total), 1) // width == iota((BLOCKS, total), 0)
    value = iota((LANES, total), 0) == offset + iota((LANES, total), 1) % width
    return owner, value.astype(F32).astype(BF)


def tap_runs():
    for b in range(KERNEL * FF // 64):
        f = b * 64
        yield f // FF, f % FF, f // TAP_RUN, TAPS + f % TAP_RUN


def read_small(me, pieces, gains, taps, table):
    off = row_of(GATHERS[0][1], SMALL_0[0])
    for core in range(2):
        for r in range(BLOCKS // 2):
            rows = pieces[2 + core][r, off : off + 16, :].astype(F32)
            slot = core * 16 + r
            for q in range(SMALL_ROWS):
                table[slot : slot + 1, q * PACK : (q + 1) * PACK] = rows[q : q + 1, :]
    table[...] = nn(owner_slots(me, 1), table[...].astype(BF))
    for ref, (offset, width) in zip(gains, GAINS):
        owner, value = gain_maps(offset, width)
        spread = nn(table[:, :LANES].astype(BF), value)
        ref[...] = jnp.sum(jnp.where(owner, spread, 0.0), axis=0, keepdims=True)
    for tap, channel, who, place in tap_runs():
        taps[tap : tap + 1, channel : channel + 64] = table[who : who + 1, place : place + 64]


def write_small(me, gains, taps, table, block, grads):
    table[...] = jnp.zeros_like(table)
    total = jnp.zeros((BLOCKS, LANES), F32)
    for gain, (offset, width) in zip(gains, GAINS):
        owner, value = gain_maps(offset, width)
        total = total + nt(jnp.where(owner, gain[...], 0.0).astype(BF), value)
    table[:, :LANES] = total
    for tap, channel, who, place in tap_runs():
        table[who : who + 1, place : place + 64] = taps[tap : tap + 1, channel : channel + 64]
    table[...] = tn(owner_slots(me, 0), table[...].astype(BF))
    block[...] = jnp.zeros_like(block)
    for slot in range(BLOCKS):
        for q in range(SMALL_ROWS):
            block[slot, q : q + 1, :] = table[slot : slot + 1, q * PACK : (q + 1) * PACK]
    at = height(sum(SUMS[3], [])) - 16
    grads[:, at : at + 16, :] = block[...].astype(BF)


def pack_kernel(names, *refs):
    shards = dict(zip(names, refs))
    for ref, halves in zip(refs[len(names) :], GATHERS):
        at = 0
        for name, j in sum(halves, []):
            b = ROWS[name]
            if name == "small":
                ref[at : at + b, :] = shards[name][...]
            else:
                ref[at : at + b, :] = shards[name][:, j * PACK : (j + 1) * PACK]
            at += b


def pack(shards):
    names = tuple(shards)
    return call(
        functools.partial(pack_kernel, names),
        [(shards[k], None) for k in names],
        [((height(sum(halves, [])), PACK), BF, None) for halves in GATHERS],
        micros=2,
    )


def front1_kernel(scal, x_ref, p0, p1, p2, p3, h1_ref, y2_ref, joined_ref, *refs):
    weights, gains, taps, table = refs[:3], refs[3:8], refs[8], refs[9]
    g1, g2 = gains[:2]

    @pl.when(pl.program_id(0) == 0)
    def _():
        read_small(scal[2], (p0, p1, p2, p3), gains, taps, table)
        unpack(scal[2], 0, (p0, p1, p2, p3), dict(zip(SHAPES[0], weights)))

    x = x_ref[...].astype(F32)
    hat, _ = normalise(x)
    joined = nn((hat * g1[...]).astype(BF), weights[0][...])
    joined_ref[...] = joined
    h1 = x + joined[:, :D] * sigmoid(joined[:, D:])
    h1_ref[...] = h1
    hat2, _ = normalise(h1)
    y2_ref[...] = (hat2 * g2[...]).astype(BF)


def front1(scal, x, pieces, ties=()):
    rows = x.shape[0]
    tile = 400
    return call(
        front1_kernel,
        [(scal, "s"), (x, tile)] + [(p, None) for p in pieces],
        [((rows, D), F32, tile), ((rows, D), BF, tile), ((rows, 2 * D), F32, tile)]
        + [(shape, BF, None) for shape in SHAPES[0].values()]
        + [((1, BLOCKS * width), F32, None) for _, width in GAINS]
        + [((KERNEL, FF), F32, None)],
        scratch=[((BLOCKS, SMALL_ROWS * PACK), F32)],
        micros=12,
        ties=ties,
        steps=rows // tile,
    )


def front2_kernel(tile, group, scal, y2_ref, g3, wide, narrow, left_ref, right_ref, mid_ref, u_ref):
    rows = y2_ref.shape[0]
    base = scal[0] * (rows - 2 * RIM) - RIM
    first = scal[1]
    i = pl.program_id(0)

    @pl.when(i == 0)
    def _():
        u_ref[0:RIM, :] = jnp.zeros((RIM, 3 * NARROW), F32)
        u_ref[RIM + rows : 2 * RIM + rows, :] = jnp.zeros((RIM, 3 * NARROW), F32)

        def narrow_step(j, carry):
            y = y2_ref[rows_at(j, tile), :]
            for k in range(3):
                u_ref[rows_at(j, tile, RIM), k * NARROW : (k + 1) * NARROW] = nn(
                    y, narrow[k * D : (k + 1) * D, :]
                )
            return carry

        lax.fori_loop(0, rows // tile, narrow_step, 0)

    around = pl.ds(pl.multiple_of(i * tile, 16), tile + 2 * RIM)
    left = nn(y2_ref[rows_at(i, tile), :], wide[...])
    left_ref[...] = left
    pos = places(base + i * tile, tile, NARROW)
    before = pltpu.roll(u_ref[around, 0:NARROW], 1, 0)[RIM : RIM + tile]
    after = pltpu.roll(u_ref[around, 2 * NARROW :], tile + 2 * RIM - 1, 0)[RIM : RIM + tile]
    right = u_ref[rows_at(i, tile, RIM), NARROW : 2 * NARROW]
    right = right + jnp.where((pos == first) | (pos == 0), 0.0, before)
    right = right + jnp.where((pos + 1 == first) | (pos + 1 == group), 0.0, after)
    right_ref[...] = right
    for q in range(0, tile, STEP):
        at = slice(q, q + STEP)
        left = gelu(left_ref[at, :])
        joined = jnp.concatenate([left[:, :NARROW] + gelu(right_ref[at, :]), left[:, NARROW:]], axis=1)
        hat, _ = normalise(joined)
        row = base + i * tile + q + iota((STEP, 1), 0)
        inside = ((row >= 0) & (row < group)).astype(F32)
        mid_ref[at, :] = (hat * inside * g3[...]).astype(BF)


def front2(scal, y2, g3, wide, narrow, group, ties=()):
    rows = y2.shape[0]
    tile = 400
    return call(
        functools.partial(front2_kernel, tile, group),
        [(scal, "s"), (y2, None), (g3, None), (wide, None), (narrow, None)],
        [((rows, FF), F32, tile), ((rows, NARROW), F32, tile), ((rows, FF), BF, tile)],
        scratch=[((rows + 2 * RIM, 3 * NARROW), F32)],
        micros=12,
        ties=ties,
        steps=rows // tile,
    )


def crosses(pos, offset, first):
    if offset > 0:
        return (pos < first) & (pos + offset >= first)
    return (pos >= first) & (pos + offset < first)


WIDTH = 4
STEP = 16


def front3_kernel(tile, n, share, scal, mid_ref, taps, h1_ref, g4, p0, p1, p2, p3, *refs):
    spread_ref, h2_ref, y4_ref = refs[:3]
    outs = refs[3 : 3 + n]
    qkv_w, point, win, qkv_s = refs[3 + n :]
    i = pl.program_id(0)

    @pl.when(i == 0)
    def _():
        unpack(scal[2], 1, (p0, p1, p2, p3), {"qkv": qkv_w, "point": point})

    s, first = scal[0], scal[1]
    begin = s * (mid_ref.shape[0] - 2 * RIM) + i * tile
    near = (first > begin - HALF) & (first < begin + tile + HALF)

    def chunk(c, carry):
        around = pl.ds(pl.multiple_of(i * tile, 16), tile + 2 * RIM)
        lanes = [pl.ds(pl.multiple_of((c * WIDTH + w) * LANES, LANES), LANES) for w in range(WIDTH)]
        for w in range(WIDTH):
            win[w] = mid_ref[around, lanes[w]].astype(F32)
        for masked in (False, True):

            @pl.when(near if masked else jnp.logical_not(near))
            def _():
                for w in range(WIDTH):
                    tap = [taps[k : k + 1, lanes[w]] for k in range(KERNEL)]
                    for r in range(0, tile, STEP):
                        pos = places(begin + r, STEP)
                        total = None
                        for k in range(KERNEL):
                            o = k - HALF
                            v = win[w, RIM + o + r : RIM + o + r + STEP, :]
                            if masked and o != 0:
                                v = jnp.where(crosses(pos, o, first), 0.0, v)
                            total = v * tap[k] if total is None else total + v * tap[k]
                        spread_ref[r : r + STEP, lanes[w]] = total.astype(BF)

        return carry

    lax.fori_loop(0, FF // (WIDTH * LANES), chunk, 0)
    h1 = h1_ref[rows_at(i, tile, RIM), :]
    branch = nn(spread_ref[...], point[...])
    h2 = jnp.concatenate([h1[:, :NARROW] + branch, h1[:, NARROW:]], axis=1)
    h2_ref[...] = h2
    hat, _ = normalise(h2)
    y4 = (hat * g4[...]).astype(BF)
    y4_ref[...] = y4
    qkv_s[...] = nn(y4, qkv_w[...]).astype(BF)
    for k in range(n):
        block = (s ^ k) // share
        for part in range(3):
            outs[k][:, part * LANES : (part + 1) * LANES] = qkv_s[
                :, pl.ds(pl.multiple_of(part * D + block * LANES, LANES), LANES)
            ]


def front3(scal, mid, taps, h1, g4, pieces, n, share, ties=()):
    rows = mid.shape[0] - 2 * RIM
    tile = 256
    return call(
        functools.partial(front3_kernel, tile, n, share),
        [(scal, "s")] + [(a, None) for a in (mid, taps, h1, g4, *pieces)],
        [((rows, FF), BF, tile), ((rows, D), F32, tile), ((rows, D), BF, tile)]
        + [((rows, 3 * LANES), BF, tile)] * n
        + [(shape, BF, None) for shape in SHAPES[1].values()],
        scratch=[((WIDTH, tile + 2 * RIM, LANES), F32), ((tile, 3 * D), BF)],
        micros=20,
        ties=ties,
        steps=rows // tile,
    )


def gather_lanes(wide_ref, n, share, s, blocks, parts):
    rows = wide_ref.shape[0]
    for k in range(n):
        block = (s ^ k) // share
        for part in range(parts):
            lanes = pl.ds(pl.multiple_of(part * D + block * LANES, LANES), LANES)
            new = blocks[k][:, part * LANES : (part + 1) * LANES]
            if share > 1:
                lane = lax.broadcasted_iota(jnp.int32, (rows, LANES), 1)
                mine = lane // (LANES // share) == (s ^ k) % share
                new = jnp.where(mine, new.astype(F32), wide_ref[:, lanes].astype(F32)).astype(BF)
            wide_ref[:, lanes] = new


def middle_kernel(n, share, scal, h2_ref, *refs):
    att = refs[:n]
    cot_ref, g5, p0, p1, p2, p3, mixed_ref, dh3_ref = refs[n : n + 8]
    datt = refs[n + 8 : 2 * n + 8]
    att_s, y5_s, inner_s, du_s, ln_out = refs[2 * n + 8 : 2 * n + 13]
    wa, wup, wdown, ln_ref = refs[2 * n + 13 :]
    s = scal[0]
    i = pl.program_id(0)

    @pl.when(i == 0)
    def _():
        unpack(scal[2], 2, (p0, p1, p2, p3), {"attn": wa, "up": wup, "down": wdown})
        ln_ref[...] = jnp.zeros_like(ln_ref)

    gather_lanes(att_s, n, share, s, att, 1)
    h3 = h2_ref[...] + nn(att_s[...], wa[...])
    hat, r = normalise(h3)
    y5 = (hat * g5[...]).astype(BF)
    y5_s[...] = y5
    value, slope = gelu_and_slope(nn(y5, wup[...]))
    inner = value.astype(BF)
    inner_s[...] = inner
    mixed_ref[...] = (h3 + nn(inner, wdown[...])).astype(BF)
    cot = cot_ref[...]
    du = (nt(cot, wdown[...]) * slope).astype(BF)
    du_s[...] = du
    dy5 = nt(du, wup[...])
    ln_ref[...] += fold8(dy5 * hat)
    dh3 = cot.astype(F32) + norm_back(dy5, hat, r, g5[...])
    dh3_ref[...] = dh3
    da = nt(dh3.astype(BF), wa[...]).astype(BF)
    for j in range(D // LANES):
        for k in range(n):

            @pl.when((s ^ k) // share == j)
            def _():
                datt[k][...] = da[:, j * LANES : (j + 1) * LANES]

    ln_out[...] = jnp.sum(ln_ref[...], axis=0, keepdims=True)


def middle(scal, h2, att, cot, g5, pieces, n, share, ties=()):
    rows = h2.shape[0]
    tile = 384
    return call(
        functools.partial(middle_kernel, n, share),
        [(scal, "s"), (h2, tile)]
        + [(a, tile) for a in (*att, cot)]
        + [(a, None) for a in (g5, *pieces)],
        [((rows, D), BF, tile), ((rows, D), F32, tile)]
        + [((rows, LANES), BF, tile)] * n
        + [((rows, c), BF, tile) for c in (D, D, FF, FF)]
        + [((1, D), F32, None)],
        scratch=[((D, D), BF), ((D, FF), BF), ((FF, D), BF), ((8, D), F32)],
        micros=20,
        ties=ties,
        steps=rows // tile,
    )


def weigh0_kernel(scal, att_s, y5_s, inner_s, du_s, cot_ref, dh3_ref, kept, given, grads):
    me = scal[2]
    att_t = att_s[...].T
    for j in range(D // PACK):
        part = nn(att_t, dh3_ref[:, j * PACK : (j + 1) * PACK].astype(BF))
        put(me, 0, grads, ("attn", j), part.astype(BF))
    y5_t = y5_s[...].T
    for j in range(FF // PACK):
        cols = slice(j * PACK, (j + 1) * PACK)
        put(me, 0, grads, ("up", j), nn(y5_t, du_s[:, cols]).astype(BF))
        down = tn(inner_s[:, cols], cot_ref[...]).astype(BF)
        for m in range(D // PACK):
            put(me, 0, grads, ("down", m), down[:, m * PACK : (m + 1) * PACK], j * PACK // 64)
    part_slots(grads, kept, given)


def weigh0(scal, att, y5, inner, du, cot, dh3, ties=()):
    return whole_call(
        weigh0_kernel,
        group_grads(0),
        [scal, att, y5, inner, du, cot, dh3],
        scratch=[group_slots(0)],
        micros=10,
        ties=ties,
    )


def back3_kernel(n, share, scal, *refs):
    blocks = refs[:n]
    dh3_ref, h2_ref, g4, qkv_w = refs[n : n + 4]
    dh2_ref, db_ref, dqkv_s, ln_out, ln_ref = refs[n + 4 :]

    @pl.when(pl.program_id(0) == 0)
    def _():
        ln_ref[...] = jnp.zeros_like(ln_ref)

    gather_lanes(dqkv_s, n, share, scal[0], blocks, 3)
    dy4 = nt(dqkv_s[...], qkv_w[...])
    hat, r = normalise(h2_ref[...])
    ln_ref[...] += fold8(dy4 * hat)
    dh2 = dh3_ref[...] + norm_back(dy4, hat, r, g4[...])
    dh2_ref[...] = dh2
    db_ref[...] = dh2[:, :NARROW].astype(BF)
    ln_out[...] = jnp.sum(ln_ref[...], axis=0, keepdims=True)


def back3(scal, blocks, dh3, h2, g4, qkv_w, n, share, ties=()):
    rows = h2.shape[0]
    tile = 384
    return call(
        functools.partial(back3_kernel, n, share),
        [(scal, "s")] + [(a, tile) for a in (*blocks, dh3, h2)] + [(g4, None), (qkv_w, None)],
        [((rows, D), F32, tile), ((rows, NARROW), BF, tile), ((rows, 3 * D), BF, tile)]
        + [((1, D), F32, None)],
        scratch=[((8, D), F32)],
        micros=6,
        ties=ties,
        steps=rows // tile,
    )


def weigh1_kernel(scal, y4_ref, dqkv_s, spread_ref, db_ref, kept, given, grads):
    me = scal[2]
    y4_t = y4_ref[...].T
    for j in range(3 * D // PACK):
        part = nn(y4_t, dqkv_s[:, j * PACK : (j + 1) * PACK])
        put(me, 1, grads, ("qkv", j), part.astype(BF))
    for j in range(FF // PACK):
        part = tn(spread_ref[:, j * PACK : (j + 1) * PACK], db_ref[...]).astype(BF)
        put(me, 1, grads, ("point", 0), part, j * PACK // 64)
    part_slots(grads, kept, given)


def weigh1(scal, y4, dqkv, spread, db, ties=()):
    return whole_call(
        weigh1_kernel,
        group_grads(1),
        [scal, y4, dqkv, spread, db],
        scratch=[group_slots(1)],
        micros=3,
        ties=ties,
    )


def back2_kernel(tile, group, scal, low_ref, db_ref, high_ref, *refs):
    taps, mid_ref, left_ref, right_ref, g3, point = refs[:6]
    dl, st, gdepth_out, ln_out = refs[6:10]
    dbx, dsp, win, dmid, dr, gdepth_ref, ln_ref = refs[10:]
    rows = db_ref.shape[0]
    ext = rows + 2 * RIM
    base = scal[0] * rows - RIM
    first = scal[1]
    i = pl.program_id(0)
    last = ext // tile - 1

    @pl.when(i == 0)
    def _():
        dbx[0:RIM, :] = low_ref[...]
        dbx[RIM : RIM + rows, :] = db_ref[...]
        dbx[RIM + rows :, :] = high_ref[...]
        dsp[0:RIM, :] = jnp.zeros((RIM, FF), F32)
        dsp[RIM + ext :, :] = jnp.zeros((RIM, FF), F32)
        dr[0:RIM, :] = jnp.zeros((RIM, NARROW), F32)
        dr[RIM + ext :, :] = jnp.zeros((RIM, NARROW), F32)
        gdepth_ref[...] = jnp.zeros_like(gdepth_ref)
        ln_ref[...] = jnp.zeros_like(ln_ref)

        def spread_step(j, carry):
            dsp[rows_at(j, tile, RIM), :] = nt(dbx[rows_at(j, tile), :], point[...])
            return carry

        lax.fori_loop(0, ext // tile, spread_step, 0)

    begin = base + i * tile
    near = (first > begin - HALF) & (first < begin + tile + HALF)
    near = near | (i == 0) | (i == last)

    def chunk(c, carry):
        around = pl.ds(pl.multiple_of(i * tile, 16), tile + 2 * RIM)
        lanes = [pl.ds(pl.multiple_of((c * WIDTH + w) * LANES, LANES), LANES) for w in range(WIDTH)]
        for w in range(WIDTH):
            win[w] = dsp[around, lanes[w]]
        for masked in (False, True):

            @pl.when(near if masked else jnp.logical_not(near))
            def _():
                for w in range(WIDTH):
                    tap = [taps[k : k + 1, lanes[w]] for k in range(KERNEL)]
                    pairs = [None] * KERNEL
                    for r in range(0, tile, STEP):
                        pos = places(begin + r, STEP)
                        local = i * tile + r + iota((STEP, LANES), 0)
                        mid = mid_ref[r : r + STEP, lanes[w]].astype(F32)
                        total = None
                        for k in range(KERNEL):
                            o = HALF - k
                            v = win[w, RIM + o + r : RIM + o + r + STEP, :]
                            if masked and o != 0:
                                v = jnp.where(crosses(pos, o, first), 0.0, v)
                            counted = v
                            if masked:
                                kept = (local + o >= RIM) & (local + o < RIM + rows)
                                counted = jnp.where(kept, v, 0.0)
                            counted = counted * mid
                            counted = counted[:8] + counted[8:]
                            pairs[k] = counted if pairs[k] is None else pairs[k] + counted
                            total = v * tap[k] if total is None else total + v * tap[k]
                        dmid[r : r + STEP, lanes[w]] = total
                    for k in range(KERNEL):
                        gdepth_ref[k * 8 : (k + 1) * 8, lanes[w]] += pairs[k]

        return carry

    lax.fori_loop(0, FF // (WIDTH * LANES), chunk, 0)
    for q in range(0, tile, STEP):
        at = slice(q, q + STEP)
        left, slope = gelu_and_slope(left_ref[at, :])
        right, slope_r = gelu_and_slope(right_ref[at, :])
        joined = jnp.concatenate([left[:, :NARROW] + right, left[:, NARROW:]], axis=1)
        hat, r = normalise(joined)
        local = i * tile + q + iota((STEP, 1), 0)
        own = ((local >= RIM) & (local < RIM + rows)).astype(F32)
        pos = base + local
        grad = dmid[at, :] * ((pos >= 0) & (pos < group)).astype(F32)
        ln_ref[...] += fold8(grad * hat * own)
        dj = norm_back(grad, hat, r, g3[...])
        dl[at, :] = (dj * slope).astype(BF)
        dr[rows_at(i, tile, RIM + q, STEP), :] = (dj[:, :NARROW] * slope_r).astype(BF).astype(F32)

    @pl.when(i == last)
    def _():
        for k in range(KERNEL):
            gdepth_out[k : k + 1, :] = jnp.sum(
                gdepth_ref[k * 8 : (k + 1) * 8, :], axis=0, keepdims=True
            )
        ln_out[...] = jnp.sum(ln_ref[...], axis=0, keepdims=True)
        part = 128

        def gather_step(j, carry):
            at = rows_at(j, part)
            around = pl.ds(pl.multiple_of(RIM + j * part, 16), part + 2 * RIM)
            pos = places(base + RIM + j * part, part, NARROW)
            v = dr[around, :]
            after = pltpu.roll(v, part + 2 * RIM - 1, 0)[RIM : RIM + part]
            before = pltpu.roll(v, 1, 0)[RIM : RIM + part]
            after = jnp.where((pos + 1 == first) | (pos + 1 == group), 0.0, after)
            before = jnp.where((pos == first) | (pos == 0), 0.0, before)
            st[at, 0:NARROW] = after.astype(BF)
            st[at, NARROW : 2 * NARROW] = v[RIM : RIM + part].astype(BF)
            st[at, 2 * NARROW :] = before.astype(BF)
            return carry

        lax.fori_loop(0, rows // part, gather_step, 0)


def back2(scal, low, db, high, taps, mid, left, right, g3, point, group, ties=()):
    rows = db.shape[0]
    ext = rows + 2 * RIM
    tile = 160
    return call(
        functools.partial(back2_kernel, tile, group),
        [(scal, "s")]
        + [(a, None) for a in (low, db, high, taps)]
        + [(a, tile) for a in (mid, left, right)]
        + [(g3, None), (point, None)],
        [((ext, FF), BF, tile), ((rows, 3 * NARROW), BF, None)]
        + [((KERNEL, FF), F32, None), ((1, FF), F32, None)],
        scratch=[
            ((ext, NARROW), BF),
            ((ext + 2 * RIM, FF), F32),
            ((WIDTH, tile + 2 * RIM, LANES), F32),
            ((tile, FF), F32),
            ((ext + 2 * RIM, NARROW), F32),
            ((8 * KERNEL, FF), F32),
            ((8, FF), F32),
        ],
        micros=44,
        ties=ties,
        steps=ext // tile,
    )


def back1_kernel(scal, dl, st, dh2_ref, h1_ref, joined_ref, x_ref, g1, g2, *refs):
    glu, wide, narrow, dx_ref, y1_ref, dj_ref, ln1_out, ln2_out, ln1_ref, ln2_ref = refs
    i = pl.program_id(0)

    @pl.when(i == 0)
    def _():
        ln1_ref[...] = jnp.zeros_like(ln1_ref)
        ln2_ref[...] = jnp.zeros_like(ln2_ref)

    dy2 = nt(dl[...], wide[...])
    for k in range(3):
        dy2 = dy2 + nt(st[:, k * NARROW : (k + 1) * NARROW], narrow[k * D : (k + 1) * D, :])
    hat2, r2 = normalise(h1_ref[...])
    ln2_ref[...] += fold8(dy2 * hat2)
    dh1 = dh2_ref[...] + norm_back(dy2, hat2, r2, g2[...])
    gate = sigmoid(joined_ref[:, D:])
    value = joined_ref[:, :D]
    dj_ref[:, :D] = (dh1 * gate).astype(BF)
    dj_ref[:, D:] = (dh1 * value * gate * (1.0 - gate)).astype(BF)
    x = x_ref[...].astype(F32)
    hat1, r1 = normalise(x)
    y1_ref[...] = (hat1 * g1[...]).astype(BF)
    dy1 = nt(dj_ref[...], glu[...])
    ln1_ref[...] += fold8(dy1 * hat1)
    dx_ref[...] = (dh1 + norm_back(dy1, hat1, r1, g1[...])).astype(dx_ref.dtype)
    ln1_out[...] = jnp.sum(ln1_ref[...], axis=0, keepdims=True)
    ln2_out[...] = jnp.sum(ln2_ref[...], axis=0, keepdims=True)


def back1(scal, dl, st, dh2, h1, joined, x, g1, g2, glu, wide, narrow, start, rows):
    tile = 384
    own, ext = (tile, start), (tile, start + RIM)
    return call(
        back1_kernel,
        [(scal, "s"), (dl, ext), (st, own), (dh2, own), (h1, ext), (joined, ext), (x, ext)]
        + [(a, None) for a in (g1, g2, glu, wide, narrow)],
        [((rows, D), BF, tile), ((rows, D), BF, tile), ((rows, 2 * D), BF, tile)]
        + [((1, D), F32, None)] * 2,
        scratch=[((8, D), F32), ((8, D), F32)],
        micros=5,
        steps=rows // tile,
    )


def weigh2_kernel(scal, dl, st, y2_ref, kept, given, grads, gn):
    me = scal[2]
    rows = st.shape[0]
    y2_t = y2_ref[RIM : RIM + rows, :].T
    for j in range(FF // PACK):
        part = nn(y2_t, dl[RIM : RIM + rows, j * PACK : (j + 1) * PACK]).astype(BF)
        put(me, 2, grads, ("wide", j), part)
    for k in range(3):
        gn[k * D : (k + 1) * D, :] = nn(y2_t, st[:, k * NARROW : (k + 1) * NARROW]).astype(BF)
    put(me, 2, grads, ("narrow", 0), gn[...])
    part_slots(grads, kept, given)


def weigh2(scal, dl, st, y2):
    return whole_call(
        weigh2_kernel,
        group_grads(2),
        [scal, dl, st, y2],
        scratch=[group_slots(2), ((3 * D, NARROW), BF)],
        micros=3,
    )


def weigh3_kernel(halves, scal, *refs):
    y1, dj, ln1, ln2 = (refs[i * halves : (i + 1) * halves] for i in range(4))
    gains, taps, kept, given = refs[4 * halves : 4 * halves + 3], *refs[4 * halves + 3 : 4 * halves + 6]
    grads, table, block, ln1_s, ln2_s = refs[4 * halves + 6 :]
    me = scal[2]
    for total, parts in ((ln1_s, ln1), (ln2_s, ln2)):
        total[...] = sum(p[...] for p in parts[1:]) + parts[0][...]
    write_small(me, (ln1_s, ln2_s, *gains), taps, table, block, grads)
    turned = [y[...].T for y in y1]
    for j in range(2 * D // PACK):
        part = None
        for y, d in zip(turned, dj):
            more = nn(y, d[:, j * PACK : (j + 1) * PACK])
            part = more if part is None else part + more
        put(me, 3, grads, ("glu", j), part.astype(BF))
    part_slots(grads, kept, given)


def weigh3(scal, y1, dj, ln1, ln2, gains, taps):
    return whole_call(
        functools.partial(weigh3_kernel, len(y1)),
        group_grads(3),
        [scal, *y1, *dj, *ln1, *ln2, *gains, taps],
        scratch=[group_slots(3), ((BLOCKS, SMALL_ROWS * PACK), F32), ((BLOCKS, 16, PACK), F32)]
        + [((1, D), F32)] * 2,
        micros=0,
    )


def lane_maps(rows, head):
    lane = lax.broadcasted_iota(jnp.int32,(rows,LANES),1)
    own = (lane >= head*HEAD) & (lane < (head+1)*HEAD)
    rel = lane - (1-head)*HEAD
    return own, rel

def id_column(base, rows, first):
    pos = base + lax.broadcasted_iota(jnp.int32,(rows,LANES),0)
    return pos >= first

def split3(v):
    hi = v.astype(BF).astype(F32)
    mid = (v-hi).astype(BF).astype(F32)
    return hi, mid, v-hi-mid

def tile_ids(start, rows, first):
    return start < first, start+rows > first

def overlap(a_start,a_rows,b_start,b_rows,first):
    a0,a1 = tile_ids(a_start,a_rows,first); b0,b1=tile_ids(b_start,b_rows,first)
    return (a0&b0)|(a1&b1)

def attend_kernel(n, heads, share, tq, tk, scal, *refs):
    qkv = refs[:n]; att = refs[n:2*n]; lse_ref = refs[2*n]
    qa, ka, va, mx_ref, m_ref, q2_ref, acc_ref = refs[2*n+1:]
    s = scal[0]; first = scal[1]
    rows = qkv[0].shape[0]
    for k in range(n):
        base = (s ^ k)*rows
        id1 = id_column(base, rows, first).astype(F32)
        q = qkv[k][:, 0:LANES].astype(F32)*(HEAD**-0.5)
        key = qkv[k][:, LANES:2*LANES].astype(F32)
        v = qkv[k][:, 2*LANES:3*LANES].astype(F32)
        for i in range(heads):
            h = i if share==1 else s % share
            own, rel = lane_maps(rows, h)
            qx = jnp.where(rel==0, 1.0-id1, jnp.where(rel==1, id1, 0.0))
            kx = jnp.where(rel==0, id1*BIG, jnp.where(rel==1, (1.0-id1)*BIG, jnp.where(rel<5,1.0,0.0)))
            qa[i, k*rows:(k+1)*rows,:] = jnp.where(own, q, qx).astype(BF)
            ka[i, k*rows:(k+1)*rows,:] = jnp.where(own, key, kx).astype(BF)
            va[i, k*rows:(k+1)*rows,:] = jnp.where(own, v, 1.0).astype(BF)
    per = rows//tq; per_k = rows//tk
    def fold(sc, best):
        for j in range(tk//LANES):
            best = jnp.maximum(best, sc[:, j*LANES:(j+1)*LANES])
        return best
    def q_step(it, carry):
        kq = it//per
        r0 = pl.multiple_of((it % per)*tq, tq)
        g0 = pl.multiple_of(it*tq, tq)
        own0 = pl.multiple_of((g0//tk)*tk, tk)
        q_start = (s ^ kq)*rows + r0
        for i in range(heads):
            for j in range(max(1,tq//tk)):
                sc = nt(qa[i, pl.ds(g0,tq),:], ka[i, pl.ds(own0+j*tk,tk),:])
                best = fold(sc, sc[:, :LANES] if j==0 else best)
            mx_ref[i] = best
            m_ref[i] = jnp.zeros((tq,LANES),F32)
        def attempt(again):
            for i in range(heads):
                h = i if share==1 else s % share
                own, rel = lane_maps(tq, h)
                m = jnp.max(mx_ref[i], axis=1, keepdims=True)
                mb = m_ref[i] + jnp.broadcast_to(m, (tq,LANES))
                m_ref[i] = mb
                hi,mid,lo = split3(-mb)
                q = qa[i, pl.ds(g0,tq),:].astype(F32)
                q2_ref[i] = jnp.where(rel==2,hi,jnp.where(rel==3,mid,jnp.where(rel==4,lo,q))).astype(BF)
            mx_ref[...] = jnp.full_like(mx_ref, -3e38)
            acc_ref[...] = jnp.zeros_like(acc_ref)
            for kt in range(n*per_k):
                k_start = (s ^ (kt//per_k))*rows + (kt%per_k)*tk
                @pl.when(overlap(q_start,tq,k_start,tk,first))
                def _():
                    for i in range(heads):
                        sc = nt(q2_ref[i], ka[i, kt*tk:(kt+1)*tk,:])
                        mx_ref[i] = fold(sc, mx_ref[i])
                        p = jnp.exp2(sc*LOG2E).astype(BF)
                        acc_ref[i] += nn(p, va[i, kt*tk:(kt+1)*tk,:])
            return (jnp.max(mx_ref[...]) > 40.0).astype(jnp.int32)
        lax.while_loop(lambda again: again > 0, attempt, jnp.int32(1))
        out = jnp.zeros((tq,LANES),F32); lse = jnp.zeros((tq,LANES),F32)
        for i in range(heads):
            h = i if share==1 else s % share
            own,_ = lane_maps(tq,h)
            acc = acc_ref[i]
            total = pltpu.roll(acc, HEAD, 1)
            out = jnp.where(own, acc/total, out)
            lse = jnp.where(own, m_ref[i]+jnp.log(total), lse)
        lse_ref[pl.ds(g0,tq),:] = lse
        for k in range(n):
            @pl.when(kq==k)
            def _():
                att[k][pl.ds(r0,tq),:] = out.astype(BF)
        return carry
    lax.fori_loop(0, n*per, q_step, 0)

def attend(scal, blocks, n, share, tq=768, tk=768, ties=()):
    rows = blocks[0].shape[0]
    heads = 2 // share
    return whole_call(
        functools.partial(attend_kernel, n, heads, share, tq, tk),
        [((rows, LANES), BF)] * n + [((n * rows, LANES), F32)],
        [scal, *blocks],
        scratch=[((heads, n * rows, LANES), BF)] * 3
        + [((heads, tq, LANES), F32)] * 2
        + [((heads, tq, LANES), BF), ((heads, tq, LANES), F32)],
        ties=ties,
        micros=36,
    )


def attend_back_kernel(n, heads, share, tq, tk, scal, *refs):
    qkv = refs[:n]; att = refs[n:2*n]; dat = refs[2*n:3*n]; lse_ref = refs[3*n]
    out = refs[3*n+1:4*n+1]
    qa, ka, va, da, dq_ref, dk_ref, dv_ref = refs[4*n+1:]
    s = scal[0]; first = scal[1]
    rows = qkv[0].shape[0]
    for k in range(n):
        base = (s ^ k)*rows
        sl = slice(k*rows,(k+1)*rows)
        id1 = id_column(base, rows, first).astype(F32)
        q = qkv[k][:, 0:LANES].astype(F32)*(HEAD**-0.5)
        key = qkv[k][:, LANES:2*LANES].astype(F32)
        v = qkv[k][:, 2*LANES:3*LANES].astype(F32)
        do = dat[k][...].astype(F32)
        prod = do*att[k][...].astype(F32)
        for i in range(heads):
            h = i if share==1 else s % share
            own, rel = lane_maps(rows, h)
            lse = pltpu.roll(lse_ref[sl,:], HEAD, 1)
            hi,mid,lo = split3(-lse)
            delta = jnp.sum(jnp.where(own,prod,0.0),axis=1,keepdims=True)
            dhi,dmid,dlo = split3(-delta)
            qx = jnp.where(rel==0, 1.0-id1, jnp.where(rel==1, id1, jnp.where(rel==2,hi,jnp.where(rel==3,mid,jnp.where(rel==4,lo,0.0)))))
            kx = jnp.where(rel==0, id1*BIG, jnp.where(rel==1, (1.0-id1)*BIG, jnp.where(rel<5,1.0,0.0)))
            vx = jnp.where(rel<3,1.0,0.0)
            dx = jnp.where(rel==0,dhi,jnp.where(rel==1,dmid,jnp.where(rel==2,dlo,0.0)))
            qa[i,sl,:] = jnp.where(own,q,qx).astype(BF)
            ka[i,sl,:] = jnp.where(own,key,kx).astype(BF)
            va[i,sl,:] = jnp.where(own,v,vx).astype(BF)
            da[i,sl,:] = jnp.where(own,do,dx).astype(BF)
    dq_ref[...] = jnp.zeros_like(dq_ref)
    per_q = rows//tq; per_k = rows//tk
    def k_step(kt, carry):
        k0 = pl.multiple_of(kt*tk, tk)
        kk = kt//per_k
        k_start = (s ^ kk)*rows + (kt % per_k)*tk
        for i in range(heads):
            dk_ref[i] = jnp.zeros((tk,LANES),F32)
            dv_ref[i] = jnp.zeros((tk,LANES),F32)
        def q_step(qt, c2):
            q0 = pl.multiple_of(qt*tq, tq)
            q_start = (s ^ (qt//per_q))*rows + (qt % per_q)*tq
            @pl.when(overlap(q_start,tq,k_start,tk,first))
            def _():
                for i in range(heads):
                    qq = qa[i,pl.ds(q0,tq),:]; kx = ka[i,pl.ds(k0,tk),:]; dd = da[i,pl.ds(q0,tq),:]
                    st = nt(kx, qq)
                    p = jnp.exp2(st*LOG2E)
                    dp = nt(va[i,pl.ds(k0,tk),:], dd)
                    ds = (p*dp).astype(BF)
                    dv_ref[i] += nn(p.astype(BF), dd)
                    dk_ref[i] += nn(ds, qq)
                    dq_ref[i,pl.ds(q0,tq),:] += tn(ds, kx)
            return c2
        lax.fori_loop(0, n*per_q, q_step, 0)
        dk = jnp.zeros((tk,LANES),F32); dv = jnp.zeros((tk,LANES),F32)
        for i in range(heads):
            h = i if share==1 else s % share
            own,_ = lane_maps(tk,h)
            dk = jnp.where(own, dk_ref[i], dk); dv = jnp.where(own, dv_ref[i], dv)
        r0 = pl.multiple_of((kt % per_k)*tk, tk)
        for k in range(n):
            @pl.when(kk==k)
            def _():
                out[k][pl.ds(r0,tk),LANES:2*LANES] = dk.astype(BF)
                out[k][pl.ds(r0,tk),2*LANES:3*LANES] = dv.astype(BF)
        return carry
    lax.fori_loop(0, n*per_k, k_step, 0)
    for k in range(n):
        sl = slice(k*rows,(k+1)*rows)
        dq = jnp.zeros((rows,LANES),F32)
        for i in range(heads):
            h = i if share==1 else s % share
            own,_ = lane_maps(rows,h)
            dq = jnp.where(own, dq_ref[i,sl,:], dq)
        out[k][:, 0:LANES] = (dq*(HEAD**-0.5)).astype(BF)

def attend_back(scal, blocks, att, datt, lse, n, share, tq=384, tk=384, ties=()):
    rows = blocks[0].shape[0]
    heads = 2 // share
    return whole_call(
        functools.partial(attend_back_kernel, n, heads, share, tq, tk),
        [((rows, 3 * LANES), BF)] * n,
        [scal, *blocks, *att, *datt, lse],
        scratch=[((heads, n * rows, LANES), BF)] * 4
        + [((heads, n * rows, LANES), F32)]
        + [((heads, tk, LANES), F32)] * 2,
        ties=ties,
        micros=58,
    )


class Links:
    def __init__(self, n_seq, n_dp):
        self.count = n_seq * n_dp
        self.direct = (n_seq, n_dp) == (4, 8)

    def flip(self, value, mask):
        return lax.ppermute(value, AXES, [(i, i ^ mask) for i in range(self.count)])

    def near(self, block):
        return jnp.stack([block] + [self.flip(block, k << 3) for k in range(1, 4)])

    def part(self, group, held):
        low = height(GATHERS[group][0])
        return [held[:, :low], held[:, low:]]

    def spread(self, held, stage):
        masks = ((4, 2), (2, 4))[stage]
        return [jnp.concatenate([h, self.flip(h, m)]) for h, m in zip(held, masks)]

    def across(self, held):
        return [held[0], self.flip(held[0], 1), held[1], self.flip(held[1], 1)]

    def gather_whole(self, group, weights):
        whole = {
            name: lax.all_gather(weights[name], AXES, axis=0, tiled=True)
            for name in dict(sum(GATHERS[group], []))
        }
        pieces = []
        for half, items in enumerate(GATHERS[group]):
            blocks = [
                whole[name][:, j * PACK : (j + 1) * PACK].reshape(BLOCKS, -1, PACK)
                for name, j in items
            ]
            pieces += list(self.by_slot(jnp.concatenate(blocks, axis=1), half))
        return pieces

    def by_slot(self, blocks, half):
        shape = blocks.shape[1:]
        order = ((3, 2, 1, 0), (3, 1, 2, 0))[half]
        return blocks.reshape(4, 2, 2, 2, *shape).transpose(*order, 4, 5).reshape(2, 16, *shape)

    def by_owner(self, slots, half):
        shape = slots.shape[1:]
        order = ((3, 2, 1, 0), (3, 1, 2, 0))[half]
        return slots.reshape(2, 2, 2, 4, *shape).transpose(*order, 4, 5).reshape(BLOCKS, *shape)

    def add(self, a, b):
        return (a.astype(F32) + b.astype(F32)).astype(BF)

    def fold(self, slots, mask):
        middle = slots.shape[0] // 2
        return self.add(slots[:middle], self.flip(slots[middle:], mask))

    def cores(self, kept, given):
        return self.add(kept, self.flip(given, 1))

    def first(self, group, kept, given):
        held = self.cores(kept, given)
        low = height(SUMS[group][0])
        return [held[:, :low], held[:, low:]]

    def straight(self, held, stage):
        return self.fold(held, (2, 4)[stage])

    def flips(self, values, mask):
        flat = self.flip(jnp.concatenate([v.reshape(-1, PACK) for v in values], axis=0), mask)
        result, at = [], 0
        for v in values:
            count = v.size // PACK
            result.append(flat[at : at + count].reshape(v.shape))
            at += count
        return result

    def next_two(self, late, early):
        a, b = (v.shape[0] // 2 for v in late)
        c, d = (v.shape[0] // 2 for v in early)
        got_y = self.flips([late[0][a:], early[1][d:]], 4)
        got_x = self.flips([late[1][b:], early[0][c:]], 2)
        late = [self.add(late[0][:a], got_y[0]), self.add(late[1][:b], got_x[0])]
        early = [self.add(early[0][:c], got_x[1]), self.add(early[1][:d], got_y[1])]
        return late, early

    def next_and_plane(self, late, held):
        a, b = (v.shape[0] // 2 for v in late)
        got_y = self.flips([late[0][a:], held[4:8]], 4)
        got_x = self.flips([late[1][b:], held[8:12]], 2)
        total = held[:4].astype(F32) + got_y[1].astype(F32) + got_x[1].astype(F32)
        total = total + self.flip(held[12:], 6).astype(F32)
        late = [self.add(late[0][:a], got_y[0]), self.add(late[1][:b], got_x[0])]
        return late, total.astype(BF)

    def next(self, held, stage):
        masks = ((2, 4), (4, 2))[stage]
        return [self.fold(h, m) for h, m in zip(held, masks)]

    def finish(self, held):
        held = jnp.concatenate(held, axis=1)
        total = held[0].astype(F32)
        for k in range(1, 4):
            total = total + self.flip(held[k], k << 3).astype(F32)
        return total

    def rows_of(self, items, total):
        parts, at = {}, 0
        for name, j in items:
            b = ROWS[name] * BLOCKS // self.count
            parts.setdefault(name, []).append(total[at : at + b])
            at += b
        return {name: jnp.concatenate(p, axis=1) for name, p in parts.items()}

    def scatter_whole(self, group, parts):
        slots = jnp.concatenate(parts)
        sent, at = [], 0
        for half, items in enumerate(SUMS[group]):
            for name, _ in items:
                blocks = self.by_owner(slots[:, at : at + ROWS[name]], half if group in SPLIT else 0)
                sent.append(blocks.reshape(self.count, -1, PACK))
                at += ROWS[name]
        sent = jnp.concatenate(sent, axis=1)
        return lax.psum_scatter(sent, AXES, scatter_dimension=0, tiled=False).astype(F32)


class Layout:
    def __init__(self, n_seq, n_dp):
        self.n_seq, self.n_dp = n_seq, n_dp
        self.where = {}
        for g in range(n_dp):
            for s in range(n_seq):
                self.where[g, s] = self.place(g, s)
        self.block = np.zeros(n_seq * n_dp, np.int32)
        for (g, s), device in self.where.items():
            self.block[device] = s

    def place(self, g, s):
        if (self.n_seq, self.n_dp) == (4, 8):
            y, x, c = g >> 2, g >> 1 & 1, g & 1
            return (2 * c + y) * 8 + (s & 1) * 4 + x * 2 + (s >> 1)
        return s * self.n_dp + g

    def pairs(self, source, target):
        return [
            (source(g, s), target(g, s))
            for g in range(self.n_dp)
            for s in range(self.n_seq)
            if target(g, s) is not None and source(g, s) is not None
        ]

    def at(self, g, s):
        return self.where.get((g, s))

    def home(self, g, s):
        return s * self.n_dp + g

    def bring(self, value):
        return lax.ppermute(value, AXES, self.pairs(self.home, self.at))

    def bring_to(self, value, step):
        return lax.ppermute(
            value, AXES, self.pairs(self.home, lambda g, s: self.at(g, s + step))
        )

    def send_home(self, value):
        return lax.ppermute(value, AXES, self.pairs(self.at, self.home))

    def to_neighbour(self, value, step):
        return lax.ppermute(value, AXES, self.pairs(self.at, lambda g, s: self.at(g, s + step)))

    def swap(self, values):
        return [values[0]] + [
            lax.ppermute(values[k], AXES, self.pairs(self.at, lambda g, s: self.at(g, s ^ k)))
            for k in range(1, self.n_seq)
        ]


NAMES = ("ln1", "ln2", "ln3", "ln4", "ln5", "glu", "wide", "narrow", "depth", "point", "qkv", "attn", "up", "down")
SMALL = ("ln1", "ln2", "ln3", "ln4", "ln5", "depth")


def sync(*values):
    return lax.optimization_barrier(values)


def small_block(arrays, blocks):
    flat = jnp.concatenate([a.reshape(blocks, -1) for a in arrays], axis=1)
    flat = jnp.pad(flat, ((0, 0), (0, 16 * PACK - flat.shape[1])))
    return flat.reshape(blocks * 16, PACK)


def on_device(tokens, cotangent, first_length, *weights):
    n = lax.axis_size("seq")
    n_dp = lax.axis_size("dp")
    share = n * LANES // D
    layout = Layout(n, n_dp)
    links = Links(n, n_dp)
    direct = links.direct
    rows = tokens.shape[1]
    group = n * rows
    here = lax.axis_index("seq") * n_dp + lax.axis_index("dp")
    me = here if direct else jnp.zeros_like(here)
    s = jnp.asarray(layout.block)[here]
    mine = dict(zip(NAMES, weights))
    if direct:
        mine["small"] = small_block([mine[k] for k in SMALL], 1)
    else:
        small = [lax.all_gather(mine[k], AXES, axis=0, tiled=True) for k in SMALL]
        mine["small"] = small_block(small, BLOCKS).reshape(links.count, -1, PACK)[here]

    tokens = tokens[0]
    digits = jnp.where(
        lax.broadcasted_iota(jnp.int32, (RIM, D), 1) < LANES,
        first_length[0] // LANES,
        first_length[0] % LANES,
    )
    sent = jnp.concatenate([tokens, digits.astype(BF)], axis=0)
    if direct:
        blocks = pack({k: mine[k] for k in mine if k not in SMALL})
        sent, blocks = sync(sent, blocks)
        held1 = links.near(blocks[0])
    x = layout.bring(sent)
    if direct:
        held1 = links.spread(links.part(0, *sync(held1)), 0)
    low = layout.bring_to(tokens[-RIM:], 1)
    high = layout.bring_to(tokens[:RIM], -1)
    if direct:
        held1, x, low, high, blocks = sync(held1, x, low, high, blocks)
        held1 = links.spread(held1, 1)
        held2 = links.near(blocks[1])
    digits = x[rows, 0 : 2 * LANES : LANES].astype(F32).astype(jnp.int32)
    first = digits[0] * LANES + digits[1]
    scal = jnp.stack([s.astype(jnp.int32), first, me.astype(jnp.int32)])
    x_ext = jnp.concatenate([low, x[:rows], high], axis=0)
    if direct:
        held1, held2, scal, x_ext = sync(held1, held2, scal, x_ext)
        pieces1 = links.across(held1)
        held2 = links.spread(links.part(1, held2), 0)
        pieces1, held2 = sync(pieces1, held2)
        held2 = links.spread(held2, 1)
    else:
        pieces1, pieces2, pieces3 = (links.gather_whole(k, mine) for k in range(3))
    h1, y2, joined, *rest = front1(scal, x_ext, pieces1)
    (glu, wide, narrow), (g1, g2, g3, g4, g5, taps) = rest[:3], rest[3:]
    if direct:
        y2, held2, blocks = sync(y2, held2, blocks)
        pieces2 = links.across(held2)
        held3 = links.near(blocks[2])
    left, right, mid = front2(scal, y2, g3, wide, narrow, group)
    if direct:
        mid, pieces2, held3 = sync(mid, pieces2, held3)
        held3 = links.spread(links.part(2, held3), 0)
    spread, h2, y4, *rest = front3(scal, mid, taps, h1, g4, pieces2, n, share)
    qkv, (qkv_w, point) = rest[:n], rest[n:]
    if direct:
        qkv, held3 = sync(qkv, held3)
    qkv = layout.swap(qkv)
    qkv, cot = sync(qkv, cotangent[0])
    cot = layout.bring(cot)
    if direct:
        held3, qkv = sync(held3, qkv)
        held3 = links.spread(held3, 1)
    *att, lse = attend(scal, qkv, n, share)
    if direct:
        att, held3, cot = sync(att, held3, cot)
        pieces3 = links.across(held3)
    else:
        att, cot = sync(att, cot)
    arrived = layout.swap(att)
    mixed, dh3, *rest = middle(scal, h2, arrived, cot, g5, pieces3, n, share)
    datt, (att_all, y5, inner, du, ln5) = rest[:n], rest[n:]
    datt, du = sync(datt, du)
    datt = layout.swap(datt)
    sum0 = weigh0(scal, att_all, y5, inner, du, cot, dh3)
    datt, sum0 = sync(datt, sum0)
    if direct:
        sum0 = links.cores(*sum0)
    dqkv = attend_back(scal, qkv, att, datt, lse, n, share)
    dqkv, sum0 = sync(dqkv, sum0)
    dqkv = layout.swap(dqkv)
    if direct:
        sum0 = links.straight(sum0, 0)
        dqkv, sum0 = sync(dqkv, sum0)
        sum0 = links.straight(sum0, 1)
    dh2, db, dqkv, ln4 = back3(scal, dqkv, dh3, h2, g4, qkv_w, n, share)
    db, dqkv = sync(db, dqkv)
    low = layout.to_neighbour(db[-RIM:], 1)
    high = layout.to_neighbour(db[:RIM], -1)
    sum1 = weigh1(scal, y4, dqkv, spread, db)
    low, high, sum1, sum0, mixed = sync(low, high, sum1, sum0, mixed)
    if direct:
        total0 = links.finish([sum0])
        sum1 = links.first(1, *sum1)
    mixed = layout.send_home(mixed)
    dl, st, gdepth, ln3 = back2(scal, low, db, high, taps, mid, left, right, g3, point, group)
    if direct:
        dl, st, total0, sum1, mixed = sync(dl, st, total0, sum1, mixed)
        sum1 = links.next(sum1, 0)
    sum2 = weigh2(scal, dl, st, y2)
    if direct:
        (dl, sum2) = sync(dl, sum2)
        sum2 = links.first(2, *sum2)
    half = rows // 2
    fixed = (scal, dl, st, dh2, h1, joined, x_ext, g1, g2, glu, wide, narrow)
    dx_a, y1_a, dj_a, ln1_a, ln2_a = back1(*fixed, 0, half)
    if direct:
        dx_a, dl, sum1, sum2 = sync(dx_a, dl, sum1, sum2)
        sum1, sum2 = links.next_two(sum1, sum2)
        fixed = (scal, dl, *fixed[2:])
    dx_a = layout.send_home(dx_a)
    dx_b, y1_b, dj_b, ln1_b, ln2_b = back1(*fixed, half, rows - half)
    if direct:
        dx_b, dj_b = sync(dx_b, dj_b)
    dx_b = layout.send_home(dx_b)
    gains = (ln3, ln4, ln5)
    sum3 = weigh3(scal, (y1_a, y1_b), (dj_a, dj_b), (ln1_a, ln1_b), (ln2_a, ln2_b), gains, gdepth)
    if direct:
        sum3, sum2, sum1, dx_a = sync(sum3, sum2, sum1, dx_a)
        sum3 = links.cores(*sum3)
    if direct:
        sum3, sum2 = sync(sum3, sum2)
        sum2, sum3 = links.next_and_plane(sum2, sum3)
        *held, dx_b = sync(*sum2, sum3, dx_b)
        sums = (total0, links.finish([*sum1, *held]))
        tables = (sum(SUMS[0], []), sum([*SUMS[1], *SUMS[2], *SUMS[3]], []))
    else:
        sums = [links.scatter_whole(k, v) for k, v in enumerate((sum0, sum1, sum2, sum3))]
        tables = [sum(items, []) for items in SUMS]
    dx = jnp.concatenate([dx_a, dx_b], axis=0)
    out = {}
    for items, total in zip(tables, sums):
        out.update(links.rows_of(items, total))
    flat = out.pop("small")
    if not direct:
        flat = lax.all_gather(flat, AXES, axis=0, tiled=True)
    flat = flat.reshape(-1, 16 * PACK)
    sizes = [width for _, width in GAINS] + [TAP_RUN]
    at = 0
    for name, size in zip(SMALL, sizes):
        part = flat[:, at : at + size].reshape(-1)
        at += size
        if not direct:
            own = mine[name].shape[0]
            part = lax.dynamic_slice(part, (here * own,), (own,))
        out[name] = part
    return (mixed[None], dx.astype(F32)[None], *(out[name] for name in NAMES))


def solution(mesh):
    token, owner, rows = P("dp", "seq", None), P(AXES), P(AXES, None)
    params = (owner,) * 5 + (rows,) * 3 + (owner,) + (rows,) * 5
    return jax.shard_map(
        on_device,
        mesh=mesh,
        in_specs=(token, token, P("dp")) + params,
        out_specs=(token, token) + params,
        check_vma=False,
    )
```

```python
import functools
import math

import jax
import jax.numpy as jnp
import numpy as np
from jax import lax
from jax.experimental import pallas as pl
from jax.experimental.pallas import tpu as pltpu
from jax.sharding import PartitionSpec as P

D = 512
HEADS = 8
FF = 2048
KERNEL = 9
HEAD = 64
NARROW = 256
HALF = KERNEL // 2
LANES = 128
PACK = 256
RIM = 16
BLOCKS = 32
F32 = jnp.float32
BF = jnp.bfloat16
LOG2E = math.log2(math.e)
BIG = -1e30
AXES = ("seq", "dp")
VMEM = 58 << 20


def nt(a, b):
    return lax.dot_general(a, b, (((1,), (1,)), ((), ())), preferred_element_type=F32)


def nn(a, b):
    return lax.dot_general(a, b, (((1,), (0,)), ((), ())), preferred_element_type=F32)


def tn(a, b):
    return lax.dot_general(a, b, (((0,), (0,)), ((), ())), preferred_element_type=F32)


def call(kernel, ins, outs, scratch=(), micros=0, ties=(), steps=None):
    if ties:
        inner, fixed, count = kernel, len(ins), len(ties)

        def kernel(*refs):
            inner(*refs[:fixed], *refs[fixed + count :])

    def spec(shape, how, once):
        if how == "s":
            return pl.BlockSpec(memory_space=pltpu.SMEM)
        if steps is None:
            return pl.BlockSpec(memory_space=pltpu.VMEM)
        if isinstance(how, tuple):
            tile, start = how
            block = tuple(pl.Element(b) for b in (tile, *shape[1:]))
            rest = (0,) * (len(shape) - 1)
            return pl.BlockSpec(block, lambda i: (pl.multiple_of(start + i * tile, 16), *rest))
        if how is None:
            zeros = (0,) * len(shape)
            mode = pl.Buffered(1) if once else None
            return pl.BlockSpec(shape, lambda i: zeros, pipeline_mode=mode)
        return pl.BlockSpec((how, *shape[1:]), lambda i: (i, *(0,) * (len(shape) - 1)))

    args = [a for a, _ in ins]
    shapes = [jax.ShapeDtypeStruct(shape, dtype) for shape, dtype, _ in outs]
    moved = sum(math.prod(a.shape) * a.dtype.itemsize for a in args + shapes) if micros else 0
    return pl.pallas_call(
        kernel,
        out_shape=shapes,
        grid=() if steps is None else (steps,),
        in_specs=[spec(a.shape, how, True) for a, how in ins]
        + [pl.BlockSpec(memory_space=pl.ANY)] * len(ties),
        out_specs=[spec(shape, how, False) for shape, _, how in outs],
        scratch_shapes=[pltpu.VMEM(shape, dtype) for shape, dtype in scratch],
        compiler_params=pltpu.CompilerParams(vmem_limit_bytes=VMEM),
        cost_estimate=pl.CostEstimate(
            flops=int(micros * 1.15e9), bytes_accessed=moved, transcendentals=0
        ),
    )(*args, *ties)


def whole_call(kernel, outs, args, scratch=(), micros=0, ties=()):
    ins = [(a, "s" if i == 0 else None) for i, a in enumerate(args)]
    outs = [(shape, dtype, None) for shape, dtype in outs]
    return call(kernel, ins, outs, scratch, micros, ties)


def normalise(v):
    mean = jnp.mean(v, axis=1, keepdims=True)
    c = v - mean
    r = lax.rsqrt(jnp.mean(c * c, axis=1, keepdims=True) + 1e-05)
    return c * r, r


def norm_back(grad, hat, r, gain):
    g = grad * gain
    a = jnp.mean(g, axis=1, keepdims=True)
    b = jnp.mean(g * hat, axis=1, keepdims=True)
    return r * (g - a - hat * b)


C0 = math.sqrt(2.0 / math.pi)
C1 = 0.044715


def gelu(x):
    return 0.5 * x * (1.0 + jnp.tanh(x * (C0 + C0 * C1 * (x * x))))


def gelu_and_slope(x):
    xx = x * x
    t = jnp.tanh(x * (C0 + C0 * C1 * xx))
    half = 0.5 * (1.0 + t)
    return x * half, half + (0.5 * x) * (1.0 - t * t) * (C0 + 3.0 * C0 * C1 * xx)


def sigmoid(x):
    return 0.5 * jnp.tanh(0.5 * x) + 0.5


def fold8(v):
    return jnp.sum(v.reshape(v.shape[0] // 8, 8, v.shape[1]), axis=0)


def rows_at(i, tile, start=0, count=None):
    return pl.ds(pl.multiple_of(start + i * tile, 16), count or tile)


def places(base, rows, lanes=LANES):
    return base + lax.broadcasted_iota(jnp.int32, (rows, lanes), 0)


ROWS = {"glu": 16, "wide": 16, "narrow": 48, "point": 64, "qkv": 16, "attn": 16, "up": 16, "down": 64, "small": 16}


def columns_of(name, *chunks):
    return [(name, j) for j in chunks]


WIDE, GLU, QKV, UP = (columns_of(n, *range(k)) for n, k in (("wide", 8), ("glu", 4), ("qkv", 6), ("up", 8)))
NARROW_0, POINT_0, SMALL_0 = (columns_of(n, 0) for n in ("narrow", "point", "small"))
ATTN, DOWN = columns_of("attn", 0, 1), columns_of("down", 0, 1)
LAST = (UP + ATTN[:1], ATTN[1:] + DOWN)
GATHERS = ((WIDE, GLU + NARROW_0 + SMALL_0), (QKV[:5], QKV[5:] + POINT_0), LAST)
SUMS = (
    LAST,
    (QKV[:5], QKV[5:] + POINT_0),
    (WIDE[:6], WIDE[6:] + NARROW_0),
    (GLU[:2], GLU[2:] + SMALL_0),
)

SPLIT = (1, 2)


def height(items):
    return sum(ROWS[name] for name, _ in items)


def row_of(items, item):
    return height(items[: items.index(item)])


def slot_bits(half, r):
    high, low, z = r >> 3, r >> 2 & 1, r & 3
    x, y = (high, low) if half == 0 else (low, high)
    return z * 8 + y * 4 + x * 2


def slot_of(half, rel):
    z, y, x, c = rel >> 3, rel >> 2 & 1, rel >> 1 & 1, rel & 1
    high, low = (x, y) if half == 0 else (y, x)
    return c * 16 + high * 8 + low * 4 + z


def unpack(me, group, pieces, wanted):
    for half, items in enumerate(GATHERS[group]):
        for core in range(2):
            piece = pieces[half * 2 + core]
            for r in range(BLOCKS // 2):
                owner = (slot_bits(half, r) + core) ^ me
                for name, j in items:
                    if name in wanted:
                        b, off = ROWS[name], row_of(items, (name, j))
                        wanted[name][
                            pl.ds(pl.multiple_of(owner * b, 16), b), j * PACK : (j + 1) * PACK
                        ] = piece[r, off : off + b, :]


def put(me, group, ref, item, value, start=0):
    half = int(item in SUMS[group][1])
    off = row_of(SUMS[group][half], item) + half * height(SUMS[group][0])
    b = ROWS[item[0]]
    for k in range(value.shape[0] // b):
        slot = slot_of(half if group in SPLIT else 0, (start + k) ^ me)
        ref[slot, off : off + b, :] = value[k * b : (k + 1) * b]


def group_grads(group):
    rows = height(sum(SUMS[group], []))
    return [((BLOCKS // 2, rows, PACK), BF)] * 2


def group_slots(group):
    return ((BLOCKS, height(sum(SUMS[group], [])), PACK), BF)


def part_slots(slots, kept, given):
    kept[...] = slots[: BLOCKS // 2]
    given[...] = slots[BLOCKS // 2 :]


SHAPES = ({"glu": (D, 2 * D), "wide": (D, FF), "narrow": (3 * D, NARROW)}, {"qkv": (D, 3 * D), "point": (FF, NARROW)})

GAINS = ((0, 16), (16, 16), (32, 64), (96, 16), (112, 16))
TAPS = 128
TAP_RUN = KERNEL * FF // BLOCKS
SMALL_ROWS = 3


def iota(shape, dim):
    return lax.broadcasted_iota(jnp.int32, shape, dim)


def owner_slots(me, half):
    shape = (BLOCKS, BLOCKS)
    return (slot_of(half, iota(shape, 0) ^ me) == iota(shape, 1)).astype(F32).astype(BF)


def gain_maps(offset, width):
    total = BLOCKS * width
    owner = iota((BLOCKS, total), 1) // width == iota((BLOCKS, total), 0)
    value = iota((LANES, total), 0) == offset + iota((LANES, total), 1) % width
    return owner, value.astype(F32).astype(BF)


def tap_runs():
    for b in range(KERNEL * FF // 64):
        f = b * 64
        yield f // FF, f % FF, f // TAP_RUN, TAPS + f % TAP_RUN


def read_small(me, pieces, gains, taps, table):
    off = row_of(GATHERS[0][1], SMALL_0[0])
    for core in range(2):
        for r in range(BLOCKS // 2):
            rows = pieces[2 + core][r, off : off + 16, :].astype(F32)
            slot = core * 16 + r
            for q in range(SMALL_ROWS):
                table[slot : slot + 1, q * PACK : (q + 1) * PACK] = rows[q : q + 1, :]
    table[...] = nn(owner_slots(me, 1), table[...].astype(BF))
    for ref, (offset, width) in zip(gains, GAINS):
        owner, value = gain_maps(offset, width)
        spread = nn(table[:, :LANES].astype(BF), value)
        ref[...] = jnp.sum(jnp.where(owner, spread, 0.0), axis=0, keepdims=True)
    for tap, channel, who, place in tap_runs():
        taps[tap : tap + 1, channel : channel + 64] = table[who : who + 1, place : place + 64]


def write_small(me, gains, taps, table, block, grads):
    table[...] = jnp.zeros_like(table)
    total = jnp.zeros((BLOCKS, LANES), F32)
    for gain, (offset, width) in zip(gains, GAINS):
        owner, value = gain_maps(offset, width)
        total = total + nt(jnp.where(owner, gain[...], 0.0).astype(BF), value)
    table[:, :LANES] = total
    for tap, channel, who, place in tap_runs():
        table[who : who + 1, place : place + 64] = taps[tap : tap + 1, channel : channel + 64]
    table[...] = tn(owner_slots(me, 0), table[...].astype(BF))
    block[...] = jnp.zeros_like(block)
    for slot in range(BLOCKS):
        for q in range(SMALL_ROWS):
            block[slot, q : q + 1, :] = table[slot : slot + 1, q * PACK : (q + 1) * PACK]
    at = height(sum(SUMS[3], [])) - 16
    grads[:, at : at + 16, :] = block[...].astype(BF)


def pack_kernel(names, *refs):
    shards = dict(zip(names, refs))
    for ref, halves in zip(refs[len(names) :], GATHERS):
        at = 0
        for name, j in sum(halves, []):
            b = ROWS[name]
            if name == "small":
                ref[at : at + b, :] = shards[name][...]
            else:
                ref[at : at + b, :] = shards[name][:, j * PACK : (j + 1) * PACK]
            at += b


def pack(shards):
    names = tuple(shards)
    return call(
        functools.partial(pack_kernel, names),
        [(shards[k], None) for k in names],
        [((height(sum(halves, [])), PACK), BF, None) for halves in GATHERS],
        micros=2,
    )


def front1_kernel(scal, x_ref, p0, p1, p2, p3, h1_ref, y2_ref, joined_ref, *refs):
    weights, gains, taps, table = refs[:3], refs[3:8], refs[8], refs[9]
    g1, g2 = gains[:2]

    @pl.when(pl.program_id(0) == 0)
    def _():
        read_small(scal[2], (p0, p1, p2, p3), gains, taps, table)
        unpack(scal[2], 0, (p0, p1, p2, p3), dict(zip(SHAPES[0], weights)))

    x = x_ref[...].astype(F32)
    hat, _ = normalise(x)
    joined = nn((hat * g1[...]).astype(BF), weights[0][...])
    joined_ref[...] = joined
    h1 = x + joined[:, :D] * sigmoid(joined[:, D:])
    h1_ref[...] = h1
    hat2, _ = normalise(h1)
    y2_ref[...] = (hat2 * g2[...]).astype(BF)


def front1(scal, x, pieces, ties=()):
    rows = x.shape[0]
    tile = 400
    return call(
        front1_kernel,
        [(scal, "s"), (x, tile)] + [(p, None) for p in pieces],
        [((rows, D), F32, tile), ((rows, D), BF, tile), ((rows, 2 * D), F32, tile)]
        + [(shape, BF, None) for shape in SHAPES[0].values()]
        + [((1, BLOCKS * width), F32, None) for _, width in GAINS]
        + [((KERNEL, FF), F32, None)],
        scratch=[((BLOCKS, SMALL_ROWS * PACK), F32)],
        micros=12,
        ties=ties,
        steps=rows // tile,
    )


def front2_kernel(tile, group, scal, y2_ref, g3, wide, narrow, left_ref, right_ref, mid_ref, u_ref):
    rows = y2_ref.shape[0]
    base = scal[0] * (rows - 2 * RIM) - RIM
    first = scal[1]
    i = pl.program_id(0)

    @pl.when(i == 0)
    def _():
        u_ref[0:RIM, :] = jnp.zeros((RIM, 3 * NARROW), F32)
        u_ref[RIM + rows : 2 * RIM + rows, :] = jnp.zeros((RIM, 3 * NARROW), F32)

        def narrow_step(j, carry):
            y = y2_ref[rows_at(j, tile), :]
            for k in range(3):
                u_ref[rows_at(j, tile, RIM), k * NARROW : (k + 1) * NARROW] = nn(
                    y, narrow[k * D : (k + 1) * D, :]
                )
            return carry

        lax.fori_loop(0, rows // tile, narrow_step, 0)

    around = pl.ds(pl.multiple_of(i * tile, 16), tile + 2 * RIM)
    left = nn(y2_ref[rows_at(i, tile), :], wide[...])
    left_ref[...] = left
    pos = places(base + i * tile, tile, NARROW)
    before = pltpu.roll(u_ref[around, 0:NARROW], 1, 0)[RIM : RIM + tile]
    after = pltpu.roll(u_ref[around, 2 * NARROW :], tile + 2 * RIM - 1, 0)[RIM : RIM + tile]
    right = u_ref[rows_at(i, tile, RIM), NARROW : 2 * NARROW]
    right = right + jnp.where((pos == first) | (pos == 0), 0.0, before)
    right = right + jnp.where((pos + 1 == first) | (pos + 1 == group), 0.0, after)
    right_ref[...] = right
    for q in range(0, tile, STEP):
        at = slice(q, q + STEP)
        left = gelu(left_ref[at, :])
        joined = jnp.concatenate([left[:, :NARROW] + gelu(right_ref[at, :]), left[:, NARROW:]], axis=1)
        hat, _ = normalise(joined)
        row = base + i * tile + q + iota((STEP, 1), 0)
        inside = ((row >= 0) & (row < group)).astype(F32)
        mid_ref[at, :] = (hat * inside * g3[...]).astype(BF)


def front2(scal, y2, g3, wide, narrow, group, ties=()):
    rows = y2.shape[0]
    tile = 400
    return call(
        functools.partial(front2_kernel, tile, group),
        [(scal, "s"), (y2, None), (g3, None), (wide, None), (narrow, None)],
        [((rows, FF), F32, tile), ((rows, NARROW), F32, tile), ((rows, FF), BF, tile)],
        scratch=[((rows + 2 * RIM, 3 * NARROW), F32)],
        micros=12,
        ties=ties,
        steps=rows // tile,
    )


def crosses(pos, offset, first):
    if offset > 0:
        return (pos < first) & (pos + offset >= first)
    return (pos >= first) & (pos + offset < first)


WIDTH = 4
STEP = 16


def front3_kernel(tile, n, share, scal, mid_ref, taps, h1_ref, g4, p0, p1, p2, p3, *refs):
    spread_ref, h2_ref, y4_ref = refs[:3]
    outs = refs[3 : 3 + n]
    qkv_w, point, win, qkv_s = refs[3 + n :]
    i = pl.program_id(0)

    @pl.when(i == 0)
    def _():
        unpack(scal[2], 1, (p0, p1, p2, p3), {"qkv": qkv_w, "point": point})

    s, first = scal[0], scal[1]
    begin = s * (mid_ref.shape[0] - 2 * RIM) + i * tile
    near = (first > begin - HALF) & (first < begin + tile + HALF)

    def chunk(c, carry):
        around = pl.ds(pl.multiple_of(i * tile, 16), tile + 2 * RIM)
        lanes = [pl.ds(pl.multiple_of((c * WIDTH + w) * LANES, LANES), LANES) for w in range(WIDTH)]
        for w in range(WIDTH):
            win[w] = mid_ref[around, lanes[w]].astype(F32)
        for masked in (False, True):

            @pl.when(near if masked else jnp.logical_not(near))
            def _():
                for w in range(WIDTH):
                    tap = [taps[k : k + 1, lanes[w]] for k in range(KERNEL)]
                    for r in range(0, tile, STEP):
                        pos = places(begin + r, STEP)
                        total = None
                        for k in range(KERNEL):
                            o = k - HALF
                            v = win[w, RIM + o + r : RIM + o + r + STEP, :]
                            if masked and o != 0:
                                v = jnp.where(crosses(pos, o, first), 0.0, v)
                            total = v * tap[k] if total is None else total + v * tap[k]
                        spread_ref[r : r + STEP, lanes[w]] = total.astype(BF)

        return carry

    lax.fori_loop(0, FF // (WIDTH * LANES), chunk, 0)
    h1 = h1_ref[rows_at(i, tile, RIM), :]
    branch = nn(spread_ref[...], point[...])
    h2 = jnp.concatenate([h1[:, :NARROW] + branch, h1[:, NARROW:]], axis=1)
    h2_ref[...] = h2
    hat, _ = normalise(h2)
    y4 = (hat * g4[...]).astype(BF)
    y4_ref[...] = y4
    qkv_s[...] = nn(y4, qkv_w[...]).astype(BF)
    for k in range(n):
        block = (s ^ k) // share
        for part in range(3):
            outs[k][:, part * LANES : (part + 1) * LANES] = qkv_s[
                :, pl.ds(pl.multiple_of(part * D + block * LANES, LANES), LANES)
            ]


def front3(scal, mid, taps, h1, g4, pieces, n, share, ties=()):
    rows = mid.shape[0] - 2 * RIM
    tile = 256
    return call(
        functools.partial(front3_kernel, tile, n, share),
        [(scal, "s")] + [(a, None) for a in (mid, taps, h1, g4, *pieces)],
        [((rows, FF), BF, tile), ((rows, D), F32, tile), ((rows, D), BF, tile)]
        + [((rows, 3 * LANES), BF, tile)] * n
        + [(shape, BF, None) for shape in SHAPES[1].values()],
        scratch=[((WIDTH, tile + 2 * RIM, LANES), F32), ((tile, 3 * D), BF)],
        micros=20,
        ties=ties,
        steps=rows // tile,
    )


def gather_lanes(wide_ref, n, share, s, blocks, parts):
    rows = wide_ref.shape[0]
    for k in range(n):
        block = (s ^ k) // share
        for part in range(parts):
            lanes = pl.ds(pl.multiple_of(part * D + block * LANES, LANES), LANES)
            new = blocks[k][:, part * LANES : (part + 1) * LANES]
            if share > 1:
                lane = lax.broadcasted_iota(jnp.int32, (rows, LANES), 1)
                mine = lane // (LANES // share) == (s ^ k) % share
                new = jnp.where(mine, new.astype(F32), wide_ref[:, lanes].astype(F32)).astype(BF)
            wide_ref[:, lanes] = new


def middle_kernel(n, share, scal, h2_ref, *refs):
    att = refs[:n]
    cot_ref, g5, p0, p1, p2, p3, mixed_ref, dh3_ref = refs[n : n + 8]
    datt = refs[n + 8 : 2 * n + 8]
    att_s, y5_s, inner_s, du_s, ln_out = refs[2 * n + 8 : 2 * n + 13]
    wa, wup, wdown, ln_ref = refs[2 * n + 13 :]
    s = scal[0]
    i = pl.program_id(0)

    @pl.when(i == 0)
    def _():
        unpack(scal[2], 2, (p0, p1, p2, p3), {"attn": wa, "up": wup, "down": wdown})
        ln_ref[...] = jnp.zeros_like(ln_ref)

    gather_lanes(att_s, n, share, s, att, 1)
    h3 = h2_ref[...] + nn(att_s[...], wa[...])
    hat, r = normalise(h3)
    y5 = (hat * g5[...]).astype(BF)
    y5_s[...] = y5
    value, slope = gelu_and_slope(nn(y5, wup[...]))
    inner = value.astype(BF)
    inner_s[...] = inner
    mixed_ref[...] = (h3 + nn(inner, wdown[...])).astype(BF)
    cot = cot_ref[...]
    du = (nt(cot, wdown[...]) * slope).astype(BF)
    du_s[...] = du
    dy5 = nt(du, wup[...])
    ln_ref[...] += fold8(dy5 * hat)
    dh3 = cot.astype(F32) + norm_back(dy5, hat, r, g5[...])
    dh3_ref[...] = dh3
    da = nt(dh3.astype(BF), wa[...]).astype(BF)
    for j in range(D // LANES):
        for k in range(n):

            @pl.when((s ^ k) // share == j)
            def _():
                datt[k][...] = da[:, j * LANES : (j + 1) * LANES]

    ln_out[...] = jnp.sum(ln_ref[...], axis=0, keepdims=True)


def middle(scal, h2, att, cot, g5, pieces, n, share, ties=()):
    rows = h2.shape[0]
    tile = 384
    return call(
        functools.partial(middle_kernel, n, share),
        [(scal, "s"), (h2, tile)]
        + [(a, tile) for a in (*att, cot)]
        + [(a, None) for a in (g5, *pieces)],
        [((rows, D), BF, tile), ((rows, D), F32, tile)]
        + [((rows, LANES), BF, tile)] * n
        + [((rows, c), BF, tile) for c in (D, D, FF, FF)]
        + [((1, D), F32, None)],
        scratch=[((D, D), BF), ((D, FF), BF), ((FF, D), BF), ((8, D), F32)],
        micros=20,
        ties=ties,
        steps=rows // tile,
    )


def weigh0_kernel(scal, att_s, y5_s, inner_s, du_s, cot_ref, dh3_ref, kept, given, grads):
    me = scal[2]
    att_t = att_s[...].T
    for j in range(D // PACK):
        part = nn(att_t, dh3_ref[:, j * PACK : (j + 1) * PACK].astype(BF))
        put(me, 0, grads, ("attn", j), part.astype(BF))
    y5_t = y5_s[...].T
    for j in range(FF // PACK):
        cols = slice(j * PACK, (j + 1) * PACK)
        put(me, 0, grads, ("up", j), nn(y5_t, du_s[:, cols]).astype(BF))
        down = tn(inner_s[:, cols], cot_ref[...]).astype(BF)
        for m in range(D // PACK):
            put(me, 0, grads, ("down", m), down[:, m * PACK : (m + 1) * PACK], j * PACK // 64)
    part_slots(grads, kept, given)


def weigh0(scal, att, y5, inner, du, cot, dh3, ties=()):
    return whole_call(
        weigh0_kernel,
        group_grads(0),
        [scal, att, y5, inner, du, cot, dh3],
        scratch=[group_slots(0)],
        micros=10,
        ties=ties,
    )


def back3_kernel(n, share, scal, *refs):
    blocks = refs[:n]
    dh3_ref, h2_ref, g4, qkv_w = refs[n : n + 4]
    dh2_ref, db_ref, dqkv_s, ln_out, ln_ref = refs[n + 4 :]

    @pl.when(pl.program_id(0) == 0)
    def _():
        ln_ref[...] = jnp.zeros_like(ln_ref)

    gather_lanes(dqkv_s, n, share, scal[0], blocks, 3)
    dy4 = nt(dqkv_s[...], qkv_w[...])
    hat, r = normalise(h2_ref[...])
    ln_ref[...] += fold8(dy4 * hat)
    dh2 = dh3_ref[...] + norm_back(dy4, hat, r, g4[...])
    dh2_ref[...] = dh2
    db_ref[...] = dh2[:, :NARROW].astype(BF)
    ln_out[...] = jnp.sum(ln_ref[...], axis=0, keepdims=True)


def back3(scal, blocks, dh3, h2, g4, qkv_w, n, share, ties=()):
    rows = h2.shape[0]
    tile = 384
    return call(
        functools.partial(back3_kernel, n, share),
        [(scal, "s")] + [(a, tile) for a in (*blocks, dh3, h2)] + [(g4, None), (qkv_w, None)],
        [((rows, D), F32, tile), ((rows, NARROW), BF, tile), ((rows, 3 * D), BF, tile)]
        + [((1, D), F32, None)],
        scratch=[((8, D), F32)],
        micros=6,
        ties=ties,
        steps=rows // tile,
    )


def weigh1_kernel(scal, y4_ref, dqkv_s, spread_ref, db_ref, kept, given, grads):
    me = scal[2]
    y4_t = y4_ref[...].T
    for j in range(3 * D // PACK):
        part = nn(y4_t, dqkv_s[:, j * PACK : (j + 1) * PACK])
        put(me, 1, grads, ("qkv", j), part.astype(BF))
    for j in range(FF // PACK):
        part = tn(spread_ref[:, j * PACK : (j + 1) * PACK], db_ref[...]).astype(BF)
        put(me, 1, grads, ("point", 0), part, j * PACK // 64)
    part_slots(grads, kept, given)


def weigh1(scal, y4, dqkv, spread, db, ties=()):
    return whole_call(
        weigh1_kernel,
        group_grads(1),
        [scal, y4, dqkv, spread, db],
        scratch=[group_slots(1)],
        micros=3,
        ties=ties,
    )


def back2_kernel(tile, group, scal, low_ref, db_ref, high_ref, *refs):
    taps, mid_ref, left_ref, right_ref, g3, point = refs[:6]
    dl, st, gdepth_out, ln_out = refs[6:10]
    dbx, dsp, win, dmid, dr, gdepth_ref, ln_ref = refs[10:]
    rows = db_ref.shape[0]
    ext = rows + 2 * RIM
    base = scal[0] * rows - RIM
    first = scal[1]
    i = pl.program_id(0)
    last = ext // tile - 1

    @pl.when(i == 0)
    def _():
        dbx[0:RIM, :] = low_ref[...]
        dbx[RIM : RIM + rows, :] = db_ref[...]
        dbx[RIM + rows :, :] = high_ref[...]
        dsp[0:RIM, :] = jnp.zeros((RIM, FF), F32)
        dsp[RIM + ext :, :] = jnp.zeros((RIM, FF), F32)
        dr[0:RIM, :] = jnp.zeros((RIM, NARROW), F32)
        dr[RIM + ext :, :] = jnp.zeros((RIM, NARROW), F32)
        gdepth_ref[...] = jnp.zeros_like(gdepth_ref)
        ln_ref[...] = jnp.zeros_like(ln_ref)

        def spread_step(j, carry):
            dsp[rows_at(j, tile, RIM), :] = nt(dbx[rows_at(j, tile), :], point[...])
            return carry

        lax.fori_loop(0, ext // tile, spread_step, 0)

    begin = base + i * tile
    near = (first > begin - HALF) & (first < begin + tile + HALF)
    near = near | (i == 0) | (i == last)

    def chunk(c, carry):
        around = pl.ds(pl.multiple_of(i * tile, 16), tile + 2 * RIM)
        lanes = [pl.ds(pl.multiple_of((c * WIDTH + w) * LANES, LANES), LANES) for w in range(WIDTH)]
        for w in range(WIDTH):
            win[w] = dsp[around, lanes[w]]
        for masked in (False, True):

            @pl.when(near if masked else jnp.logical_not(near))
            def _():
                for w in range(WIDTH):
                    tap = [taps[k : k + 1, lanes[w]] for k in range(KERNEL)]
                    pairs = [None] * KERNEL
                    for r in range(0, tile, STEP):
                        pos = places(begin + r, STEP)
                        local = i * tile + r + iota((STEP, LANES), 0)
                        mid = mid_ref[r : r + STEP, lanes[w]].astype(F32)
                        total = None
                        for k in range(KERNEL):
                            o = HALF - k
                            v = win[w, RIM + o + r : RIM + o + r + STEP, :]
                            if masked and o != 0:
                                v = jnp.where(crosses(pos, o, first), 0.0, v)
                            counted = v
                            if masked:
                                kept = (local + o >= RIM) & (local + o < RIM + rows)
                                counted = jnp.where(kept, v, 0.0)
                            counted = counted * mid
                            counted = counted[:8] + counted[8:]
                            pairs[k] = counted if pairs[k] is None else pairs[k] + counted
                            total = v * tap[k] if total is None else total + v * tap[k]
                        dmid[r : r + STEP, lanes[w]] = total
                    for k in range(KERNEL):
                        gdepth_ref[k * 8 : (k + 1) * 8, lanes[w]] += pairs[k]

        return carry

    lax.fori_loop(0, FF // (WIDTH * LANES), chunk, 0)
    for q in range(0, tile, STEP):
        at = slice(q, q + STEP)
        left, slope = gelu_and_slope(left_ref[at, :])
        right, slope_r = gelu_and_slope(right_ref[at, :])
        joined = jnp.concatenate([left[:, :NARROW] + right, left[:, NARROW:]], axis=1)
        hat, r = normalise(joined)
        local = i * tile + q + iota((STEP, 1), 0)
        own = ((local >= RIM) & (local < RIM + rows)).astype(F32)
        pos = base + local
        grad = dmid[at, :] * ((pos >= 0) & (pos < group)).astype(F32)
        ln_ref[...] += fold8(grad * hat * own)
        dj = norm_back(grad, hat, r, g3[...])
        dl[at, :] = (dj * slope).astype(BF)
        dr[rows_at(i, tile, RIM + q, STEP), :] = (dj[:, :NARROW] * slope_r).astype(BF).astype(F32)

    @pl.when(i == last)
    def _():
        for k in range(KERNEL):
            gdepth_out[k : k + 1, :] = jnp.sum(
                gdepth_ref[k * 8 : (k + 1) * 8, :], axis=0, keepdims=True
            )
        ln_out[...] = jnp.sum(ln_ref[...], axis=0, keepdims=True)
        part = 128

        def gather_step(j, carry):
            at = rows_at(j, part)
            around = pl.ds(pl.multiple_of(RIM + j * part, 16), part + 2 * RIM)
            pos = places(base + RIM + j * part, part, NARROW)
            v = dr[around, :]
            after = pltpu.roll(v, part + 2 * RIM - 1, 0)[RIM : RIM + part]
            before = pltpu.roll(v, 1, 0)[RIM : RIM + part]
            after = jnp.where((pos + 1 == first) | (pos + 1 == group), 0.0, after)
            before = jnp.where((pos == first) | (pos == 0), 0.0, before)
            st[at, 0:NARROW] = after.astype(BF)
            st[at, NARROW : 2 * NARROW] = v[RIM : RIM + part].astype(BF)
            st[at, 2 * NARROW :] = before.astype(BF)
            return carry

        lax.fori_loop(0, rows // part, gather_step, 0)


def back2(scal, low, db, high, taps, mid, left, right, g3, point, group, ties=()):
    rows = db.shape[0]
    ext = rows + 2 * RIM
    tile = 80
    return call(
        functools.partial(back2_kernel, tile, group),
        [(scal, "s")]
        + [(a, None) for a in (low, db, high, taps)]
        + [(a, tile) for a in (mid, left, right)]
        + [(g3, None), (point, None)],
        [((ext, FF), BF, tile), ((rows, 3 * NARROW), BF, None)]
        + [((KERNEL, FF), F32, None), ((1, FF), F32, None)],
        scratch=[
            ((ext, NARROW), BF),
            ((ext + 2 * RIM, FF), F32),
            ((WIDTH, tile + 2 * RIM, LANES), F32),
            ((tile, FF), F32),
            ((ext + 2 * RIM, NARROW), F32),
            ((8 * KERNEL, FF), F32),
            ((8, FF), F32),
        ],
        micros=44,
        ties=ties,
        steps=ext // tile,
    )


def back1_kernel(scal, dl, st, dh2_ref, h1_ref, joined_ref, x_ref, g1, g2, *refs):
    glu, wide, narrow, dx_ref, y1_ref, dj_ref, ln1_out, ln2_out, ln1_ref, ln2_ref = refs
    i = pl.program_id(0)

    @pl.when(i == 0)
    def _():
        ln1_ref[...] = jnp.zeros_like(ln1_ref)
        ln2_ref[...] = jnp.zeros_like(ln2_ref)

    dy2 = nt(dl[...], wide[...])
    for k in range(3):
        dy2 = dy2 + nt(st[:, k * NARROW : (k + 1) * NARROW], narrow[k * D : (k + 1) * D, :])
    hat2, r2 = normalise(h1_ref[...])
    ln2_ref[...] += fold8(dy2 * hat2)
    dh1 = dh2_ref[...] + norm_back(dy2, hat2, r2, g2[...])
    gate = sigmoid(joined_ref[:, D:])
    value = joined_ref[:, :D]
    dj_ref[:, :D] = (dh1 * gate).astype(BF)
    dj_ref[:, D:] = (dh1 * value * gate * (1.0 - gate)).astype(BF)
    x = x_ref[...].astype(F32)
    hat1, r1 = normalise(x)
    y1_ref[...] = (hat1 * g1[...]).astype(BF)
    dy1 = nt(dj_ref[...], glu[...])
    ln1_ref[...] += fold8(dy1 * hat1)
    dx_ref[...] = (dh1 + norm_back(dy1, hat1, r1, g1[...])).astype(dx_ref.dtype)
    ln1_out[...] = jnp.sum(ln1_ref[...], axis=0, keepdims=True)
    ln2_out[...] = jnp.sum(ln2_ref[...], axis=0, keepdims=True)


def back1(scal, dl, st, dh2, h1, joined, x, g1, g2, glu, wide, narrow, start, rows):
    tile = 384
    own, ext = (tile, start), (tile, start + RIM)
    return call(
        back1_kernel,
        [(scal, "s"), (dl, ext), (st, own), (dh2, own), (h1, ext), (joined, ext), (x, ext)]
        + [(a, None) for a in (g1, g2, glu, wide, narrow)],
        [((rows, D), BF, tile), ((rows, D), BF, tile), ((rows, 2 * D), BF, tile)]
        + [((1, D), F32, None)] * 2,
        scratch=[((8, D), F32), ((8, D), F32)],
        micros=5,
        steps=rows // tile,
    )


def weigh2_kernel(scal, dl, st, y2_ref, kept, given, grads, gn):
    me = scal[2]
    rows = st.shape[0]
    y2_t = y2_ref[RIM : RIM + rows, :].T
    for j in range(FF // PACK):
        part = nn(y2_t, dl[RIM : RIM + rows, j * PACK : (j + 1) * PACK]).astype(BF)
        put(me, 2, grads, ("wide", j), part)
    for k in range(3):
        gn[k * D : (k + 1) * D, :] = nn(y2_t, st[:, k * NARROW : (k + 1) * NARROW]).astype(BF)
    put(me, 2, grads, ("narrow", 0), gn[...])
    part_slots(grads, kept, given)


def weigh2(scal, dl, st, y2):
    return whole_call(
        weigh2_kernel,
        group_grads(2),
        [scal, dl, st, y2],
        scratch=[group_slots(2), ((3 * D, NARROW), BF)],
        micros=3,
    )


def weigh3_kernel(halves, scal, *refs):
    y1, dj, ln1, ln2 = (refs[i * halves : (i + 1) * halves] for i in range(4))
    gains, taps, kept, given = refs[4 * halves : 4 * halves + 3], *refs[4 * halves + 3 : 4 * halves + 6]
    grads, table, block, ln1_s, ln2_s = refs[4 * halves + 6 :]
    me = scal[2]
    for total, parts in ((ln1_s, ln1), (ln2_s, ln2)):
        total[...] = sum(p[...] for p in parts[1:]) + parts[0][...]
    write_small(me, (ln1_s, ln2_s, *gains), taps, table, block, grads)
    turned = [y[...].T for y in y1]
    for j in range(2 * D // PACK):
        part = None
        for y, d in zip(turned, dj):
            more = nn(y, d[:, j * PACK : (j + 1) * PACK])
            part = more if part is None else part + more
        put(me, 3, grads, ("glu", j), part.astype(BF))
    part_slots(grads, kept, given)


def weigh3(scal, y1, dj, ln1, ln2, gains, taps):
    return whole_call(
        functools.partial(weigh3_kernel, len(y1)),
        group_grads(3),
        [scal, *y1, *dj, *ln1, *ln2, *gains, taps],
        scratch=[group_slots(3), ((BLOCKS, SMALL_ROWS * PACK), F32), ((BLOCKS, 16, PACK), F32)]
        + [((1, D), F32)] * 2,
        micros=0,
    )


def lane_maps(rows, head):
    lane = lax.broadcasted_iota(jnp.int32,(rows,LANES),1)
    own = (lane >= head*HEAD) & (lane < (head+1)*HEAD)
    rel = lane - (1-head)*HEAD
    return own, rel

def id_column(base, rows, first):
    pos = base + lax.broadcasted_iota(jnp.int32,(rows,LANES),0)
    return pos >= first

def split3(v):
    hi = v.astype(BF).astype(F32)
    mid = (v-hi).astype(BF).astype(F32)
    return hi, mid, v-hi-mid

def tile_ids(start, rows, first):
    return start < first, start+rows > first

def overlap(a_start,a_rows,b_start,b_rows,first):
    a0,a1 = tile_ids(a_start,a_rows,first); b0,b1=tile_ids(b_start,b_rows,first)
    return (a0&b0)|(a1&b1)

def attend_kernel(n, heads, share, tq, tk, scal, *refs):
    qkv = refs[:n]; att = refs[n:2*n]; lse_ref = refs[2*n]
    qa, ka, va, mx_ref, m_ref, q2_ref, acc_ref = refs[2*n+1:]
    s = scal[0]; first = scal[1]
    rows = qkv[0].shape[0]
    for k in range(n):
        base = (s ^ k)*rows
        id1 = id_column(base, rows, first).astype(F32)
        q = qkv[k][:, 0:LANES].astype(F32)*(HEAD**-0.5)
        key = qkv[k][:, LANES:2*LANES].astype(F32)
        v = qkv[k][:, 2*LANES:3*LANES].astype(F32)
        for i in range(heads):
            h = i if share==1 else s % share
            own, rel = lane_maps(rows, h)
            qx = jnp.where(rel==0, 1.0-id1, jnp.where(rel==1, id1, 0.0))
            kx = jnp.where(rel==0, id1*BIG, jnp.where(rel==1, (1.0-id1)*BIG, jnp.where(rel<5,1.0,0.0)))
            qa[i, k*rows:(k+1)*rows,:] = jnp.where(own, q, qx).astype(BF)
            ka[i, k*rows:(k+1)*rows,:] = jnp.where(own, key, kx).astype(BF)
            va[i, k*rows:(k+1)*rows,:] = jnp.where(own, v, 1.0).astype(BF)
    per = rows//tq; per_k = rows//tk
    def fold(sc, best):
        for j in range(tk//LANES):
            best = jnp.maximum(best, sc[:, j*LANES:(j+1)*LANES])
        return best
    def q_step(it, carry):
        kq = it//per
        r0 = pl.multiple_of((it % per)*tq, tq)
        g0 = pl.multiple_of(it*tq, tq)
        own0 = pl.multiple_of((g0//tk)*tk, tk)
        q_start = (s ^ kq)*rows + r0
        for i in range(heads):
            for j in range(max(1,tq//tk)):
                sc = nt(qa[i, pl.ds(g0,tq),:], ka[i, pl.ds(own0+j*tk,tk),:])
                best = fold(sc, sc[:, :LANES] if j==0 else best)
            mx_ref[i] = best
            m_ref[i] = jnp.zeros((tq,LANES),F32)
        def attempt(again):
            for i in range(heads):
                h = i if share==1 else s % share
                own, rel = lane_maps(tq, h)
                m = jnp.max(mx_ref[i], axis=1, keepdims=True)
                mb = m_ref[i] + jnp.broadcast_to(m, (tq,LANES))
                m_ref[i] = mb
                hi,mid,lo = split3(-mb)
                q = qa[i, pl.ds(g0,tq),:].astype(F32)
                q2_ref[i] = jnp.where(rel==2,hi,jnp.where(rel==3,mid,jnp.where(rel==4,lo,q))).astype(BF)
            mx_ref[...] = jnp.full_like(mx_ref, -3e38)
            acc_ref[...] = jnp.zeros_like(acc_ref)
            for kt in range(n*per_k):
                k_start = (s ^ (kt//per_k))*rows + (kt%per_k)*tk
                @pl.when(overlap(q_start,tq,k_start,tk,first))
                def _():
                    for i in range(heads):
                        sc = nt(q2_ref[i], ka[i, kt*tk:(kt+1)*tk,:])
                        mx_ref[i] = fold(sc, mx_ref[i])
                        p = jnp.exp2(sc*LOG2E).astype(BF)
                        acc_ref[i] += nn(p, va[i, kt*tk:(kt+1)*tk,:])
            return (jnp.max(mx_ref[...]) > 40.0).astype(jnp.int32)
        lax.while_loop(lambda again: again > 0, attempt, jnp.int32(1))
        out = jnp.zeros((tq,LANES),F32); lse = jnp.zeros((tq,LANES),F32)
        for i in range(heads):
            h = i if share==1 else s % share
            own,_ = lane_maps(tq,h)
            acc = acc_ref[i]
            total = pltpu.roll(acc, HEAD, 1)
            out = jnp.where(own, acc/total, out)
            lse = jnp.where(own, m_ref[i]+jnp.log(total), lse)
        lse_ref[pl.ds(g0,tq),:] = lse
        for k in range(n):
            @pl.when(kq==k)
            def _():
                att[k][pl.ds(r0,tq),:] = out.astype(BF)
        return carry
    lax.fori_loop(0, n*per, q_step, 0)

def attend(scal, blocks, n, share, tq=768, tk=768, ties=()):
    rows = blocks[0].shape[0]
    heads = 2 // share
    return whole_call(
        functools.partial(attend_kernel, n, heads, share, tq, tk),
        [((rows, LANES), BF)] * n + [((n * rows, LANES), F32)],
        [scal, *blocks],
        scratch=[((heads, n * rows, LANES), BF)] * 3
        + [((heads, tq, LANES), F32)] * 2
        + [((heads, tq, LANES), BF), ((heads, tq, LANES), F32)],
        ties=ties,
        micros=36,
    )


def attend_back_kernel(n, heads, share, tq, tk, scal, *refs):
    qkv = refs[:n]; att = refs[n:2*n]; dat = refs[2*n:3*n]; lse_ref = refs[3*n]
    out = refs[3*n+1:4*n+1]
    qa, ka, va, da, dq_ref, dk_ref, dv_ref = refs[4*n+1:]
    s = scal[0]; first = scal[1]
    rows = qkv[0].shape[0]
    for k in range(n):
        base = (s ^ k)*rows
        sl = slice(k*rows,(k+1)*rows)
        id1 = id_column(base, rows, first).astype(F32)
        q = qkv[k][:, 0:LANES].astype(F32)*(HEAD**-0.5)
        key = qkv[k][:, LANES:2*LANES].astype(F32)
        v = qkv[k][:, 2*LANES:3*LANES].astype(F32)
        do = dat[k][...].astype(F32)
        prod = do*att[k][...].astype(F32)
        for i in range(heads):
            h = i if share==1 else s % share
            own, rel = lane_maps(rows, h)
            lse = pltpu.roll(lse_ref[sl,:], HEAD, 1)
            hi,mid,lo = split3(-lse)
            delta = jnp.sum(jnp.where(own,prod,0.0),axis=1,keepdims=True)
            dhi,dmid,dlo = split3(-delta)
            qx = jnp.where(rel==0, 1.0-id1, jnp.where(rel==1, id1, jnp.where(rel==2,hi,jnp.where(rel==3,mid,jnp.where(rel==4,lo,0.0)))))
            kx = jnp.where(rel==0, id1*BIG, jnp.where(rel==1, (1.0-id1)*BIG, jnp.where(rel<5,1.0,0.0)))
            vx = jnp.where(rel<3,1.0,0.0)
            dx = jnp.where(rel==0,dhi,jnp.where(rel==1,dmid,jnp.where(rel==2,dlo,0.0)))
            qa[i,sl,:] = jnp.where(own,q,qx).astype(BF)
            ka[i,sl,:] = jnp.where(own,key,kx).astype(BF)
            va[i,sl,:] = jnp.where(own,v,vx).astype(BF)
            da[i,sl,:] = jnp.where(own,do,dx).astype(BF)
    dq_ref[...] = jnp.zeros_like(dq_ref)
    per_q = rows//tq; per_k = rows//tk
    def k_step(kt, carry):
        k0 = pl.multiple_of(kt*tk, tk)
        kk = kt//per_k
        k_start = (s ^ kk)*rows + (kt % per_k)*tk
        for i in range(heads):
            dk_ref[i] = jnp.zeros((tk,LANES),F32)
            dv_ref[i] = jnp.zeros((tk,LANES),F32)
        def q_step(qt, c2):
            q0 = pl.multiple_of(qt*tq, tq)
            q_start = (s ^ (qt//per_q))*rows + (qt % per_q)*tq
            @pl.when(overlap(q_start,tq,k_start,tk,first))
            def _():
                for i in range(heads):
                    qq = qa[i,pl.ds(q0,tq),:]; kx = ka[i,pl.ds(k0,tk),:]; dd = da[i,pl.ds(q0,tq),:]
                    st = nt(kx, qq)
                    p = jnp.exp2(st*LOG2E)
                    dp = nt(va[i,pl.ds(k0,tk),:], dd)
                    ds = (p*dp).astype(BF)
                    dv_ref[i] += nn(p.astype(BF), dd)
                    dk_ref[i] += nn(ds, qq)
                    dq_ref[i,pl.ds(q0,tq),:] += tn(ds, kx)
            return c2
        lax.fori_loop(0, n*per_q, q_step, 0)
        dk = jnp.zeros((tk,LANES),F32); dv = jnp.zeros((tk,LANES),F32)
        for i in range(heads):
            h = i if share==1 else s % share
            own,_ = lane_maps(tk,h)
            dk = jnp.where(own, dk_ref[i], dk); dv = jnp.where(own, dv_ref[i], dv)
        r0 = pl.multiple_of((kt % per_k)*tk, tk)
        for k in range(n):
            @pl.when(kk==k)
            def _():
                out[k][pl.ds(r0,tk),LANES:2*LANES] = dk.astype(BF)
                out[k][pl.ds(r0,tk),2*LANES:3*LANES] = dv.astype(BF)
        return carry
    lax.fori_loop(0, n*per_k, k_step, 0)
    for k in range(n):
        sl = slice(k*rows,(k+1)*rows)
        dq = jnp.zeros((rows,LANES),F32)
        for i in range(heads):
            h = i if share==1 else s % share
            own,_ = lane_maps(rows,h)
            dq = jnp.where(own, dq_ref[i,sl,:], dq)
        out[k][:, 0:LANES] = (dq*(HEAD**-0.5)).astype(BF)

def attend_back(scal, blocks, att, datt, lse, n, share, tq=384, tk=384, ties=()):
    rows = blocks[0].shape[0]
    heads = 2 // share
    return whole_call(
        functools.partial(attend_back_kernel, n, heads, share, tq, tk),
        [((rows, 3 * LANES), BF)] * n,
        [scal, *blocks, *att, *datt, lse],
        scratch=[((heads, n * rows, LANES), BF)] * 4
        + [((heads, n * rows, LANES), F32)]
        + [((heads, tk, LANES), F32)] * 2,
        ties=ties,
        micros=58,
    )


class Links:
    def __init__(self, n_seq, n_dp):
        self.count = n_seq * n_dp
        self.direct = (n_seq, n_dp) == (4, 8)

    def flip(self, value, mask):
        return lax.ppermute(value, AXES, [(i, i ^ mask) for i in range(self.count)])

    def near(self, block):
        return jnp.stack([block] + [self.flip(block, k << 3) for k in range(1, 4)])

    def part(self, group, held):
        low = height(GATHERS[group][0])
        return [held[:, :low], held[:, low:]]

    def spread(self, held, stage):
        masks = ((4, 2), (2, 4))[stage]
        return [jnp.concatenate([h, self.flip(h, m)]) for h, m in zip(held, masks)]

    def across(self, held):
        return [held[0], self.flip(held[0], 1), held[1], self.flip(held[1], 1)]

    def gather_whole(self, group, weights):
        whole = {
            name: lax.all_gather(weights[name], AXES, axis=0, tiled=True)
            for name in dict(sum(GATHERS[group], []))
        }
        pieces = []
        for half, items in enumerate(GATHERS[group]):
            blocks = [
                whole[name][:, j * PACK : (j + 1) * PACK].reshape(BLOCKS, -1, PACK)
                for name, j in items
            ]
            pieces += list(self.by_slot(jnp.concatenate(blocks, axis=1), half))
        return pieces

    def by_slot(self, blocks, half):
        shape = blocks.shape[1:]
        order = ((3, 2, 1, 0), (3, 1, 2, 0))[half]
        return blocks.reshape(4, 2, 2, 2, *shape).transpose(*order, 4, 5).reshape(2, 16, *shape)

    def by_owner(self, slots, half):
        shape = slots.shape[1:]
        order = ((3, 2, 1, 0), (3, 1, 2, 0))[half]
        return slots.reshape(2, 2, 2, 4, *shape).transpose(*order, 4, 5).reshape(BLOCKS, *shape)

    def add(self, a, b):
        return (a.astype(F32) + b.astype(F32)).astype(BF)

    def fold(self, slots, mask):
        middle = slots.shape[0] // 2
        return self.add(slots[:middle], self.flip(slots[middle:], mask))

    def cores(self, kept, given):
        return self.add(kept, self.flip(given, 1))

    def first(self, group, kept, given):
        held = self.cores(kept, given)
        low = height(SUMS[group][0])
        return [held[:, :low], held[:, low:]]

    def straight(self, held, stage):
        return self.fold(held, (2, 4)[stage])

    def flips(self, values, mask):
        flat = self.flip(jnp.concatenate([v.reshape(-1, PACK) for v in values], axis=0), mask)
        result, at = [], 0
        for v in values:
            count = v.size // PACK
            result.append(flat[at : at + count].reshape(v.shape))
            at += count
        return result

    def next_two(self, late, early):
        a, b = (v.shape[0] // 2 for v in late)
        c, d = (v.shape[0] // 2 for v in early)
        got_y = self.flips([late[0][a:], early[1][d:]], 4)
        got_x = self.flips([late[1][b:], early[0][c:]], 2)
        late = [self.add(late[0][:a], got_y[0]), self.add(late[1][:b], got_x[0])]
        early = [self.add(early[0][:c], got_x[1]), self.add(early[1][:d], got_y[1])]
        return late, early

    def next_and_plane(self, late, held):
        a, b = (v.shape[0] // 2 for v in late)
        got_y = self.flips([late[0][a:], held[4:8]], 4)
        got_x = self.flips([late[1][b:], held[8:12]], 2)
        total = held[:4].astype(F32) + got_y[1].astype(F32) + got_x[1].astype(F32)
        total = total + self.flip(held[12:], 6).astype(F32)
        late = [self.add(late[0][:a], got_y[0]), self.add(late[1][:b], got_x[0])]
        return late, total.astype(BF)

    def next(self, held, stage):
        masks = ((2, 4), (4, 2))[stage]
        return [self.fold(h, m) for h, m in zip(held, masks)]

    def finish(self, held):
        held = jnp.concatenate(held, axis=1)
        total = held[0].astype(F32)
        for k in range(1, 4):
            total = total + self.flip(held[k], k << 3).astype(F32)
        return total

    def rows_of(self, items, total):
        parts, at = {}, 0
        for name, j in items:
            b = ROWS[name] * BLOCKS // self.count
            parts.setdefault(name, []).append(total[at : at + b])
            at += b
        return {name: jnp.concatenate(p, axis=1) for name, p in parts.items()}

    def scatter_whole(self, group, parts):
        slots = jnp.concatenate(parts)
        sent, at = [], 0
        for half, items in enumerate(SUMS[group]):
            for name, _ in items:
                blocks = self.by_owner(slots[:, at : at + ROWS[name]], half if group in SPLIT else 0)
                sent.append(blocks.reshape(self.count, -1, PACK))
                at += ROWS[name]
        sent = jnp.concatenate(sent, axis=1)
        return lax.psum_scatter(sent, AXES, scatter_dimension=0, tiled=False).astype(F32)


class Layout:
    def __init__(self, n_seq, n_dp):
        self.n_seq, self.n_dp = n_seq, n_dp
        self.where = {}
        for g in range(n_dp):
            for s in range(n_seq):
                self.where[g, s] = self.place(g, s)
        self.block = np.zeros(n_seq * n_dp, np.int32)
        for (g, s), device in self.where.items():
            self.block[device] = s

    def place(self, g, s):
        if (self.n_seq, self.n_dp) == (4, 8):
            y, x, c = g >> 2, g >> 1 & 1, g & 1
            return (2 * c + y) * 8 + (s & 1) * 4 + x * 2 + (s >> 1)
        return s * self.n_dp + g

    def pairs(self, source, target):
        return [
            (source(g, s), target(g, s))
            for g in range(self.n_dp)
            for s in range(self.n_seq)
            if target(g, s) is not None and source(g, s) is not None
        ]

    def at(self, g, s):
        return self.where.get((g, s))

    def home(self, g, s):
        return s * self.n_dp + g

    def bring(self, value):
        return lax.ppermute(value, AXES, self.pairs(self.home, self.at))

    def bring_to(self, value, step):
        return lax.ppermute(
            value, AXES, self.pairs(self.home, lambda g, s: self.at(g, s + step))
        )

    def send_home(self, value):
        return lax.ppermute(value, AXES, self.pairs(self.at, self.home))

    def to_neighbour(self, value, step):
        return lax.ppermute(value, AXES, self.pairs(self.at, lambda g, s: self.at(g, s + step)))

    def swap(self, values):
        return [values[0]] + [
            lax.ppermute(values[k], AXES, self.pairs(self.at, lambda g, s: self.at(g, s ^ k)))
            for k in range(1, self.n_seq)
        ]


NAMES = ("ln1", "ln2", "ln3", "ln4", "ln5", "glu", "wide", "narrow", "depth", "point", "qkv", "attn", "up", "down")
SMALL = ("ln1", "ln2", "ln3", "ln4", "ln5", "depth")


def sync(*values):
    return lax.optimization_barrier(values)


def small_block(arrays, blocks):
    flat = jnp.concatenate([a.reshape(blocks, -1) for a in arrays], axis=1)
    flat = jnp.pad(flat, ((0, 0), (0, 16 * PACK - flat.shape[1])))
    return flat.reshape(blocks * 16, PACK)


def on_device(tokens, cotangent, first_length, *weights):
    n = lax.axis_size("seq")
    n_dp = lax.axis_size("dp")
    share = n * LANES // D
    layout = Layout(n, n_dp)
    links = Links(n, n_dp)
    direct = links.direct
    rows = tokens.shape[1]
    group = n * rows
    here = lax.axis_index("seq") * n_dp + lax.axis_index("dp")
    me = here if direct else jnp.zeros_like(here)
    s = jnp.asarray(layout.block)[here]
    mine = dict(zip(NAMES, weights))
    if direct:
        mine["small"] = small_block([mine[k] for k in SMALL], 1)
    else:
        small = [lax.all_gather(mine[k], AXES, axis=0, tiled=True) for k in SMALL]
        mine["small"] = small_block(small, BLOCKS).reshape(links.count, -1, PACK)[here]

    tokens = tokens[0]
    digits = jnp.where(
        lax.broadcasted_iota(jnp.int32, (RIM, D), 1) < LANES,
        first_length[0] // LANES,
        first_length[0] % LANES,
    )
    sent = jnp.concatenate([tokens, digits.astype(BF)], axis=0)
    if direct:
        blocks = pack({k: mine[k] for k in mine if k not in SMALL})
        sent, blocks = sync(sent, blocks)
        held1 = links.near(blocks[0])
    x = layout.bring(sent)
    if direct:
        held1 = links.spread(links.part(0, *sync(held1)), 0)
    low = layout.bring_to(tokens[-RIM:], 1)
    high = layout.bring_to(tokens[:RIM], -1)
    if direct:
        held1, x, low, high, blocks = sync(held1, x, low, high, blocks)
        held1 = links.spread(held1, 1)
        held2 = links.near(blocks[1])
    digits = x[rows, 0 : 2 * LANES : LANES].astype(F32).astype(jnp.int32)
    first = digits[0] * LANES + digits[1]
    scal = jnp.stack([s.astype(jnp.int32), first, me.astype(jnp.int32)])
    x_ext = jnp.concatenate([low, x[:rows], high], axis=0)
    if direct:
        held1, held2, scal, x_ext = sync(held1, held2, scal, x_ext)
        pieces1 = links.across(held1)
        held2 = links.spread(links.part(1, held2), 0)
        pieces1, held2 = sync(pieces1, held2)
        held2 = links.spread(held2, 1)
    else:
        pieces1, pieces2, pieces3 = (links.gather_whole(k, mine) for k in range(3))
    h1, y2, joined, *rest = front1(scal, x_ext, pieces1)
    (glu, wide, narrow), (g1, g2, g3, g4, g5, taps) = rest[:3], rest[3:]
    if direct:
        y2, held2, blocks = sync(y2, held2, blocks)
        pieces2 = links.across(held2)
        held3 = links.near(blocks[2])
    left, right, mid = front2(scal, y2, g3, wide, narrow, group)
    if direct:
        mid, pieces2, held3 = sync(mid, pieces2, held3)
        held3 = links.spread(links.part(2, held3), 0)
    spread, h2, y4, *rest = front3(scal, mid, taps, h1, g4, pieces2, n, share)
    qkv, (qkv_w, point) = rest[:n], rest[n:]
    if direct:
        qkv, held3 = sync(qkv, held3)
    qkv = layout.swap(qkv)
    qkv, cot = sync(qkv, cotangent[0])
    cot = layout.bring(cot)
    if direct:
        held3, qkv = sync(held3, qkv)
        held3 = links.spread(held3, 1)
    *att, lse = attend(scal, qkv, n, share)
    if direct:
        att, held3, cot = sync(att, held3, cot)
        pieces3 = links.across(held3)
    else:
        att, cot = sync(att, cot)
    arrived = layout.swap(att)
    mixed, dh3, *rest = middle(scal, h2, arrived, cot, g5, pieces3, n, share)
    datt, (att_all, y5, inner, du, ln5) = rest[:n], rest[n:]
    datt, du = sync(datt, du)
    datt = layout.swap(datt)
    sum0 = weigh0(scal, att_all, y5, inner, du, cot, dh3)
    datt, sum0 = sync(datt, sum0)
    if direct:
        sum0 = links.cores(*sum0)
    dqkv = attend_back(scal, qkv, att, datt, lse, n, share)
    dqkv, sum0 = sync(dqkv, sum0)
    dqkv = layout.swap(dqkv)
    if direct:
        sum0 = links.straight(sum0, 0)
        dqkv, sum0 = sync(dqkv, sum0)
        sum0 = links.straight(sum0, 1)
    dh2, db, dqkv, ln4 = back3(scal, dqkv, dh3, h2, g4, qkv_w, n, share)
    db, dqkv = sync(db, dqkv)
    low = layout.to_neighbour(db[-RIM:], 1)
    high = layout.to_neighbour(db[:RIM], -1)
    sum1 = weigh1(scal, y4, dqkv, spread, db)
    low, high, sum1, sum0, mixed = sync(low, high, sum1, sum0, mixed)
    if direct:
        total0 = links.finish([sum0])
        sum1 = links.first(1, *sum1)
    mixed = layout.send_home(mixed)
    dl, st, gdepth, ln3 = back2(scal, low, db, high, taps, mid, left, right, g3, point, group)
    if direct:
        dl, st, total0, sum1, mixed = sync(dl, st, total0, sum1, mixed)
        sum1 = links.next(sum1, 0)
    sum2 = weigh2(scal, dl, st, y2)
    if direct:
        (dl, sum2) = sync(dl, sum2)
        sum2 = links.first(2, *sum2)
    half = rows // 2
    fixed = (scal, dl, st, dh2, h1, joined, x_ext, g1, g2, glu, wide, narrow)
    dx_a, y1_a, dj_a, ln1_a, ln2_a = back1(*fixed, 0, half)
    if direct:
        dx_a, dl, sum1, sum2 = sync(dx_a, dl, sum1, sum2)
        sum1, sum2 = links.next_two(sum1, sum2)
        fixed = (scal, dl, *fixed[2:])
    dx_a = layout.send_home(dx_a)
    dx_b, y1_b, dj_b, ln1_b, ln2_b = back1(*fixed, half, rows - half)
    if direct:
        dx_b, dj_b = sync(dx_b, dj_b)
    dx_b = layout.send_home(dx_b)
    gains = (ln3, ln4, ln5)
    sum3 = weigh3(scal, (y1_a, y1_b), (dj_a, dj_b), (ln1_a, ln1_b), (ln2_a, ln2_b), gains, gdepth)
    if direct:
        sum3, sum2, sum1, dx_a = sync(sum3, sum2, sum1, dx_a)
        sum3 = links.cores(*sum3)
    if direct:
        sum3, sum2 = sync(sum3, sum2)
        sum2, sum3 = links.next_and_plane(sum2, sum3)
        *held, dx_b = sync(*sum2, sum3, dx_b)
        sums = (total0, links.finish([*sum1, *held]))
        tables = (sum(SUMS[0], []), sum([*SUMS[1], *SUMS[2], *SUMS[3]], []))
    else:
        sums = [links.scatter_whole(k, v) for k, v in enumerate((sum0, sum1, sum2, sum3))]
        tables = [sum(items, []) for items in SUMS]
    dx = jnp.concatenate([dx_a, dx_b], axis=0)
    out = {}
    for items, total in zip(tables, sums):
        out.update(links.rows_of(items, total))
    flat = out.pop("small")
    if not direct:
        flat = lax.all_gather(flat, AXES, axis=0, tiled=True)
    flat = flat.reshape(-1, 16 * PACK)
    sizes = [width for _, width in GAINS] + [TAP_RUN]
    at = 0
    for name, size in zip(SMALL, sizes):
        part = flat[:, at : at + size].reshape(-1)
        at += size
        if not direct:
            own = mine[name].shape[0]
            part = lax.dynamic_slice(part, (here * own,), (own,))
        out[name] = part
    return (mixed[None], dx.astype(F32)[None], *(out[name] for name in NAMES))


def solution(mesh):
    token, owner, rows = P("dp", "seq", None), P(AXES), P(AXES, None)
    params = (owner,) * 5 + (rows,) * 3 + (owner,) + (rows,) * 5
    return jax.shard_map(
        on_device,
        mesh=mesh,
        in_specs=(token, token, P("dp")) + params,
        out_specs=(token, token) + params,
        check_vma=False,
    )
```
